128 devices in a mesh: seq: 64 (over x, y, z_hi, core), ch: 2 (over z_lo).
Axes of the slice: x: 4, y: 4, z: 4 (z_hi: 2, z_lo: 2; z = z_hi * 2 + z_lo), core: 2. Of those that a mesh axis runs over, the one named last changes fastest.
Arguments:
- inputs: bfloat16 [64, 2048, 652], P('seq', None, 'ch'), may hold values from -6 to 6
- offsets: int32 [64], P('seq'), may hold values from 0 to 683, as said below
- owners: int32 [64], replicated, may hold values from 0 to 63, each once
- cotangent: bfloat16 [64, 1024, 768], P('seq', None, 'ch'), may hold values from -6 to 6
- norm1_gain: float32 [652], P('ch'), may hold values from 0.5 to 1.5
- norm1_bias: float32 [652], P('ch'), may hold values from -4 to 4
- norm1_moments: float32 [2, 2, 652], P(None, None, 'ch'), as said below
- norm2_gain: float32 [768], P('ch'), may hold values from 0.5 to 1.5
- norm2_bias: float32 [768], P('ch'), may hold values from -4 to 4
- norm2_moments: float32 [2, 2, 768], P(None, None, 'ch'), as said below
- norm3_gain: float32 [384], P('ch'), may hold values from 0.5 to 1.5
- norm3_bias: float32 [384], P('ch'), may hold values from -4 to 4
- norm3_moments: float32 [2, 2, 384], P(None, None, 'ch'), as said below
- conv1_copy: bfloat16 [5, 652, 768], P(None, None, 'ch'), may hold values from -0.109375 to 0.109375
- conv1_master: float32 [5, 652, 768], P(None, None, ('seq', 'ch')), may hold values from -0.109375 to 0.109375
- conv1_first: float32 [5, 652, 768], P(None, None, ('seq', 'ch')), may hold values from -96 to 96
- conv1_second: float32 [5, 652, 768], P(None, None, ('seq', 'ch')), may hold values from 622.592 to 4980.736
- conv1_average: float32 [5, 652, 768], P(None, None, ('seq', 'ch')), may hold values from -0.109375 to 0.109375
- basis1: float32 [652, 652], replicated, as said below
- conv2_copy: bfloat16 [3, 768, 384], P(None, None, 'ch'), may hold values from -0.125 to 0.125
- conv2_master: float32 [3, 768, 384], P(None, None, ('seq', 'ch')), may hold values from -0.125 to 0.125
- conv2_first: float32 [3, 768, 384], P(None, None, ('seq', 'ch')), may hold values from -96 to 96
- conv2_second: float32 [3, 768, 384], P(None, None, ('seq', 'ch')), may hold values from 622.592 to 4980.736
- conv2_average: float32 [3, 768, 384], P(None, None, ('seq', 'ch')), may hold values from -0.125 to 0.125
- basis2: float32 [768, 768], replicated, as said below
- project_copy: bfloat16 [768, 384], P(None, 'ch'), may hold values from -0.3125 to 0.3125
- project_master: float32 [768, 384], P(None, ('seq', 'ch')), may hold values from -0.3125 to 0.3125
- project_first: float32 [768, 384], P(None, ('seq', 'ch')), may hold values from -96 to 96
- project_second: float32 [768, 384], P(None, ('seq', 'ch')), may hold values from 622.592 to 4980.736
- project_average: float32 [768, 384], P(None, ('seq', 'ch')), may hold values from -0.3125 to 0.3125
- basis3: float32 [768, 768], replicated, as said below
Outputs:
- output: bfloat16 [64, 1024, 768], P('seq', None, 'ch')
- input_grad: float32 [64, 2048, 652], P('seq', None, 'ch')
- norm1_new_values: float32 [2, 652], P(None, 'ch')
- norm1_new_first: float32 [2, 652], P(None, 'ch')
- norm1_new_second: float32 [2, 652], P(None, 'ch')
- norm2_new_values: float32 [2, 768], P(None, 'ch')
- norm2_new_first: float32 [2, 768], P(None, 'ch')
- norm2_new_second: float32 [2, 768], P(None, 'ch')
- norm3_new_values: float32 [2, 384], P(None, 'ch')
- norm3_new_first: float32 [2, 384], P(None, 'ch')
- norm3_new_second: float32 [2, 384], P(None, 'ch')
- conv1_new_master: float32 [5, 652, 768], P(None, None, ('seq', 'ch'))
- conv1_new_copy: bfloat16 [5, 652, 768], P(None, None, 'ch')
- conv1_new_first: float32 [5, 652, 768], P(None, None, ('seq', 'ch'))
- conv1_new_second: float32 [5, 652, 768], P(None, None, ('seq', 'ch'))
- conv1_new_average: float32 [5, 652, 768], P(None, None, ('seq', 'ch'))
- conv2_new_master: float32 [3, 768, 384], P(None, None, ('seq', 'ch'))
- conv2_new_copy: bfloat16 [3, 768, 384], P(None, None, 'ch')
- conv2_new_first: float32 [3, 768, 384], P(None, None, ('seq', 'ch'))
- conv2_new_second: float32 [3, 768, 384], P(None, None, ('seq', 'ch'))
- conv2_new_average: float32 [3, 768, 384], P(None, None, ('seq', 'ch'))
- project_new_master: float32 [768, 384], P(None, ('seq', 'ch'))
- project_new_copy: bfloat16 [768, 384], P(None, 'ch')
- project_new_first: float32 [768, 384], P(None, ('seq', 'ch'))
- project_new_second: float32 [768, 384], P(None, ('seq', 'ch'))
- project_new_average: float32 [768, 384], P(None, ('seq', 'ch'))
The draws below stay inside these ranges and needn't reach their ends.
Inputs may be any that keep to these rules, and one draw needn't show every extreme that they name: offsets[s] counts the leading padded bins of sequence s; one sequence has none and at least one has 683. `owners`: a permutation of the indices along seq. `basis1`: orthogonal. `basis2`: orthogonal. `basis3`: orthogonal. `norm1_moments`: second moments positive. `norm2_moments`: second moments positive. `norm3_moments`: second moments positive.
All inputs are finite; a program needn't handle non-finite values.
Results may differ from the reference program's by a relative error of at most 0.017.
Values may be sent and summed in bfloat16 or wider, within the bound.
A program may use at most 192 MiB of HBM per device.

```python
import math
import jax
import jax.numpy as jnp
from jax import lax

C0 = 652
C1 = 768
H = 384
LEN = 1024
STEP = 8
SEQS = 64
TOKENS = 65536
N_SEQ = 64
N_CH = 2


def draw_offsets(key, part):
    key = jax.random.fold_in(key, 11)
    seq_index = jnp.arange(SEQS, dtype=jnp.int32)
    shortest = LEN // 3
    valid_bins = shortest + (LEN - shortest) * seq_index // (SEQS - 1)
    jitter = jax.random.randint(key, (SEQS,), 0, LEN // 8 + 1)
    interior = (seq_index > 0) & (seq_index < SEQS - 1)
    valid_bins = jnp.where(interior, jnp.maximum(valid_bins - jitter, shortest), valid_bins)
    return (LEN - valid_bins).astype(jnp.int32)


def cosine_basis(key, dimension):
    columns = jax.random.permutation(key, dimension)
    flips = jnp.where(jax.random.bernoulli(jax.random.fold_in(key, 1), 0.5, (dimension,)), 1.0, -1.0)
    row_index = jnp.arange(dimension, dtype=jnp.float32)[:, None]
    frequency = columns.astype(jnp.float32)[None, :]
    scales = jnp.where(frequency == 0.0, math.sqrt(1.0 / dimension), math.sqrt(2.0 / dimension))
    values = scales * flips[None, :] * jnp.cos(math.pi * (2.0 * row_index + 1.0) * frequency / (2.0 * dimension))
    return values.astype(jnp.float32)


def draw_basis1(key, part):
    key = jax.random.fold_in(key, 21)
    return cosine_basis(key, C0)


def draw_basis2(key, part):
    key = jax.random.fold_in(key, 22)
    return cosine_basis(key, C1)


def draw_basis3(key, part):
    key = jax.random.fold_in(key, 23)
    return cosine_basis(key, C1)


def norm_moment_draw(key, channels):
    typical = 0.5 * math.sqrt(1.0 * TOKENS)
    first_part = jax.random.normal(jax.random.fold_in(key, 1), (2, channels), jnp.float32) * (0.111 * typical)
    exponent = jax.random.uniform(jax.random.fold_in(key, 2), (2, channels), jnp.float32, math.log(0.5 * 0.0526), math.log(4.0 * 0.0526))
    second_part = typical * typical * jnp.exp(exponent)
    return jnp.stack([first_part, second_part]).astype(jnp.float32)


def draw_norm1_moments(key, part):
    key = jax.random.fold_in(key, 31)
    return norm_moment_draw(key, C0)


def draw_norm2_moments(key, part):
    key = jax.random.fold_in(key, 32)
    return norm_moment_draw(key, C1)


def draw_norm3_moments(key, part):
    key = jax.random.fold_in(key, 33)
    return norm_moment_draw(key, H)


def level_of(own_key, extent, cuts, least, top_value):
    loudness = 1.0
    for position, shards_of in cuts:
        steps = jax.random.uniform(jax.random.fold_in(jax.random.fold_in(own_key, 6), position), (shards_of,), jnp.float32, least / len(cuts), top_value / len(cuts))
        loudness = loudness * jnp.repeat(jnp.exp(steps), extent[position] // shards_of).reshape((-1,) + (1,) * (len(extent) - 1 - position))
    return loudness


def scatter_about(key, shape, scale, bound, cuts=(), held_as=jnp.bfloat16):
    array = jax.random.normal(key, shape, jnp.float32) * scale
    if len(cuts) > 0:
        array = level_of(key, shape, cuts, -0.22, 0.18) * array
    return jnp.clip(array, min=-bound, max=bound).astype(held_as)


def setup_inputs(seed: int = 0) -> dict:
    keys = jax.random.split(jax.random.key(seed), 32)
    return {
        "inputs": scatter_about(keys[0], (SEQS, 2 * LEN, C0), 1.0, 6.0, ((0, 64), (2, 2))),
        "offsets": draw_offsets(jax.random.fold_in(keys[31], 71), 0),
        "owners": jax.random.permutation(keys[2], N_SEQ).astype(jnp.int32),
        "cotangent": scatter_about(keys[3], (SEQS, LEN, C1), 1.0, 6.0, ((0, 64), (2, 2))),
        "norm1_gain": jnp.clip(1.0 + 0.1 * jax.random.normal(keys[4], (C0,), jnp.float32), 0.5, 1.5),
        "norm1_bias": scatter_about(keys[5], (C0,), 0.3, 4.0, ((0, 2),), jnp.float32),
        "norm1_moments": draw_norm1_moments(jax.random.fold_in(keys[31], 71), 0),
        "norm2_gain": jnp.clip(1.0 + 0.1 * jax.random.normal(keys[7], (C1,), jnp.float32), 0.5, 1.5),
        "norm2_bias": scatter_about(keys[8], (C1,), 0.3, 4.0, ((0, 2),), jnp.float32),
        "norm2_moments": draw_norm2_moments(jax.random.fold_in(keys[31], 71), 0),
        "norm3_gain": jnp.clip(1.0 + 0.1 * jax.random.normal(keys[10], (H,), jnp.float32), 0.5, 1.5),
        "norm3_bias": scatter_about(keys[11], (H,), 0.3, 4.0, ((0, 2),), jnp.float32),
        "norm3_moments": draw_norm3_moments(jax.random.fold_in(keys[31], 71), 0),
        "conv1_copy": scatter_about(keys[13], (5, C0, C1), (5 * C0) ** -0.5, 0.109375, ((2, 2),)),
        "conv1_master": scatter_about(keys[14], (5, C0, C1), (5 * C0) ** -0.5, 0.109375, ((2, 128),), jnp.float32),
        "conv1_first": scatter_about(keys[15], (5, C0, C1), (0.067 * TOKENS ** 0.5), 96.0, ((2, 128),), jnp.float32),
        "conv1_second": jnp.clip(jnp.exp(math.log(4980.736) - 2.0794415 * jax.random.uniform(keys[16], (5, C0, C1), jnp.float32) ** level_of(keys[16], (5, C0, C1), ((2, 128),), -0.2, 0.2)), 622.592, 4980.736),
        "conv1_average": scatter_about(keys[17], (5, C0, C1), (5 * C0) ** -0.5, 0.109375, ((2, 128),), jnp.float32),
        "basis1": draw_basis1(jax.random.fold_in(keys[31], 71), 0),
        "conv2_copy": scatter_about(keys[19], (3, C1, H), (3 * C1) ** -0.5, 0.125, ((2, 2),)),
        "conv2_master": scatter_about(keys[20], (3, C1, H), (3 * C1) ** -0.5, 0.125, ((2, 128),), jnp.float32),
        "conv2_first": scatter_about(keys[21], (3, C1, H), (0.067 * TOKENS ** 0.5), 96.0, ((2, 128),), jnp.float32),
        "conv2_second": jnp.clip(jnp.exp(math.log(4980.736) - 2.0794415 * jax.random.uniform(keys[22], (3, C1, H), jnp.float32) ** level_of(keys[22], (3, C1, H), ((2, 128),), -0.2, 0.2)), 622.592, 4980.736),
        "conv2_average": scatter_about(keys[23], (3, C1, H), (3 * C1) ** -0.5, 0.125, ((2, 128),), jnp.float32),
        "basis2": draw_basis2(jax.random.fold_in(keys[31], 71), 0),
        "project_copy": scatter_about(keys[25], (C1, H), H ** -0.5, 0.3125, ((1, 2),)),
        "project_master": scatter_about(keys[26], (C1, H), H ** -0.5, 0.3125, ((1, 128),), jnp.float32),
        "project_first": scatter_about(keys[27], (C1, H), (0.067 * TOKENS ** 0.5), 96.0, ((1, 128),), jnp.float32),
        "project_second": jnp.clip(jnp.exp(math.log(4980.736) - 2.0794415 * jax.random.uniform(keys[28], (C1, H), jnp.float32) ** level_of(keys[28], (C1, H), ((1, 128),), -0.2, 0.2)), 622.592, 4980.736),
        "project_average": scatter_about(keys[29], (C1, H), H ** -0.5, 0.3125, ((1, 128),), jnp.float32),
        "basis3": draw_basis3(jax.random.fold_in(keys[31], 71), 0),
    }


@jax.custom_vjp
def low(v):
    return lax.optimization_barrier(v.astype(jnp.bfloat16)).astype(jnp.float32)

@jax.custom_vjp
def low_back(v):
    return v

def low_keep(v):
    return (low(v), None)

def low_pass(kept, grad):
    return (grad,)

def back_keep(v):
    return (v, None)

def back_low(kept, grad):
    return (low(grad),)
low.defvjp(low_keep, low_pass)
low_back.defvjp(back_keep, back_low)
highest = lax.Precision.HIGHEST
eps_norm = 1e-05
beta_one = 0.9
beta_two = 0.95
adam_eps = 1e-08
decay_rate = 0.01
average_rate = 0.9
norm_rate = 0.05

def batch_norm(values, validity, population, gain_values, bias_values):
    center = lax.optimization_barrier(jnp.sum(values * validity, axis=(0, 1))) / population
    spread = lax.optimization_barrier(jnp.sum(validity * (values - center) ** 2, axis=(0, 1))) / population
    scaled = (values - center) * lax.rsqrt(spread + eps_norm)
    return jax.nn.gelu(scaled * gain_values + bias_values) * validity

def convolve(values, weight):
    taps_count = weight.shape[0]
    margin = (taps_count - 1) // 2
    length = values.shape[1]
    padded = jnp.pad(values, ((0, 0), (margin, margin), (0, 0)))
    summed = jnp.zeros(values.shape[:2] + (weight.shape[2],), jnp.float32)
    for tap_index in range(taps_count):
        summed = summed + jnp.einsum('spi,io->spo', padded[:, tap_index:tap_index + length], weight[tap_index], precision=highest)
    return summed

def forward(inputs, norm1_gain, norm1_bias, norm2_gain, norm2_bias, norm3_gain, norm3_bias, conv1_copy, conv2_copy, project_copy, in_valid, bin_valid, bin_count):
    normed_in = low(batch_norm(inputs, in_valid, 2.0 * bin_count, norm1_gain, norm1_bias))
    hidden1 = low_back(convolve(normed_in, conv1_copy))
    paired = hidden1.reshape(hidden1.shape[0], hidden1.shape[1] // 2, 2, hidden1.shape[2])
    pooled = jax.nn.logsumexp(paired, axis=2) - math.log(2.0)
    normed_mid = low(batch_norm(pooled, bin_valid, bin_count, norm2_gain, norm2_bias))
    hidden2 = low_back(convolve(normed_mid, conv2_copy))
    normed_out = low(batch_norm(hidden2, bin_valid, bin_count, norm3_gain, norm3_bias))
    branch = jnp.einsum('sph,oh->spo', normed_out, project_copy, precision=highest)
    return pooled + branch

def to_slots(matrix, owners):
    leading = matrix.shape[:-1]
    block_width = matrix.shape[-1] // (N_SEQ * N_CH)
    blocks = matrix.reshape(leading + (N_CH, N_SEQ, block_width))
    blocks = jnp.take(blocks, owners, axis=len(leading) + 1)
    blocks = jnp.swapaxes(blocks, len(leading), len(leading) + 1)
    return blocks.reshape(matrix.shape)

def from_slots(matrix, owners):
    leading = matrix.shape[:-1]
    block_width = matrix.shape[-1] // (N_SEQ * N_CH)
    inverse = jnp.argsort(owners).astype(jnp.int32)
    blocks = matrix.reshape(leading + (N_SEQ, N_CH, block_width))
    blocks = jnp.swapaxes(blocks, len(leading), len(leading) + 1)
    blocks = jnp.take(blocks, inverse, axis=len(leading) + 1)
    return blocks.reshape(matrix.shape)

def rotated_adam(gradient, master, first_moment, second, average, rotation, step_rate):
    turned = jnp.einsum('ij,...iw->...jw', rotation, gradient, precision=highest)
    first_new = beta_one * first_moment + (1.0 - beta_one) * turned
    second_new = beta_two * second + (1.0 - beta_two) * turned * turned
    direction = first_new / (1.0 - beta_one ** STEP) / (jnp.sqrt(second_new / (1.0 - beta_two ** STEP)) + adam_eps)
    update = jnp.einsum('ij,...jw->...iw', rotation, direction, precision=highest)
    master_new = master - step_rate * (update + decay_rate * master)
    average_new = average_rate * average + (1.0 - average_rate) * master_new
    return (master_new, first_new, second_new, average_new)

def norm_adam(gradient, parameters, moments):
    first_new = beta_one * moments[0] + (1.0 - beta_one) * gradient
    second_new = beta_two * moments[1] + (1.0 - beta_two) * gradient * gradient
    direction = first_new / (1.0 - beta_one ** STEP) / (jnp.sqrt(second_new / (1.0 - beta_two ** STEP)) + adam_eps)
    return (parameters - norm_rate * direction, first_new, second_new)

def reference(inputs, offsets, owners, cotangent, norm1_gain, norm1_bias, norm1_moments, norm2_gain, norm2_bias, norm2_moments, norm3_gain, norm3_bias, norm3_moments, conv1_copy, conv1_master, conv1_first, conv1_second, conv1_average, basis1, conv2_copy, conv2_master, conv2_first, conv2_second, conv2_average, basis2, project_copy, project_master, project_first, project_second, project_average, basis3):
    positions = jnp.arange(LEN, dtype=jnp.int32)
    bin_valid = (positions[None, :] >= offsets[:, None]).astype(jnp.float32)[:, :, None]
    in_valid = jnp.repeat(bin_valid, 2, axis=1)
    bin_count = jnp.sum(bin_valid)
    primals = (inputs.astype(jnp.float32), norm1_gain, norm1_bias, norm2_gain, norm2_bias, norm3_gain, norm3_bias, conv1_copy.astype(jnp.float32), conv2_copy.astype(jnp.float32), project_copy.astype(jnp.float32))

    def closed(*weights):
        return forward(*weights, in_valid, bin_valid, bin_count)
    block_out, pullback = jax.vjp(closed, *primals)
    gradients = pullback(cotangent.astype(jnp.float32))
    norm1_state = norm_adam(jnp.stack([gradients[1], gradients[2]]), jnp.stack([norm1_gain, norm1_bias]), norm1_moments)
    norm2_state = norm_adam(jnp.stack([gradients[3], gradients[4]]), jnp.stack([norm2_gain, norm2_bias]), norm2_moments)
    norm3_state = norm_adam(jnp.stack([gradients[5], gradients[6]]), jnp.stack([norm3_gain, norm3_bias]), norm3_moments)
    first_result = rotated_adam(to_slots(gradients[7], owners), conv1_master, conv1_first, conv1_second, conv1_average, basis1, 0.02)
    second_result = rotated_adam(to_slots(gradients[8], owners), conv2_master, conv2_first, conv2_second, conv2_average, basis2, 0.02)
    third_result = rotated_adam(to_slots(gradients[9], owners), project_master, project_first, project_second, project_average, basis3, 0.05)
    return (block_out.astype(jnp.bfloat16), gradients[0], norm1_state[0], norm1_state[1], norm1_state[2], norm2_state[0], norm2_state[1], norm2_state[2], norm3_state[0], norm3_state[1], norm3_state[2], first_result[0], from_slots(first_result[0], owners).astype(jnp.bfloat16), first_result[1], first_result[2], first_result[3], second_result[0], from_slots(second_result[0], owners).astype(jnp.bfloat16), second_result[1], second_result[2], second_result[3], third_result[0], from_slots(third_result[0], owners).astype(jnp.bfloat16), third_result[1], third_result[2], third_result[3])
```

```python
import math

import jax
import jax.numpy as jnp
import numpy as np
from jax import lax
from jax.experimental import pallas as pl
from jax.experimental.pallas import tpu as pltpu
from jax.sharding import Mesh
from jax.sharding import PartitionSpec as P

STEP = 8
SEQ = ("seq_0", "seq_1", "seq_2", "seq_3")
SEQ_CH = ("seq_0", "seq_1", "seq_2", "seq_3", "ch")
MESH = pl.DeviceIdType.MESH
bf16 = jnp.bfloat16
f32 = jnp.float32

eps_norm = 1e-05
beta_one = 0.9
beta_two = 0.95
adam_eps = 1e-08
decay_rate = 0.01
average_rate = 0.9
norm_rate = 0.05

C0, C1, H = 652, 768, 384
HALF0, HALF1, HALFH = 326, 384, 192
BINS = 1024
OWN = 512
WIN = 528
LANES = 1152
PAD = 768

GELU_K = math.sqrt(2.0 / math.pi)
GELU_C = 0.044715


def gelu(v):
    return 0.5 * v * (1.0 + jnp.tanh(GELU_K * (v + GELU_C * (v * v * v))))


def gelu_slope(v):
    square = v * v
    t = jnp.tanh(GELU_K * v * (1.0 + GELU_C * square))
    return 0.5 * (1.0 + t) + 0.5 * GELU_K * v * (1.0 - t * t) * (1.0 + 3.0 * GELU_C * square)


def dot(a, b, dims=((1,), (0,))):
    return lax.dot_general(a, b, (dims, ((), ())), preferred_element_type=f32)


def iota(shape, dim):
    return lax.broadcasted_iota(jnp.int32, shape, dim)


class Place:
    def __init__(self):
        self.x, self.y, self.zh, self.c, self.zl = [lax.axis_index(n) for n in SEQ_CH]
        self.z = 2 * self.zh + self.zl
        self.e = 2 * self.z + self.c
        self.g = 4 * self.x + self.y

    def at(self, **other):
        v = {"x": self.x, "y": self.y, "z": self.z, "c": self.c}
        v.update(other)
        z = v["z"]
        return (v["x"], v["y"], lax.div(z, 2), v["c"], lax.rem(z, 2))


def remote(src, dst, send, recv, device):
    return pltpu.make_async_remote_copy(
        src_ref=src, dst_ref=dst, send_sem=send, recv_sem=recv, device_id=device, device_id_type=MESH
    )


def column_peers(p):
    out = []
    for k in range(1, 8):
        z = lax.rem(p.z + k // 2, 4)
        c = lax.rem(p.c + k % 2, 2)
        out.append((p.at(z=z, c=c), z, c))
    return out


def plane_peers(p):
    out = []
    for k in range(1, 16):
        x = lax.rem(p.x + k // 4, 4)
        y = lax.rem(p.y + k % 4, 4)
        out.append((p.at(x=x, y=y), x, y))
    return out


class Total:
    def __init__(self, p, bufs, sems):
        self.p = p
        self.b1, self.b2 = bufs
        self.s1, self.r1, self.s2, self.r2 = sems

    def start(self, value):
        p = self.p
        self.b1[p.e] = value
        self.c1 = []
        for k, (device, _, _) in enumerate(column_peers(p)):
            cp = remote(self.b1.at[p.e], self.b1.at[p.e], self.s1.at[k], self.r1.at[p.e], device)
            cp.start()
            self.c1.append(cp)

    def middle(self):
        p = self.p
        for device, z, c in column_peers(p):
            e = 2 * z + c
            remote(self.b1.at[e], self.b1.at[e], self.s1.at[0], self.r1.at[e], device).wait_recv()
        total = self.b1[0]
        for k in range(1, 8):
            total = total + self.b1[k]
        for cp in self.c1:
            cp.wait_send()
        self.b2[p.g] = total
        self.c2 = []
        for k, (device, _, _) in enumerate(plane_peers(p)):
            cp = remote(self.b2.at[p.g], self.b2.at[p.g], self.s2.at[k], self.r2.at[p.g], device)
            cp.start()
            self.c2.append(cp)

    def end(self):
        p = self.p
        for device, x, y in plane_peers(p):
            g = 4 * x + y
            remote(self.b2.at[g], self.b2.at[g], self.s2.at[0], self.r2.at[g], device).wait_recv()
        total = self.b2[0]
        for k in range(1, 16):
            total = total + self.b2[k]
        for cp in self.c2:
            cp.wait_send()
        return total


TAP_CORE = (0, 0, 1, 1, 0)
UNIT_CORE = (0, 1, 0, 1)


def step_kernel(
    xt, offs, cot, w1, w2, wp, pvec, owners_row, e1, bw1, e2, bw2,
    out, gin, s1, s2, stats,
    xw, raw, aa, ww1, ww2, wwp, pooled, diff, cc, mm, hid, og, no, hh, mid, gg, gp, perm,
    slope, sl_send, sl_home, ob, small, offw, acc, tr,
    a1a, a1b, ab1, ab2,
    ss, rs, ls, as1, ar1, as2, ar2,
):
    p = Place()
    c, zl = p.c, p.zl
    flip = p.at(z=3 - p.z)
    direct = p.at(z=p.z + 1 - 2 * zl)
    other_core = p.at(c=1 - c)

    bar = pltpu.get_barrier_semaphore()
    for device, _, _ in column_peers(p):
        pl.semaphore_signal(bar, inc=1, device_id=device, device_id_type=MESH)
    for device, _, _ in plane_peers(p):
        pl.semaphore_signal(bar, inc=1, device_id=device, device_id_type=MESH)

    own_w = [
        pltpu.make_async_copy(w1, ww1.at[:, :, pl.ds(pl.multiple_of(384 * zl, 128), 384)], ls.at[0]),
        pltpu.make_async_copy(w2, ww2.at[:, pl.ds(pl.multiple_of(192 * zl, 16), 192), :], ls.at[1]),
        pltpu.make_async_copy(wp, wwp.at[pl.ds(pl.multiple_of(192 * zl, 16), 192), :], ls.at[2]),
    ]
    for cp in own_w:
        cp.start()

    pl.semaphore_wait(bar, 22)

    is_self = c == zl
    not_self = c != zl
    home_chip = 2 * p.zh + c

    def window(j):
        return xt.at[:, pl.ds(pl.multiple_of(896 * j, 128), LANES)]

    def cot_window(j):
        return cot.at[pl.ds(pl.multiple_of(496 * j, 16), WIN), :]

    cc_mine = cc.at[:, pl.ds(pl.multiple_of(384 * zl, 128), 384)]
    x_a = remote(window(c), xw.at[zl], ss.at[0], rs.at[0 + zl], p.at(z=home_chip, c=c))
    x_b = remote(window(1 - c), xw.at[zl], ss.at[1], rs.at[0 + zl], p.at(z=home_chip, c=1 - c))
    c_a = remote(cot_window(c), cc_mine, ss.at[2], rs.at[2 + zl], p.at(z=home_chip, c=c))
    c_b = remote(cot_window(1 - c), cc_mine, ss.at[3], rs.at[2 + zl], p.at(z=home_chip, c=1 - c))
    o_a = remote(offs, offw, ss.at[4], rs.at[4], other_core)

    @pl.when(not_self)
    def _():
        x_a.start()

    @pl.when(is_self)
    def _():
        pltpu.make_async_copy(window(c), xw.at[zl], rs.at[0 + zl]).start()

    x_b.start()
    o_a.start()

    my_lanes = pl.ds(pl.multiple_of(384 * zl, 128), 384)
    its_lanes = pl.ds(pl.multiple_of(384 - 384 * zl, 128), 384)
    my_rows = pl.ds(pl.multiple_of(192 * zl, 16), 192)
    its_rows = pl.ds(pl.multiple_of(192 - 192 * zl, 16), 192)

    def tap_over(t):
        to = direct if t == 4 else flip
        return remote(w1.at[t], ww1.at[t, :, my_lanes], ss.at[5 + t], rs.at[5 + t], to)

    def tap_here(t):
        return remote(
            ww1.at[t, :, its_lanes], ww1.at[t, :, its_lanes], ss.at[10 + t], rs.at[10 + t], other_core
        )

    def unit_ref(u, rows):
        return ww2.at[u, rows, :] if u < 3 else wwp.at[rows, :]

    def unit_over(u):
        return remote(
            w2.at[u] if u < 3 else wp, unit_ref(u, my_rows), ss.at[15 + u], rs.at[15 + u], flip
        )

    def unit_here(u):
        return remote(
            unit_ref(u, its_rows), unit_ref(u, its_rows), ss.at[19 + u], rs.at[19 + u], other_core
        )

    for t in range(5):
        pl.when(c == TAP_CORE[t])(lambda t=t: tap_over(t).start())

    @pl.when(not_self)
    def _():
        c_a.start()

    @pl.when(is_self)
    def _():
        pltpu.make_async_copy(cot_window(c), cc_mine, rs.at[2 + zl]).start()

    c_b.start()
    for u in range(4):
        pl.when(c == UNIT_CORE[u])(lambda u=u: unit_over(u).start())

    off_home = offs[0:1, 0:1]
    total_s = jnp.zeros((8, HALF0), f32)
    total_q = jnp.zeros((8, HALF0), f32)
    for k in range(8):
        lanes = pl.ds(256 * k, 256)
        mask = ((iota((8, 256), 1) + 256 * k).astype(f32) >= 2.0 * off_home).astype(bf16)
        xb = xt[:, lanes]
        xf = xb.astype(f32)
        sq = xf * xf
        hi = sq.astype(bf16)
        lo = (sq - hi.astype(f32)).astype(bf16)
        nt = ((1,), (1,))
        total_s = total_s + dot(mask, xb, nt)
        total_q = total_q + (dot(mask, hi, nt) + dot(mask, lo, nt))
    small[...] = jnp.zeros_like(small)
    small[0:1, 0:HALF0] = total_s[0:1]
    small[1:2, 0:HALF0] = total_q[0:1]
    here = small[...]
    here = jnp.where(zl == 0, here, pltpu.roll(here, HALF0, 1))
    count = jnp.maximum(BINS - off_home, 0.0)
    lane8 = iota((8, PAD), 1)
    row8 = iota((8, PAD), 0)
    here = here + jnp.where((lane8 == PAD - 1) & (row8 == 0), count, 0.0)
    t1 = Total(p, (a1a, a1b), (as1.at[0], ar1.at[0], as2.at[0], ar2.at[0]))
    t1.start(here + pvec[...])
    t1.middle()

    nat1 = dot(owners_row[...], e1[...])[0:1] * 6.0 + bw1[0:1]
    nat2 = dot(owners_row[...], e2[...])[0:1] * 3.0 + bw2[0:1]
    for k in range(6):
        perm[pl.ds(128 * k, 128), :] = (
            (iota((128, PAD), 0) + 128 * k).astype(f32) == nat1
        ).astype(bf16)
    perm2 = (iota((H, H), 0).astype(f32) == nat2).astype(bf16)

    row = iota((128, 128), 0)
    pick = (iota((128, 128), 1) == jnp.where(row < 64, 2 * row, 2 * row - 127)).astype(bf16)
    for k in range(2):
        remote(xw.at[k], xw.at[k], ss.at[0], rs.at[0 + k], other_core).wait_recv()
    tr[...] = jnp.zeros_like(tr)
    for k in range(9):
        lanes = pl.ds(128 * k, 128)
        tr[0, :, 0:HALF0] = dot(pick, xw[0, :, lanes], ((1,), (1,)))
        tr[1, :, 0:HALF0] = dot(pick, xw[1, :, lanes], ((1,), (1,)))
        both = (tr[0] + pltpu.roll(tr[1], HALF0, 1)).astype(bf16)
        raw[0, pl.ds(64 * k, 64), :] = both[0:64]
        raw[1, pl.ds(64 * k, 64), :] = both[64:128]

    first = t1.end()
    n1 = first[0:1, PAD - 1 : PAD]
    n2 = 0.5 * n1
    inv_n1 = 1.0 / n1
    inv_n2 = 1.0 / n2
    real = iota((1, PAD), 1) < C0
    mean1 = jnp.where(real, first[0:1], 0.0) * inv_n1
    var1 = first[1:2] * inv_n1 - mean1 * mean1
    rs1 = lax.rsqrt(var1 + eps_norm)
    gain1, bias1 = first[2:3], first[3:4]
    gain2, bias2 = first[4:5], first[5:6]
    gain3, bias3 = first[6:7, 0:H], first[6:7, H : 2 * H]

    remote(offs, offw, ss.at[4], rs.at[4], other_core).wait()
    off = jnp.where(is_self, offs[0:1, 0:1], offw[0:1, 0:1])

    bin0 = 496 * c
    own0 = pl.multiple_of(16 * c, 16)
    raw0 = pl.multiple_of(48 * c, 16)
    rawown = pl.multiple_of(64 * c, 16)

    def valid_mask(rows, at=0):
        return ((iota((rows, 1), 0) + (bin0 + at)).astype(f32) >= off).astype(f32)

    def own_mask(rows, at=0):
        r = iota((rows, 1), 0) + at
        return ((r >= 16 * c) & (r < 16 * c + OWN)).astype(f32)

    not_first = (iota((WIN, 1), 0) > 0).astype(f32)
    not_last = (iota((WIN, 1), 0) < WIN - 1).astype(f32)

    def before(v):
        return (pltpu.roll(v, 1, 0) * not_first).astype(bf16)

    def after(v):
        return (pltpu.roll(v, WIN - 1, 0) * not_last).astype(bf16)

    small[0:1] = rs1 * gain1
    small[1:2] = bias1 - mean1 * (rs1 * gain1)
    small[2:3] = mean1
    small[3:4] = rs1

    @pl.loop(0, 6)
    def _(k):
        lanes = pl.ds(pl.multiple_of(128 * k, 128), 128)
        scale, shift = small[0:1, lanes], small[1:2, lanes]
        valid = valid_mask(WIN)
        for par in range(2):
            v = raw[par, pl.ds(raw0, WIN), lanes].astype(f32)
            v = gelu(v * scale + shift) * valid
            aa[par, :, lanes] = before(v)
            aa[2 + par, :, lanes] = v.astype(bf16)
            aa[4 + par, :, lanes] = after(v)

    own_w[0].wait()
    for t in range(5):

        def there(t=t):
            cp = tap_over(t)
            remote(
                ww1.at[t, :, its_lanes], ww1.at[t, :, its_lanes], ss.at[5 + t], rs.at[5 + t], flip
            ).wait_recv()
            tap_here(t).start()
            cp.wait_send()

        pl.when(c == TAP_CORE[t])(there)
    for t in range(5):
        pl.when(c == TAP_CORE[t])(lambda t=t: tap_here(t).wait_send())
        pl.when(c != TAP_CORE[t])(lambda t=t: tap_here(t).wait_recv())

    acc[...] = jnp.zeros_like(acc)

    @pl.loop(0, 3)
    def _(k):
        rows = pl.ds(pl.multiple_of(176 * k, 16), 176)
        h0 = jnp.zeros((176, C1), f32)
        for t in range(5):
            h0 = h0 + dot(aa[t, rows, 0:C0], ww1[t])
        h1 = jnp.zeros((176, C1), f32)
        for t in range(5):
            h1 = h1 + dot(aa[t + 1, rows, 0:C0], ww1[t])
        d = h0 - h1
        v = jnp.maximum(h0, h1) + (jnp.log(1.0 + jnp.exp(-jnp.abs(d))) - math.log(2.0))
        diff[rows, :] = d
        pooled[rows, :] = v
        m = valid_mask(176, 176 * k) * own_mask(176, 176 * k)
        vm = v * m
        acc[0:1] += jnp.sum(vm, axis=0, keepdims=True)
        acc[1:2] += jnp.sum(vm * v, axis=0, keepdims=True)

    t2 = Total(p, (ab1.at[0], ab2.at[0]), (as1.at[1], ar1.at[1], as2.at[1], ar2.at[1]))
    t2.start(acc[0:2])
    t2.middle()
    own_w[1].wait()
    own_w[2].wait()
    for u in range(4):

        def there_u(u=u):
            remote(
                unit_ref(u, its_rows), unit_ref(u, its_rows), ss.at[15 + u], rs.at[15 + u], flip
            ).wait_recv()
            unit_here(u).start()
            unit_over(u).wait_send()

        pl.when(c == UNIT_CORE[u])(there_u)
    for k in range(2):
        part = cc.at[:, pl.ds(384 * k, 384)]
        remote(part, part, ss.at[0], rs.at[2 + k], other_core).wait_recv()
    for u in range(4):
        pl.when(c == UNIT_CORE[u])(lambda u=u: unit_here(u).wait_send())
        pl.when(c != UNIT_CORE[u])(lambda u=u: unit_here(u).wait_recv())
    og[...] = dot(cc[...], wwp[...], ((1,), (1,)))

    @pl.when(not_self)
    def _():
        x_a.wait_send()
        c_a.wait_send()

    x_b.wait_send()
    c_b.wait_send()

    second = t2.end()
    mean2 = second[0:1] * inv_n2
    var2 = second[1:2] * inv_n2 - mean2 * mean2
    rs2 = lax.rsqrt(var2 + eps_norm)
    acc[2:3] = rs2 * gain2
    acc[3:4] = bias2 - mean2 * (rs2 * gain2)
    acc[4:5] = mean2
    acc[5:6] = rs2

    @pl.loop(0, 6)
    def _(k):
        lanes = pl.ds(pl.multiple_of(128 * k, 128), 128)
        v = gelu(pooled[:, lanes] * acc[2:3, lanes] + acc[3:4, lanes]) * valid_mask(WIN)
        mm[0, :, lanes] = before(v)
        mm[1, :, lanes] = v.astype(bf16)
        mm[2, :, lanes] = after(v)

    h2 = jnp.zeros((WIN, H), f32)
    for t in range(3):
        h2 = h2 + dot(mm[t], ww2[t], ((1,), (1,)))
    hid[...] = h2
    m = valid_mask(WIN) * own_mask(WIN)
    h2m = h2 * m
    acc[6:7, 0:H] = jnp.sum(h2m, axis=0, keepdims=True)
    acc[6:7, H : 2 * H] = jnp.sum(h2m * h2, axis=0, keepdims=True)
    t3 = Total(p, (ab1.at[1], ab2.at[1]), (as1.at[2], ar1.at[2], as2.at[2], ar2.at[2]))
    t3.start(acc[6:8])
    t3.middle()
    third = t3.end()
    mean3 = third[0:1, 0:H] * inv_n2
    var3 = third[0:1, H : 2 * H] * inv_n2 - mean3 * mean3
    rs3 = lax.rsqrt(var3 + eps_norm)
    valid = valid_mask(WIN)
    own = own_mask(WIN)
    h2 = hid[...]
    scaled = (h2 - mean3) * rs3
    pre = scaled * gain3 + bias3
    no[...] = (gelu(pre) * valid).astype(bf16)
    slopes = gelu_slope(pre) * og[...] * valid
    og[...] = slopes
    hid[...] = scaled
    acc[6:7, 0:H] = jnp.sum(slopes * scaled * own, axis=0, keepdims=True)
    acc[6:7, H : 2 * H] = jnp.sum(slopes * own, axis=0, keepdims=True)
    t4 = Total(p, (ab1.at[2], ab2.at[2]), (as1.at[3], ar1.at[3], as2.at[3], ar2.at[3]))
    t4.start(acc[6:8])
    ob[...] = (pooled[...] + dot(no[...], wwp[...])).astype(bf16)
    t4.middle()
    out_rows = pl.ds(pl.multiple_of(512 * c, 16), OWN)
    own_rows = pl.ds(own0, OWN)

    def out_copy(k):
        return remote(
            ob.at[own_rows, pl.ds(384 * k, 384)],
            out.at[out_rows, :],
            ss.at[23 + k],
            rs.at[23 + c],
            p.at(z=2 * p.zh + k, c=zl),
        )

    def to_self(k):
        return (zl == k) & is_self

    for k in range(2):
        pl.when(jnp.logical_not(to_self(k)))(lambda k=k: out_copy(k).start())

        def local(k=k):
            pltpu.make_async_copy(
                ob.at[own_rows, pl.ds(384 * k, 384)], out.at[out_rows, :], rs.at[23 + c]
            ).start()

        pl.when(to_self(k))(local)

    def put2(m, value):
        s2[:, pl.ds(24 * m, 24), :] = value.astype(bf16).reshape(16, 24, C1)

    tn = ((0,), (0,))
    nop = dot(no[own_rows, :], perm2).astype(bf16)
    put2(3, dot(nop, cc[own_rows, :], tn))
    fourth = t4.end()
    stats[4:5] = fourth[0:1]
    gain_mean = fourth[0:1, 0:H] * inv_n2
    bias_mean = fourth[0:1, H : 2 * H] * inv_n2
    hg = valid_mask(WIN) * (gain3 * rs3) * (og[...] - bias_mean - hid[...] * gain_mean)
    hh[0] = after(hg)
    hh[1] = hg.astype(bf16)
    hh[2] = before(hg)
    mid_grad = jnp.zeros((WIN, C1), f32)
    for t in range(3):
        mid_grad = mid_grad + dot(hh[t], ww2[t])
    mid[...] = mid_grad

    @pl.loop(0, 6)
    def _(k):
        lanes = pl.ds(pl.multiple_of(128 * k, 128), 128)
        v = pooled[:, lanes]
        slopes = gelu_slope(v * acc[2:3, lanes] + acc[3:4, lanes]) * mid[:, lanes] * valid_mask(WIN)
        scaled = (v - acc[4:5, lanes]) * acc[5:6, lanes]
        mid[:, lanes] = slopes
        pooled[:, lanes] = scaled
        mine = slopes * own_mask(WIN)
        acc[0:1, lanes] = jnp.sum(mine * scaled, axis=0, keepdims=True)
        acc[1:2, lanes] = jnp.sum(mine, axis=0, keepdims=True)

    t5 = Total(p, (ab1.at[3], ab2.at[3]), (as1.at[4], ar1.at[4], as2.at[4], ar2.at[4]))
    t5.start(acc[0:2])
    hp = dot(hh[1, own_rows, :], perm2).astype(bf16)
    put2(0, dot(hp, mm[0, own_rows, :], tn))
    t5.middle()
    for t in range(1, 3):
        put2(t, dot(hp, mm[t, own_rows, :], tn))
    fifth = t5.end()
    stats[2:4] = fifth
    acc[0:2] = fifth * inv_n2

    @pl.loop(0, 6)
    def _(k):
        lanes = pl.ds(pl.multiple_of(128 * k, 128), 128)
        back = acc[2:3, lanes] * (
            mid[:, lanes] - acc[1:2, lanes] - pooled[:, lanes] * acc[0:1, lanes]
        )
        pg = cc[:, lanes].astype(f32) + back * valid_mask(WIN)
        even = 1.0 / (1.0 + jnp.exp(-diff[:, lanes]))
        ge = pg * even
        go = pg * (1.0 - even)
        gg[0, :, lanes] = after(go)
        gg[1, :, lanes] = after(ge)
        gg[2, :, lanes] = go.astype(bf16)
        gg[3, :, lanes] = ge.astype(bf16)
        gg[4, :, lanes] = before(go)
        gg[5, :, lanes] = before(ge)

    gp[0] = dot(gg[3, own_rows, :], perm[...]).astype(bf16)
    gp[1] = dot(gg[2, own_rows, :], perm[...]).astype(bf16)
    for t in range(5):
        part = dot(gp[0], aa[t, own_rows, 0:C0], tn) + dot(gp[1], aa[t + 1, own_rows, 0:C0], tn)
        s1[t, :, 0:C0] = part.astype(bf16)
        s1[t, :, C0:PAD] = jnp.zeros((C1, PAD - C0), bf16)

    small[4:6] = jnp.zeros((2, PAD), f32)
    for par in range(2):
        for k in range(2):
            rows = pl.ds(pl.multiple_of(own0 + 256 * k, 16), 256)
            v = jnp.zeros((256, C0), f32)
            for t in range(5):
                v = v + dot(gg[t + 1 - par, rows, :], ww1[t], ((1,), (1,)))
            slope[:, 0:C0] = v
            slope[:, C0:PAD] = jnp.zeros((256, PAD - C0), f32)

            @pl.loop(0, 6)
            def _(q, par=par, k=k):
                lanes = pl.ds(pl.multiple_of(128 * q, 128), 128)
                xv = raw[par, pl.ds(pl.multiple_of(rawown + 256 * k, 16), 256), lanes].astype(f32)
                valid = valid_mask(256, 16 * c + 256 * k)
                slopes = gelu_slope(xv * small[0:1, lanes] + small[1:2, lanes]) * slope[:, lanes] * valid
                scaled = (xv - small[2:3, lanes]) * small[3:4, lanes]
                slope[:, lanes] = slopes
                small[4:5, lanes] += jnp.sum(slopes * scaled, axis=0, keepdims=True)
                small[5:6, lanes] += jnp.sum(slopes, axis=0, keepdims=True)

            dst = pl.ds(256 * k, 256)
            sl_send[0, par, dst, :] = slope[:, 0:384].astype(bf16)
            sl_send[1, par, dst, :] = pltpu.roll(slope[...], PAD - HALF0, 1)[:, 0:384].astype(bf16)

    t6 = Total(p, (ab1.at[4], ab2.at[4]), (as1.at[5], ar1.at[5], as2.at[5], ar2.at[5]))
    t6.start(small[4:6])

    def slope_copy(k):
        return remote(
            sl_send.at[k], sl_home.at[c], ss.at[25 + k], rs.at[25 + c], p.at(z=2 * p.zh + k, c=zl)
        )

    for k in range(2):
        pl.when(jnp.logical_not(to_self(k)))(lambda k=k: slope_copy(k).start())

        def local_s(k=k):
            pltpu.make_async_copy(sl_send.at[k], sl_home.at[c], rs.at[25 + c]).start()

        pl.when(to_self(k))(local_s)
    t6.middle()
    sixth = t6.end()
    stats[0:2] = sixth
    stats[5:8] = jnp.zeros((3, PAD), f32)

    small[4:6] = sixth * inv_n1
    small[6:7] = rs1 * gain1
    vec = small[...]
    vec = jnp.where(zl == 0, vec, pltpu.roll(vec, PAD - HALF0, 1))
    tr[0, 0:8, :] = vec
    cols = jnp.transpose(tr[0, :, 0:384])
    mean_c = cols[0:HALF0, 2:3]
    rs_c = cols[0:HALF0, 3:4]
    gm_c = cols[0:HALF0, 4:5]
    bm_c = cols[0:HALF0, 5:6]
    scale_c = cols[0:HALF0, 6:7]
    for j in range(2):
        remote(sl_home.at[j], sl_home.at[j], ss.at[0], rs.at[25 + j], other_core).wait_recv()
    rowq = iota((128, 256), 0)
    laneq = iota((128, 256), 1)
    put_even = (laneq == 2 * rowq).astype(bf16)
    put_odd = (laneq == 2 * rowq + 1).astype(bf16)
    for j in range(2):
        for k in range(4):
            bins = pl.ds(128 * k, 128)
            st = dot(sl_home[j, 0, bins, :], put_even, tn) + dot(sl_home[j, 1, bins, :], put_odd, tn)
            lanes = pl.ds(1024 * j + 256 * k, 256)
            xf = xt[:, lanes].astype(f32)
            scaled = (xf - mean_c) * rs_c
            ok = ((iota((1, 256), 1) + (1024 * j + 256 * k)).astype(f32) >= 2.0 * off_home).astype(f32)
            gin[:, lanes] = ok * (scale_c * (st[0:HALF0] - bm_c - scaled * gm_c))

    for k in range(2):

        def sent(k=k):
            out_copy(k).wait_send()
            slope_copy(k).wait_send()

        pl.when(jnp.logical_not(to_self(k)))(sent)
    for j in range(2):
        rows = out.at[pl.ds(512 * j, 512), :]
        remote(rows, rows, ss.at[0], rs.at[23 + j], other_core).wait_recv()


VMEM = pl.BlockSpec(memory_space=pltpu.VMEM)
ANY = pl.BlockSpec(memory_space=pl.ANY)


def run_step(xt, offs, cot, w1, w2, wp, pvec, owners_row, consts):
    shape = jax.ShapeDtypeStruct
    dma = pltpu.SemaphoreType.DMA
    scratch = [
        pltpu.VMEM((2, HALF0, LANES), bf16),
        pltpu.VMEM((2, 576, PAD), bf16),
        pltpu.VMEM((6, WIN, PAD), bf16),
        pltpu.VMEM((5, C0, C1), bf16),
        pltpu.VMEM((3, H, C1), bf16),
        pltpu.VMEM((H, C1), bf16),
        pltpu.VMEM((WIN, C1), f32),
        pltpu.VMEM((WIN, C1), f32),
        pltpu.VMEM((WIN, C1), bf16),
        pltpu.VMEM((3, WIN, C1), bf16),
        pltpu.VMEM((WIN, H), f32),
        pltpu.VMEM((WIN, H), f32),
        pltpu.VMEM((WIN, H), bf16),
        pltpu.VMEM((3, WIN, H), bf16),
        pltpu.VMEM((WIN, C1), f32),
        pltpu.VMEM((6, WIN, C1), bf16),
        pltpu.VMEM((2, OWN, C1), bf16),
        pltpu.VMEM((C1, C1), bf16),
        pltpu.VMEM((256, PAD), f32),
        pltpu.VMEM((2, 2, OWN, 384), bf16),
        pltpu.VMEM((2, 2, OWN, 384), bf16),
        pltpu.VMEM((WIN, C1), bf16),
        pltpu.VMEM((8, PAD), f32),
        pltpu.VMEM((8, 128), f32),
        pltpu.VMEM((8, PAD), f32),
        pltpu.VMEM((2, 128, PAD), f32),
        pltpu.VMEM((8, 8, PAD), f32),
        pltpu.VMEM((16, 8, PAD), f32),
        pltpu.VMEM((5, 8, 2, PAD), f32),
        pltpu.VMEM((5, 16, 2, PAD), f32),
        dma((32,)),
        dma((32,)),
        dma((4,)),
        dma((6, 8)),
        dma((6, 8)),
        dma((6, 16)),
        dma((6, 16)),
    ]
    return pl.pallas_call(
        step_kernel,
        out_shape=(
            shape((BINS, 384), bf16),
            shape((HALF0, 2 * BINS), f32),
            shape((5, C1, PAD), bf16),
            shape((16, 96, C1), bf16),
            shape((8, PAD), f32),
        ),
        in_specs=[VMEM, VMEM, ANY, ANY, ANY, ANY] + [VMEM] * 6,
        out_specs=(ANY, VMEM, VMEM, VMEM, VMEM),
        scratch_shapes=scratch,
        compiler_params=pltpu.CompilerParams(
            collective_id=0, has_side_effects=True, vmem_limit_bytes=63 * 2**20
        ),
    )(xt, offs, cot, w1, w2, wp, pvec, owners_row, consts["e1"], consts["bw1"], consts["e2"], consts["bw2"])


def adam_block(first, second, turned):
    first_new = beta_one * first + (1.0 - beta_one) * turned
    second_new = beta_two * second + (1.0 - beta_two) * turned * turned
    direction = (
        first_new
        / (1.0 - beta_one**STEP)
        / (jnp.sqrt(second_new / (1.0 - beta_two**STEP)) + adam_eps)
    )
    return first_new, second_new, direction


def master_block(master, update, rate, average):
    master_new = master - rate * (update + decay_rate * master)
    return master_new, average_rate * average + (1.0 - average_rate) * master_new


def tail_kernel(
    s1, s2, b1, b2, b3,
    m1, f1, q1, a1, m2, f2, q2, a2, m3, f3, q3, a3,
    owners_row, owners_col, rep1, rep2, ec1, bwc1, e3, bw3,
    cp1, cp2, cp3,
    nm1, nf1, nq1, na1, nm2, nf2, nq2, na2, nm3, nf3, nq3, na3,
    t1, t2, ra1, ua, ra2, rb1, rb2, ub1, ub2, rb3, rb4, pz, rz, dd, upd, nb, ga,
    ss, rs, ls,
):
    p = Place()
    x, y, zh, zl, z, c = p.x, p.y, p.zh, p.zl, p.z, p.c
    other_core = p.at(c=1 - c)
    xs = [(p.at(x=lax.rem(x + k, 4)), lax.rem(x + k, 4)) for k in (1, 2, 3)]
    ys = [(p.at(y=lax.rem(y + k, 4)), lax.rem(y + k, 4)) for k in (1, 2, 3)]
    column = column_peers(p)
    bar = pltpu.get_barrier_semaphore()
    for device, *_ in xs + ys + column:
        pl.semaphore_signal(bar, inc=1, device_id=device, device_id_type=MESH)
    pl.semaphore_wait(bar, 13)

    mine = pl.ds(pl.multiple_of(384 * c, 128), 384)
    others = pl.ds(pl.multiple_of(384 - 384 * c, 128), 384)
    ca = remote(s1.at[:, :, :, :, others], t1, ss.at[0], rs.at[0], other_core)
    cb = remote(s2.at[:, :, :, others], t2, ss.at[1], rs.at[1], other_core)
    ca.start()
    cb.start()
    ca.wait()
    cb.wait()
    for t in range(5):
        t1[t] = (t1[t].astype(f32) + s1[t, :, :, :, mine].astype(f32)).astype(bf16)
    t2[...] = (t2[...].astype(f32) + s2[:, :, :, mine].astype(f32)).astype(bf16)

    sent = []
    for k in range(3):
        xd, xi = xs[k]
        yd, yi = ys[k]
        sent.append(remote(t1.at[0:4, xi], ra1.at[k], ss.at[2 + k], rs.at[2 + k], xd))
        sent.append(remote(t1.at[4, :, yi], rb1.at[k], ss.at[5 + k], rs.at[5 + k], yd))
        sent.append(remote(t2.at[:, yi], rb2.at[k], ss.at[8 + k], rs.at[8 + k], yd))
    for cp in sent:
        cp.start()
    for cp in sent:
        cp.wait_recv()

    def total(own, parts):
        v = own.astype(f32)
        for k in range(3):
            v = v + parts[k].astype(f32)
        return v

    for t in range(4):
        ua[t] = total(t1[t, x], [ra1[k, t] for k in range(3)]).astype(bf16)
    ub1[...] = total(t1[4, :, y], [rb1[k] for k in range(3)]).astype(bf16)
    ub2[...] = total(t2[:, y], [rb2[k] for k in range(3)]).astype(bf16)
    late = []
    for k in range(3):
        xd, xi = xs[k]
        yd, yi = ys[k]
        late.append(remote(ua.at[:, yi], ra2.at[k], ss.at[11 + k], rs.at[11 + k], yd))
        late.append(remote(ub1.at[xi], rb3.at[k], ss.at[14 + k], rs.at[14 + k], xd))
        late.append(remote(ub2.at[xi], rb4.at[k], ss.at[17 + k], rs.at[17 + k], xd))
    for cp in late:
        cp.start()
    for cp in late:
        cp.wait_recv()
    va = total(ua[:, y], [ra2[k] for k in range(3)]).astype(bf16).reshape(192, 384)
    vb = total(ub1[x], [rb3[k] for k in range(3)]).astype(bf16)
    vc = total(ub2[x], [rb4[k] for k in range(3)]).astype(bf16)
    r1 = rep1[...]
    g1 = dot(r1[:, 0:192], va) + dot(r1[:, 192:240], vb)
    g2 = dot(rep2[...], vc)
    for e in range(8):
        pz[e, 0:48] = g1[48 * e : 48 * e + 48].astype(bf16)
        pz[e, 48:80] = g2[32 * e : 32 * e + 32].astype(bf16)
    near = []
    for k, (device, zi, ci) in enumerate(column):
        near.append(remote(pz.at[2 * zi + ci], rz.at[p.e], ss.at[20 + k], rs.at[20 + p.e], device))
    for cp in near:
        cp.start()
    rz[p.e] = pz[p.e]
    for device, zi, ci in column:
        e = 2 * zi + ci
        remote(rz.at[e], rz.at[e], ss.at[0], rs.at[20 + e], device).wait_recv()
    halves = []
    for half in range(2):
        v = rz[half].astype(f32)
        for k in range(1, 4):
            v = v + rz[2 * k + half].astype(f32)
        halves.append(v)
    grad = jnp.concatenate(halves, axis=1)

    nt = ((1,), (1,))
    basis1 = b1[...].astype(bf16)
    turned = dot(grad[0:40, 0:C0].astype(bf16), basis1)
    dd[...] = jnp.zeros_like(dd)
    for t in range(5):
        first_new, second_new, direction = adam_block(f1[t], q1[t], turned[8 * t : 8 * t + 6])
        nf1[t] = first_new
        nq1[t] = second_new
        dd[8 * t : 8 * t + 6, 0:C0] = direction
    update = dot(dd[0:40, 0:C0].astype(bf16), basis1, nt)
    nb[...] = jnp.zeros_like(nb)
    for t in range(5):
        master_new, average_new = master_block(m1[t], update[8 * t : 8 * t + 6], 0.02, a1[t])
        nm1[t] = master_new
        na1[t] = average_new
        nb[8 * t : 8 * t + 6, 0:C0] = master_new
    basis2 = b2[...].astype(bf16)
    turned = dot(grad[48:72].astype(bf16), basis2)
    for t in range(3):
        first_new, second_new, direction = adam_block(f2[t], q2[t], turned[8 * t : 8 * t + 3])
        nf2[t] = first_new
        nq2[t] = second_new
        dd[8 * t : 8 * t + 3, :] = direction
    update = dot(dd[0:24].astype(bf16), basis2, nt)
    for t in range(3):
        master_new, average_new = master_block(m2[t], update[8 * t : 8 * t + 3], 0.02, a2[t])
        nm2[t] = master_new
        na2[t] = average_new
        nb[40 + 4 * t : 43 + 4 * t, :] = master_new
    basis3 = b3[...].astype(bf16)
    turned = dot(grad[72:80].astype(bf16), basis3)
    first_new, second_new, direction = adam_block(f3[...], q3[...], turned[0:3])
    nf3[...] = first_new
    nq3[...] = second_new
    dd[0:8] = jnp.zeros((8, PAD), f32)
    dd[0:3] = direction
    update = dot(dd[0:8].astype(bf16), basis3, nt)
    master_new, average_new = master_block(m3[...], update[0:3], 0.05, a3[...])
    nm3[...] = master_new
    na3[...] = average_new
    nb[52:55, :] = master_new

    ga[c, x, y, zh] = nb[...].astype(bf16)
    mine_ga = ga.at[c, x, y, zh]
    zcp = remote(mine_ga, mine_ga, ss.at[28], rs.at[28], p.at(z=lax.rem(z + 2, 4)))
    zcp.start()
    zcp.wait()
    up, low = pl.ds(0, 32), pl.ds(32, 32)
    cps = []
    for k in range(3):
        xd, xi = xs[k]
        yd, yi = ys[k]
        va_ = ga.at[c, x, y, :, up]
        vb_ = ga.at[c, x, y, :, low]
        cps.append(remote(va_, va_, ss.at[29 + k], rs.at[29 + k], yd))
        cps.append(remote(vb_, vb_, ss.at[32 + k], rs.at[32 + k], xd))
    for cp in cps:
        cp.start()
    for k in range(3):
        yi = lax.rem(y + 3 - k, 4)
        xi = lax.rem(x + 3 - k, 4)
        va_ = ga.at[c, x, yi, :, up]
        vb_ = ga.at[c, xi, y, :, low]
        remote(va_, va_, ss.at[0], rs.at[29 + k], other_core).wait_recv()
        remote(vb_, vb_, ss.at[0], rs.at[32 + k], other_core).wait_recv()
    cps2 = []
    for k in range(3):
        xd, xi = xs[k]
        yd, yi = ys[k]
        va_ = ga.at[c, x, :, :, up]
        vb_ = ga.at[c, :, y, :, low]
        cps2.append(remote(va_, va_, ss.at[35 + k], rs.at[35 + k], xd))
        cps2.append(remote(vb_, vb_, ss.at[38 + k], rs.at[38 + k], yd))
    for cp in cps2:
        cp.start()

    natc = dot(ec1[...], owners_col[...]) * 6.0 + bwc1[...]
    lane = iota((512, 128), 1)
    place1 = jnp.concatenate(
        [((lane + 128 * k).astype(f32) == natc).astype(bf16) for k in range(3)], axis=1
    )
    natr = dot(owners_row[...], e3[...])[0:1] * 3.0 + bw3[0:1]
    place2 = (iota((768, 1024), 0).astype(f32) == natr).astype(bf16)
    for k in range(3):
        yi = lax.rem(y + 3 - k, 4)
        xi = lax.rem(x + 3 - k, 4)
        va_ = ga.at[c, xi, :, :, up]
        vb_ = ga.at[c, :, yi, :, low]
        remote(va_, va_, ss.at[0], rs.at[35 + k], other_core).wait_recv()
        remote(vb_, vb_, ss.at[0], rs.at[38 + k], other_core).wait_recv()
    both = remote(ga.at[c], ga.at[c], ss.at[41], rs.at[41], other_core)
    both.start()
    remote(ga.at[1 - c], ga.at[1 - c], ss.at[0], rs.at[41], other_core).wait_recv()
    tn = ((0,), (0,))
    for t in range(5):
        block = ga[:, :, :, :, 8 * t : 8 * t + 8, :].reshape(512, PAD)
        cp1[t] = dot(block[:, 0:C0], place1, tn).astype(bf16)
    block = ga[:, :, :, :, 40:56, :].reshape(1024, PAD)
    copy2 = dot(place2, block).astype(bf16)
    for t in range(3):
        cp2[t] = copy2[192 * t : 192 * t + 192]
    cp3[...] = copy2[576:768]
    for cp in sent + late + near + cps + cps2 + [both]:
        cp.wait_send()


def run_tail(s1, s2, bases, states, owners_row, owners_col, consts):
    shape = jax.ShapeDtypeStruct
    dma = pltpu.SemaphoreType.DMA
    scratch = [
        pltpu.VMEM((5, 4, 4, 48, 384), bf16),
        pltpu.VMEM((4, 4, 96, 384), bf16),
        pltpu.VMEM((3, 4, 4, 48, 384), bf16),
        pltpu.VMEM((4, 4, 48, 384), bf16),
        pltpu.VMEM((3, 4, 48, 384), bf16),
        pltpu.VMEM((3, 4, 48, 384), bf16),
        pltpu.VMEM((3, 4, 96, 384), bf16),
        pltpu.VMEM((4, 48, 384), bf16),
        pltpu.VMEM((4, 96, 384), bf16),
        pltpu.VMEM((3, 48, 384), bf16),
        pltpu.VMEM((3, 96, 384), bf16),
        pltpu.VMEM((8, 80, 384), bf16),
        pltpu.VMEM((8, 80, 384), bf16),
        pltpu.VMEM((40, PAD), f32),
        pltpu.VMEM((8, 128), f32),
        pltpu.VMEM((64, PAD), f32),
        pltpu.VMEM((2, 4, 4, 2, 64, PAD), bf16),
        dma((44,)),
        dma((44,)),
        dma((4,)),
    ]
    wide = [shape(a.shape, f32) for a in states]
    return pl.pallas_call(
        tail_kernel,
        out_shape=(
            shape((5, C0, 384), bf16),
            shape((3, HALFH, C1), bf16),
            shape((HALFH, C1), bf16),
            *wide,
        ),
        in_specs=[VMEM] * (5 + 12 + 8),
        out_specs=tuple([VMEM] * 15),
        scratch_shapes=scratch,
        compiler_params=pltpu.CompilerParams(
            collective_id=1, has_side_effects=True, vmem_limit_bytes=63 * 2**20
        ),
    )(
        s1, s2, *bases, *states, owners_row, owners_col,
        consts["rep1"], consts["rep2"], consts["ec1"], consts["bwc1"], consts["e3"], consts["bw3"],
    )


def make_consts():
    e1 = np.zeros((64, 768), np.float32)
    bw1 = np.zeros((8, 768), np.float32)
    e2 = np.zeros((64, 384), np.float32)
    bw2 = np.zeros((8, 384), np.float32)
    for s in range(64):
        g, zh, c = s // 4, (s // 2) % 2, s % 2
        for b in range(2):
            e = (2 * zh + b) * 2 + c
            for w in range(6):
                e1[s, (g * 8 + e) * 6 + w] = 1
                bw1[:, (g * 8 + e) * 6 + w] = b * 384 + w
            for w in range(3):
                e2[s, (g * 8 + e) * 3 + w] = 1
                bw2[:, (g * 8 + e) * 3 + w] = b * 192 + w
    rep1 = np.zeros((8 * 48, 240), np.float32)
    rep2 = np.zeros((8 * 32, 96), np.float32)
    for e in range(8):
        for t in range(5):
            for w in range(6):
                rep1[e * 48 + t * 8 + w, t * 48 + e * 6 + w] = 1
        for m in range(4):
            for w in range(3):
                rep2[e * 32 + m * 8 + w, m * 24 + e * 3 + w] = 1
    ec1 = np.zeros((512, 64), np.float32)
    bwc1 = np.full((512, 128), -4096.0, np.float32)
    e3 = np.zeros((64, 1024), np.float32)
    bw3 = np.full((8, 1024), -4096.0, np.float32)
    for k in range(64):
        c, g, zh = k // 32, (k // 2) % 16, k % 2
        s = g * 4 + zh * 2 + c
        ec1[8 * k : 8 * k + 8, s] = 1
        for w in range(6):
            bwc1[8 * k + w] = w
        e3[s, 16 * k : 16 * k + 16] = 1
        for m in range(4):
            for w in range(3):
                bw3[:, 16 * k + 4 * m + w] = 192 * m + w
    low = lambda a: jnp.asarray(a, bf16)
    return {
        "e1": low(e1), "bw1": jnp.asarray(bw1), "e2": low(e2), "bw2": jnp.asarray(bw2),
        "rep1": low(rep1), "rep2": low(rep2), "ec1": low(ec1), "bwc1": jnp.asarray(bwc1),
        "e3": low(e3), "bw3": jnp.asarray(bw3),
    }


def norm_adam(gradient, parameters, moments):
    first_new = beta_one * moments[0] + (1.0 - beta_one) * gradient
    second_new = beta_two * moments[1] + (1.0 - beta_two) * gradient * gradient
    direction = (
        first_new
        / (1.0 - beta_one**STEP)
        / (jnp.sqrt(second_new / (1.0 - beta_two**STEP)) + adam_eps)
    )
    return (parameters - norm_rate * direction, first_new, second_new)


def local(
    inputs, offsets, owners, cotangent,
    norm1_gain, norm1_bias, norm1_moments,
    norm2_gain, norm2_bias, norm2_moments,
    norm3_gain, norm3_bias, norm3_moments,
    conv1_copy, conv1_master, conv1_first, conv1_second, conv1_average, basis1,
    conv2_copy, conv2_master, conv2_first, conv2_second, conv2_average, basis2,
    project_copy, project_master, project_first, project_second, project_average, basis3,
):
    consts = make_consts()
    zl = lax.axis_index("ch")
    leader = lax.axis_index(SEQ) == 0

    def in_half(v, half, at=0):
        wide = jnp.zeros((PAD,), f32)
        return lax.dynamic_update_slice(wide, v, (at + zl * half,))

    rows = jnp.stack(
        [
            in_half(norm1_gain, HALF0),
            in_half(norm1_bias, HALF0),
            in_half(norm2_gain, HALF1),
            in_half(norm2_bias, HALF1),
            in_half(norm3_gain, HALFH) + in_half(norm3_bias, HALFH, H),
        ]
    )
    pvec = jnp.pad(jnp.where(leader, rows, 0.0), ((2, 1), (0, 0)))
    offs = jnp.broadcast_to(offsets.astype(f32)[:, None], (8, 128))
    owners_low = owners.astype(bf16)
    owners_row = jnp.broadcast_to(owners_low[None], (8, 64))
    owners_col = jnp.broadcast_to(owners_low[:, None], (64, 128))
    out, gin, s1, s2, stats = run_step(
        jnp.swapaxes(inputs[0], 0, 1), offs, cotangent[0], conv1_copy,
        jnp.swapaxes(conv2_copy, 1, 2), jnp.swapaxes(project_copy, 0, 1),
        pvec, owners_row, consts,
    )
    flip2 = lambda a: jnp.swapaxes(a, -1, -2)
    states = [
        conv1_master, conv1_first, conv1_second, conv1_average,
        conv2_master, conv2_first, conv2_second, conv2_average,
        project_master, project_first, project_second, project_average,
    ]
    cp1, cp2, cp3, *new = run_tail(
        s1.reshape(5, 4, 4, 48, PAD), s2.reshape(4, 4, 96, C1), (basis1, basis2, basis3),
        [flip2(a) for a in states], owners_row, owners_col, consts,
    )
    nm1, nf1, nq1, na1, nm2, nf2, nq2, na2, nm3, nf3, nq3, na3 = [flip2(a) for a in new]

    def my_half(v, half):
        return lax.dynamic_slice(v, (0, zl * half), (2, half))

    g3 = stats[4].reshape(2, H)
    s_1 = norm_adam(my_half(stats[0:2], HALF0), jnp.stack([norm1_gain, norm1_bias]), norm1_moments)
    s_2 = norm_adam(my_half(stats[2:4], HALF1), jnp.stack([norm2_gain, norm2_bias]), norm2_moments)
    s_3 = norm_adam(my_half(g3, HALFH), jnp.stack([norm3_gain, norm3_bias]), norm3_moments)
    return (
        out[None], jnp.swapaxes(gin, 0, 1)[None], *s_1, *s_2, *s_3,
        nm1, cp1, nf1, nq1, na1,
        nm2, flip2(cp2), nf2, nq2, na2,
        nm3, flip2(cp3), nf3, nq3, na3,
    )


def solution(mesh):
    finer = Mesh(mesh.devices.reshape(4, 4, 2, 2, mesh.shape["ch"]), SEQ_CH)
    owner3 = P(None, None, SEQ_CH)
    owner2 = P(None, SEQ_CH)
    half3 = P(None, None, "ch")
    in_specs = (
        P(SEQ, None, "ch"), P(SEQ), P(), P(SEQ, None, "ch"),
        P("ch"), P("ch"), half3, P("ch"), P("ch"), half3, P("ch"), P("ch"), half3,
        half3, owner3, owner3, owner3, owner3, P(),
        half3, owner3, owner3, owner3, owner3, P(),
        P(None, "ch"), owner2, owner2, owner2, owner2, P(),
    )
    vec = P(None, "ch")
    out_specs = (
        P(SEQ, None, "ch"), P(SEQ, None, "ch"), *[vec] * 9,
        owner3, half3, owner3, owner3, owner3,
        owner3, half3, owner3, owner3, owner3,
        owner2, vec, owner2, owner2, owner2,
    )
    return jax.shard_map(local, mesh=finer, in_specs=in_specs, out_specs=out_specs, check_vma=False)
```

```python
import math

import jax
import jax.numpy as jnp
import numpy as np
from jax import lax
from jax.experimental import pallas as pl
from jax.experimental.pallas import tpu as pltpu
from jax.sharding import Mesh
from jax.sharding import PartitionSpec as P

STEP = 8
SEQ = ("seq_0", "seq_1", "seq_2", "seq_3")
SEQ_CH = ("seq_0", "seq_1", "seq_2", "seq_3", "ch")
MESH = pl.DeviceIdType.MESH
bf16 = jnp.bfloat16
f32 = jnp.float32

eps_norm = 1e-05
beta_one = 0.9
beta_two = 0.95
adam_eps = 1e-08
decay_rate = 0.01
average_rate = 0.9
norm_rate = 0.05

C0, C1, H = 652, 768, 384
HALF0, HALF1, HALFH = 326, 384, 192
BINS = 1024
OWN = 512
WIN = 528
LANES = 1152
PAD = 768

GELU_K = math.sqrt(2.0 / math.pi)
GELU_C = 0.044715


def gelu(v):
    return 0.5 * v * (1.0 + jnp.tanh(GELU_K * (v + GELU_C * (v * v * v))))


def gelu_slope(v):
    square = v * v
    t = jnp.tanh(GELU_K * v * (1.0 + GELU_C * square))
    return 0.5 * (1.0 + t) + 0.5 * GELU_K * v * (1.0 - t * t) * (1.0 + 3.0 * GELU_C * square)


def dot(a, b, dims=((1,), (0,))):
    return lax.dot_general(a, b, (dims, ((), ())), preferred_element_type=f32)


def iota(shape, dim):
    return lax.broadcasted_iota(jnp.int32, shape, dim)


class Place:
    def __init__(self):
        self.x, self.y, self.zh, self.c, self.zl = [lax.axis_index(n) for n in SEQ_CH]
        self.z = 2 * self.zh + self.zl
        self.e = 2 * self.z + self.c
        self.g = 4 * self.x + self.y

    def at(self, **other):
        v = {"x": self.x, "y": self.y, "z": self.z, "c": self.c}
        v.update(other)
        z = v["z"]
        return (v["x"], v["y"], lax.div(z, 2), v["c"], lax.rem(z, 2))


def remote(src, dst, send, recv, device):
    return pltpu.make_async_remote_copy(
        src_ref=src, dst_ref=dst, send_sem=send, recv_sem=recv, device_id=device, device_id_type=MESH
    )


def column_peers(p):
    out = []
    for k in range(1, 8):
        z = lax.rem(p.z + k // 2, 4)
        c = lax.rem(p.c + k % 2, 2)
        out.append((p.at(z=z, c=c), z, c))
    return out


def plane_peers(p):
    out = []
    for k in range(1, 16):
        x = lax.rem(p.x + k // 4, 4)
        y = lax.rem(p.y + k % 4, 4)
        out.append((p.at(x=x, y=y), x, y))
    return out


class Total:
    def __init__(self, p, bufs, sems):
        self.p = p
        self.b1, self.b2 = bufs
        self.s1, self.r1, self.s2, self.r2 = sems

    def start(self, value):
        p = self.p
        self.b1[p.e] = value
        self.c1 = []
        for k, (device, _, _) in enumerate(column_peers(p)):
            cp = remote(self.b1.at[p.e], self.b1.at[p.e], self.s1.at[k], self.r1.at[p.e], device)
            cp.start()
            self.c1.append(cp)

    def middle(self):
        p = self.p
        for device, z, c in column_peers(p):
            e = 2 * z + c
            remote(self.b1.at[e], self.b1.at[e], self.s1.at[0], self.r1.at[e], device).wait_recv()
        total = self.b1[0]
        for k in range(1, 8):
            total = total + self.b1[k]
        for cp in self.c1:
            cp.wait_send()
        self.b2[p.g] = total
        self.c2 = []
        for k, (device, _, _) in enumerate(plane_peers(p)):
            cp = remote(self.b2.at[p.g], self.b2.at[p.g], self.s2.at[k], self.r2.at[p.g], device)
            cp.start()
            self.c2.append(cp)

    def end(self):
        p = self.p
        for device, x, y in plane_peers(p):
            g = 4 * x + y
            remote(self.b2.at[g], self.b2.at[g], self.s2.at[0], self.r2.at[g], device).wait_recv()
        total = self.b2[0]
        for k in range(1, 16):
            total = total + self.b2[k]
        for cp in self.c2:
            cp.wait_send()
        return total


TAP_CORE = (0, 0, 1, 1, 0)
UNIT_CORE = (0, 1, 0, 1)


def step_kernel(
    xt, offsets, owners, cot, w1, w2, wp, pg1, pb1, pg2, pb2, pg3, pb3,
    e1, bw1, e2, bw2, rep1, rep2,
    out, sl_home, grad, stats,
    s1, s2, xw, raw, aa, ww1, ww2, wwp, pooled, diff, cc, hid, og, no, hh, mid, gg, gp, perm,
    slope, small, offs, offw, acc, tr,
    t1, t2, ra, rb, rd, re, ua, uc, va, pz, rz,
    a1a, a1b, ab1, ab2,
    ss, rs, ls, as1, ar1, as2, ar2, gs, gr,
):
    mm = gg.at[0:3]
    p = Place()
    offs[...] = jnp.broadcast_to(offsets[...].astype(f32), (8, 128))
    c, zl = p.c, p.zl
    flip = p.at(z=3 - p.z)
    direct = p.at(z=p.z + 1 - 2 * zl)
    other_core = p.at(c=1 - c)

    bar = pltpu.get_barrier_semaphore()
    for device, _, _ in column_peers(p):
        pl.semaphore_signal(bar, inc=1, device_id=device, device_id_type=MESH)
    for device, _, _ in plane_peers(p):
        pl.semaphore_signal(bar, inc=1, device_id=device, device_id_type=MESH)

    own_w = [
        pltpu.make_async_copy(w1, ww1.at[:, :, pl.ds(pl.multiple_of(384 * zl, 128), 384)], ls.at[0]),
        pltpu.make_async_copy(w2, ww2.at[:, pl.ds(pl.multiple_of(192 * zl, 16), 192), :], ls.at[1]),
        pltpu.make_async_copy(wp, wwp.at[pl.ds(pl.multiple_of(192 * zl, 16), 192), :], ls.at[2]),
    ]
    for cp in own_w:
        cp.start()

    pl.semaphore_wait(bar, 22)

    is_self = c == zl
    not_self = c != zl
    home_chip = 2 * p.zh + c

    def window(j):
        return xt.at[:, pl.ds(pl.multiple_of(896 * j, 128), LANES)]

    def cot_window(j):
        return cot.at[pl.ds(pl.multiple_of(496 * j, 16), WIN), :]

    cc_mine = cc.at[:, pl.ds(pl.multiple_of(384 * zl, 128), 384)]
    x_a = remote(window(c), xw.at[zl], ss.at[0], rs.at[0 + zl], p.at(z=home_chip, c=c))
    x_b = remote(window(1 - c), xw.at[zl], ss.at[1], rs.at[0 + zl], p.at(z=home_chip, c=1 - c))
    c_a = remote(cot_window(c), cc_mine, ss.at[2], rs.at[2 + zl], p.at(z=home_chip, c=c))
    c_b = remote(cot_window(1 - c), cc_mine, ss.at[3], rs.at[2 + zl], p.at(z=home_chip, c=1 - c))
    o_a = remote(offs, offw, ss.at[4], rs.at[4], other_core)

    @pl.when(not_self)
    def _():
        x_a.start()

    @pl.when(is_self)
    def _():
        pltpu.make_async_copy(window(c), xw.at[zl], rs.at[0 + zl]).start()

    x_b.start()
    o_a.start()

    mine = pl.ds(pl.multiple_of(384 * c, 128), 384)
    others = pl.ds(pl.multiple_of(384 - 384 * c, 128), 384)
    my_lanes = pl.ds(pl.multiple_of(384 * zl, 128), 384)
    its_lanes = pl.ds(pl.multiple_of(384 - 384 * zl, 128), 384)
    my_rows = pl.ds(pl.multiple_of(192 * zl, 16), 192)
    its_rows = pl.ds(pl.multiple_of(192 - 192 * zl, 16), 192)

    def tap_over(t):
        to = direct if t == 4 else flip
        return remote(w1.at[t], ww1.at[t, :, my_lanes], ss.at[5 + t], rs.at[5 + t], to)

    def tap_here(t):
        return remote(
            ww1.at[t, :, its_lanes], ww1.at[t, :, its_lanes], ss.at[10 + t], rs.at[10 + t], other_core
        )

    def unit_ref(u, rows):
        return ww2.at[u, rows, :] if u < 3 else wwp.at[rows, :]

    def unit_over(u):
        return remote(
            w2.at[u] if u < 3 else wp, unit_ref(u, my_rows), ss.at[15 + u], rs.at[15 + u], flip
        )

    def unit_here(u):
        return remote(
            unit_ref(u, its_rows), unit_ref(u, its_rows), ss.at[19 + u], rs.at[19 + u], other_core
        )

    for t in range(5):
        pl.when(c == TAP_CORE[t])(lambda t=t: tap_over(t).start())

    @pl.when(not_self)
    def _():
        c_a.start()

    @pl.when(is_self)
    def _():
        pltpu.make_async_copy(cot_window(c), cc_mine, rs.at[2 + zl]).start()

    c_b.start()
    for u in range(4):
        pl.when(c == UNIT_CORE[u])(lambda u=u: unit_over(u).start())

    off_home = offs[0:1, 0:1]
    total_s = jnp.zeros((8, HALF0), f32)
    total_q = jnp.zeros((8, HALF0), f32)
    for k in range(8):
        lanes = pl.ds(256 * k, 256)
        mask = ((iota((8, 256), 1) + 256 * k).astype(f32) >= 2.0 * off_home).astype(bf16)
        xb = xt[:, lanes]
        xf = xb.astype(f32)
        sq = xf * xf
        hi = sq.astype(bf16)
        lo = (sq - hi.astype(f32)).astype(bf16)
        nt = ((1,), (1,))
        total_s = total_s + dot(mask, xb, nt)
        total_q = total_q + (dot(mask, hi, nt) + dot(mask, lo, nt))
    small[...] = jnp.zeros_like(small)
    small[0:1, 0:HALF0] = total_s[0:1]
    small[1:2, 0:HALF0] = total_q[0:1]
    small[2:3, 0:HALF0] = pg1[...].reshape(1, HALF0)
    small[3:4, 0:HALF0] = pb1[...].reshape(1, HALF0)
    small[4:5, 0:HALF1] = pg2[...].reshape(1, HALF1)
    small[5:6, 0:HALF1] = pb2[...].reshape(1, HALF1)
    small[6:7, 0:HALFH] = pg3[...].reshape(1, HALFH)
    small[6:7, H : H + HALFH] = pb3[...].reshape(1, HALFH)
    here = small[...]
    half_row = iota((8, PAD), 0)
    moved = jnp.where(
        half_row < 4,
        pltpu.roll(here, HALF0, 1),
        jnp.where(half_row < 6, pltpu.roll(here, HALF1, 1), pltpu.roll(here, HALFH, 1)),
    )
    here = jnp.where(zl == 0, here, moved)
    leader = (p.g == 0) & (p.zh == 0) & (c == 0)
    here = jnp.where((half_row < 2) | leader, here, 0.0)
    count = jnp.maximum(BINS - off_home, 0.0)
    lane8 = iota((8, PAD), 1)
    row8 = iota((8, PAD), 0)
    here = here + jnp.where((lane8 == PAD - 1) & (row8 == 0), count, 0.0)
    all1 = Total(p, (a1a, a1b), (as1.at[0], ar1.at[0], as2.at[0], ar2.at[0]))
    all1.start(here)
    all1.middle()

    owners_row = jnp.broadcast_to(owners[...].astype(f32), (8, 64)).astype(bf16)
    nat1 = dot(owners_row, e1[...])[0:1] * 6.0 + bw1[0:1]
    nat2 = dot(owners_row, e2[...])[0:1] * 3.0 + bw2[0:1]
    for k in range(6):
        perm[pl.ds(128 * k, 128), :] = (
            (iota((128, PAD), 0) + 128 * k).astype(f32) == nat1
        ).astype(bf16)
    perm2 = (iota((H, H), 0).astype(f32) == nat2).astype(bf16)

    row = iota((128, 128), 0)
    pick = (iota((128, 128), 1) == jnp.where(row < 64, 2 * row, 2 * row - 127)).astype(bf16)
    for k in range(2):
        remote(xw.at[k], xw.at[k], ss.at[0], rs.at[0 + k], other_core).wait_recv()
    tr[...] = jnp.zeros_like(tr)
    for k in range(9):
        lanes = pl.ds(128 * k, 128)
        tr[0, :, 0:HALF0] = dot(pick, xw[0, :, lanes], ((1,), (1,)))
        tr[1, :, 0:HALF0] = dot(pick, xw[1, :, lanes], ((1,), (1,)))
        both = (tr[0] + pltpu.roll(tr[1], HALF0, 1)).astype(bf16)
        raw[0, pl.ds(64 * k, 64), :] = both[0:64]
        raw[1, pl.ds(64 * k, 64), :] = both[64:128]

    first = all1.end()
    n1 = first[0:1, PAD - 1 : PAD]
    n2 = 0.5 * n1
    inv_n1 = 1.0 / n1
    inv_n2 = 1.0 / n2
    real = iota((1, PAD), 1) < C0
    mean1 = jnp.where(real, first[0:1], 0.0) * inv_n1
    var1 = first[1:2] * inv_n1 - mean1 * mean1
    rs1 = lax.rsqrt(var1 + eps_norm)
    gain1, bias1 = first[2:3], first[3:4]
    gain2, bias2 = first[4:5], first[5:6]
    gain3, bias3 = first[6:7, 0:H], first[6:7, H : 2 * H]

    remote(offs, offw, ss.at[4], rs.at[4], other_core).wait()
    off = jnp.where(is_self, offs[0:1, 0:1], offw[0:1, 0:1])

    bin0 = 496 * c
    own0 = pl.multiple_of(16 * c, 16)
    raw0 = pl.multiple_of(48 * c, 16)
    rawown = pl.multiple_of(64 * c, 16)

    def valid_mask(rows, at=0):
        return ((iota((rows, 1), 0) + (bin0 + at)).astype(f32) >= off).astype(f32)

    def own_mask(rows, at=0):
        r = iota((rows, 1), 0) + at
        return ((r >= 16 * c) & (r < 16 * c + OWN)).astype(f32)

    not_first = (iota((WIN, 1), 0) > 0).astype(f32)
    not_last = (iota((WIN, 1), 0) < WIN - 1).astype(f32)

    def before(v):
        return (pltpu.roll(v, 1, 0) * not_first).astype(bf16)

    def after(v):
        return (pltpu.roll(v, WIN - 1, 0) * not_last).astype(bf16)

    small[0:1] = rs1 * gain1
    small[1:2] = bias1 - mean1 * (rs1 * gain1)
    small[2:3] = mean1
    small[3:4] = rs1

    @pl.loop(0, 6)
    def _(k):
        lanes = pl.ds(pl.multiple_of(128 * k, 128), 128)
        scale, shift = small[0:1, lanes], small[1:2, lanes]
        valid = valid_mask(WIN)
        for par in range(2):
            v = raw[par, pl.ds(raw0, WIN), lanes].astype(f32)
            v = gelu(v * scale + shift) * valid
            aa[par, :, lanes] = before(v)
            aa[2 + par, :, lanes] = v.astype(bf16)
            aa[4 + par, :, lanes] = after(v)

    own_w[0].wait()
    for t in range(5):

        def there(t=t):
            cp = tap_over(t)
            remote(
                ww1.at[t, :, its_lanes], ww1.at[t, :, its_lanes], ss.at[5 + t], rs.at[5 + t], flip
            ).wait_recv()
            tap_here(t).start()
            cp.wait_send()

        pl.when(c == TAP_CORE[t])(there)
    for t in range(5):
        pl.when(c == TAP_CORE[t])(lambda t=t: tap_here(t).wait_send())
        pl.when(c != TAP_CORE[t])(lambda t=t: tap_here(t).wait_recv())

    acc[...] = jnp.zeros_like(acc)

    @pl.loop(0, 3)
    def _(k):
        rows = pl.ds(pl.multiple_of(176 * k, 16), 176)
        h0 = jnp.zeros((176, C1), f32)
        for t in range(5):
            h0 = h0 + dot(aa[t, rows, 0:C0], ww1[t])
        h1 = jnp.zeros((176, C1), f32)
        for t in range(5):
            h1 = h1 + dot(aa[t + 1, rows, 0:C0], ww1[t])
        d = h0 - h1
        v = jnp.maximum(h0, h1) + (jnp.log(1.0 + jnp.exp(-jnp.abs(d))) - math.log(2.0))
        diff[rows, :] = d
        pooled[rows, :] = v
        m = valid_mask(176, 176 * k) * own_mask(176, 176 * k)
        vm = v * m
        acc[0:1] += jnp.sum(vm, axis=0, keepdims=True)
        acc[1:2] += jnp.sum(vm * v, axis=0, keepdims=True)

    all2 = Total(p, (ab1.at[0], ab2.at[0]), (as1.at[1], ar1.at[1], as2.at[1], ar2.at[1]))
    all2.start(acc[0:2])
    all2.middle()
    own_w[1].wait()
    own_w[2].wait()
    for u in range(4):

        def there_u(u=u):
            remote(
                unit_ref(u, its_rows), unit_ref(u, its_rows), ss.at[15 + u], rs.at[15 + u], flip
            ).wait_recv()
            unit_here(u).start()
            unit_over(u).wait_send()

        pl.when(c == UNIT_CORE[u])(there_u)
    for k in range(2):
        part = cc.at[:, pl.ds(384 * k, 384)]
        remote(part, part, ss.at[0], rs.at[2 + k], other_core).wait_recv()
    for u in range(4):
        pl.when(c == UNIT_CORE[u])(lambda u=u: unit_here(u).wait_send())
        pl.when(c != UNIT_CORE[u])(lambda u=u: unit_here(u).wait_recv())
    og[...] = dot(cc[...], wwp[...], ((1,), (1,)))

    @pl.when(not_self)
    def _():
        x_a.wait_send()
        c_a.wait_send()

    x_b.wait_send()
    c_b.wait_send()

    second = all2.end()
    mean2 = second[0:1] * inv_n2
    var2 = second[1:2] * inv_n2 - mean2 * mean2
    rs2 = lax.rsqrt(var2 + eps_norm)
    acc[2:3] = rs2 * gain2
    acc[3:4] = bias2 - mean2 * (rs2 * gain2)
    acc[4:5] = mean2
    acc[5:6] = rs2

    @pl.loop(0, 6)
    def _(k):
        lanes = pl.ds(pl.multiple_of(128 * k, 128), 128)
        v = gelu(pooled[:, lanes] * acc[2:3, lanes] + acc[3:4, lanes]) * valid_mask(WIN)
        mm[0, :, lanes] = before(v)
        mm[1, :, lanes] = v.astype(bf16)
        mm[2, :, lanes] = after(v)

    h2 = jnp.zeros((WIN, H), f32)
    for t in range(3):
        h2 = h2 + dot(mm[t], ww2[t], ((1,), (1,)))
    hid[...] = h2
    m = valid_mask(WIN) * own_mask(WIN)
    h2m = h2 * m
    acc[6:7, 0:H] = jnp.sum(h2m, axis=0, keepdims=True)
    acc[6:7, H : 2 * H] = jnp.sum(h2m * h2, axis=0, keepdims=True)
    all3 = Total(p, (ab1.at[1], ab2.at[1]), (as1.at[2], ar1.at[2], as2.at[2], ar2.at[2]))
    all3.start(acc[6:8])
    all3.middle()
    third = all3.end()
    mean3 = third[0:1, 0:H] * inv_n2
    var3 = third[0:1, H : 2 * H] * inv_n2 - mean3 * mean3
    rs3 = lax.rsqrt(var3 + eps_norm)
    valid = valid_mask(WIN)
    own = own_mask(WIN)
    h2 = hid[...]
    scaled = (h2 - mean3) * rs3
    pre = scaled * gain3 + bias3
    no[...] = (gelu(pre) * valid).astype(bf16)
    slopes = gelu_slope(pre) * og[...] * valid
    og[...] = slopes
    hid[...] = scaled
    acc[6:7, 0:H] = jnp.sum(slopes * scaled * own, axis=0, keepdims=True)
    acc[6:7, H : 2 * H] = jnp.sum(slopes * own, axis=0, keepdims=True)
    all4 = Total(p, (ab1.at[2], ab2.at[2]), (as1.at[3], ar1.at[3], as2.at[3], ar2.at[3]))
    all4.start(acc[6:8])
    out_rows = pl.ds(pl.multiple_of(512 * c, 16), OWN)
    own_rows = pl.ds(own0, OWN)
    gp[0] = (pooled[own_rows, :] + dot(no[own_rows, :], wwp[...])).astype(bf16)
    all4.middle()

    def out_copy(k):
        return remote(
            gp.at[0, :, pl.ds(384 * k, 384)],
            out.at[out_rows, :],
            ss.at[23 + k],
            rs.at[23 + c],
            p.at(z=2 * p.zh + k, c=zl),
        )

    def out_local(k):
        return pltpu.make_async_copy(
            gp.at[0, :, pl.ds(384 * k, 384)], out.at[out_rows, :], ls.at[3]
        )

    def to_self(k):
        return (zl == k) & is_self

    for k in range(2):
        pl.when(jnp.logical_not(to_self(k)))(lambda k=k: out_copy(k).start())

        pl.when(to_self(k))(lambda k=k: out_local(k).start())

    def put2(m, value):
        s2[:, :, pl.ds(24 * m, 24), :] = value.astype(bf16).reshape(4, 4, 24, C1)

    tn = ((0,), (0,))
    nop = dot(no[own_rows, :], perm2).astype(bf16)
    put2(3, dot(nop, cc[own_rows, :], tn))
    fourth = all4.end()
    stats[4:5] = fourth[0:1]
    gain_mean = fourth[0:1, 0:H] * inv_n2
    bias_mean = fourth[0:1, H : 2 * H] * inv_n2
    hg = valid_mask(WIN) * (gain3 * rs3) * (og[...] - bias_mean - hid[...] * gain_mean)
    hh[0] = after(hg)
    hh[1] = hg.astype(bf16)
    hh[2] = before(hg)
    mid_grad = jnp.zeros((WIN, C1), f32)
    for t in range(3):
        mid_grad = mid_grad + dot(hh[t], ww2[t])
    mid[...] = mid_grad

    @pl.loop(0, 6)
    def _(k):
        lanes = pl.ds(pl.multiple_of(128 * k, 128), 128)
        v = pooled[:, lanes]
        slopes = gelu_slope(v * acc[2:3, lanes] + acc[3:4, lanes]) * mid[:, lanes] * valid_mask(WIN)
        scaled = (v - acc[4:5, lanes]) * acc[5:6, lanes]
        mid[:, lanes] = slopes
        pooled[:, lanes] = scaled
        mine = slopes * own_mask(WIN)
        acc[0:1, lanes] = jnp.sum(mine * scaled, axis=0, keepdims=True)
        acc[1:2, lanes] = jnp.sum(mine, axis=0, keepdims=True)

    all5 = Total(p, (ab1.at[3], ab2.at[3]), (as1.at[4], ar1.at[4], as2.at[4], ar2.at[4]))
    all5.start(acc[0:2])
    hp = dot(hh[1, own_rows, :], perm2).astype(bf16)
    put2(0, dot(hp, mm[0, own_rows, :], tn))
    all5.middle()
    for t in range(1, 3):
        put2(t, dot(hp, mm[t, own_rows, :], tn))
    s2_over = remote(s2.at[:, :, :, others], t2, gs.at[0], gr.at[0], other_core)
    s2_over.start()
    fifth = all5.end()
    stats[2:4] = fifth
    acc[0:2] = fifth * inv_n2

    @pl.loop(0, 6)
    def _(k):
        lanes = pl.ds(pl.multiple_of(128 * k, 128), 128)
        back = acc[2:3, lanes] * (
            mid[:, lanes] - acc[1:2, lanes] - pooled[:, lanes] * acc[0:1, lanes]
        )
        pg = cc[:, lanes].astype(f32) + back * valid_mask(WIN)
        even = 1.0 / (1.0 + jnp.exp(-diff[:, lanes]))
        ge = pg * even
        go = pg * (1.0 - even)
        gg[0, :, lanes] = after(go)
        gg[1, :, lanes] = after(ge)
        gg[2, :, lanes] = go.astype(bf16)
        gg[3, :, lanes] = ge.astype(bf16)
        gg[4, :, lanes] = before(go)
        gg[5, :, lanes] = before(ge)

    def total(own, parts):
        v = own.astype(f32)
        for part in parts:
            v = v + part.astype(f32)
        return v.astype(bf16)

    def along(k, axis):
        if axis == "x":
            i = lax.rem(p.x + k + 1, 4)
            return p.at(x=i), i
        i = lax.rem(p.y + k + 1, 4)
        return p.at(y=i), i

    s2_over.wait()
    t2[...] = total(t2[...], [s2[:, :, :, mine]])
    flying = []

    def send(src, dst, sem, device):
        cp = remote(src, dst, gs.at[sem], gr.at[sem], device)
        cp.start()
        flying.append(cp)

    def arrived(dst, sem):
        remote(dst, dst, gs.at[0], gr.at[sem], other_core).wait_recv()

    for k in range(3):
        device, i = along(k, "y")
        send(t2.at[:, i], rd.at[k], 1 + k, device)

    for k in range(2):

        def out_sent(k=k):
            out_copy(k).wait_send()

        pl.when(jnp.logical_not(to_self(k)))(out_sent)
        pl.when(to_self(k))(lambda k=k: out_local(k).wait())
    gp[0] = dot(gg[3, own_rows, :], perm[...]).astype(bf16)
    gp[1] = dot(gg[2, own_rows, :], perm[...]).astype(bf16)

    TAP_AXIS = ("x", "y", "x", "y", "x")

    def to_core(t):
        return remote(s1.at[t, :, :, :, others], t1.at[t], gs.at[7 + t], gr.at[7 + t], other_core)

    def to_axis(t):
        to_core(t).wait_recv()
        t1[t] = total(t1[t], [s1[t, :, :, :, mine]])
        for k in range(3):
            device, i = along(k, TAP_AXIS[t])
            src = t1.at[t, i] if TAP_AXIS[t] == "x" else t1.at[t, :, i]
            send(src, ra.at[t, k], 12 + 3 * t + k, device)

    def to_other_axis(t):
        for k in range(3):
            arrived(ra.at[t, k], 12 + 3 * t + k)
        own_part = t1[t, p.x] if TAP_AXIS[t] == "x" else t1[t, :, p.y]
        ua[t] = total(own_part, [ra[t, k] for k in range(3)])
        for k in range(3):
            device, i = along(k, "y" if TAP_AXIS[t] == "x" else "x")
            send(ua.at[t, i], rb.at[t, k], 27 + 3 * t + k, device)

    def last_of(t):
        for k in range(3):
            arrived(rb.at[t, k], 27 + 3 * t + k)
        own_part = ua[t, p.y] if TAP_AXIS[t] == "x" else ua[t, p.x]
        va[t] = total(own_part, [rb[t, k] for k in range(3)])

    for t in range(5):
        part = dot(gp[0], aa[t, own_rows, 0:C0], tn) + dot(gp[1], aa[t + 1, own_rows, 0:C0], tn)
        part = part.astype(bf16).reshape(4, 4, 48, C0)
        s1[t, :, :, :, 0:C0] = part
        s1[t, :, :, :, C0:PAD] = jnp.zeros((4, 4, 48, PAD - C0), bf16)
        to_core(t).start()
        if t > 0:
            to_axis(t - 1)
    to_axis(4)
    for k in range(3):
        arrived(rd.at[k], 1 + k)
    uc[...] = total(t2[:, p.y], [rd[k] for k in range(3)])
    for k in range(3):
        device, i = along(k, "x")
        send(uc.at[i], re.at[k], 4 + k, device)

    def slope_part(half, par, k):
        return (
            gp.at[par, pl.ds(256 * k, 256), pl.ds(384 * half, 384)],
            sl_home.at[c, par, pl.ds(256 * k, 256), :],
        )

    def slope_copy(half, par, k):
        src, dst = slope_part(half, par, k)
        n = 2 * par + k
        return remote(src, dst, ss.at[25 + 4 * half + n], rs.at[25 + 4 * c + n], p.at(z=2 * p.zh + half, c=zl))

    def slope_local(half, par, k):
        src, dst = slope_part(half, par, k)
        return pltpu.make_async_copy(src, dst, rs.at[25 + 4 * c + 2 * par + k])

    small[4:6] = jnp.zeros((2, PAD), f32)
    for par in range(2):
        for k in range(2):
            rows = pl.ds(pl.multiple_of(own0 + 256 * k, 16), 256)
            v = jnp.zeros((256, C0), f32)
            for t in range(5):
                v = v + dot(gg[t + 1 - par, rows, :], ww1[t], ((1,), (1,)))
            slope[:, 0:C0] = v
            slope[:, C0:PAD] = jnp.zeros((256, PAD - C0), f32)

            @pl.loop(0, 6)
            def _(q, par=par, k=k):
                lanes = pl.ds(pl.multiple_of(128 * q, 128), 128)
                xv = raw[par, pl.ds(pl.multiple_of(rawown + 256 * k, 16), 256), lanes].astype(f32)
                valid = valid_mask(256, 16 * c + 256 * k)
                slopes = gelu_slope(xv * small[0:1, lanes] + small[1:2, lanes]) * slope[:, lanes] * valid
                scaled = (xv - small[2:3, lanes]) * small[3:4, lanes]
                slope[:, lanes] = slopes
                small[4:5, lanes] += jnp.sum(slopes * scaled, axis=0, keepdims=True)
                small[5:6, lanes] += jnp.sum(slopes, axis=0, keepdims=True)

            dst = pl.ds(256 * k, 256)
            gp[par, dst, 0:384] = slope[:, 0:384].astype(bf16)
            gp[par, dst, 384:768] = pltpu.roll(slope[...], PAD - HALF0, 1)[:, 0:384].astype(bf16)
            for half in range(2):

                def send_slope(half=half, par=par, k=k):
                    slope_copy(half, par, k).start()

                def keep_slope(half=half, par=par, k=k):
                    slope_local(half, par, k).start()

                pl.when(jnp.logical_not(to_self(half)))(send_slope)
                pl.when(to_self(half))(keep_slope)
            if (par, k) == (1, 0):
                to_other_axis(0)
                to_other_axis(1)

    all6 = Total(p, (ab1.at[4], ab2.at[4]), (as1.at[5], ar1.at[5], as2.at[5], ar2.at[5]))
    all6.start(small[4:6])

    to_other_axis(2)
    all6.middle()
    to_other_axis(3)
    for t in range(2):
        last_of(t)
    sixth = all6.end()
    stats[0:2] = sixth
    stats[5:6] = mean1
    stats[6:7] = rs1
    stats[7:8] = rs1 * gain1
    stats[8:10] = sixth * inv_n1
    stats[10:16] = jnp.zeros((6, PAD), f32)
    to_other_axis(4)
    for k in range(3):
        arrived(re.at[k], 4 + k)
    vc = total(uc[p.x], [re[k] for k in range(3)])
    for t in range(2, 5):
        last_of(t)
    g1 = dot(rep1[...], va[...].reshape(240, 384))
    g2 = dot(rep2[...], vc)
    for e in range(8):
        pz[e, 0:48] = g1[48 * e : 48 * e + 48].astype(bf16)
        pz[e, 48:80] = g2[32 * e : 32 * e + 32].astype(bf16)
    for k, (device, zi, ci) in enumerate(column_peers(p)):
        cp = remote(pz.at[2 * zi + ci], rz.at[p.e], gs.at[42 + k], gr.at[42 + p.e], device)
        cp.start()
        flying.append(cp)
    rz[p.e] = pz[p.e]
    for device, zi, ci in column_peers(p):
        e = 2 * zi + ci
        arrived(rz.at[e], 42 + e)
    for half in range(2):
        v = rz[half].astype(f32)
        for k in range(1, 4):
            v = v + rz[2 * k + half].astype(f32)
        grad[:, 384 * half : 384 * half + 384] = v

    for t in range(5):
        to_core(t).wait_send()
    for cp in flying:
        cp.wait_send()
    for half in range(2):
        for par in range(2):
            for k in range(2):

                def slope_sent(half=half, par=par, k=k):
                    slope_copy(half, par, k).wait_send()

                pl.when(jnp.logical_not(to_self(half)))(slope_sent)
    for j in range(2):

        def out_here(j=j):
            rows = out.at[pl.ds(512 * j, 512), :]
            remote(rows, rows, ss.at[0], rs.at[23 + j], other_core).wait_recv()

        pl.when(jnp.logical_not(is_self & (c == j)))(out_here)
    for j in range(2):
        for par in range(2):
            for k in range(2):
                part = sl_home.at[j, par, pl.ds(256 * k, 256), :]
                remote(part, part, ss.at[0], rs.at[25 + 4 * j + 2 * par + k], other_core).wait_recv()


VMEM = pl.BlockSpec(memory_space=pltpu.VMEM)
ANY = pl.BlockSpec(memory_space=pl.ANY)


def run_step(xt, offsets, owners, cot, w1, w2, wp, params, consts):
    shape = jax.ShapeDtypeStruct
    dma = pltpu.SemaphoreType.DMA
    scratch = [
        pltpu.VMEM((5, 4, 4, 48, PAD), bf16),
        pltpu.VMEM((4, 4, 96, C1), bf16),
        pltpu.VMEM((2, HALF0, LANES), bf16),
        pltpu.VMEM((2, 576, PAD), bf16),
        pltpu.VMEM((6, WIN, PAD), bf16),
        pltpu.VMEM((5, C0, C1), bf16),
        pltpu.VMEM((3, H, C1), bf16),
        pltpu.VMEM((H, C1), bf16),
        pltpu.VMEM((WIN, C1), f32),
        pltpu.VMEM((WIN, C1), f32),
        pltpu.VMEM((WIN, C1), bf16),
        pltpu.VMEM((WIN, H), f32),
        pltpu.VMEM((WIN, H), f32),
        pltpu.VMEM((WIN, H), bf16),
        pltpu.VMEM((3, WIN, H), bf16),
        pltpu.VMEM((WIN, C1), f32),
        pltpu.VMEM((6, WIN, C1), bf16),
        pltpu.VMEM((2, OWN, C1), bf16),
        pltpu.VMEM((C1, C1), bf16),
        pltpu.VMEM((256, PAD), f32),
        pltpu.VMEM((8, PAD), f32),
        pltpu.VMEM((8, 128), f32),
        pltpu.VMEM((8, 128), f32),
        pltpu.VMEM((8, PAD), f32),
        pltpu.VMEM((2, 128, PAD), f32),
        pltpu.VMEM((5, 4, 4, 48, 384), bf16),
        pltpu.VMEM((4, 4, 96, 384), bf16),
        pltpu.VMEM((5, 3, 4, 48, 384), bf16),
        pltpu.VMEM((5, 3, 48, 384), bf16),
        pltpu.VMEM((3, 4, 96, 384), bf16),
        pltpu.VMEM((3, 96, 384), bf16),
        pltpu.VMEM((5, 4, 48, 384), bf16),
        pltpu.VMEM((4, 96, 384), bf16),
        pltpu.VMEM((5, 48, 384), bf16),
        pltpu.VMEM((8, 80, 384), bf16),
        pltpu.VMEM((8, 80, 384), bf16),
        pltpu.VMEM((8, 8, PAD), f32),
        pltpu.VMEM((16, 8, PAD), f32),
        pltpu.VMEM((5, 8, 2, PAD), f32),
        pltpu.VMEM((5, 16, 2, PAD), f32),
        dma((40,)),
        dma((40,)),
        dma((4,)),
        dma((6, 8)),
        dma((6, 8)),
        dma((6, 16)),
        dma((6, 16)),
        dma((52,)),
        dma((52,)),
    ]
    return pl.pallas_call(
        step_kernel,
        out_shape=(
            shape((BINS, 384), bf16),
            shape((2, 2, OWN, 384), bf16),
            shape((80, PAD), f32),
            shape((16, PAD), f32),
        ),
        in_specs=[VMEM, VMEM, VMEM, ANY, ANY, ANY, ANY] + [VMEM] * 12,
        out_specs=(ANY, ANY, VMEM, VMEM),
        scratch_shapes=scratch,
        compiler_params=pltpu.CompilerParams(
            collective_id=0, has_side_effects=True, vmem_limit_bytes=63 * 2**20
        ),
    )(
        xt, offsets, owners, cot, w1, w2, wp, *params,
        *[consts[n] for n in ("e1", "bw1", "e2", "bw2", "rep1", "rep2")],
    )


def adam_block(first, second, turned):
    first_new = beta_one * first + (1.0 - beta_one) * turned
    second_new = beta_two * second + (1.0 - beta_two) * turned * turned
    direction = (
        first_new
        / (1.0 - beta_one**STEP)
        / (jnp.sqrt(second_new / (1.0 - beta_two**STEP)) + adam_eps)
    )
    return first_new, second_new, direction


def master_block(master, update, rate, average):
    master_new = master - rate * (update + decay_rate * master)
    return master_new, average_rate * average + (1.0 - average_rate) * master_new


def owner_kernel(
    grad, b1, b2, b3,
    m1, f1, q1, a1, m2, f2, q2, a2, m3, f3, q3, a3, pack_a, pack_b,
    ga, gb, nm1, nf1, nq1, na1, nm2, nf2, nq2, na2, nm3, nf3, nq3, na3,
    dd, nb, near, fa, fb, pa, pb,
    ss, rs, ls,
):
    p = Place()
    x, y, zh, zl, z, c = p.x, p.y, p.zh, p.zl, p.z, p.c
    other_core = p.at(c=1 - c)
    over = p.at(z=lax.rem(z + 2, 4))
    xs = [(p.at(x=lax.rem(x + k, 4)), lax.rem(x + k, 4)) for k in (1, 2, 3)]
    ys = [(p.at(y=lax.rem(y + k, 4)), lax.rem(y + k, 4)) for k in (1, 2, 3)]
    bar = pltpu.get_barrier_semaphore()
    for device in [d for d, _ in xs + ys] + [other_core, over]:
        pl.semaphore_signal(bar, inc=1, device_id=device, device_id_type=MESH)

    nt = ((1,), (1,))
    nb[...] = jnp.zeros_like(nb)
    dd[...] = jnp.zeros_like(dd)
    basis1 = b1[...].astype(bf16)
    turned = dot(grad[0:40, 0:C0].astype(bf16), basis1)
    for t in range(5):
        first_new, second_new, direction = adam_block(f1[t], q1[t], turned[8 * t : 8 * t + 6])
        nf1[t] = first_new
        nq1[t] = second_new
        dd[8 * t : 8 * t + 6, 0:C0] = direction
    update = dot(dd[0:40, 0:C0].astype(bf16), basis1, nt)
    row_of = (0, 8, 16, 32, 40)
    for t in range(5):
        master_new, average_new = master_block(m1[t], update[8 * t : 8 * t + 6], 0.02, a1[t])
        nm1[t] = master_new
        na1[t] = average_new
        nb[row_of[t] : row_of[t] + 6, 0:C0] = master_new
    basis2 = b2[...].astype(bf16)
    turned = dot(grad[48:72].astype(bf16), basis2)
    for t in range(3):
        first_new, second_new, direction = adam_block(f2[t], q2[t], turned[8 * t : 8 * t + 3])
        nf2[t] = first_new
        nq2[t] = second_new
        dd[40 + 8 * t : 43 + 8 * t, :] = direction
    update = dot(dd[40:64].astype(bf16), basis2, nt)
    for t in range(3):
        master_new, average_new = master_block(m2[t], update[8 * t : 8 * t + 3], 0.02, a2[t])
        nm2[t] = master_new
        na2[t] = average_new
        nb[48 + 4 * t : 51 + 4 * t, :] = master_new
    basis3 = b3[...].astype(bf16)
    turned = dot(grad[72:80].astype(bf16), basis3)
    first_new, second_new, direction = adam_block(f3[...], q3[...], turned[0:3])
    nf3[...] = first_new
    nq3[...] = second_new
    dd[64:67] = direction
    update = dot(dd[64:72].astype(bf16), basis3, nt)
    master_new, average_new = master_block(m3[...], update[0:3], 0.05, a3[...])
    nm3[...] = master_new
    na3[...] = average_new
    nb[24:27, :] = master_new

    pl.semaphore_wait(bar, 8)
    flying = []

    def send(src, dst, sem, device, at=None):
        cp = remote(src, dst, ss.at[sem], rs.at[sem if at is None else at], device)
        cp.start()
        flying.append(cp)

    def arrived(dst, sem):
        remote(dst, dst, ss.at[0], rs.at[sem], other_core).wait_recv()

    near[zh] = nb[...].astype(bf16)
    send(near.at[zh], near.at[zh], 0, over)
    arrived(near.at[1 - zh], 0)
    fa[y] = near[:, 0:32]
    fb[x] = near[:, 32:64]
    for k in range(3):
        send(near.at[:, pl.ds(0, 32)], fa.at[y], 1 + k, ys[k][0])
        send(near.at[:, pl.ds(32, 32)], fb.at[x], 4 + k, xs[k][0])
    for k in range(3):
        arrived(fa.at[lax.rem(y + 3 - k, 4)], 1 + k)
    pa[...] = dot(pack_a[...], fa[...].reshape(256, PAD)).astype(bf16)
    for k in range(3):
        send(pa, ga.at[c, x], 7 + k, xs[k][0])
    for k in range(3):
        arrived(fb.at[lax.rem(x + 3 - k, 4)], 4 + k)
    pb[...] = dot(pack_b[...], fb[...].reshape(256, PAD)).astype(bf16)
    for k in range(3):
        send(pb, gb.at[c, y], 10 + k, ys[k][0])
    send(pa, ga.at[c, x], 13, other_core, at=13)
    send(pb, gb.at[c, y], 17, other_core, at=17)
    keep = [
        pltpu.make_async_copy(pa, ga.at[c, x], ls.at[0]),
        pltpu.make_async_copy(pb, gb.at[c, y], ls.at[1]),
    ]
    for cp in keep:
        cp.start()
    for k in range(3):
        i = lax.rem(x + 3 - k, 4)
        arrived(ga.at[c, i], 7 + k)
        send(ga.at[c, i], ga.at[c, i], 14 + k, other_core)
        i = lax.rem(y + 3 - k, 4)
        arrived(gb.at[c, i], 10 + k)
        send(gb.at[c, i], gb.at[c, i], 18 + k, other_core)
    arrived(ga.at[1 - c, x], 13)
    arrived(gb.at[1 - c, y], 17)
    for k in range(3):
        arrived(ga.at[1 - c, lax.rem(x + 3 - k, 4)], 14 + k)
        arrived(gb.at[1 - c, lax.rem(y + 3 - k, 4)], 18 + k)
    for cp in keep:
        cp.wait()
    for cp in flying:
        cp.wait_send()


def run_owner(grad, bases, states, consts):
    shape = jax.ShapeDtypeStruct
    dma = pltpu.SemaphoreType.DMA
    scratch = [
        pltpu.VMEM((72, PAD), f32),
        pltpu.VMEM((64, PAD), f32),
        pltpu.VMEM((2, 64, PAD), bf16),
        pltpu.VMEM((4, 2, 32, PAD), bf16),
        pltpu.VMEM((4, 2, 32, PAD), bf16),
        pltpu.VMEM((176, PAD), bf16),
        pltpu.VMEM((176, PAD), bf16),
        dma((24,)),
        dma((24,)),
        dma((2,)),
    ]
    gathered = shape((2, 4, 176, PAD), bf16)
    return pl.pallas_call(
        owner_kernel,
        out_shape=(gathered, gathered, *[shape(a.shape, f32) for a in states]),
        in_specs=[VMEM] * (4 + 12 + 2),
        out_specs=(ANY, ANY, *[VMEM] * 12),
        scratch_shapes=scratch,
        compiler_params=pltpu.CompilerParams(
            collective_id=1, has_side_effects=True, vmem_limit_bytes=63 * 2**20
        ),
    )(grad, *bases, *states, consts["pack_a"], consts["pack_b"])


def norm_block(gradient, parameters, moments):
    first_new, second_new, direction = adam_block(moments[0], moments[1], gradient)
    return parameters - norm_rate * direction, first_new, second_new


def finish_kernel(
    xt, offsets, owners, slopes, stats, ga, gb, out_in, *rest,
):
    p = Place()
    zl = p.zl
    params = rest[0:6]
    moments = rest[6:9]
    rep_a, rep_b, at_a, at_b, rep2a, rep2b, at2a, at2b = rest[9:17]
    states_in = rest[17:29]
    out, gin, v1, v1f, v1s, v2, v2f, v2s, v3, v3f, v3s, cp1, cp2, cp3 = rest[29:43]
    states_out = rest[43:55]
    gav, gbv, held, tr, ls = rest[55:]
    copies = [
        pltpu.make_async_copy(ga, gav, ls.at[0]),
        pltpu.make_async_copy(gb, gbv, ls.at[1]),
    ]
    for cp in copies:
        cp.start()
    out[...] = out_in[...]
    for k in range(12):
        states_out[k][...] = states_in[k][...]

    vec = stats[...]
    v326 = jnp.where(zl == 0, vec, pltpu.roll(vec, PAD - HALF0, 1))
    tr[0:16, :] = v326[:, 0:384]
    tr[16:128, :] = jnp.zeros((112, 384), f32)
    cols = jnp.transpose(tr[...])
    mean_c = cols[0:HALF0, 5:6]
    rs_c = cols[0:HALF0, 6:7]
    scale_c = cols[0:HALF0, 7:8]
    gm_c = cols[0:HALF0, 8:9]
    bm_c = cols[0:HALF0, 9:10]
    off_home = offsets[...].astype(f32)
    tn = ((0,), (0,))
    rowq = iota((128, 256), 0)
    laneq = iota((128, 256), 1)
    put_even = (laneq == 2 * rowq).astype(bf16)
    put_odd = (laneq == 2 * rowq + 1).astype(bf16)
    back = []
    for j in range(2):
        for k in range(4):
            bins = pl.ds(128 * k, 128)
            st = dot(slopes[j, 0, bins, :], put_even, tn) + dot(slopes[j, 1, bins, :], put_odd, tn)
            lanes = pl.ds(1024 * j + 256 * k, 256)
            xf = xt[:, lanes].astype(f32)
            scaled = (xf - mean_c) * rs_c
            ok = ((iota((1, 256), 1) + (1024 * j + 256 * k)).astype(f32) >= 2.0 * off_home).astype(f32)
            held[:, lanes] = ok * (scale_c * (st[0:HALF0] - bm_c - scaled * gm_c))
        half = pl.ds(1024 * j, 1024)
        back.append(pltpu.make_async_copy(held.at[:, half], gin.at[:, 0, half], ls.at[2 + j]))
        back[j].start()

    grads1 = v326[0:2, 0:HALF0]
    v384 = jnp.where(zl == 0, vec, pltpu.roll(vec, PAD - HALF1, 1))
    grads2 = v384[2:4, 0:HALF1]
    v192 = jnp.where(zl == 0, vec, pltpu.roll(vec, PAD - HALFH, 1))
    halves = [(grads1[0:1], grads1[1:2]), (grads2[0:1], grads2[1:2]), (v192[4:5, 0:HALFH], v192[4:5, H : H + HALFH])]
    outs = [(v1, v1f, v1s), (v2, v2f, v2s), (v3, v3f, v3s)]
    for n in range(3):
        for r in range(2):
            old = (moments[n][0, r : r + 1, :], moments[n][1, r : r + 1, :])
            new = norm_block(halves[n][r], params[2 * n + r][...].reshape(1, -1), old)
            for q in range(3):
                outs[n][q][r : r + 1, :] = new[q]

    own_row = jnp.broadcast_to(owners[...].astype(f32), (8, 64))

    def column(rep, at, width):
        own = jnp.sum(rep[...].astype(f32) * own_row[0:1], axis=1, keepdims=True)
        return own * float(width) + at[...]

    lane = iota((384, 384), 1).astype(f32)
    place_a = (lane == column(rep_a, at_a, 6)).astype(bf16)
    place_b = (lane == column(rep_b, at_b, 6)).astype(bf16)
    own8 = own_row.astype(bf16)
    place2a = (iota((HALFH, 256), 0).astype(f32) == (dot(own8, rep2a[...])[0:1] * 3.0 + at2a[...])).astype(bf16)
    place2b = (
        iota((3 * HALFH, 640), 0).astype(f32) == (dot(own8, rep2b[...])[0:1] * 3.0 + at2b[...])
    ).astype(bf16)
    copies[0].wait()
    copies[1].wait()
    for t in range(3):
        block = gav[:, :, 48 * t : 48 * t + 48, :].reshape(384, PAD)
        cp1[t] = dot(block[:, 0:C0], place_a, tn).astype(bf16)
    for t in range(2):
        block = gbv[:, :, 48 * t : 48 * t + 48, :].reshape(384, PAD)
        cp1[3 + t] = dot(block[:, 0:C0], place_b, tn).astype(bf16)
    cp3[...] = dot(place2a, gav[:, :, 144:176, :].reshape(256, PAD)).astype(bf16)
    two = dot(place2b, gbv[:, :, 96:176, :].reshape(640, PAD)).astype(bf16)
    for t in range(3):
        cp2[t] = two[HALFH * t : HALFH * t + HALFH]
    for cp in back:
        cp.wait()


def run_finish(xt, offsets, owners, slopes, stats, ga, gb, out, params, moments, states, consts):
    shape = jax.ShapeDtypeStruct
    vec = [shape((2, n), f32) for n in (HALF0,) * 3 + (HALF1,) * 3 + (HALFH,) * 3]
    names = ("rep_a", "rep_b", "at_a", "at_b", "rep2a", "rep2b", "at2a", "at2b")
    return pl.pallas_call(
        finish_kernel,
        out_shape=(
            shape((BINS, 384), bf16),
            shape((HALF0, 1, 2 * BINS), f32),
            *vec,
            shape((5, C0, 384), bf16),
            shape((3, HALFH, C1), bf16),
            shape((HALFH, C1), bf16),
            *[shape(a.shape, f32) for a in states],
        ),
        in_specs=[VMEM] * 5 + [ANY] * 2 + [VMEM] * 30,
        out_specs=(VMEM, ANY, *[VMEM] * 24),
        scratch_shapes=[
            pltpu.VMEM((2, 4, 176, PAD), bf16),
            pltpu.VMEM((2, 4, 176, PAD), bf16),
            pltpu.VMEM((HALF0, 2 * BINS), f32),
            pltpu.VMEM((128, 384), f32),
            pltpu.SemaphoreType.DMA((4,)),
        ],
        compiler_params=pltpu.CompilerParams(vmem_limit_bytes=63 * 2**20),
    )(
        xt, offsets, owners, slopes, stats, ga, gb, out, *params, *moments,
        *[consts[n] for n in names], *states,
    )


def make_consts():
    e1 = np.zeros((64, 768), np.float32)
    bw1 = np.zeros((8, 768), np.float32)
    e2 = np.zeros((64, 384), np.float32)
    bw2 = np.zeros((8, 384), np.float32)
    for s in range(64):
        g, zh, c = s // 4, (s // 2) % 2, s % 2
        for b in range(2):
            e = (2 * zh + b) * 2 + c
            for w in range(6):
                e1[s, (g * 8 + e) * 6 + w] = 1
                bw1[:, (g * 8 + e) * 6 + w] = b * 384 + w
            for w in range(3):
                e2[s, (g * 8 + e) * 3 + w] = 1
                bw2[:, (g * 8 + e) * 3 + w] = b * 192 + w
    rep1 = np.zeros((8 * 48, 240), np.float32)
    rep2 = np.zeros((8 * 32, 96), np.float32)
    for e in range(8):
        for t in range(5):
            for w in range(6):
                rep1[e * 48 + t * 8 + w, t * 48 + e * 6 + w] = 1
        for m in range(4):
            for w in range(3):
                rep2[e * 32 + m * 8 + w, m * 24 + e * 3 + w] = 1
    pack_a = np.zeros((176, 256), np.float32)
    pack_b = np.zeros((176, 256), np.float32)
    for o in range(8):
        for w in range(6):
            for t in range(3):
                pack_a[t * 48 + o * 6 + w, o * 32 + 8 * t + w] = 1
            for t in range(2):
                pack_b[t * 48 + o * 6 + w, o * 32 + 8 * t + w] = 1
        for w in range(3):
            pack_a[144 + o * 3 + w, o * 32 + 24 + w] = 1
            for m in range(3):
                pack_b[96 + m * 24 + o * 3 + w, o * 32 + 16 + 4 * m + w] = 1
    rep_a = np.zeros((384, 64), np.float32)
    rep_b = np.zeros((384, 64), np.float32)
    at_a = np.zeros((384, 1), np.float32)
    rep2a = np.zeros((64, 256), np.float32)
    at2a = np.full((1, 256), -4096.0, np.float32)
    rep2b = np.zeros((64, 640), np.float32)
    at2b = np.full((1, 640), -4096.0, np.float32)
    for c in range(2):
        for i in range(4):
            for o in range(8):
                j, zh = o // 2, o % 2
                s_a = ((i * 4 + j) * 2 + zh) * 2 + c
                s_b = ((j * 4 + i) * 2 + zh) * 2 + c
                for w in range(6):
                    r = (c * 4 + i) * 48 + o * 6 + w
                    rep_a[r, s_a] = 1
                    rep_b[r, s_b] = 1
                    at_a[r, 0] = w
                for w in range(3):
                    r = (c * 4 + i) * 32 + o * 3 + w
                    rep2a[s_a, r] = 1
                    at2a[0, r] = w
                    for m in range(3):
                        r = (c * 4 + i) * 80 + m * 24 + o * 3 + w
                        rep2b[s_b, r] = 1
                        at2b[0, r] = m * 192 + w
    low = lambda a: jnp.asarray(a, bf16)
    return {
        "e1": low(e1), "bw1": jnp.asarray(bw1), "e2": low(e2), "bw2": jnp.asarray(bw2),
        "rep1": low(rep1), "rep2": low(rep2), "pack_a": low(pack_a), "pack_b": low(pack_b),
        "rep_a": low(rep_a), "rep_b": low(rep_b), "at_a": jnp.asarray(at_a), "at_b": jnp.asarray(at_a),
        "rep2a": low(rep2a), "rep2b": low(rep2b), "at2a": jnp.asarray(at2a), "at2b": jnp.asarray(at2b),
    }


def local(
    inputs, offsets, owners, cotangent,
    norm1_gain, norm1_bias, norm1_moments,
    norm2_gain, norm2_bias, norm2_moments,
    norm3_gain, norm3_bias, norm3_moments,
    conv1_copy, conv1_master, conv1_first, conv1_second, conv1_average, basis1,
    conv2_copy, conv2_master, conv2_first, conv2_second, conv2_average, basis2,
    project_copy, project_master, project_first, project_second, project_average, basis3,
):
    consts = make_consts()
    flip2 = lambda a: jnp.swapaxes(a, -1, -2)
    xt = flip2(inputs[0])
    offsets = offsets[None]
    owners = owners[None]
    params = [norm1_gain, norm1_bias, norm2_gain, norm2_bias, norm3_gain, norm3_bias]
    out, slopes, grad, stats = run_step(
        xt, offsets, owners, cotangent[0], conv1_copy, flip2(conv2_copy), flip2(project_copy), params, consts
    )
    states = [
        conv1_master, conv1_first, conv1_second, conv1_average,
        conv2_master, conv2_first, conv2_second, conv2_average,
        project_master, project_first, project_second, project_average,
    ]
    ga, gb, *new = run_owner(grad, (basis1, basis2, basis3), [flip2(a) for a in states], consts)
    result = run_finish(
        xt, offsets, owners, slopes, stats, ga, gb, out, params,
        (norm1_moments, norm2_moments, norm3_moments), new, consts,
    )
    out, gin, *vec = result[0:11]
    cp1, cp2, cp3 = result[11:14]
    nm1, nf1, nq1, na1, nm2, nf2, nq2, na2, nm3, nf3, nq3, na3 = [flip2(a) for a in result[14:]]
    return (
        out[None], jnp.transpose(gin, (1, 2, 0)), *vec,
        nm1, cp1, nf1, nq1, na1,
        nm2, flip2(cp2), nf2, nq2, na2,
        nm3, flip2(cp3), nf3, nq3, na3,
    )


def solution(mesh):
    finer = Mesh(mesh.devices.reshape(4, 4, 2, 2, mesh.shape["ch"]), SEQ_CH)
    owner3 = P(None, None, SEQ_CH)
    owner2 = P(None, SEQ_CH)
    half3 = P(None, None, "ch")
    in_specs = (
        P(SEQ, None, "ch"), P(SEQ), P(), P(SEQ, None, "ch"),
        P("ch"), P("ch"), half3, P("ch"), P("ch"), half3, P("ch"), P("ch"), half3,
        half3, owner3, owner3, owner3, owner3, P(),
        half3, owner3, owner3, owner3, owner3, P(),
        P(None, "ch"), owner2, owner2, owner2, owner2, P(),
    )
    vec = P(None, "ch")
    out_specs = (
        P(SEQ, None, "ch"), P(SEQ, None, "ch"), *[vec] * 9,
        owner3, half3, owner3, owner3, owner3,
        owner3, half3, owner3, owner3, owner3,
        owner2, vec, owner2, owner2, owner2,
    )
    return jax.shard_map(local, mesh=finer, in_specs=in_specs, out_specs=out_specs, check_vma=False)
```

```python
import math

import jax
import jax.numpy as jnp
import numpy as np
from jax import lax
from jax.experimental import pallas as pl
from jax.experimental.pallas import tpu as pltpu
from jax.sharding import Mesh
from jax.sharding import PartitionSpec as P

STEP = 8
SEQ = ("seq_0", "seq_1", "seq_2", "seq_3")
SEQ_CH = ("seq_0", "seq_1", "seq_2", "seq_3", "ch")
MESH = pl.DeviceIdType.MESH
bf16 = jnp.bfloat16
f32 = jnp.float32

eps_norm = 1e-05
beta_one = 0.9
beta_two = 0.95
adam_eps = 1e-08
decay_rate = 0.01
average_rate = 0.9
norm_rate = 0.05

C0, C1, H = 652, 768, 384
HALF0, HALF1, HALFH = 326, 384, 192
BINS = 1024
OWN = 512
WIN = 528
LANES = 1152
PAD = 768

GELU_K = math.sqrt(2.0 / math.pi)
GELU_C = 0.044715


def gelu(v):
    return 0.5 * v * (1.0 + jnp.tanh(GELU_K * (v + GELU_C * (v * v * v))))


def gelu_slope(v):
    square = v * v
    t = jnp.tanh(GELU_K * v * (1.0 + GELU_C * square))
    return 0.5 * (1.0 + t) + 0.5 * GELU_K * v * (1.0 - t * t) * (1.0 + 3.0 * GELU_C * square)


def dot(a, b, dims=((1,), (0,))):
    return lax.dot_general(a, b, (dims, ((), ())), preferred_element_type=f32)


def iota(shape, dim):
    return lax.broadcasted_iota(jnp.int32, shape, dim)


def adam_block(first, second, turned):
    first_new = beta_one * first + (1.0 - beta_one) * turned
    second_new = beta_two * second + (1.0 - beta_two) * turned * turned
    direction = (
        first_new
        / (1.0 - beta_one**STEP)
        / (jnp.sqrt(second_new / (1.0 - beta_two**STEP)) + adam_eps)
    )
    return first_new, second_new, direction


def master_block(master, update, rate, average):
    master_new = master - rate * (update + decay_rate * master)
    return master_new, average_rate * average + (1.0 - average_rate) * master_new


class Place:
    def __init__(self):
        self.x, self.y, self.zh, self.c, self.zl = [lax.axis_index(n) for n in SEQ_CH]
        self.z = 2 * self.zh + self.zl
        self.e = 2 * self.z + self.c
        self.g = 4 * self.x + self.y

    def at(self, **other):
        v = {"x": self.x, "y": self.y, "z": self.z, "c": self.c}
        v.update(other)
        z = v["z"]
        return (v["x"], v["y"], lax.div(z, 2), v["c"], lax.rem(z, 2))


def remote(src, dst, send, recv, device):
    return pltpu.make_async_remote_copy(
        src_ref=src, dst_ref=dst, send_sem=send, recv_sem=recv, device_id=device, device_id_type=MESH
    )


def column_peers(p):
    out = []
    for k in range(1, 8):
        z = lax.rem(p.z + k // 2, 4)
        c = lax.rem(p.c + k % 2, 2)
        out.append((p.at(z=z, c=c), z, c))
    return out


def plane_peers(p):
    out = []
    for k in range(1, 16):
        x = lax.rem(p.x + k // 4, 4)
        y = lax.rem(p.y + k % 4, 4)
        out.append((p.at(x=x, y=y), x, y))
    return out


def other_peers(p):
    over = lax.rem(p.z + 2, 4)
    out = [p.at(x=lax.rem(p.x + k, 4), c=1 - p.c) for k in (1, 2, 3)]
    out += [p.at(x=lax.rem(p.x + k, 4), z=over) for k in (1, 2, 3)]
    out += [p.at(y=lax.rem(p.y + k, 4), z=over) for k in (1, 2, 3)]
    return out


class Total:
    def __init__(self, p, bufs, sems):
        self.p = p
        self.b1, self.b2 = bufs
        self.s1, self.r1, self.s2, self.r2 = sems

    def start(self, value):
        p = self.p
        self.b1[p.e] = value
        self.c1 = []
        for k, (device, _, _) in enumerate(column_peers(p)):
            cp = remote(self.b1.at[p.e], self.b1.at[p.e], self.s1.at[k], self.r1.at[p.e], device)
            cp.start()
            self.c1.append(cp)

    def middle(self):
        p = self.p
        for device, z, c in column_peers(p):
            e = 2 * z + c
            remote(self.b1.at[e], self.b1.at[e], self.s1.at[0], self.r1.at[e], device).wait_recv()
        total = self.b1[0]
        for k in range(1, 8):
            total = total + self.b1[k]
        for cp in self.c1:
            cp.wait_send()
        self.b2[p.g] = total
        self.c2 = []
        for k, (device, _, _) in enumerate(plane_peers(p)):
            cp = remote(self.b2.at[p.g], self.b2.at[p.g], self.s2.at[k], self.r2.at[p.g], device)
            cp.start()
            self.c2.append(cp)

    def end(self):
        p = self.p
        for device, x, y in plane_peers(p):
            g = 4 * x + y
            remote(self.b2.at[g], self.b2.at[g], self.s2.at[0], self.r2.at[g], device).wait_recv()
        total = self.b2[0]
        for k in range(1, 16):
            total = total + self.b2[k]
        for cp in self.c2:
            cp.wait_send()
        return total


TAP_CORE = (0, 0, 1, 1, 0)
UNIT_CORE = (0, 1, 0, 1)


def step_kernel(
    xt, offsets, owners, cot, w1, w2, wp, pg1, pb1, pg2, pb2, pg3, pb3,
    e1, bw1, e2, bw2, rep1, rep2, pack1, pack2, b1, b2, b3,
    m1, f1, q1, a1, m2, f2, q2, a2, m3, f3, q3, a3,
    out, sl_home, stats, ga1, gb1, ga2, gb2,
    nm1, nf1, nq1, na1, nm2, nf2, nq2, na2, nm3, nf3, nq3, na3,
    s1, s2, xw, raw, aa, ww1, ww2, wwp, pooled, diff, cc, hid, og, no, hh, mid, gg, gp,
    slope, small, offs, offw, acc, tr, dv, dm,
    t1, t2, ra, rb, rd, re, ua, uc, va, pz, rz, pz2, rz2,
    b1f, bb1, grad, dd, nb, near1, near2, fa1, fb1, fa2, fb2, pa1, pb1_, pa2, pb2_,
    a1a, a1b, ab1, ab2,
    ss, rs, ls, as1, ar1, as2, ar2, gs, gr, hs, hr, bs,
):
    mm = gg.at[0:3]
    p = Place()
    offs[...] = jnp.broadcast_to(offsets[...].astype(f32), (8, 128))
    c, zl = p.c, p.zl
    flip = p.at(z=3 - p.z)
    direct = p.at(z=p.z + 1 - 2 * zl)
    other_core = p.at(c=1 - c)

    bar = pltpu.get_barrier_semaphore()
    for device, _, _ in column_peers(p):
        pl.semaphore_signal(bar, inc=1, device_id=device, device_id_type=MESH)
    for device, _, _ in plane_peers(p):
        pl.semaphore_signal(bar, inc=1, device_id=device, device_id_type=MESH)
    for device in other_peers(p):
        pl.semaphore_signal(bar, inc=1, device_id=device, device_id_type=MESH)

    mine = pl.ds(pl.multiple_of(384 * c, 128), 384)
    others = pl.ds(pl.multiple_of(384 - 384 * c, 128), 384)
    my_lanes = pl.ds(pl.multiple_of(384 * zl, 128), 384)
    its_lanes = pl.ds(pl.multiple_of(384 - 384 * zl, 128), 384)
    my_rows = pl.ds(pl.multiple_of(192 * zl, 16), 192)
    its_rows = pl.ds(pl.multiple_of(192 - 192 * zl, 16), 192)

    def unit_ref(u, rows):
        return ww2.at[u, rows, :] if u < 3 else wwp.at[rows, :]

    own_w = [pltpu.make_async_copy(w1.at[t], ww1.at[t, :, my_lanes], ls.at[t]) for t in range(5)]
    own_w += [
        pltpu.make_async_copy(w2.at[u] if u < 3 else wp, unit_ref(u, my_rows), ls.at[5 + u])
        for u in range(4)
    ]
    for cp in own_w:
        cp.start()

    pl.semaphore_wait(bar, 31)

    is_self = c == zl
    not_self = c != zl
    home_chip = 2 * p.zh + c

    def window(j, part):
        at = 896 * j + (0, 256)[part]
        return xt.at[:, pl.ds(pl.multiple_of(at, 128), (256, LANES - 256)[part])]

    def window_there(k, part):
        return xw.at[k, :, pl.ds((0, 256)[part], (256, LANES - 256)[part])]

    def cot_window(j):
        return cot.at[pl.ds(pl.multiple_of(496 * j, 16), WIN), :]

    cc_mine = cc.at[:, pl.ds(pl.multiple_of(384 * zl, 128), 384)]
    x_a = [
        remote(window(c, h), window_there(zl, h), ss.at[33 * h], rs.at[33 * h + zl], p.at(z=home_chip, c=c))
        for h in range(2)
    ]
    x_b = [
        remote(
            window(1 - c, h), window_there(zl, h), ss.at[33 * h + 1], rs.at[33 * h + zl],
            p.at(z=home_chip, c=1 - c),
        )
        for h in range(2)
    ]
    c_a = remote(cot_window(c), cc_mine, ss.at[2], rs.at[2 + zl], p.at(z=home_chip, c=c))
    c_b = remote(cot_window(1 - c), cc_mine, ss.at[3], rs.at[2 + zl], p.at(z=home_chip, c=1 - c))
    o_a = remote(offs, offw, ss.at[4], rs.at[4], other_core)

    def send_windows(h):
        pl.when(not_self)(lambda: x_a[h].start())

        def keep():
            pltpu.make_async_copy(window(c, h), window_there(zl, h), rs.at[33 * h + zl]).start()

        pl.when(is_self)(keep)
        x_b[h].start()

    send_windows(0)
    o_a.start()

    def tap_over(t):
        to = direct if t == 4 else flip
        return remote(ww1.at[t, :, my_lanes], ww1.at[t, :, my_lanes], ss.at[5 + t], rs.at[5 + t], to)

    def tap_here(t):
        return remote(
            ww1.at[t, :, its_lanes], ww1.at[t, :, its_lanes], ss.at[10 + t], rs.at[10 + t], other_core
        )

    def unit_over(u):
        return remote(
            unit_ref(u, my_rows), unit_ref(u, my_rows), ss.at[15 + u], rs.at[15 + u], flip
        )

    def unit_here(u):
        return remote(
            unit_ref(u, its_rows), unit_ref(u, its_rows), ss.at[19 + u], rs.at[19 + u], other_core
        )

    own_w[5].wait()
    pl.when(c == 0)(lambda: unit_over(0).start())

    off_home = offs[0:1, 0:1]
    total_s = jnp.zeros((8, HALF0), f32)
    total_q = jnp.zeros((8, HALF0), f32)
    for k in range(8):
        lanes = pl.ds(256 * k, 256)
        mask = ((iota((8, 256), 1) + 256 * k).astype(f32) >= 2.0 * off_home).astype(bf16)
        xb = xt[:, lanes]
        xf = xb.astype(f32)
        sq = xf * xf
        hi = sq.astype(bf16)
        lo = (sq - hi.astype(f32)).astype(bf16)
        nt = ((1,), (1,))
        total_s = total_s + dot(mask, xb, nt)
        total_q = total_q + (dot(mask, hi, nt) + dot(mask, lo, nt))
    small[...] = jnp.zeros_like(small)
    small[0:1, 0:HALF0] = total_s[0:1]
    small[1:2, 0:HALF0] = total_q[0:1]
    small[2:3, 0:HALF0] = pg1[...].reshape(1, HALF0)
    small[3:4, 0:HALF0] = pb1[...].reshape(1, HALF0)
    small[4:5, 0:HALF1] = pg2[...].reshape(1, HALF1)
    small[5:6, 0:HALF1] = pb2[...].reshape(1, HALF1)
    small[6:7, 0:HALFH] = pg3[...].reshape(1, HALFH)
    small[6:7, H : H + HALFH] = pb3[...].reshape(1, HALFH)
    here = small[...]
    half_row = iota((8, PAD), 0)
    moved = jnp.where(
        half_row < 4,
        pltpu.roll(here, HALF0, 1),
        jnp.where(half_row < 6, pltpu.roll(here, HALF1, 1), pltpu.roll(here, HALFH, 1)),
    )
    here = jnp.where(zl == 0, here, moved)
    leader = (p.g == 0) & (p.zh == 0) & (c == 0)
    here = jnp.where((half_row < 2) | leader, here, 0.0)
    count = jnp.maximum(BINS - off_home, 0.0)
    lane8 = iota((8, PAD), 1)
    row8 = iota((8, PAD), 0)
    here = here + jnp.where((lane8 == PAD - 1) & (row8 == 0), count, 0.0)
    all1 = Total(p, (a1a, a1b), (as1.at[0], ar1.at[0], as2.at[0], ar2.at[0]))
    all1.start(here)
    send_windows(1)
    for t in range(5):
        own_w[t].wait()
        pl.when(c == TAP_CORE[t])(lambda t=t: tap_over(t).start())

    @pl.when(not_self)
    def _():
        c_a.start()

    @pl.when(is_self)
    def _():
        pltpu.make_async_copy(cot_window(c), cc_mine, rs.at[2 + zl]).start()

    c_b.start()
    for u in range(1, 4):
        own_w[5 + u].wait()
        pl.when(c == UNIT_CORE[u])(lambda u=u: unit_over(u).start())
    all1.middle()

    owners_row = jnp.broadcast_to(owners[...].astype(f32), (8, 64)).astype(bf16)
    nat1 = dot(owners_row, e1[...])[0:1] * 6.0 + bw1[0:1]
    nat2 = dot(owners_row, e2[...])[0:1] * 3.0 + bw2[0:1]
    for k in range(4):
        s1[4, k] = ((iota((192, PAD), 0) + 192 * k).astype(f32) == nat1).astype(bf16).reshape(4, 48, PAD)
    perm2 = (iota((H, H), 0).astype(f32) == nat2).astype(bf16)

    row = iota((128, 128), 0)
    pick = (iota((128, 128), 1) == jnp.where(row < 64, 2 * row, 2 * row - 127)).astype(bf16)
    for k in range(2):
        for h in range(2):
            part = window_there(k, h)
            remote(part, part, ss.at[0], rs.at[33 * h + k], other_core).wait_recv()
    tr[...] = jnp.zeros_like(tr)
    for k in range(9):
        lanes = pl.ds(128 * k, 128)
        tr[0, :, 0:HALF0] = dot(pick, xw[0, :, lanes], ((1,), (1,)))
        tr[1, :, 0:HALF0] = dot(pick, xw[1, :, lanes], ((1,), (1,)))
        both = (tr[0] + pltpu.roll(tr[1], HALF0, 1)).astype(bf16)
        raw[0, pl.ds(64 * k, 64), :] = both[0:64]
        raw[1, pl.ds(64 * k, 64), :] = both[64:128]

    first = all1.end()
    n1 = first[0:1, PAD - 1 : PAD]
    n2 = 0.5 * n1
    inv_n1 = 1.0 / n1
    inv_n2 = 1.0 / n2
    real = iota((1, PAD), 1) < C0
    mean1 = jnp.where(real, first[0:1], 0.0) * inv_n1
    var1 = first[1:2] * inv_n1 - mean1 * mean1
    rs1 = lax.rsqrt(var1 + eps_norm)
    gain1, bias1 = first[2:3], first[3:4]
    gain2, bias2 = first[4:5], first[5:6]
    gain3, bias3 = first[6:7, 0:H], first[6:7, H : 2 * H]

    remote(offs, offw, ss.at[4], rs.at[4], other_core).wait()
    off = jnp.where(is_self, offs[0:1, 0:1], offw[0:1, 0:1])

    bin0 = 496 * c
    own0 = pl.multiple_of(16 * c, 16)
    raw0 = pl.multiple_of(48 * c, 16)
    rawown = pl.multiple_of(64 * c, 16)

    def valid_mask(rows, at=0):
        return ((iota((rows, 1), 0) + (bin0 + at)).astype(f32) >= off).astype(f32)

    def own_mask(rows, at=0):
        r = iota((rows, 1), 0) + at
        return ((r >= 16 * c) & (r < 16 * c + OWN)).astype(f32)

    not_first = (iota((WIN, 1), 0) > 0).astype(f32)
    not_last = (iota((WIN, 1), 0) < WIN - 1).astype(f32)

    def before(v):
        return (pltpu.roll(v, 1, 0) * not_first).astype(bf16)

    def after(v):
        return (pltpu.roll(v, WIN - 1, 0) * not_last).astype(bf16)

    small[0:1] = rs1 * gain1
    small[1:2] = bias1 - mean1 * (rs1 * gain1)
    small[2:3] = mean1
    small[3:4] = rs1

    @pl.loop(0, 6)
    def _(k):
        lanes = pl.ds(pl.multiple_of(128 * k, 128), 128)
        scale, shift = small[0:1, lanes], small[1:2, lanes]
        valid = valid_mask(WIN)
        for par in range(2):
            v = raw[par, pl.ds(raw0, WIN), lanes].astype(f32)
            v = gelu(v * scale + shift) * valid
            aa[par, :, lanes] = before(v)
            aa[2 + par, :, lanes] = v.astype(bf16)
            aa[4 + par, :, lanes] = after(v)

    for t in range(5):

        def there(t=t):
            cp = tap_over(t)
            remote(
                ww1.at[t, :, its_lanes], ww1.at[t, :, its_lanes], ss.at[5 + t], rs.at[5 + t], flip
            ).wait_recv()
            tap_here(t).start()
            cp.wait_send()

        pl.when(c == TAP_CORE[t])(there)
    for t in range(5):
        pl.when(c == TAP_CORE[t])(lambda t=t: tap_here(t).wait_send())
        pl.when(c != TAP_CORE[t])(lambda t=t: tap_here(t).wait_recv())

    acc[...] = jnp.zeros_like(acc)

    @pl.loop(0, 3)
    def _(k):
        rows = pl.ds(pl.multiple_of(176 * k, 16), 176)
        h0 = jnp.zeros((176, C1), f32)
        for t in range(5):
            h0 = h0 + dot(aa[t, rows, 0:C0], ww1[t])
        h1 = jnp.zeros((176, C1), f32)
        for t in range(5):
            h1 = h1 + dot(aa[t + 1, rows, 0:C0], ww1[t])
        d = h0 - h1
        v = jnp.maximum(h0, h1) + (jnp.log(1.0 + jnp.exp(-jnp.abs(d))) - math.log(2.0))
        diff[rows, :] = d
        pooled[rows, :] = v
        m = valid_mask(176, 176 * k) * own_mask(176, 176 * k)
        vm = v * m
        acc[0:1] += jnp.sum(vm, axis=0, keepdims=True)
        acc[1:2] += jnp.sum(vm * v, axis=0, keepdims=True)

    all2 = Total(p, (ab1.at[0], ab2.at[0]), (as1.at[1], ar1.at[1], as2.at[1], ar2.at[1]))
    all2.start(acc[0:2])

    def early_slopes(par):
        @pl.loop(0, 6)
        def _(q):
            lanes = pl.ds(pl.multiple_of(128 * q, 128), 128)
            xv = raw[par, pl.ds(rawown, OWN), lanes].astype(f32)
            turn = gelu_slope(xv * small[0:1, lanes] + small[1:2, lanes])
            dv[par, :, lanes] = (turn * valid_mask(OWN, 16 * c)).astype(bf16)

    early_slopes(0)
    all2.middle()
    for u in range(4):

        def there_u(u=u):
            remote(
                unit_ref(u, its_rows), unit_ref(u, its_rows), ss.at[15 + u], rs.at[15 + u], flip
            ).wait_recv()
            unit_here(u).start()
            unit_over(u).wait_send()

        pl.when(c == UNIT_CORE[u])(there_u)
    for k in range(2):
        part = cc.at[:, pl.ds(384 * k, 384)]
        remote(part, part, ss.at[0], rs.at[2 + k], other_core).wait_recv()
    for u in range(4):
        pl.when(c == UNIT_CORE[u])(lambda u=u: unit_here(u).wait_send())
        pl.when(c != UNIT_CORE[u])(lambda u=u: unit_here(u).wait_recv())
    og[...] = dot(cc[...], wwp[...], ((1,), (1,)))
    early_slopes(1)

    @pl.when(not_self)
    def _():
        x_a[0].wait_send()
        x_a[1].wait_send()
        c_a.wait_send()

    x_b[0].wait_send()
    x_b[1].wait_send()
    c_b.wait_send()

    second = all2.end()
    mean2 = second[0:1] * inv_n2
    var2 = second[1:2] * inv_n2 - mean2 * mean2
    rs2 = lax.rsqrt(var2 + eps_norm)
    acc[2:3] = rs2 * gain2
    acc[3:4] = bias2 - mean2 * (rs2 * gain2)
    acc[4:5] = mean2
    acc[5:6] = rs2

    @pl.loop(0, 6)
    def _(k):
        lanes = pl.ds(pl.multiple_of(128 * k, 128), 128)
        v = gelu(pooled[:, lanes] * acc[2:3, lanes] + acc[3:4, lanes]) * valid_mask(WIN)
        mm[0, :, lanes] = before(v)
        mm[1, :, lanes] = v.astype(bf16)
        mm[2, :, lanes] = after(v)

    h2 = jnp.zeros((WIN, H), f32)
    for t in range(3):
        h2 = h2 + dot(mm[t], ww2[t], ((1,), (1,)))
    hid[...] = h2
    m = valid_mask(WIN) * own_mask(WIN)
    h2m = h2 * m
    acc[6:7, 0:H] = jnp.sum(h2m, axis=0, keepdims=True)
    acc[6:7, H : 2 * H] = jnp.sum(h2m * h2, axis=0, keepdims=True)
    all3 = Total(p, (ab1.at[1], ab2.at[1]), (as1.at[2], ar1.at[2], as2.at[2], ar2.at[2]))
    all3.start(acc[6:8])

    def basis_rows(src, first, size, buf, sem):
        return pltpu.make_async_copy(src.at[pl.ds(first, size)], buf, bs.at[sem])

    slope_buf = [slope.at[pl.ds(0, 128)], slope.at[pl.ds(128, 128)]]
    rows_buf = slope_buf + [tr.at[0], tr.at[1]]

    def rounds(n):
        got = []
        for k in range(4):
            block = 4 * n + k
            src = b2 if block < 6 else b3
            got.append(basis_rows(src, 128 * (block % 6), 128, rows_buf[k], k))
        return got

    def keep_round(n):
        for k, cp in enumerate(rounds(n)):
            cp.wait()
            block = 4 * n + k
            half, at = block // 3, 128 * (block % 3)
            value = rows_buf[k][...].astype(bf16)
            if half < 3:
                ww2[half, pl.ds(at, 128), :] = value
            else:
                wwp[pl.ds(at, 128), :] = value

    first_basis = pltpu.make_async_copy(b1, b1f, bs.at[4])
    first_basis.start()

    @pl.loop(0, 6)
    def _(q):
        lanes = pl.ds(pl.multiple_of(128 * q, 128), 128)
        turn = gelu_slope(pooled[:, lanes] * acc[2:3, lanes] + acc[3:4, lanes])
        dm[:, lanes] = (turn * valid_mask(WIN)).astype(bf16)

    all3.middle()

    @pl.loop(0, 6)
    def _(q):
        lanes = pl.ds(pl.multiple_of(128 * q, 128), 128)
        diff[:, lanes] = 1.0 / (1.0 + jnp.exp(-diff[:, lanes]))

    first_basis.wait()
    bb1[...] = b1f[...].astype(bf16)
    third = all3.end()
    mean3 = third[0:1, 0:H] * inv_n2
    var3 = third[0:1, H : 2 * H] * inv_n2 - mean3 * mean3
    rs3 = lax.rsqrt(var3 + eps_norm)
    valid = valid_mask(WIN)
    own = own_mask(WIN)
    h2 = hid[...]
    scaled = (h2 - mean3) * rs3
    pre = scaled * gain3 + bias3
    no[...] = (gelu(pre) * valid).astype(bf16)
    slopes = gelu_slope(pre) * og[...] * valid
    og[...] = slopes
    hid[...] = scaled
    acc[6:7, 0:H] = jnp.sum(slopes * scaled * own, axis=0, keepdims=True)
    acc[6:7, H : 2 * H] = jnp.sum(slopes * own, axis=0, keepdims=True)
    all4 = Total(p, (ab1.at[2], ab2.at[2]), (as1.at[3], ar1.at[3], as2.at[3], ar2.at[3]))
    all4.start(acc[6:8])
    out_rows = pl.ds(pl.multiple_of(512 * c, 16), OWN)
    own_rows = pl.ds(own0, OWN)
    gp[0] = (pooled[own_rows, :] + dot(no[own_rows, :], wwp[...])).astype(bf16)
    all4.middle()

    def out_copy(k):
        return remote(
            gp.at[0, :, pl.ds(384 * k, 384)],
            out.at[out_rows, :],
            ss.at[23 + k],
            rs.at[23 + c],
            p.at(z=2 * p.zh + k, c=zl),
        )

    def out_local(k):
        return pltpu.make_async_copy(
            gp.at[0, :, pl.ds(384 * k, 384)], out.at[out_rows, :], ls.at[9]
        )

    def to_self(k):
        return (zl == k) & is_self

    for k in range(2):
        pl.when(jnp.logical_not(to_self(k)))(lambda k=k: out_copy(k).start())

        pl.when(to_self(k))(lambda k=k: out_local(k).start())

    def put2(m, value):
        s2[:, :, pl.ds(24 * m, 24), :] = value.astype(bf16).reshape(4, 4, 24, C1)

    tn = ((0,), (0,))
    nop = dot(no[own_rows, :], perm2).astype(bf16)
    put2(3, dot(nop, cc[own_rows, :], tn))
    for cp in rounds(0):
        cp.start()
    fourth = all4.end()
    stats[4:5] = fourth[0:1]
    gain_mean = fourth[0:1, 0:H] * inv_n2
    bias_mean = fourth[0:1, H : 2 * H] * inv_n2
    hg = valid_mask(WIN) * (gain3 * rs3) * (og[...] - bias_mean - hid[...] * gain_mean)
    hh[0] = after(hg)
    hh[1] = hg.astype(bf16)
    hh[2] = before(hg)
    mid_grad = jnp.zeros((WIN, C1), f32)
    for t in range(3):
        mid_grad = mid_grad + dot(hh[t], ww2[t])
    mid[...] = mid_grad

    @pl.loop(0, 6)
    def _(k):
        lanes = pl.ds(pl.multiple_of(128 * k, 128), 128)
        v = pooled[:, lanes]
        slopes = dm[:, lanes].astype(f32) * mid[:, lanes]
        scaled = (v - acc[4:5, lanes]) * acc[5:6, lanes]
        mid[:, lanes] = slopes
        pooled[:, lanes] = scaled
        mine = slopes * own_mask(WIN)
        acc[0:1, lanes] = jnp.sum(mine * scaled, axis=0, keepdims=True)
        acc[1:2, lanes] = jnp.sum(mine, axis=0, keepdims=True)

    all5 = Total(p, (ab1.at[3], ab2.at[3]), (as1.at[4], ar1.at[4], as2.at[4], ar2.at[4]))
    all5.start(acc[0:2])
    hp = dot(hh[1, own_rows, :], perm2).astype(bf16)
    put2(0, dot(hp, mm[0, own_rows, :], tn))
    keep_round(0)
    all5.middle()
    for cp in rounds(1):
        cp.start()
    for t in range(1, 3):
        put2(t, dot(hp, mm[t, own_rows, :], tn))
    s2_over = remote(s2.at[:, :, :, others], t2, gs.at[0], gr.at[0], other_core)
    s2_over.start()
    keep_round(1)
    for cp in rounds(2):
        cp.start()
    fifth = all5.end()
    stats[2:4] = fifth
    acc[0:2] = fifth * inv_n2

    @pl.loop(0, 6)
    def _(k):
        lanes = pl.ds(pl.multiple_of(128 * k, 128), 128)
        back = acc[2:3, lanes] * (
            mid[:, lanes] - acc[1:2, lanes] - pooled[:, lanes] * acc[0:1, lanes]
        )
        pg = cc[:, lanes].astype(f32) + back * valid_mask(WIN)
        even = diff[:, lanes]
        ge = pg * even
        go = pg * (1.0 - even)
        gg[0, :, lanes] = after(go)
        gg[1, :, lanes] = after(ge)
        gg[2, :, lanes] = go.astype(bf16)
        gg[3, :, lanes] = ge.astype(bf16)
        gg[4, :, lanes] = before(go)
        gg[5, :, lanes] = before(ge)

    def total(own, parts):
        v = own.astype(f32)
        for part in parts:
            v = v + part.astype(f32)
        return v.astype(bf16)

    def along(k, axis):
        if axis == "x":
            i = lax.rem(p.x + k + 1, 4)
            return p.at(x=i), i
        if axis == "z":
            i = lax.rem(p.z + k + 1, 4)
            return p.at(z=i), i
        i = lax.rem(p.y + k + 1, 4)
        return p.at(y=i), i

    s2_over.wait()
    t2[...] = total(t2[...], [s2[:, :, :, mine]])
    flying = []

    def send(src, dst, sem, device):
        cp = remote(src, dst, gs.at[sem], gr.at[sem], device)
        cp.start()
        flying.append(cp)

    def arrived(dst, sem):
        remote(dst, dst, gs.at[0], gr.at[sem], other_core).wait_recv()

    for k in range(3):
        device, i = along(k, "z")
        send(t2.at[i], rd.at[k], 1 + k, device)
    keep_round(2)

    for k in range(2):

        def out_sent(k=k):
            out_copy(k).wait_send()

        pl.when(jnp.logical_not(to_self(k)))(out_sent)
        pl.when(to_self(k))(lambda k=k: out_local(k).wait())
    perm = s1[4].reshape(PAD, PAD)
    gp[0] = dot(gg[3, own_rows, :], perm).astype(bf16)
    gp[1] = dot(gg[2, own_rows, :], perm).astype(bf16)

    TAP_AXIS = ("x", "y", "x", "y", "x")

    def to_core(t):
        return remote(s1.at[t, :, :, :, others], t1.at[t], gs.at[7 + t], gr.at[7 + t], other_core)

    def to_axis(t):
        to_core(t).wait_recv()
        t1[t] = total(t1[t], [s1[t, :, :, :, mine]])
        for k in range(3):
            device, i = along(k, TAP_AXIS[t])
            src = t1.at[t, i] if TAP_AXIS[t] == "x" else t1.at[t, :, i]
            send(src, ra.at[t, k], 12 + 3 * t + k, device)

    def to_other_axis(t):
        for k in range(3):
            arrived(ra.at[t, k], 12 + 3 * t + k)
        own_part = t1[t, p.x] if TAP_AXIS[t] == "x" else t1[t, :, p.y]
        ua[t] = total(own_part, [ra[t, k] for k in range(3)])
        for k in range(3):
            device, i = along(k, "y" if TAP_AXIS[t] == "x" else "x")
            send(ua.at[t, i], rb.at[t, k], 27 + 3 * t + k, device)

    def last_of(t):
        for k in range(3):
            arrived(rb.at[t, k], 27 + 3 * t + k)
        own_part = ua[t, p.y] if TAP_AXIS[t] == "x" else ua[t, p.x]
        va[t] = total(own_part, [rb[t, k] for k in range(3)])

    for t in range(5):
        part = dot(gp[0], aa[t, own_rows, 0:C0], tn) + dot(gp[1], aa[t + 1, own_rows, 0:C0], tn)
        part = part.astype(bf16).reshape(4, 4, 48, C0)
        s1[t, :, :, :, 0:C0] = part
        s1[t, :, :, :, C0:PAD] = jnp.zeros((4, 4, 48, PAD - C0), bf16)
        to_core(t).start()
        if t > 0:
            to_axis(t - 1)
    to_axis(4)

    def second_of_two():
        for k in range(3):
            arrived(rd.at[k], 1 + k)
        uc[...] = total(t2[p.z], [rd[k] for k in range(3)])
        for k in range(3):
            device, i = along(k, "y")
            send(uc.at[i], re.at[k], 4 + k, device)

    def xc_peers():
        for k in range(1, 8):
            xi = lax.rem(p.x + k // 2, 4)
            ci = lax.rem(c + k % 2, 2)
            yield p.at(x=xi, c=ci), 2 * xi + ci

    def slope_part(half, par, k):
        return (
            gp.at[par, pl.ds(256 * k, 256), pl.ds(384 * half, 384)],
            sl_home.at[c, par, pl.ds(256 * k, 256), :],
        )

    def slope_copy(half, par, k):
        src, dst = slope_part(half, par, k)
        n = 2 * par + k
        return remote(src, dst, ss.at[25 + 4 * half + n], rs.at[25 + 4 * c + n], p.at(z=2 * p.zh + half, c=zl))

    def slope_local(half, par, k):
        src, dst = slope_part(half, par, k)
        return pltpu.make_async_copy(src, dst, rs.at[25 + 4 * c + 2 * par + k])

    small[4:6] = jnp.zeros((2, PAD), f32)
    for par in range(2):
        for k in range(2):
            rows = pl.ds(pl.multiple_of(own0 + 256 * k, 16), 256)
            v = jnp.zeros((256, C0), f32)
            for t in range(5):
                v = v + dot(gg[t + 1 - par, rows, :], ww1[t], ((1,), (1,)))
            slope[:, 0:C0] = v
            slope[:, C0:PAD] = jnp.zeros((256, PAD - C0), f32)

            @pl.loop(0, 6)
            def _(q, par=par, k=k):
                lanes = pl.ds(pl.multiple_of(128 * q, 128), 128)
                xv = raw[par, pl.ds(pl.multiple_of(rawown + 256 * k, 16), 256), lanes].astype(f32)
                slopes = dv[par, pl.ds(256 * k, 256), lanes].astype(f32) * slope[:, lanes]
                scaled = (xv - small[2:3, lanes]) * small[3:4, lanes]
                slope[:, lanes] = slopes
                small[4:5, lanes] += jnp.sum(slopes * scaled, axis=0, keepdims=True)
                small[5:6, lanes] += jnp.sum(slopes, axis=0, keepdims=True)

            dst = pl.ds(256 * k, 256)
            gp[par, dst, 0:384] = slope[:, 0:384].astype(bf16)
            gp[par, dst, 384:768] = pltpu.roll(slope[...], PAD - HALF0, 1)[:, 0:384].astype(bf16)
            if (par, k) == (0, 1):
                second_of_two()
            if (par, k) == (1, 0):
                to_other_axis(0)
                to_other_axis(1)

    def send_slopes(par):
        for half in range(2):
            for k in range(2):

                def send_slope(half=half, k=k):
                    slope_copy(half, par, k).start()

                def keep_slope(half=half, k=k):
                    slope_local(half, par, k).start()

                pl.when(jnp.logical_not(to_self(half)))(send_slope)
                pl.when(to_self(half))(keep_slope)

    all6 = Total(p, (ab1.at[4], ab2.at[4]), (as1.at[5], ar1.at[5], as2.at[5], ar2.at[5]))
    all6.start(small[4:6])

    to_other_axis(2)
    to_other_axis(3)
    all6.middle()
    send_slopes(0)
    for k in range(3):
        arrived(re.at[k], 4 + k)
    g2 = dot(rep2[...], total(uc[p.y], [re[k] for k in range(3)]))
    e2_own = 2 * p.x + c
    for e in range(8):
        pz2[e] = g2[32 * e : 32 * e + 32].astype(bf16)
    for k, (device, e) in enumerate(xc_peers()):
        cp = remote(pz2.at[e], rz2.at[e2_own], gs.at[50 + k], gr.at[50 + e2_own], device)
        cp.start()
        flying.append(cp)
    rz2[e2_own] = pz2[e2_own]
    to_other_axis(4)
    for t in range(4):
        last_of(t)

    def summed(parts, half):
        v = parts[half].astype(f32)
        for k in range(1, 4):
            v = v + parts[2 * k + half].astype(f32)
        return v

    for _, e in xc_peers():
        arrived(rz2.at[e], 50 + e)
    for half in range(2):
        grad[48:80, 384 * half : 384 * half + 384] = summed(rz2, half)
    nt = ((1,), (1,))
    nb[...] = jnp.zeros_like(nb)
    dd[...] = jnp.zeros_like(dd)

    def turn2(v):
        return dot(v[:, 0:384], ww2[0]) + dot(v[:, 384:768], ww2[1])

    def turn3(v):
        return dot(v[:, 0:384], ww2[2]) + dot(v[:, 384:768], wwp[...])

    turned = turn2(grad[48:72].astype(bf16))
    for t in range(3):
        first_new, second_new, direction = adam_block(f2[t], q2[t], turned[8 * t : 8 * t + 3])
        nf2[t] = first_new
        nq2[t] = second_new
        dd[40 + 8 * t : 43 + 8 * t, :] = direction
    turned = turn3(grad[72:80].astype(bf16))
    first_new, second_new, direction = adam_block(f3[...], q3[...], turned[0:3])
    nf3[...] = first_new
    nq3[...] = second_new
    dd[64:67] = direction
    d2 = dd[40:64].astype(bf16)
    update = jnp.concatenate([dot(d2, ww2[0], nt), dot(d2, ww2[1], nt)], axis=1)
    row_of_two = (68, 80, 84)
    for t in range(3):
        master_new, average_new = master_block(m2[t], update[8 * t : 8 * t + 3], 0.02, a2[t])
        nm2[t] = master_new
        na2[t] = average_new
        nb[row_of_two[t] : row_of_two[t] + 3, :] = master_new
    d3 = dd[64:72].astype(bf16)
    update = jnp.concatenate([dot(d3, ww2[2], nt), dot(d3, wwp[...], nt)], axis=1)
    master_new, average_new = master_block(m3[...], update[0:3], 0.05, a3[...])
    nm3[...] = master_new
    na3[...] = average_new
    nb[64:67, :] = master_new

    def hop(src, dst, send_at, recv_at, device):
        cp = remote(src, dst, hs.at[send_at], hr.at[recv_at], device)
        cp.start()
        flying.append(cp)

    def landed(dst, sem):
        remote(dst, dst, hs.at[0], hr.at[sem], other_core).wait_recv()

    qa = 2 * p.y + p.zh
    qb = 2 * p.x + p.zh

    def near_peers(axis):
        for k in range(1, 8):
            i = lax.rem((p.y if axis == "y" else p.x) + k // 2, 4)
            zh = lax.rem(p.zh + k % 2, 2)
            z = 2 * zh + zl
            yield (p.at(y=i, z=z) if axis == "y" else p.at(x=i, z=z)), 2 * i + zh

    def gather_near(near, fa, fb, rows, base):
        fa[qa] = near[0:rows]
        fb[qb] = near[rows : 2 * rows]
        for k, (device, _) in enumerate(near_peers("y")):
            hop(near.at[pl.ds(0, rows)], fa.at[qa], base + k, base + qa, device)
        for k, (device, _) in enumerate(near_peers("x")):
            hop(near.at[pl.ds(rows, rows)], fb.at[qb], base + 8 + k, base + 8 + qb, device)

    def gather_far(fa, fb, pack, pa, pb, parts_a, parts_b, ga, gb, base):
        for _, q in near_peers("y"):
            landed(fa.at[q], base + q)
        pa[...] = dot(pack, fa[...].reshape(8 * fa.shape[1], PAD)).astype(bf16)
        for k in range(3):
            device, _ = along(k, "x")
            for n, part in enumerate(parts_a):
                hop(pa.at[part], ga.at[(c, p.x) + part], base + 16 + 8 * n + k, base + 16 + 8 * n + p.x, device)
        for _, q in near_peers("x"):
            landed(fb.at[q], base + 8 + q)
        pb[...] = dot(pack, fb[...].reshape(8 * fb.shape[1], PAD)).astype(bf16)
        for k in range(3):
            device, _ = along(k, "y")
            for n, part in enumerate(parts_b):
                hop(pb.at[part], gb.at[(c, p.y) + part], base + 20 + 8 * n + k, base + 20 + 8 * n + p.y, device)
        kept = []
        for n, part in enumerate(parts_a):
            hop(pa.at[part], ga.at[(c, p.x) + part], base + 35 + 8 * n, base + 32 + 8 * n + p.x, other_core)
            kept.append(pltpu.make_async_copy(pa.at[part], ga.at[(c, p.x) + part], bs.at[8 + n]))
        for n, part in enumerate(parts_b):
            hop(pb.at[part], gb.at[(c, p.y) + part], base + 39 + 8 * n, base + 36 + 8 * n + p.y, other_core)
            kept.append(pltpu.make_async_copy(pb.at[part], gb.at[(c, p.y) + part], bs.at[10 + n]))
        for cp in kept:
            cp.start()
        return kept

    def gather_over(parts_a, parts_b, ga, gb, base):
        for k in range(3):
            _, i = along(2 - k, "x")
            for n, part in enumerate(parts_a):
                ref = ga.at[(c, i) + part]
                landed(ref, base + 16 + 8 * n + i)
                hop(ref, ref, base + 32 + 8 * n + k, base + 32 + 8 * n + i, other_core)
            _, i = along(2 - k, "y")
            for n, part in enumerate(parts_b):
                ref = gb.at[(c, i) + part]
                landed(ref, base + 20 + 8 * n + i)
                hop(ref, ref, base + 36 + 8 * n + k, base + 36 + 8 * n + i, other_core)

    def gather_end(parts_a, parts_b, ga, gb, base):
        for i in range(4):
            for n, part in enumerate(parts_a):
                landed(ga.at[(1 - c, i) + part], base + 32 + 8 * n + i)
            for n, part in enumerate(parts_b):
                landed(gb.at[(1 - c, i) + part], base + 36 + 8 * n + i)

    whole2 = ((slice(None), slice(None)),)
    near2[...] = nb[64:96].astype(bf16)
    gather_near(near2, fa2, fb2, 16, 0)

    last_of(4)
    g1 = dot(rep1[...], va[...].reshape(240, 384))
    for e in range(8):
        pz[e] = g1[48 * e : 48 * e + 48].astype(bf16)
    for k, (device, zi, ci) in enumerate(column_peers(p)):
        cp = remote(pz.at[2 * zi + ci], rz.at[p.e], gs.at[42 + k], gr.at[42 + p.e], device)
        cp.start()
        flying.append(cp)
    rz[p.e] = pz[p.e]
    kept2 = gather_far(fa2, fb2, pack2[...], pa2, pb2_, whole2, whole2, ga2, gb2, 0)
    sixth = all6.end()
    stats[0:2] = sixth
    stats[5:6] = mean1
    stats[6:7] = rs1
    stats[7:8] = rs1 * gain1
    stats[8:10] = sixth * inv_n1
    stats[10:16] = jnp.zeros((6, PAD), f32)

    for device, zi, ci in column_peers(p):
        e = 2 * zi + ci
        arrived(rz.at[e], 42 + e)
    for half in range(2):
        grad[0:48, 384 * half : 384 * half + 384] = summed(rz, half)
    turned = dot(grad[0:40, 0:C0].astype(bf16), bb1[...])
    for t in range(5):
        first_new, second_new, direction = adam_block(f1[t], q1[t], turned[8 * t : 8 * t + 6])
        nf1[t] = first_new
        nq1[t] = second_new
        dd[8 * t : 8 * t + 6, 0:C0] = direction
    update = dot(dd[0:40, 0:C0].astype(bf16), bb1[...], nt)
    row_of = (0, 8, 16, 32, 40)
    for t in range(5):
        master_new, average_new = master_block(m1[t], update[8 * t : 8 * t + 6], 0.02, a1[t])
        nm1[t] = master_new
        na1[t] = average_new
        nb[row_of[t] : row_of[t] + 6, 0:C0] = master_new
        if t == 2:
            nb[48:54, 0:C0] = master_new
    near1[...] = nb[0:64].astype(bf16)
    gather_near(near1, fa1, fb1, 32, 48)
    send_slopes(1)
    gather_over(whole2, whole2, ga2, gb2, 0)
    taps2 = (pl.ds(0, 96), slice(None))
    parts_a = (taps2, (pl.ds(96, 48), pl.ds(0, 384)))
    parts_b = (taps2, (pl.ds(96, 48), pl.ds(384, 384)))
    kept1 = gather_far(fa1, fb1, pack1[...], pa1, pb1_, parts_a, parts_b, ga1, gb1, 48)
    gather_over(parts_a, parts_b, ga1, gb1, 48)
    gather_end(whole2, whole2, ga2, gb2, 0)
    gather_end(parts_a, parts_b, ga1, gb1, 48)
    for cp in kept1 + kept2:
        cp.wait()

    for t in range(5):
        to_core(t).wait_send()
    for cp in flying:
        cp.wait_send()
    for half in range(2):
        for par in range(2):
            for k in range(2):

                def slope_sent(half=half, par=par, k=k):
                    slope_copy(half, par, k).wait_send()

                pl.when(jnp.logical_not(to_self(half)))(slope_sent)
    for j in range(2):

        def out_here(j=j):
            rows = out.at[pl.ds(512 * j, 512), :]
            remote(rows, rows, ss.at[0], rs.at[23 + j], other_core).wait_recv()

        pl.when(jnp.logical_not(is_self & (c == j)))(out_here)
    for j in range(2):
        for par in range(2):
            for k in range(2):
                part = sl_home.at[j, par, pl.ds(256 * k, 256), :]
                remote(part, part, ss.at[0], rs.at[25 + 4 * j + 2 * par + k], other_core).wait_recv()


VMEM = pl.BlockSpec(memory_space=pltpu.VMEM)
ANY = pl.BlockSpec(memory_space=pl.ANY)


def run_step(xt, offsets, owners, cot, w1, w2, wp, params, bases, states, consts):
    shape = jax.ShapeDtypeStruct
    dma = pltpu.SemaphoreType.DMA
    scratch = [
        pltpu.VMEM((5, 4, 4, 48, PAD), bf16),
        pltpu.VMEM((4, 4, 96, C1), bf16),
        pltpu.VMEM((2, HALF0, LANES), bf16),
        pltpu.VMEM((2, 576, PAD), bf16),
        pltpu.VMEM((6, WIN, PAD), bf16),
        pltpu.VMEM((5, C0, C1), bf16),
        pltpu.VMEM((3, H, C1), bf16),
        pltpu.VMEM((H, C1), bf16),
        pltpu.VMEM((WIN, C1), f32),
        pltpu.VMEM((WIN, C1), f32),
        pltpu.VMEM((WIN, C1), bf16),
        pltpu.VMEM((WIN, H), f32),
        pltpu.VMEM((WIN, H), f32),
        pltpu.VMEM((WIN, H), bf16),
        pltpu.VMEM((3, WIN, H), bf16),
        pltpu.VMEM((WIN, C1), f32),
        pltpu.VMEM((6, WIN, C1), bf16),
        pltpu.VMEM((2, OWN, C1), bf16),
        pltpu.VMEM((256, PAD), f32),
        pltpu.VMEM((8, PAD), f32),
        pltpu.VMEM((8, 128), f32),
        pltpu.VMEM((8, 128), f32),
        pltpu.VMEM((8, PAD), f32),
        pltpu.VMEM((2, 128, PAD), f32),
        pltpu.VMEM((2, OWN, PAD), bf16),
        pltpu.VMEM((WIN, C1), bf16),
        pltpu.VMEM((5, 4, 4, 48, 384), bf16),
        pltpu.VMEM((4, 4, 96, 384), bf16),
        pltpu.VMEM((5, 3, 4, 48, 384), bf16),
        pltpu.VMEM((5, 3, 48, 384), bf16),
        pltpu.VMEM((3, 4, 96, 384), bf16),
        pltpu.VMEM((3, 96, 384), bf16),
        pltpu.VMEM((5, 4, 48, 384), bf16),
        pltpu.VMEM((4, 96, 384), bf16),
        pltpu.VMEM((5, 48, 384), bf16),
        pltpu.VMEM((8, 48, 384), bf16),
        pltpu.VMEM((8, 48, 384), bf16),
        pltpu.VMEM((8, 32, 384), bf16),
        pltpu.VMEM((8, 32, 384), bf16),
        pltpu.VMEM((C0, C0), f32),
        pltpu.VMEM((C0, C0), bf16),
        pltpu.VMEM((80, PAD), f32),
        pltpu.VMEM((72, PAD), f32),
        pltpu.VMEM((96, PAD), f32),
        pltpu.VMEM((64, PAD), bf16),
        pltpu.VMEM((32, PAD), bf16),
        pltpu.VMEM((8, 32, PAD), bf16),
        pltpu.VMEM((8, 32, PAD), bf16),
        pltpu.VMEM((8, 16, PAD), bf16),
        pltpu.VMEM((8, 16, PAD), bf16),
        pltpu.VMEM((144, PAD), bf16),
        pltpu.VMEM((144, PAD), bf16),
        pltpu.VMEM((48, PAD), bf16),
        pltpu.VMEM((48, PAD), bf16),
        pltpu.VMEM((8, 8, PAD), f32),
        pltpu.VMEM((16, 8, PAD), f32),
        pltpu.VMEM((5, 8, 2, PAD), f32),
        pltpu.VMEM((5, 16, 2, PAD), f32),
        dma((40,)),
        dma((40,)),
        dma((10,)),
        dma((6, 8)),
        dma((6, 8)),
        dma((6, 16)),
        dma((6, 16)),
        dma((60,)),
        dma((60,)),
        dma((96,)),
        dma((96,)),
        dma((12,)),
    ]
    one = shape((2, 4, 144, PAD), bf16)
    two = shape((2, 4, 48, PAD), bf16)
    return pl.pallas_call(
        step_kernel,
        out_shape=(
            shape((BINS, 384), bf16),
            shape((2, 2, OWN, 384), bf16),
            shape((16, PAD), f32),
            one,
            one,
            two,
            two,
            *[shape(a.shape, f32) for a in states],
        ),
        in_specs=[VMEM, VMEM, VMEM, ANY, ANY, ANY, ANY] + [VMEM] * 14 + [ANY] * 3 + [VMEM] * 12,
        out_specs=(ANY, ANY, VMEM, ANY, ANY, ANY, ANY, *[VMEM] * 12),
        scratch_shapes=scratch,
        compiler_params=pltpu.CompilerParams(
            collective_id=0, has_side_effects=True, vmem_limit_bytes=63 * 2**20
        ),
    )(
        xt, offsets, owners, cot, w1, w2, wp, *params,
        *[consts[n] for n in ("e1", "bw1", "e2", "bw2", "rep1", "rep2", "pack1", "pack2")],
        *bases, *states,
    )


def norm_block(gradient, parameters, moments):
    first_new, second_new, direction = adam_block(moments[0], moments[1], gradient)
    return parameters - norm_rate * direction, first_new, second_new


def finish_kernel(
    xt, offsets, owners, slopes, stats, ga1, gb1, ga2, gb2, out_in, *rest,
):
    p = Place()
    zl = p.zl
    params = rest[0:6]
    moments = rest[6:9]
    rep_a, rep_b, at_a, at_b, rep2a, rep2b, at2a, at2b = rest[9:17]
    states_in = rest[17:29]
    out, gin, v1, v1f, v1s, v2, v2f, v2s, v3, v3f, v3s, cp1, cp2, cp3 = rest[29:43]
    states_out = rest[43:55]
    gav, gbv, gav2, gbv2, held, tr, ls = rest[55:]
    third_a = (slice(None), slice(None), pl.ds(96, 48), pl.ds(0, 384))
    third_b = (slice(None), slice(None), pl.ds(96, 48), pl.ds(384, 384))
    taps2 = (slice(None), slice(None), pl.ds(0, 96))
    copies = [
        pltpu.make_async_copy(ga1.at[taps2], gav.at[taps2], ls.at[0]),
        pltpu.make_async_copy(gb1.at[taps2], gbv.at[taps2], ls.at[1]),
        pltpu.make_async_copy(ga1.at[third_a], gav.at[third_a], ls.at[4]),
        pltpu.make_async_copy(gb1.at[third_b], gbv.at[third_b], ls.at[5]),
        pltpu.make_async_copy(ga2, gav2, ls.at[6]),
        pltpu.make_async_copy(gb2, gbv2, ls.at[7]),
    ]
    for cp in copies:
        cp.start()
    out[...] = out_in[...]
    for k in range(12):
        states_out[k][...] = states_in[k][...]

    vec = stats[...]
    v326 = jnp.where(zl == 0, vec, pltpu.roll(vec, PAD - HALF0, 1))
    tr[0:16, :] = v326[:, 0:384]
    tr[16:128, :] = jnp.zeros((112, 384), f32)
    cols = jnp.transpose(tr[...])
    mean_c = cols[0:HALF0, 5:6]
    rs_c = cols[0:HALF0, 6:7]
    scale_c = cols[0:HALF0, 7:8]
    gm_c = cols[0:HALF0, 8:9]
    bm_c = cols[0:HALF0, 9:10]
    off_home = offsets[...].astype(f32)
    tn = ((0,), (0,))
    rowq = iota((128, 256), 0)
    laneq = iota((128, 256), 1)
    put_even = (laneq == 2 * rowq).astype(bf16)
    put_odd = (laneq == 2 * rowq + 1).astype(bf16)
    back = []
    for j in range(2):
        for k in range(4):
            bins = pl.ds(128 * k, 128)
            st = dot(slopes[j, 0, bins, :], put_even, tn) + dot(slopes[j, 1, bins, :], put_odd, tn)
            lanes = pl.ds(1024 * j + 256 * k, 256)
            xf = xt[:, lanes].astype(f32)
            scaled = (xf - mean_c) * rs_c
            ok = ((iota((1, 256), 1) + (1024 * j + 256 * k)).astype(f32) >= 2.0 * off_home).astype(f32)
            held[:, lanes] = ok * (scale_c * (st[0:HALF0] - bm_c - scaled * gm_c))
        half = pl.ds(1024 * j, 1024)
        back.append(pltpu.make_async_copy(held.at[:, half], gin.at[:, 0, half], ls.at[2 + j]))
        back[j].start()

    grads1 = v326[0:2, 0:HALF0]
    v384 = jnp.where(zl == 0, vec, pltpu.roll(vec, PAD - HALF1, 1))
    grads2 = v384[2:4, 0:HALF1]
    v192 = jnp.where(zl == 0, vec, pltpu.roll(vec, PAD - HALFH, 1))
    halves = [(grads1[0:1], grads1[1:2]), (grads2[0:1], grads2[1:2]), (v192[4:5, 0:HALFH], v192[4:5, H : H + HALFH])]
    outs = [(v1, v1f, v1s), (v2, v2f, v2s), (v3, v3f, v3s)]
    for n in range(3):
        for r in range(2):
            old = (moments[n][0, r : r + 1, :], moments[n][1, r : r + 1, :])
            new = norm_block(halves[n][r], params[2 * n + r][...].reshape(1, -1), old)
            for q in range(3):
                outs[n][q][r : r + 1, :] = new[q]

    own_row = jnp.broadcast_to(owners[...].astype(f32), (8, 64))

    def column(rep, at, width):
        own = jnp.sum(rep[...].astype(f32) * own_row[0:1], axis=1, keepdims=True)
        return own * float(width) + at[...]

    lane = iota((384, 384), 1).astype(f32)
    place_a = (lane == column(rep_a, at_a, 6)).astype(bf16)
    place_b = (lane == column(rep_b, at_b, 6)).astype(bf16)
    own8 = own_row.astype(bf16)
    place2a = (iota((H, H), 0).astype(f32) == (dot(own8, rep2a[...])[0:1] * 3.0 + at2a[...])).astype(bf16)
    place2b = (iota((H, H), 0).astype(f32) == (dot(own8, rep2b[...])[0:1] * 3.0 + at2b[...])).astype(bf16)
    for cp in copies:
        cp.wait()
    for t in range(2):
        block = gav[:, :, 48 * t : 48 * t + 48, :].reshape(384, PAD)
        cp1[t] = dot(block[:, 0:C0], place_a, tn).astype(bf16)
        block = gbv[:, :, 48 * t : 48 * t + 48, :].reshape(384, PAD)
        cp1[3 + t] = dot(block[:, 0:C0], place_b, tn).astype(bf16)
    cp1[2, 0:384] = dot(gav[:, :, 96:144, 0:384].reshape(384, 384), place_a, tn).astype(bf16)
    cp1[2, 384:C0] = dot(gbv[:, :, 96:144, 384:C0].reshape(384, C0 - 384), place_b, tn).astype(bf16)
    two = dot(place2a, gav2[...].reshape(384, PAD)).astype(bf16)
    cp3[...] = two[0:HALFH]
    cp2[0] = two[HALFH:H]
    two = dot(place2b, gbv2[...].reshape(384, PAD)).astype(bf16)
    cp2[1] = two[0:HALFH]
    cp2[2] = two[HALFH:H]
    for cp in back:
        cp.wait()


def run_finish(xt, offsets, owners, slopes, stats, gathered, out, params, moments, states, consts):
    shape = jax.ShapeDtypeStruct
    vec = [shape((2, n), f32) for n in (HALF0,) * 3 + (HALF1,) * 3 + (HALFH,) * 3]
    names = ("rep_a", "rep_b", "at_a", "at_b", "rep2a", "rep2b", "at2a", "at2b")
    return pl.pallas_call(
        finish_kernel,
        out_shape=(
            shape((BINS, 384), bf16),
            shape((HALF0, 1, 2 * BINS), f32),
            *vec,
            shape((5, C0, 384), bf16),
            shape((3, HALFH, C1), bf16),
            shape((HALFH, C1), bf16),
            *[shape(a.shape, f32) for a in states],
        ),
        in_specs=[VMEM] * 5 + [ANY] * 4 + [VMEM] * 30,
        out_specs=(VMEM, ANY, *[VMEM] * 24),
        scratch_shapes=[
            pltpu.VMEM((2, 4, 144, PAD), bf16),
            pltpu.VMEM((2, 4, 144, PAD), bf16),
            pltpu.VMEM((2, 4, 48, PAD), bf16),
            pltpu.VMEM((2, 4, 48, PAD), bf16),
            pltpu.VMEM((HALF0, 2 * BINS), f32),
            pltpu.VMEM((128, 384), f32),
            pltpu.SemaphoreType.DMA((8,)),
        ],
        compiler_params=pltpu.CompilerParams(vmem_limit_bytes=63 * 2**20),
    )(
        xt, offsets, owners, slopes, stats, *gathered, out, *params, *moments,
        *[consts[n] for n in names], *states,
    )


def make_consts():
    e1 = np.zeros((64, 768), np.float32)
    bw1 = np.zeros((8, 768), np.float32)
    e2 = np.zeros((64, 384), np.float32)
    bw2 = np.zeros((8, 384), np.float32)
    for s in range(64):
        g, zh, c = s // 4, (s // 2) % 2, s % 2
        for b in range(2):
            e = (2 * zh + b) * 2 + c
            for w in range(6):
                e1[s, (g * 8 + e) * 6 + w] = 1
                bw1[:, (g * 8 + e) * 6 + w] = b * 384 + w
            block = ((2 * zh + b) * 4 + g % 4) * 8 + (g // 4) * 2 + c
            for w in range(3):
                e2[s, block * 3 + w] = 1
                bw2[:, block * 3 + w] = b * 192 + w
    rep1 = np.zeros((8 * 48, 240), np.float32)
    rep2 = np.zeros((8 * 32, 96), np.float32)
    for e in range(8):
        for t in range(5):
            for w in range(6):
                rep1[e * 48 + t * 8 + w, t * 48 + e * 6 + w] = 1
        for m in range(4):
            for w in range(3):
                rep2[e * 32 + m * 8 + w, m * 24 + e * 3 + w] = 1
    pack1 = np.zeros((144, 256), np.float32)
    pack2 = np.zeros((48, 128), np.float32)
    for o in range(8):
        for w in range(6):
            for t in range(3):
                pack1[t * 48 + o * 6 + w, o * 32 + 8 * t + w] = 1
        for w in range(3):
            for m in range(2):
                pack2[m * 24 + o * 3 + w, o * 16 + 4 * m + w] = 1
    rep_a = np.zeros((384, 64), np.float32)
    rep_b = np.zeros((384, 64), np.float32)
    at_a = np.zeros((384, 1), np.float32)
    rep2a = np.zeros((64, 384), np.float32)
    rep2b = np.zeros((64, 384), np.float32)
    at2 = np.zeros((1, 384), np.float32)
    for c in range(2):
        for i in range(4):
            for o in range(8):
                j, zh = o // 2, o % 2
                s_a = ((i * 4 + j) * 2 + zh) * 2 + c
                s_b = ((j * 4 + i) * 2 + zh) * 2 + c
                for w in range(6):
                    r = (c * 4 + i) * 48 + o * 6 + w
                    rep_a[r, s_a] = 1
                    rep_b[r, s_b] = 1
                    at_a[r, 0] = w
                for m in range(2):
                    for w in range(3):
                        r = (c * 4 + i) * 48 + m * 24 + o * 3 + w
                        rep2a[s_a, r] = 1
                        rep2b[s_b, r] = 1
                        at2[0, r] = m * 192 + w
    low = lambda a: jnp.asarray(a, bf16)
    return {
        "e1": low(e1), "bw1": jnp.asarray(bw1), "e2": low(e2), "bw2": jnp.asarray(bw2),
        "rep1": low(rep1), "rep2": low(rep2), "pack1": low(pack1), "pack2": low(pack2),
        "rep_a": low(rep_a), "rep_b": low(rep_b), "at_a": jnp.asarray(at_a), "at_b": jnp.asarray(at_a),
        "rep2a": low(rep2a), "rep2b": low(rep2b), "at2a": jnp.asarray(at2), "at2b": jnp.asarray(at2),
    }


def local(
    inputs, offsets, owners, cotangent,
    norm1_gain, norm1_bias, norm1_moments,
    norm2_gain, norm2_bias, norm2_moments,
    norm3_gain, norm3_bias, norm3_moments,
    conv1_copy, conv1_master, conv1_first, conv1_second, conv1_average, basis1,
    conv2_copy, conv2_master, conv2_first, conv2_second, conv2_average, basis2,
    project_copy, project_master, project_first, project_second, project_average, basis3,
):
    consts = make_consts()
    flip2 = lambda a: jnp.swapaxes(a, -1, -2)
    xt = flip2(inputs[0])
    offsets = offsets[None]
    owners = owners[None]
    params = [norm1_gain, norm1_bias, norm2_gain, norm2_bias, norm3_gain, norm3_bias]
    states = [
        conv1_master, conv1_first, conv1_second, conv1_average,
        conv2_master, conv2_first, conv2_second, conv2_average,
        project_master, project_first, project_second, project_average,
    ]
    out, slopes, stats, *more = run_step(
        xt, offsets, owners, cotangent[0], conv1_copy, flip2(conv2_copy), flip2(project_copy), params,
        (basis1, basis2, basis3), [flip2(a) for a in states], consts,
    )
    gathered, new = more[0:4], more[4:]
    result = run_finish(
        xt, offsets, owners, slopes, stats, gathered, out, params,
        (norm1_moments, norm2_moments, norm3_moments), new, consts,
    )
    out, gin, *vec = result[0:11]
    cp1, cp2, cp3 = result[11:14]
    nm1, nf1, nq1, na1, nm2, nf2, nq2, na2, nm3, nf3, nq3, na3 = [flip2(a) for a in result[14:]]
    return (
        out[None], jnp.transpose(gin, (1, 2, 0)), *vec,
        nm1, cp1, nf1, nq1, na1,
        nm2, flip2(cp2), nf2, nq2, na2,
        nm3, flip2(cp3), nf3, nq3, na3,
    )


def solution(mesh):
    finer = Mesh(mesh.devices.reshape(4, 4, 2, 2, mesh.shape["ch"]), SEQ_CH)
    owner3 = P(None, None, SEQ_CH)
    owner2 = P(None, SEQ_CH)
    half3 = P(None, None, "ch")
    in_specs = (
        P(SEQ, None, "ch"), P(SEQ), P(), P(SEQ, None, "ch"),
        P("ch"), P("ch"), half3, P("ch"), P("ch"), half3, P("ch"), P("ch"), half3,
        half3, owner3, owner3, owner3, owner3, P(),
        half3, owner3, owner3, owner3, owner3, P(),
        P(None, "ch"), owner2, owner2, owner2, owner2, P(),
    )
    vec = P(None, "ch")
    out_specs = (
        P(SEQ, None, "ch"), P(SEQ, None, "ch"), *[vec] * 9,
        owner3, half3, owner3, owner3, owner3,
        owner3, half3, owner3, owner3, owner3,
        owner2, vec, owner2, owner2, owner2,
    )
    return jax.shard_map(local, mesh=finer, in_specs=in_specs, out_specs=out_specs, check_vma=False)
```

```python
import math

import jax
import jax.numpy as jnp
import numpy as np
from jax import lax
from jax.experimental import pallas as pl
from jax.experimental.pallas import tpu as pltpu
from jax.sharding import Mesh
from jax.sharding import PartitionSpec as P

STEP = 8
SEQ = ("seq_0", "seq_1", "seq_2", "seq_3")
SEQ_CH = ("seq_0", "seq_1", "seq_2", "seq_3", "ch")
MESH = pl.DeviceIdType.MESH
bf16 = jnp.bfloat16
f32 = jnp.float32

eps_norm = 1e-05
beta_one = 0.9
beta_two = 0.95
adam_eps = 1e-08
decay_rate = 0.01
average_rate = 0.9
norm_rate = 0.05

C0, C1, H = 652, 768, 384
HALF0, HALF1, HALFH = 326, 384, 192
BINS = 1024
OWN = 512
WIN = 528
LANES = 1152
PAD = 768

GELU_K = math.sqrt(2.0 / math.pi)
GELU_C = 0.044715


def gelu(v):
    return 0.5 * v * (1.0 + jnp.tanh(GELU_K * (v + GELU_C * (v * v * v))))


def gelu_slope(v):
    square = v * v
    t = jnp.tanh(GELU_K * v * (1.0 + GELU_C * square))
    return 0.5 * (1.0 + t) + 0.5 * GELU_K * v * (1.0 - t * t) * (1.0 + 3.0 * GELU_C * square)


def dot(a, b, dims=((1,), (0,))):
    return lax.dot_general(a, b, (dims, ((), ())), preferred_element_type=f32)


def iota(shape, dim):
    return lax.broadcasted_iota(jnp.int32, shape, dim)


def adam_block(first, second, turned):
    first_new = beta_one * first + (1.0 - beta_one) * turned
    second_new = beta_two * second + (1.0 - beta_two) * turned * turned
    direction = (
        first_new
        / (1.0 - beta_one**STEP)
        / (jnp.sqrt(second_new / (1.0 - beta_two**STEP)) + adam_eps)
    )
    return first_new, second_new, direction


def master_block(master, update, rate, average):
    master_new = master - rate * (update + decay_rate * master)
    return master_new, average_rate * average + (1.0 - average_rate) * master_new


class Place:
    def __init__(self):
        self.x, self.y, self.zh, self.c, self.zl = [lax.axis_index(n) for n in SEQ_CH]
        self.z = 2 * self.zh + self.zl
        self.e = 2 * self.z + self.c
        self.g = 4 * self.x + self.y

    def at(self, **other):
        v = {"x": self.x, "y": self.y, "z": self.z, "c": self.c}
        v.update(other)
        z = v["z"]
        return (v["x"], v["y"], lax.div(z, 2), v["c"], lax.rem(z, 2))


def remote(src, dst, send, recv, device):
    return pltpu.make_async_remote_copy(
        src_ref=src, dst_ref=dst, send_sem=send, recv_sem=recv, device_id=device, device_id_type=MESH
    )


def column_peers(p):
    out = []
    for k in range(1, 8):
        z = lax.rem(p.z + k // 2, 4)
        c = lax.rem(p.c + k % 2, 2)
        out.append((p.at(z=z, c=c), z, c))
    return out


def plane_peers(p):
    out = []
    for k in range(1, 16):
        x = lax.rem(p.x + k // 4, 4)
        y = lax.rem(p.y + k % 4, 4)
        out.append((p.at(x=x, y=y), x, y))
    return out


def other_peers(p):
    over = lax.rem(p.z + 2, 4)
    out = [p.at(x=lax.rem(p.x + k, 4), c=1 - p.c) for k in (1, 2, 3)]
    out += [p.at(x=lax.rem(p.x + k, 4), z=over) for k in (1, 2, 3)]
    out += [p.at(y=lax.rem(p.y + k, 4), z=over) for k in (1, 2, 3)]
    return out


class Total:
    def __init__(self, p, bufs, sems):
        self.p = p
        self.b1, self.b2 = bufs
        self.s1, self.r1, self.s2, self.r2 = sems

    def start(self, value):
        p = self.p
        self.b1[p.e] = value
        self.c1 = []
        for k, (device, _, _) in enumerate(column_peers(p)):
            cp = remote(self.b1.at[p.e], self.b1.at[p.e], self.s1.at[k], self.r1.at[p.e], device)
            cp.start()
            self.c1.append(cp)

    def middle(self):
        p = self.p
        for device, z, c in column_peers(p):
            e = 2 * z + c
            remote(self.b1.at[e], self.b1.at[e], self.s1.at[0], self.r1.at[e], device).wait_recv()
        total = self.b1[0]
        for k in range(1, 8):
            total = total + self.b1[k]
        for cp in self.c1:
            cp.wait_send()
        self.b2[p.g] = total
        self.c2 = []
        for k, (device, _, _) in enumerate(plane_peers(p)):
            cp = remote(self.b2.at[p.g], self.b2.at[p.g], self.s2.at[k], self.r2.at[p.g], device)
            cp.start()
            self.c2.append(cp)

    def end(self):
        p = self.p
        for device, x, y in plane_peers(p):
            g = 4 * x + y
            remote(self.b2.at[g], self.b2.at[g], self.s2.at[0], self.r2.at[g], device).wait_recv()
        total = self.b2[0]
        for k in range(1, 16):
            total = total + self.b2[k]
        for cp in self.c2:
            cp.wait_send()
        return total


TAP_CORE = (0, 0, 1, 1, 0)
UNIT_CORE = (0, 1, 0, 1)


def step_kernel(
    xt, offsets, owners, cot, w1, w2, wp, pg1, pb1, pg2, pb2, pg3, pb3,
    e1, bw1, e2, bw2, rep1, rep2, pack1, pack2, b1, b2, b3,
    *rest,
):
    states_in = rest[0:12]
    out, sl_home, stats, ga1, gb1, ga2, gb2 = rest[12:19]
    states_out = rest[19:31]
    held_in = rest[31:43]
    held_out = rest[43:55]
    step_body(
        xt, offsets, owners, cot, w1, w2, wp, pg1, pb1, pg2, pb2, pg3, pb3,
        e1, bw1, e2, bw2, rep1, rep2, pack1, pack2, b1, b2, b3,
        states_in, states_out, held_in, held_out,
        out, sl_home, stats, ga1, gb1, ga2, gb2, *rest[55:],
    )


def step_body(
    xt, offsets, owners, cot, w1, w2, wp, pg1, pb1, pg2, pb2, pg3, pb3,
    e1, bw1, e2, bw2, rep1, rep2, pack1, pack2, b1, b2, b3,
    states_in, states_out, held_in, held_out,
    out, sl_home, stats, ga1, gb1, ga2, gb2,
    s1, s2, xw, raw, aa, ww1, ww2, wwp, pooled, diff, cc, hid, og, no, hh, mid, gg, gp,
    slope, small, offs, offw, acc, tr, dv,
    t1, t2, ra, rb, rd, re, ua, uc, va, pz, rz, pz2, rz2,
    b1f, bb1, grad, dd, nb, near1, near2, fa1, fb1, fa2, fb2, pa1, pb1_, pa2, pb2_,
    a1a, a1b, ab1, ab2,
    ss, rs, ls, as1, ar1, as2, ar2, gs, gr, hs, hr, bs, ns,
):
    m1, f1, q1, a1, m2, f2, q2, a2, m3, f3, q3, a3 = held_in
    nm1, nf1, nq1, na1, nm2, nf2, nq2, na2, nm3, nf3, nq3, na3 = held_out
    loads = [pltpu.make_async_copy(states_in[k], held_in[k], ns.at[k]) for k in range(12)]
    stores = [pltpu.make_async_copy(held_out[k], states_out[k], ns.at[12 + k]) for k in range(12)]
    mm = gg.at[0:3]
    p = Place()
    offs[...] = jnp.broadcast_to(offsets[...].astype(f32), (8, 128))
    c, zl = p.c, p.zl
    flip = p.at(z=3 - p.z)
    direct = p.at(z=p.z + 1 - 2 * zl)
    other_core = p.at(c=1 - c)

    bar = pltpu.get_barrier_semaphore()
    for device, _, _ in column_peers(p):
        pl.semaphore_signal(bar, inc=1, device_id=device, device_id_type=MESH)
    for device, _, _ in plane_peers(p):
        pl.semaphore_signal(bar, inc=1, device_id=device, device_id_type=MESH)
    for device in other_peers(p):
        pl.semaphore_signal(bar, inc=1, device_id=device, device_id_type=MESH)

    mine = pl.ds(pl.multiple_of(384 * c, 128), 384)
    others = pl.ds(pl.multiple_of(384 - 384 * c, 128), 384)
    my_lanes = pl.ds(pl.multiple_of(384 * zl, 128), 384)
    its_lanes = pl.ds(pl.multiple_of(384 - 384 * zl, 128), 384)
    my_rows = pl.ds(pl.multiple_of(192 * zl, 16), 192)
    its_rows = pl.ds(pl.multiple_of(192 - 192 * zl, 16), 192)

    def unit_ref(u, rows):
        return ww2.at[u, rows, :] if u < 3 else wwp.at[rows, :]

    own_w = [pltpu.make_async_copy(w1.at[t], ww1.at[t, :, my_lanes], ls.at[t]) for t in range(5)]
    own_w += [
        pltpu.make_async_copy(w2.at[u] if u < 3 else wp, unit_ref(u, my_rows), ls.at[5 + u])
        for u in range(4)
    ]
    for cp in own_w:
        cp.start()

    pl.semaphore_wait(bar, 31)

    is_self = c == zl
    not_self = c != zl
    home_chip = 2 * p.zh + c

    def window(j, part):
        at = 896 * j + (0, 256)[part]
        return xt.at[:, pl.ds(pl.multiple_of(at, 128), (256, LANES - 256)[part])]

    def window_there(k, part):
        return xw.at[k, :, pl.ds((0, 256)[part], (256, LANES - 256)[part])]

    def cot_window(j):
        return cot.at[pl.ds(pl.multiple_of(496 * j, 16), WIN), :]

    cc_mine = cc.at[:, pl.ds(pl.multiple_of(384 * zl, 128), 384)]
    x_a = [
        remote(window(c, h), window_there(zl, h), ss.at[33 * h], rs.at[33 * h + zl], p.at(z=home_chip, c=c))
        for h in range(2)
    ]
    x_b = [
        remote(
            window(1 - c, h), window_there(zl, h), ss.at[33 * h + 1], rs.at[33 * h + zl],
            p.at(z=home_chip, c=1 - c),
        )
        for h in range(2)
    ]
    c_a = remote(cot_window(c), cc_mine, ss.at[2], rs.at[2 + zl], p.at(z=home_chip, c=c))
    c_b = remote(cot_window(1 - c), cc_mine, ss.at[3], rs.at[2 + zl], p.at(z=home_chip, c=1 - c))
    o_a = remote(offs, offw, ss.at[4], rs.at[4], other_core)

    def send_windows(h):
        pl.when(not_self)(lambda: x_a[h].start())

        def keep():
            pltpu.make_async_copy(window(c, h), window_there(zl, h), rs.at[33 * h + zl]).start()

        pl.when(is_self)(keep)
        x_b[h].start()

    send_windows(0)
    o_a.start()

    def tap_over(t):
        to = direct if t == 4 else flip
        return remote(ww1.at[t, :, my_lanes], ww1.at[t, :, my_lanes], ss.at[5 + t], rs.at[5 + t], to)

    def tap_here(t):
        return remote(
            ww1.at[t, :, its_lanes], ww1.at[t, :, its_lanes], ss.at[10 + t], rs.at[10 + t], other_core
        )

    def unit_over(u):
        return remote(
            unit_ref(u, my_rows), unit_ref(u, my_rows), ss.at[15 + u], rs.at[15 + u], flip
        )

    def unit_here(u):
        return remote(
            unit_ref(u, its_rows), unit_ref(u, its_rows), ss.at[19 + u], rs.at[19 + u], other_core
        )

    own_w[0].wait()
    pl.when(c == 0)(lambda: tap_over(0).start())

    for cp in loads:
        cp.start()

    off_home = offs[0:1, 0:1]
    total_s = jnp.zeros((8, HALF0), f32)
    total_q = jnp.zeros((8, HALF0), f32)
    for k in range(8):
        lanes = pl.ds(256 * k, 256)
        mask = ((iota((8, 256), 1) + 256 * k).astype(f32) >= 2.0 * off_home).astype(bf16)
        xb = xt[:, lanes]
        xf = xb.astype(f32)
        sq = xf * xf
        hi = sq.astype(bf16)
        lo = (sq - hi.astype(f32)).astype(bf16)
        nt = ((1,), (1,))
        total_s = total_s + dot(mask, xb, nt)
        total_q = total_q + (dot(mask, hi, nt) + dot(mask, lo, nt))
    small[...] = jnp.zeros_like(small)
    small[0:1, 0:HALF0] = total_s[0:1]
    small[1:2, 0:HALF0] = total_q[0:1]
    small[2:3, 0:HALF0] = pg1[...].reshape(1, HALF0)
    small[3:4, 0:HALF0] = pb1[...].reshape(1, HALF0)
    small[4:5, 0:HALF1] = pg2[...].reshape(1, HALF1)
    small[5:6, 0:HALF1] = pb2[...].reshape(1, HALF1)
    small[6:7, 0:HALFH] = pg3[...].reshape(1, HALFH)
    small[6:7, H : H + HALFH] = pb3[...].reshape(1, HALFH)
    here = small[...]
    half_row = iota((8, PAD), 0)
    moved = jnp.where(
        half_row < 4,
        pltpu.roll(here, HALF0, 1),
        jnp.where(half_row < 6, pltpu.roll(here, HALF1, 1), pltpu.roll(here, HALFH, 1)),
    )
    here = jnp.where(zl == 0, here, moved)
    leader = (p.g == 0) & (p.zh == 0) & (c == 0)
    here = jnp.where((half_row < 2) | leader, here, 0.0)
    count = jnp.maximum(BINS - off_home, 0.0)
    lane8 = iota((8, PAD), 1)
    row8 = iota((8, PAD), 0)
    here = here + jnp.where((lane8 == PAD - 1) & (row8 == 0), count, 0.0)
    all1 = Total(p, (a1a, a1b), (as1.at[0], ar1.at[0], as2.at[0], ar2.at[0]))
    all1.start(here)
    send_windows(1)
    for t in range(1, 5):
        own_w[t].wait()
        pl.when(c == TAP_CORE[t])(lambda t=t: tap_over(t).start())

    @pl.when(not_self)
    def _():
        c_a.start()

    @pl.when(is_self)
    def _():
        pltpu.make_async_copy(cot_window(c), cc_mine, rs.at[2 + zl]).start()

    c_b.start()
    for u in range(4):
        own_w[5 + u].wait()
        pl.when(c == UNIT_CORE[u])(lambda u=u: unit_over(u).start())
    all1.middle()

    owners_row = jnp.broadcast_to(owners[...].astype(f32), (8, 64)).astype(bf16)
    nat1 = dot(owners_row, e1[...])[0:1] * 6.0 + bw1[0:1]
    nat2 = dot(owners_row, e2[...])[0:1] * 3.0 + bw2[0:1]
    for k in range(4):
        s1[4, k] = ((iota((192, PAD), 0) + 192 * k).astype(f32) == nat1).astype(bf16).reshape(4, 48, PAD)
    perm2 = (iota((H, H), 0).astype(f32) == nat2).astype(bf16)

    row = iota((128, 128), 0)
    pick = (iota((128, 128), 1) == jnp.where(row < 64, 2 * row, 2 * row - 127)).astype(bf16)
    def window_here(k):
        for h in range(2):
            part = window_there(k, h)
            remote(part, part, ss.at[0], rs.at[33 * h + k], other_core).wait_recv()

    tr[...] = jnp.zeros_like(tr)

    def blocks(k, second):
        for b in range(9):
            buf = b % 2
            tr[buf, :, 0:HALF0] = dot(pick, xw[k, :, pl.ds(128 * b, 128)], ((1,), (1,)))
            bins = pl.ds(64 * b, 64)

            def put(value, bins=bins):
                value = value.astype(bf16)
                for par in range(2):
                    part = value[64 * par : 64 * par + 64]
                    raw[par, bins, :] = raw[par, bins, :] + part if second else part

            pl.when(k == 0)(lambda: put(tr[buf]))
            pl.when(k == 1)(lambda: put(pltpu.roll(tr[buf], HALF0, 1)))

    window_here(zl)
    blocks(zl, False)
    first = all1.end()
    n1 = first[0:1, PAD - 1 : PAD]
    n2 = 0.5 * n1
    inv_n1 = 1.0 / n1
    inv_n2 = 1.0 / n2
    real = iota((1, PAD), 1) < C0
    mean1 = jnp.where(real, first[0:1], 0.0) * inv_n1
    var1 = first[1:2] * inv_n1 - mean1 * mean1
    rs1 = lax.rsqrt(var1 + eps_norm)
    gain1, bias1 = first[2:3], first[3:4]
    gain2, bias2 = first[4:5], first[5:6]
    gain3, bias3 = first[6:7, 0:H], first[6:7, H : 2 * H]

    remote(offs, offw, ss.at[4], rs.at[4], other_core).wait()
    off = jnp.where(is_self, offs[0:1, 0:1], offw[0:1, 0:1])

    bin0 = 496 * c
    own0 = pl.multiple_of(16 * c, 16)
    raw0 = pl.multiple_of(48 * c, 16)
    rawown = pl.multiple_of(64 * c, 16)

    def valid_mask(rows, at=0):
        return ((iota((rows, 1), 0) + (bin0 + at)).astype(f32) >= off).astype(f32)

    def own_mask(rows, at=0):
        r = iota((rows, 1), 0) + at
        return ((r >= 16 * c) & (r < 16 * c + OWN)).astype(f32)

    not_first = (iota((WIN, 1), 0) > 0).astype(f32)
    not_last = (iota((WIN, 1), 0) < WIN - 1).astype(f32)

    def before(v):
        return (pltpu.roll(v, 1, 0) * not_first).astype(bf16)

    def after(v):
        return (pltpu.roll(v, WIN - 1, 0) * not_last).astype(bf16)

    small[0:1] = rs1 * gain1
    small[1:2] = bias1 - mean1 * (rs1 * gain1)
    small[2:3] = mean1
    small[3:4] = rs1

    def norm_tile(q):
        lanes = pl.ds(pl.multiple_of(128 * q, 128), 128)
        scale, shift = small[0:1, lanes], small[1:2, lanes]
        valid = valid_mask(WIN)
        for par in range(2):
            v = raw[par, pl.ds(raw0, WIN), lanes].astype(f32)
            v = gelu(v * scale + shift) * valid
            aa[par, :, lanes] = before(v)
            aa[2 + par, :, lanes] = v.astype(bf16)
            aa[4 + par, :, lanes] = after(v)

    def pass_on(t):
        def there():
            part = ww1.at[t, :, its_lanes]
            remote(part, part, ss.at[5 + t], rs.at[5 + t], flip).wait_recv()
            tap_here(t).start()

        pl.when(c == TAP_CORE[t])(there)

    @pl.loop(0, 2)
    def _(k):
        norm_tile(3 * zl + k)

    pass_on(0)
    window_here(1 - zl)
    blocks(1 - zl, True)
    pass_on(1)
    pass_on(2)

    @pl.loop(0, 4)
    def _(k):
        norm_tile(jnp.where(zl == 0, k + 2, jnp.where(k < 3, k, 5)))

    pass_on(3)
    pass_on(4)
    for t in range(5):
        pl.when(c != TAP_CORE[t])(lambda t=t: tap_here(t).wait_recv())

    acc[...] = jnp.zeros_like(acc)

    @pl.loop(0, 3)
    def _(k):
        rows = pl.ds(pl.multiple_of(176 * k, 16), 176)
        h0 = jnp.zeros((176, C1), f32)
        for t in range(5):
            h0 = h0 + dot(aa[t, rows, 0:C0], ww1[t])
        h1 = jnp.zeros((176, C1), f32)
        for t in range(5):
            h1 = h1 + dot(aa[t + 1, rows, 0:C0], ww1[t])
        d = h0 - h1
        v = jnp.maximum(h0, h1) + (jnp.log(1.0 + jnp.exp(-jnp.abs(d))) - math.log(2.0))
        diff[rows, :] = d
        pooled[rows, :] = v
        m = valid_mask(176, 176 * k) * own_mask(176, 176 * k)
        vm = v * m
        acc[0:1] += jnp.sum(vm, axis=0, keepdims=True)
        acc[1:2] += jnp.sum(vm * v, axis=0, keepdims=True)

    all2 = Total(p, (ab1.at[0], ab2.at[0]), (as1.at[1], ar1.at[1], as2.at[1], ar2.at[1]))
    all2.start(acc[0:2])

    def early_slopes(par):
        @pl.loop(0, 6)
        def _(q):
            lanes = pl.ds(pl.multiple_of(128 * q, 128), 128)
            xv = raw[par, pl.ds(rawown, OWN), lanes].astype(f32)
            turn = gelu_slope(xv * small[0:1, lanes] + small[1:2, lanes])
            dv[par, :, lanes] = (turn * valid_mask(OWN, 16 * c)).astype(bf16)

    early_slopes(0)
    all2.middle()
    for u in range(4):

        def there_u(u=u):
            remote(
                unit_ref(u, its_rows), unit_ref(u, its_rows), ss.at[15 + u], rs.at[15 + u], flip
            ).wait_recv()
            unit_here(u).start()

        pl.when(c == UNIT_CORE[u])(there_u)
    for k in range(2):
        part = cc.at[:, pl.ds(384 * k, 384)]
        remote(part, part, ss.at[0], rs.at[2 + k], other_core).wait_recv()
    for u in range(4):
        pl.when(c == UNIT_CORE[u])(lambda u=u: unit_here(u).wait_send())
        pl.when(c != UNIT_CORE[u])(lambda u=u: unit_here(u).wait_recv())
    og[...] = dot(cc[...], wwp[...], ((1,), (1,)))
    early_slopes(1)

    @pl.when(not_self)
    def _():
        x_a[0].wait_send()
        x_a[1].wait_send()
        c_a.wait_send()

    x_b[0].wait_send()
    x_b[1].wait_send()
    c_b.wait_send()
    for t in range(5):

        def tap_sent(t=t):
            tap_over(t).wait_send()
            tap_here(t).wait_send()

        pl.when(c == TAP_CORE[t])(tap_sent)
    for u in range(4):
        pl.when(c == UNIT_CORE[u])(lambda u=u: unit_over(u).wait_send())

    second = all2.end()
    mean2 = second[0:1] * inv_n2
    var2 = second[1:2] * inv_n2 - mean2 * mean2
    rs2 = lax.rsqrt(var2 + eps_norm)
    acc[2:3] = rs2 * gain2
    acc[3:4] = bias2 - mean2 * (rs2 * gain2)
    acc[4:5] = mean2
    acc[5:6] = rs2

    @pl.loop(0, 6)
    def _(k):
        lanes = pl.ds(pl.multiple_of(128 * k, 128), 128)
        v = gelu(pooled[:, lanes] * acc[2:3, lanes] + acc[3:4, lanes]) * valid_mask(WIN)
        mm[0, :, lanes] = before(v)
        mm[1, :, lanes] = v.astype(bf16)
        mm[2, :, lanes] = after(v)

    h2 = jnp.zeros((WIN, H), f32)
    for t in range(3):
        h2 = h2 + dot(mm[t], ww2[t], ((1,), (1,)))
    hid[...] = h2
    m = valid_mask(WIN) * own_mask(WIN)
    h2m = h2 * m
    acc[6:7, 0:H] = jnp.sum(h2m, axis=0, keepdims=True)
    acc[6:7, H : 2 * H] = jnp.sum(h2m * h2, axis=0, keepdims=True)
    all3 = Total(p, (ab1.at[1], ab2.at[1]), (as1.at[2], ar1.at[2], as2.at[2], ar2.at[2]))
    all3.start(acc[6:8])

    def basis_rows(src, first, size, buf, sem):
        return pltpu.make_async_copy(src.at[pl.ds(first, size)], buf, bs.at[sem])

    slope_buf = [slope.at[pl.ds(0, 128)], slope.at[pl.ds(128, 128)]]
    rows_buf = slope_buf + [tr.at[0], tr.at[1]]

    def rounds(n):
        got = []
        for k in range(4):
            block = 4 * n + k
            src = b2 if block < 6 else b3
            got.append(basis_rows(src, 128 * (block % 6), 128, rows_buf[k], k))
        return got

    def keep_round(n):
        for k, cp in enumerate(rounds(n)):
            cp.wait()
            block = 4 * n + k
            half, at = block // 3, 128 * (block % 3)
            value = rows_buf[k][...].astype(bf16)
            if half < 3:
                ww2[half, pl.ds(at, 128), :] = value
            else:
                wwp[pl.ds(at, 128), :] = value

    first_basis = pltpu.make_async_copy(b1, b1f, bs.at[4])
    first_basis.start()

    @pl.loop(0, 6)
    def _(q):
        lanes = pl.ds(pl.multiple_of(128 * q, 128), 128)
        turn = gelu_slope(pooled[:, lanes] * acc[2:3, lanes] + acc[3:4, lanes])
        turn = (turn * valid_mask(WIN)).astype(bf16)
        xw[0, 0:272, lanes] = turn[0:272]
        xw[1, 0:256, lanes] = turn[272:WIN]

    all3.middle()

    @pl.loop(0, 6)
    def _(q):
        lanes = pl.ds(pl.multiple_of(128 * q, 128), 128)
        diff[:, lanes] = 1.0 / (1.0 + jnp.exp(-diff[:, lanes]))

    first_basis.wait()
    bb1[...] = b1f[...].astype(bf16)
    third = all3.end()
    mean3 = third[0:1, 0:H] * inv_n2
    var3 = third[0:1, H : 2 * H] * inv_n2 - mean3 * mean3
    rs3 = lax.rsqrt(var3 + eps_norm)
    valid = valid_mask(WIN)
    own = own_mask(WIN)
    h2 = hid[...]
    scaled = (h2 - mean3) * rs3
    pre = scaled * gain3 + bias3
    no[...] = (gelu(pre) * valid).astype(bf16)
    slopes = gelu_slope(pre) * og[...] * valid
    og[...] = slopes
    hid[...] = scaled
    acc[6:7, 0:H] = jnp.sum(slopes * scaled * own, axis=0, keepdims=True)
    acc[6:7, H : 2 * H] = jnp.sum(slopes * own, axis=0, keepdims=True)
    all4 = Total(p, (ab1.at[2], ab2.at[2]), (as1.at[3], ar1.at[3], as2.at[3], ar2.at[3]))
    all4.start(acc[6:8])
    out_rows = pl.ds(pl.multiple_of(512 * c, 16), OWN)
    own_rows = pl.ds(own0, OWN)
    gp[0] = (pooled[own_rows, :] + dot(no[own_rows, :], wwp[...])).astype(bf16)
    all4.middle()

    def out_copy(k):
        return remote(
            gp.at[0, :, pl.ds(384 * k, 384)],
            out.at[out_rows, :],
            ss.at[23 + k],
            rs.at[23 + c],
            p.at(z=2 * p.zh + k, c=zl),
        )

    def out_local(k):
        return pltpu.make_async_copy(
            gp.at[0, :, pl.ds(384 * k, 384)], out.at[out_rows, :], ls.at[9]
        )

    def to_self(k):
        return (zl == k) & is_self

    for k in range(2):
        pl.when(jnp.logical_not(to_self(k)))(lambda k=k: out_copy(k).start())

        pl.when(to_self(k))(lambda k=k: out_local(k).start())

    def put2(m, value):
        s2[:, :, pl.ds(24 * m, 24), :] = value.astype(bf16).reshape(4, 4, 24, C1)

    tn = ((0,), (0,))
    nop = dot(no[own_rows, :], perm2).astype(bf16)
    put2(3, dot(nop, cc[own_rows, :], tn))
    for cp in rounds(0):
        cp.start()
    fourth = all4.end()
    stats[4:5] = fourth[0:1]
    gain_mean = fourth[0:1, 0:H] * inv_n2
    bias_mean = fourth[0:1, H : 2 * H] * inv_n2
    hg = valid_mask(WIN) * (gain3 * rs3) * (og[...] - bias_mean - hid[...] * gain_mean)
    hh[0] = after(hg)
    hh[1] = hg.astype(bf16)
    hh[2] = before(hg)
    mid_grad = jnp.zeros((WIN, C1), f32)
    for t in range(3):
        mid_grad = mid_grad + dot(hh[t], ww2[t])
    mid[...] = mid_grad

    @pl.loop(0, 6)
    def _(k):
        lanes = pl.ds(pl.multiple_of(128 * k, 128), 128)
        v = pooled[:, lanes]
        turn = jnp.concatenate([xw[0, 0:272, lanes], xw[1, 0:256, lanes]], axis=0)
        slopes = turn.astype(f32) * mid[:, lanes]
        scaled = (v - acc[4:5, lanes]) * acc[5:6, lanes]
        mid[:, lanes] = slopes
        pooled[:, lanes] = scaled
        mine = slopes * own_mask(WIN)
        acc[0:1, lanes] = jnp.sum(mine * scaled, axis=0, keepdims=True)
        acc[1:2, lanes] = jnp.sum(mine, axis=0, keepdims=True)

    all5 = Total(p, (ab1.at[3], ab2.at[3]), (as1.at[4], ar1.at[4], as2.at[4], ar2.at[4]))
    all5.start(acc[0:2])
    hp = dot(hh[1, own_rows, :], perm2).astype(bf16)
    put2(0, dot(hp, mm[0, own_rows, :], tn))
    keep_round(0)
    all5.middle()
    for cp in rounds(1):
        cp.start()
    for t in range(1, 3):
        put2(t, dot(hp, mm[t, own_rows, :], tn))
    s2_over = remote(s2.at[:, :, :, others], t2, gs.at[0], gr.at[0], other_core)
    s2_over.start()
    keep_round(1)
    for cp in rounds(2):
        cp.start()
    fifth = all5.end()
    stats[2:4] = fifth
    acc[0:2] = fifth * inv_n2

    @pl.loop(0, 6)
    def _(k):
        lanes = pl.ds(pl.multiple_of(128 * k, 128), 128)
        back = acc[2:3, lanes] * (
            mid[:, lanes] - acc[1:2, lanes] - pooled[:, lanes] * acc[0:1, lanes]
        )
        pg = cc[:, lanes].astype(f32) + back * valid_mask(WIN)
        even = diff[:, lanes]
        ge = pg * even
        go = pg * (1.0 - even)
        gg[0, :, lanes] = after(go)
        gg[1, :, lanes] = after(ge)
        gg[2, :, lanes] = go.astype(bf16)
        gg[3, :, lanes] = ge.astype(bf16)
        gg[4, :, lanes] = before(go)
        gg[5, :, lanes] = before(ge)

    def total(own, parts):
        v = own.astype(f32)
        for part in parts:
            v = v + part.astype(f32)
        return v.astype(bf16)

    def along(k, axis):
        if axis == "x":
            i = lax.rem(p.x + k + 1, 4)
            return p.at(x=i), i
        if axis == "z":
            i = lax.rem(p.z + k + 1, 4)
            return p.at(z=i), i
        i = lax.rem(p.y + k + 1, 4)
        return p.at(y=i), i

    s2_over.wait()
    t2[...] = total(t2[...], [s2[:, :, :, mine]])
    flying = []

    def send(src, dst, sem, device):
        cp = remote(src, dst, gs.at[sem], gr.at[sem], device)
        cp.start()
        flying.append(cp)

    def arrived(dst, sem):
        remote(dst, dst, gs.at[0], gr.at[sem], other_core).wait_recv()

    for k in range(3):
        device, i = along(k, "z")
        send(t2.at[i], rd.at[k], 1 + k, device)
    keep_round(2)

    for k in range(2):

        def out_sent(k=k):
            out_copy(k).wait_send()

        pl.when(jnp.logical_not(to_self(k)))(out_sent)
        pl.when(to_self(k))(lambda k=k: out_local(k).wait())
    perm = s1[4].reshape(PAD, PAD)
    gp[0] = dot(gg[3, own_rows, :], perm).astype(bf16)
    gp[1] = dot(gg[2, own_rows, :], perm).astype(bf16)

    TAP_AXIS = ("x", "y", "x", "y", "x")

    def to_core(t):
        return remote(s1.at[t, :, :, :, others], t1.at[t], gs.at[7 + t], gr.at[7 + t], other_core)

    def to_axis(t):
        to_core(t).wait_recv()
        t1[t] = total(t1[t], [s1[t, :, :, :, mine]])
        for k in range(3):
            device, i = along(k, TAP_AXIS[t])
            src = t1.at[t, i] if TAP_AXIS[t] == "x" else t1.at[t, :, i]
            send(src, ra.at[t, k], 12 + 3 * t + k, device)

    def to_other_axis(t):
        for k in range(3):
            arrived(ra.at[t, k], 12 + 3 * t + k)
        own_part = t1[t, p.x] if TAP_AXIS[t] == "x" else t1[t, :, p.y]
        ua[t] = total(own_part, [ra[t, k] for k in range(3)])
        for k in range(3):
            device, i = along(k, "y" if TAP_AXIS[t] == "x" else "x")
            send(ua.at[t, i], rb.at[t, k], 27 + 3 * t + k, device)

    def last_of(t):
        for k in range(3):
            arrived(rb.at[t, k], 27 + 3 * t + k)
        own_part = ua[t, p.y] if TAP_AXIS[t] == "x" else ua[t, p.x]
        va[t] = total(own_part, [rb[t, k] for k in range(3)])

    for t in range(5):
        part = dot(gp[0], aa[t, own_rows, 0:C0], tn) + dot(gp[1], aa[t + 1, own_rows, 0:C0], tn)
        part = part.astype(bf16).reshape(4, 4, 48, C0)
        s1[t, :, :, :, 0:C0] = part
        s1[t, :, :, :, C0:PAD] = jnp.zeros((4, 4, 48, PAD - C0), bf16)
        to_core(t).start()
        if t > 0:
            to_axis(t - 1)
    to_axis(4)

    def second_of_two():
        for k in range(3):
            arrived(rd.at[k], 1 + k)
        uc[...] = total(t2[p.z], [rd[k] for k in range(3)])
        for k in range(3):
            device, i = along(k, "y")
            send(uc.at[i], re.at[k], 4 + k, device)

    def xc_peers():
        for k in range(1, 8):
            xi = lax.rem(p.x + k // 2, 4)
            ci = lax.rem(c + k % 2, 2)
            yield p.at(x=xi, c=ci), 2 * xi + ci

    def slope_part(half, par, k):
        return (
            gp.at[par, pl.ds(256 * k, 256), pl.ds(384 * half, 384)],
            sl_home.at[c, par, pl.ds(256 * k, 256), :],
        )

    def slope_copy(half, par, k):
        src, dst = slope_part(half, par, k)
        n = 2 * par + k
        return remote(src, dst, ss.at[25 + 4 * half + n], rs.at[25 + 4 * c + n], p.at(z=2 * p.zh + half, c=zl))

    def slope_local(half, par, k):
        src, dst = slope_part(half, par, k)
        return pltpu.make_async_copy(src, dst, rs.at[25 + 4 * c + 2 * par + k])

    def send_slopes(par):
        for half in range(2):
            for k in range(2):

                def send_slope(half=half, k=k):
                    slope_copy(half, par, k).start()

                def keep_slope(half=half, k=k):
                    slope_local(half, par, k).start()

                pl.when(jnp.logical_not(to_self(half)))(send_slope)
                pl.when(to_self(half))(keep_slope)

    small[4:6] = jnp.zeros((2, PAD), f32)
    for par in range(2):
        for k in range(2):
            rows = pl.ds(pl.multiple_of(own0 + 256 * k, 16), 256)
            v = jnp.zeros((256, C0), f32)
            for t in range(5):
                v = v + dot(gg[t + 1 - par, rows, :], ww1[t], ((1,), (1,)))
            slope[:, 0:C0] = v
            slope[:, C0:PAD] = jnp.zeros((256, PAD - C0), f32)

            @pl.loop(0, 6)
            def _(q, par=par, k=k):
                lanes = pl.ds(pl.multiple_of(128 * q, 128), 128)
                xv = raw[par, pl.ds(pl.multiple_of(rawown + 256 * k, 16), 256), lanes].astype(f32)
                slopes = dv[par, pl.ds(256 * k, 256), lanes].astype(f32) * slope[:, lanes]
                scaled = (xv - small[2:3, lanes]) * small[3:4, lanes]
                slope[:, lanes] = slopes
                small[4:5, lanes] += jnp.sum(slopes * scaled, axis=0, keepdims=True)
                small[5:6, lanes] += jnp.sum(slopes, axis=0, keepdims=True)

            dst = pl.ds(256 * k, 256)
            gp[par, dst, 0:384] = slope[:, 0:384].astype(bf16)
            gp[par, dst, 384:768] = pltpu.roll(slope[...], PAD - HALF0, 1)[:, 0:384].astype(bf16)
            if (par, k) == (0, 1):
                second_of_two()
                send_slopes(0)
            if (par, k) == (1, 0):
                to_other_axis(0)
                to_other_axis(1)

    all6 = Total(p, (ab1.at[4], ab2.at[4]), (as1.at[5], ar1.at[5], as2.at[5], ar2.at[5]))
    all6.start(small[4:6])

    to_other_axis(2)
    to_other_axis(3)
    for k in range(3):
        arrived(re.at[k], 4 + k)
    g2 = dot(rep2[...], total(uc[p.y], [re[k] for k in range(3)]))
    e2_own = 2 * p.x + c
    for e in range(8):
        pz2[e] = g2[32 * e : 32 * e + 32].astype(bf16)
    for k, (device, e) in enumerate(xc_peers()):
        cp = remote(pz2.at[e], rz2.at[e2_own], gs.at[50 + k], gr.at[50 + e2_own], device)
        cp.start()
        flying.append(cp)
    rz2[e2_own] = pz2[e2_own]
    for t in range(2):
        last_of(t)
    to_other_axis(4)
    for t in range(2, 5):
        last_of(t)
    g1 = dot(rep1[...], va[...].reshape(240, 384))
    for e in range(8):
        pz[e] = g1[48 * e : 48 * e + 48].astype(bf16)
    for k, (device, zi, ci) in enumerate(column_peers(p)):
        cp = remote(pz.at[2 * zi + ci], rz.at[p.e], gs.at[42 + k], gr.at[42 + p.e], device)
        cp.start()
        flying.append(cp)
    rz[p.e] = pz[p.e]
    all6.middle()

    def summed(parts, half):
        v = parts[half].astype(f32)
        for k in range(1, 4):
            v = v + parts[2 * k + half].astype(f32)
        return v

    for cp in loads:
        cp.wait()
    for _, e in xc_peers():
        arrived(rz2.at[e], 50 + e)
    for half in range(2):
        grad[48:80, 384 * half : 384 * half + 384] = summed(rz2, half)
    nt = ((1,), (1,))
    nb[...] = jnp.zeros_like(nb)
    dd[...] = jnp.zeros_like(dd)

    def turn2(v):
        return dot(v[:, 0:384], ww2[0]) + dot(v[:, 384:768], ww2[1])

    def turn3(v):
        return dot(v[:, 0:384], ww2[2]) + dot(v[:, 384:768], wwp[...])

    turned = turn2(grad[48:72].astype(bf16))
    for t in range(3):
        first_new, second_new, direction = adam_block(f2[t], q2[t], turned[8 * t : 8 * t + 3])
        nf2[t] = first_new
        nq2[t] = second_new
        dd[40 + 8 * t : 43 + 8 * t, :] = direction
    turned = turn3(grad[72:80].astype(bf16))
    first_new, second_new, direction = adam_block(f3[...], q3[...], turned[0:3])
    nf3[...] = first_new
    nq3[...] = second_new
    dd[64:67] = direction
    d2 = dd[40:64].astype(bf16)
    update = jnp.concatenate([dot(d2, ww2[0], nt), dot(d2, ww2[1], nt)], axis=1)
    row_of_two = (68, 80, 84)
    for t in range(3):
        master_new, average_new = master_block(m2[t], update[8 * t : 8 * t + 3], 0.02, a2[t])
        nm2[t] = master_new
        na2[t] = average_new
        nb[row_of_two[t] : row_of_two[t] + 3, :] = master_new
    d3 = dd[64:72].astype(bf16)
    update = jnp.concatenate([dot(d3, ww2[2], nt), dot(d3, wwp[...], nt)], axis=1)
    master_new, average_new = master_block(m3[...], update[0:3], 0.05, a3[...])
    nm3[...] = master_new
    na3[...] = average_new
    nb[64:67, :] = master_new
    for cp in stores[4:12]:
        cp.start()

    def hop(src, dst, send_at, recv_at, device):
        cp = remote(src, dst, hs.at[send_at], hr.at[recv_at], device)
        cp.start()
        flying.append(cp)

    def landed(dst, sem):
        remote(dst, dst, hs.at[0], hr.at[sem], other_core).wait_recv()

    qa = 2 * p.y + p.zh
    qb = 2 * p.x + p.zh

    def near_peers(axis):
        for k in range(1, 8):
            i = lax.rem((p.y if axis == "y" else p.x) + k // 2, 4)
            zh = lax.rem(p.zh + k % 2, 2)
            z = 2 * zh + zl
            yield (p.at(y=i, z=z) if axis == "y" else p.at(x=i, z=z)), 2 * i + zh

    def gather_near(near, fa, fb, rows, base):
        fa[qa] = near[0:rows]
        fb[qb] = near[rows : 2 * rows]
        for k, (device, _) in enumerate(near_peers("y")):
            hop(near.at[pl.ds(0, rows)], fa.at[qa], base + k, base + qa, device)
        for k, (device, _) in enumerate(near_peers("x")):
            hop(near.at[pl.ds(rows, rows)], fb.at[qb], base + 8 + k, base + 8 + qb, device)

    def gather_far(fa, fb, pack, pa, pb, parts_a, parts_b, ga, gb, base):
        for _, q in near_peers("y"):
            landed(fa.at[q], base + q)
        pa[...] = dot(pack, fa[...].reshape(8 * fa.shape[1], PAD)).astype(bf16)
        for k in range(3):
            device, _ = along(k, "x")
            for n, part in enumerate(parts_a):
                hop(pa.at[part], ga.at[(c, p.x) + part], base + 16 + 8 * n + k, base + 16 + 8 * n + p.x, device)
        for _, q in near_peers("x"):
            landed(fb.at[q], base + 8 + q)
        pb[...] = dot(pack, fb[...].reshape(8 * fb.shape[1], PAD)).astype(bf16)
        for k in range(3):
            device, _ = along(k, "y")
            for n, part in enumerate(parts_b):
                hop(pb.at[part], gb.at[(c, p.y) + part], base + 20 + 8 * n + k, base + 20 + 8 * n + p.y, device)
        kept = []
        for n, part in enumerate(parts_a):
            hop(pa.at[part], ga.at[(c, p.x) + part], base + 35 + 8 * n, base + 32 + 8 * n + p.x, other_core)
            kept.append(pltpu.make_async_copy(pa.at[part], ga.at[(c, p.x) + part], bs.at[8 + n]))
        for n, part in enumerate(parts_b):
            hop(pb.at[part], gb.at[(c, p.y) + part], base + 39 + 8 * n, base + 36 + 8 * n + p.y, other_core)
            kept.append(pltpu.make_async_copy(pb.at[part], gb.at[(c, p.y) + part], bs.at[10 + n]))
        for cp in kept:
            cp.start()
        return kept

    def gather_over(parts_a, parts_b, ga, gb, base):
        for k in range(3):
            _, i = along(2 - k, "x")
            for n, part in enumerate(parts_a):
                ref = ga.at[(c, i) + part]
                landed(ref, base + 16 + 8 * n + i)
                hop(ref, ref, base + 32 + 8 * n + k, base + 32 + 8 * n + i, other_core)
            _, i = along(2 - k, "y")
            for n, part in enumerate(parts_b):
                ref = gb.at[(c, i) + part]
                landed(ref, base + 20 + 8 * n + i)
                hop(ref, ref, base + 36 + 8 * n + k, base + 36 + 8 * n + i, other_core)

    def gather_end(parts_a, parts_b, ga, gb, base):
        for i in range(4):
            for n, part in enumerate(parts_a):
                landed(ga.at[(1 - c, i) + part], base + 32 + 8 * n + i)
            for n, part in enumerate(parts_b):
                landed(gb.at[(1 - c, i) + part], base + 36 + 8 * n + i)

    whole2 = ((slice(None), slice(None)),)
    near2[...] = nb[64:96].astype(bf16)
    gather_near(near2, fa2, fb2, 16, 0)

    for device, zi, ci in column_peers(p):
        e = 2 * zi + ci
        arrived(rz.at[e], 42 + e)
    for half in range(2):
        grad[0:48, 384 * half : 384 * half + 384] = summed(rz, half)
    turned = dot(grad[0:40, 0:C0].astype(bf16), bb1[...])
    for t in range(5):
        first_new, second_new, direction = adam_block(f1[t], q1[t], turned[8 * t : 8 * t + 6])
        nf1[t] = first_new
        nq1[t] = second_new
        dd[8 * t : 8 * t + 6, 0:C0] = direction
    update = dot(dd[0:40, 0:C0].astype(bf16), bb1[...], nt)
    row_of = (0, 8, 16, 32, 40)
    for t in range(5):
        master_new, average_new = master_block(m1[t], update[8 * t : 8 * t + 6], 0.02, a1[t])
        nm1[t] = master_new
        na1[t] = average_new
        nb[row_of[t] : row_of[t] + 6, 0:C0] = master_new
        if t == 2:
            nb[48:54, 0:C0] = master_new
    for cp in stores[0:4]:
        cp.start()
    near1[...] = nb[0:64].astype(bf16)
    gather_near(near1, fa1, fb1, 32, 48)
    send_slopes(1)
    kept2 = gather_far(fa2, fb2, pack2[...], pa2, pb2_, whole2, whole2, ga2, gb2, 0)
    sixth = all6.end()
    stats[0:2] = sixth
    stats[5:6] = mean1
    stats[6:7] = rs1
    stats[7:8] = rs1 * gain1
    stats[8:10] = sixth * inv_n1
    stats[10:16] = jnp.zeros((6, PAD), f32)
    taps2 = (pl.ds(0, 96), slice(None))
    parts_a = (taps2, (pl.ds(96, 48), pl.ds(0, 384)))
    parts_b = (taps2, (pl.ds(96, 48), pl.ds(384, 384)))
    kept1 = gather_far(fa1, fb1, pack1[...], pa1, pb1_, parts_a, parts_b, ga1, gb1, 48)
    gather_over(whole2, whole2, ga2, gb2, 0)
    gather_over(parts_a, parts_b, ga1, gb1, 48)
    gather_end(whole2, whole2, ga2, gb2, 0)
    gather_end(parts_a, parts_b, ga1, gb1, 48)
    for cp in kept1 + kept2 + stores:
        cp.wait()

    for t in range(5):
        to_core(t).wait_send()
    for cp in flying:
        cp.wait_send()
    for half in range(2):
        for par in range(2):
            for k in range(2):

                def slope_sent(half=half, par=par, k=k):
                    slope_copy(half, par, k).wait_send()

                pl.when(jnp.logical_not(to_self(half)))(slope_sent)
    for j in range(2):

        def out_here(j=j):
            rows = out.at[pl.ds(512 * j, 512), :]
            remote(rows, rows, ss.at[0], rs.at[23 + j], other_core).wait_recv()

        pl.when(jnp.logical_not(is_self & (c == j)))(out_here)
    for j in range(2):
        for par in range(2):
            for k in range(2):
                part = sl_home.at[j, par, pl.ds(256 * k, 256), :]
                remote(part, part, ss.at[0], rs.at[25 + 4 * j + 2 * par + k], other_core).wait_recv()


VMEM = pl.BlockSpec(memory_space=pltpu.VMEM)
ANY = pl.BlockSpec(memory_space=pl.ANY)


def run_step(xt, offsets, owners, cot, w1, w2, wp, params, bases, states, consts):
    shape = jax.ShapeDtypeStruct
    dma = pltpu.SemaphoreType.DMA
    scratch = [pltpu.VMEM(a.shape, f32) for a in states] * 2
    scratch += [
        pltpu.VMEM((5, 4, 4, 48, PAD), bf16),
        pltpu.VMEM((4, 4, 96, C1), bf16),
        pltpu.VMEM((2, HALF0, LANES), bf16),
        pltpu.VMEM((2, 576, PAD), bf16),
        pltpu.VMEM((6, WIN, PAD), bf16),
        pltpu.VMEM((5, C0, C1), bf16),
        pltpu.VMEM((3, H, C1), bf16),
        pltpu.VMEM((H, C1), bf16),
        pltpu.VMEM((WIN, C1), f32),
        pltpu.VMEM((WIN, C1), f32),
        pltpu.VMEM((WIN, C1), bf16),
        pltpu.VMEM((WIN, H), f32),
        pltpu.VMEM((WIN, H), f32),
        pltpu.VMEM((WIN, H), bf16),
        pltpu.VMEM((3, WIN, H), bf16),
        pltpu.VMEM((WIN, C1), f32),
        pltpu.VMEM((6, WIN, C1), bf16),
        pltpu.VMEM((2, OWN, C1), bf16),
        pltpu.VMEM((256, PAD), f32),
        pltpu.VMEM((8, PAD), f32),
        pltpu.VMEM((8, 128), f32),
        pltpu.VMEM((8, 128), f32),
        pltpu.VMEM((8, PAD), f32),
        pltpu.VMEM((2, 128, PAD), f32),
        pltpu.VMEM((2, OWN, PAD), bf16),
        pltpu.VMEM((5, 4, 4, 48, 384), bf16),
        pltpu.VMEM((4, 4, 96, 384), bf16),
        pltpu.VMEM((5, 3, 4, 48, 384), bf16),
        pltpu.VMEM((5, 3, 48, 384), bf16),
        pltpu.VMEM((3, 4, 96, 384), bf16),
        pltpu.VMEM((3, 96, 384), bf16),
        pltpu.VMEM((5, 4, 48, 384), bf16),
        pltpu.VMEM((4, 96, 384), bf16),
        pltpu.VMEM((5, 48, 384), bf16),
        pltpu.VMEM((8, 48, 384), bf16),
        pltpu.VMEM((8, 48, 384), bf16),
        pltpu.VMEM((8, 32, 384), bf16),
        pltpu.VMEM((8, 32, 384), bf16),
        pltpu.VMEM((C0, C0), f32),
        pltpu.VMEM((C0, C0), bf16),
        pltpu.VMEM((80, PAD), f32),
        pltpu.VMEM((72, PAD), f32),
        pltpu.VMEM((96, PAD), f32),
        pltpu.VMEM((64, PAD), bf16),
        pltpu.VMEM((32, PAD), bf16),
        pltpu.VMEM((8, 32, PAD), bf16),
        pltpu.VMEM((8, 32, PAD), bf16),
        pltpu.VMEM((8, 16, PAD), bf16),
        pltpu.VMEM((8, 16, PAD), bf16),
        pltpu.VMEM((144, PAD), bf16),
        pltpu.VMEM((144, PAD), bf16),
        pltpu.VMEM((48, PAD), bf16),
        pltpu.VMEM((48, PAD), bf16),
        pltpu.VMEM((8, 8, PAD), f32),
        pltpu.VMEM((16, 8, PAD), f32),
        pltpu.VMEM((5, 8, 2, PAD), f32),
        pltpu.VMEM((5, 16, 2, PAD), f32),
        dma((40,)),
        dma((40,)),
        dma((10,)),
        dma((6, 8)),
        dma((6, 8)),
        dma((6, 16)),
        dma((6, 16)),
        dma((60,)),
        dma((60,)),
        dma((96,)),
        dma((96,)),
        dma((12,)),
        dma((24,)),
    ]
    one = shape((2, 4, 144, PAD), bf16)
    two = shape((2, 4, 48, PAD), bf16)
    return pl.pallas_call(
        step_kernel,
        out_shape=(
            shape((BINS, 384), bf16),
            shape((2, 2, OWN, 384), bf16),
            shape((16, PAD), f32),
            one,
            one,
            two,
            two,
            *[shape(a.shape, f32) for a in states],
        ),
        in_specs=[VMEM, VMEM, VMEM, ANY, ANY, ANY, ANY] + [VMEM] * 14 + [ANY] * 15,
        out_specs=(ANY, ANY, VMEM, *[ANY] * 16),
        scratch_shapes=scratch,
        compiler_params=pltpu.CompilerParams(
            collective_id=0, has_side_effects=True, vmem_limit_bytes=63 * 2**20
        ),
    )(
        xt, offsets, owners, cot, w1, w2, wp, *params,
        *[consts[n] for n in ("e1", "bw1", "e2", "bw2", "rep1", "rep2", "pack1", "pack2")],
        *bases, *states,
    )


def norm_block(gradient, parameters, moments):
    first_new, second_new, direction = adam_block(moments[0], moments[1], gradient)
    return parameters - norm_rate * direction, first_new, second_new


def finish_kernel(
    xt_in, offsets, owners, slopes_in, stats, ga1, gb1, ga2, gb2, out_in, *rest,
):
    p = Place()
    zl = p.zl
    params = rest[0:6]
    moments = rest[6:9]
    rep_a, rep_b, at_a, at_b, rep2a, rep2b, at2a, at2b = rest[9:17]
    states_in = rest[17:29]
    out, gin, v1, v1f, v1s, v2, v2f, v2s, v3, v3f, v3s, cp1, cp2, cp3 = rest[29:43]
    states_out = rest[43:55]
    gav, gbv, gav2, gbv2, held, tr, xt, slopes, outv, cp1v, cp2v, cp3v, *held_states, ls, ns = rest[55:]
    third_a = (slice(None), slice(None), pl.ds(96, 48), pl.ds(0, 384))
    third_b = (slice(None), slice(None), pl.ds(96, 48), pl.ds(384, 384))
    taps2 = (slice(None), slice(None), pl.ds(0, 96))
    copies = [
        pltpu.make_async_copy(ga1.at[taps2], gav.at[taps2], ls.at[0]),
        pltpu.make_async_copy(gb1.at[taps2], gbv.at[taps2], ls.at[1]),
        pltpu.make_async_copy(ga1.at[third_a], gav.at[third_a], ls.at[4]),
        pltpu.make_async_copy(gb1.at[third_b], gbv.at[third_b], ls.at[5]),
        pltpu.make_async_copy(ga2, gav2, ls.at[6]),
        pltpu.make_async_copy(gb2, gbv2, ls.at[7]),
    ]
    first = [
        pltpu.make_async_copy(xt_in, xt, ls.at[8]),
        pltpu.make_async_copy(slopes_in.at[0], slopes.at[0], ls.at[9]),
        pltpu.make_async_copy(slopes_in.at[1], slopes.at[1], ls.at[10]),
    ]
    passed_in = [(out_in, outv)] + list(zip(states_in, held_states))
    passed_out = [(outv, out)] + list(zip(held_states, states_out))
    ins = [pltpu.make_async_copy(a, b, ns.at[k]) for k, (a, b) in enumerate(passed_in)]
    outs_ = [pltpu.make_async_copy(a, b, ns.at[13 + k]) for k, (a, b) in enumerate(passed_out)]
    for cp in first + copies + ins:
        cp.start()

    vec = stats[...]
    v326 = jnp.where(zl == 0, vec, pltpu.roll(vec, PAD - HALF0, 1))
    tr[0:16, :] = v326[:, 0:384]
    tr[16:128, :] = jnp.zeros((112, 384), f32)
    cols = jnp.transpose(tr[...])
    mean_c = cols[0:HALF0, 5:6]
    rs_c = cols[0:HALF0, 6:7]
    scale_c = cols[0:HALF0, 7:8]
    gm_c = cols[0:HALF0, 8:9]
    bm_c = cols[0:HALF0, 9:10]
    off_home = offsets[...].astype(f32)
    tn = ((0,), (0,))
    rowq = iota((128, 256), 0)
    laneq = iota((128, 256), 1)
    put_even = (laneq == 2 * rowq).astype(bf16)
    put_odd = (laneq == 2 * rowq + 1).astype(bf16)
    back = []
    first[0].wait()
    for j in range(2):
        first[1 + j].wait()
        for k in range(4):
            bins = pl.ds(128 * k, 128)
            st = dot(slopes[j, 0, bins, :], put_even, tn) + dot(slopes[j, 1, bins, :], put_odd, tn)
            lanes = pl.ds(1024 * j + 256 * k, 256)
            xf = xt[:, lanes].astype(f32)
            scaled = (xf - mean_c) * rs_c
            ok = ((iota((1, 256), 1) + (1024 * j + 256 * k)).astype(f32) >= 2.0 * off_home).astype(f32)
            held[:, lanes] = ok * (scale_c * (st[0:HALF0] - bm_c - scaled * gm_c))
        half = pl.ds(1024 * j, 1024)
        back.append(pltpu.make_async_copy(held.at[:, half], gin.at[:, 0, half], ls.at[2 + j]))
        back[j].start()
    for cp, on in zip(ins, outs_):
        cp.wait()
        on.start()

    grads1 = v326[0:2, 0:HALF0]
    v384 = jnp.where(zl == 0, vec, pltpu.roll(vec, PAD - HALF1, 1))
    grads2 = v384[2:4, 0:HALF1]
    v192 = jnp.where(zl == 0, vec, pltpu.roll(vec, PAD - HALFH, 1))
    halves = [(grads1[0:1], grads1[1:2]), (grads2[0:1], grads2[1:2]), (v192[4:5, 0:HALFH], v192[4:5, H : H + HALFH])]
    outs = [(v1, v1f, v1s), (v2, v2f, v2s), (v3, v3f, v3s)]
    for n in range(3):
        for r in range(2):
            old = (moments[n][0, r : r + 1, :], moments[n][1, r : r + 1, :])
            new = norm_block(halves[n][r], params[2 * n + r][...].reshape(1, -1), old)
            for q in range(3):
                outs[n][q][r : r + 1, :] = new[q]

    own_row = jnp.broadcast_to(owners[...].astype(f32), (8, 64))

    def column(rep, at, width):
        own = jnp.sum(rep[...].astype(f32) * own_row[0:1], axis=1, keepdims=True)
        return own * float(width) + at[...]

    lane = iota((384, 384), 1).astype(f32)
    place_a = (lane == column(rep_a, at_a, 6)).astype(bf16)
    place_b = (lane == column(rep_b, at_b, 6)).astype(bf16)
    own8 = own_row.astype(bf16)
    place2a = (iota((H, H), 0).astype(f32) == (dot(own8, rep2a[...])[0:1] * 3.0 + at2a[...])).astype(bf16)
    place2b = (iota((H, H), 0).astype(f32) == (dot(own8, rep2b[...])[0:1] * 3.0 + at2b[...])).astype(bf16)
    for cp in copies:
        cp.wait()

    def give(held_ref, result, sem):
        cp = pltpu.make_async_copy(held_ref, result, ls.at[sem])
        cp.start()
        back.append(cp)

    for t in range(2):
        block = gav[:, :, 48 * t : 48 * t + 48, :].reshape(384, PAD)
        cp1v[t] = dot(block[:, 0:C0], place_a, tn).astype(bf16)
        give(cp1v.at[t], cp1.at[t], 11 + 2 * t)
        block = gbv[:, :, 48 * t : 48 * t + 48, :].reshape(384, PAD)
        cp1v[3 + t] = dot(block[:, 0:C0], place_b, tn).astype(bf16)
        give(cp1v.at[3 + t], cp1.at[3 + t], 12 + 2 * t)
    cp1v[2, 0:384] = dot(gav[:, :, 96:144, 0:384].reshape(384, 384), place_a, tn).astype(bf16)
    cp1v[2, 384:C0] = dot(gbv[:, :, 96:144, 384:C0].reshape(384, C0 - 384), place_b, tn).astype(bf16)
    give(cp1v.at[2], cp1.at[2], 15)
    two = dot(place2a, gav2[...].reshape(384, PAD)).astype(bf16)
    cp3v[...] = two[0:HALFH]
    cp2v[0] = two[HALFH:H]
    two = dot(place2b, gbv2[...].reshape(384, PAD)).astype(bf16)
    cp2v[1] = two[0:HALFH]
    cp2v[2] = two[HALFH:H]
    give(cp3v, cp3, 16)
    give(cp2v, cp2, 17)
    back.extend(outs_)
    for cp in back:
        cp.wait()


def run_finish(xt, offsets, owners, slopes, stats, gathered, out, params, moments, states, consts):
    shape = jax.ShapeDtypeStruct
    vec = [shape((2, n), f32) for n in (HALF0,) * 3 + (HALF1,) * 3 + (HALFH,) * 3]
    names = ("rep_a", "rep_b", "at_a", "at_b", "rep2a", "rep2b", "at2a", "at2b")
    return pl.pallas_call(
        finish_kernel,
        out_shape=(
            shape((BINS, 384), bf16),
            shape((HALF0, 1, 2 * BINS), f32),
            *vec,
            shape((5, C0, 384), bf16),
            shape((3, HALFH, C1), bf16),
            shape((HALFH, C1), bf16),
            *[shape(a.shape, f32) for a in states],
        ),
        in_specs=[ANY, VMEM, VMEM, ANY, VMEM] + [ANY] * 5 + [VMEM] * 17 + [ANY] * 12,
        out_specs=(ANY, ANY, *[VMEM] * 9, *[ANY] * 15),
        scratch_shapes=[
            pltpu.VMEM((2, 4, 144, PAD), bf16),
            pltpu.VMEM((2, 4, 144, PAD), bf16),
            pltpu.VMEM((2, 4, 48, PAD), bf16),
            pltpu.VMEM((2, 4, 48, PAD), bf16),
            pltpu.VMEM((HALF0, 2 * BINS), f32),
            pltpu.VMEM((128, 384), f32),
            pltpu.VMEM((HALF0, 2 * BINS), bf16),
            pltpu.VMEM((2, 2, OWN, 384), bf16),
            pltpu.VMEM((BINS, 384), bf16),
            pltpu.VMEM((5, C0, 384), bf16),
            pltpu.VMEM((3, HALFH, C1), bf16),
            pltpu.VMEM((HALFH, C1), bf16),
            *[pltpu.VMEM(a.shape, f32) for a in states],
            pltpu.SemaphoreType.DMA((20,)),
            pltpu.SemaphoreType.DMA((26,)),
        ],
        compiler_params=pltpu.CompilerParams(vmem_limit_bytes=63 * 2**20),
    )(
        xt, offsets, owners, slopes, stats, *gathered, out, *params, *moments,
        *[consts[n] for n in names], *states,
    )


def make_consts():
    e1 = np.zeros((64, 768), np.float32)
    bw1 = np.zeros((8, 768), np.float32)
    e2 = np.zeros((64, 384), np.float32)
    bw2 = np.zeros((8, 384), np.float32)
    for s in range(64):
        g, zh, c = s // 4, (s // 2) % 2, s % 2
        for b in range(2):
            e = (2 * zh + b) * 2 + c
            for w in range(6):
                e1[s, (g * 8 + e) * 6 + w] = 1
                bw1[:, (g * 8 + e) * 6 + w] = b * 384 + w
            block = ((2 * zh + b) * 4 + g % 4) * 8 + (g // 4) * 2 + c
            for w in range(3):
                e2[s, block * 3 + w] = 1
                bw2[:, block * 3 + w] = b * 192 + w
    rep1 = np.zeros((8 * 48, 240), np.float32)
    rep2 = np.zeros((8 * 32, 96), np.float32)
    for e in range(8):
        for t in range(5):
            for w in range(6):
                rep1[e * 48 + t * 8 + w, t * 48 + e * 6 + w] = 1
        for m in range(4):
            for w in range(3):
                rep2[e * 32 + m * 8 + w, m * 24 + e * 3 + w] = 1
    pack1 = np.zeros((144, 256), np.float32)
    pack2 = np.zeros((48, 128), np.float32)
    for o in range(8):
        for w in range(6):
            for t in range(3):
                pack1[t * 48 + o * 6 + w, o * 32 + 8 * t + w] = 1
        for w in range(3):
            for m in range(2):
                pack2[m * 24 + o * 3 + w, o * 16 + 4 * m + w] = 1
    rep_a = np.zeros((384, 64), np.float32)
    rep_b = np.zeros((384, 64), np.float32)
    at_a = np.zeros((384, 1), np.float32)
    rep2a = np.zeros((64, 384), np.float32)
    rep2b = np.zeros((64, 384), np.float32)
    at2 = np.zeros((1, 384), np.float32)
    for c in range(2):
        for i in range(4):
            for o in range(8):
                j, zh = o // 2, o % 2
                s_a = ((i * 4 + j) * 2 + zh) * 2 + c
                s_b = ((j * 4 + i) * 2 + zh) * 2 + c
                for w in range(6):
                    r = (c * 4 + i) * 48 + o * 6 + w
                    rep_a[r, s_a] = 1
                    rep_b[r, s_b] = 1
                    at_a[r, 0] = w
                for m in range(2):
                    for w in range(3):
                        r = (c * 4 + i) * 48 + m * 24 + o * 3 + w
                        rep2a[s_a, r] = 1
                        rep2b[s_b, r] = 1
                        at2[0, r] = m * 192 + w
    low = lambda a: jnp.asarray(a, bf16)
    return {
        "e1": low(e1), "bw1": jnp.asarray(bw1), "e2": low(e2), "bw2": jnp.asarray(bw2),
        "rep1": low(rep1), "rep2": low(rep2), "pack1": low(pack1), "pack2": low(pack2),
        "rep_a": low(rep_a), "rep_b": low(rep_b), "at_a": jnp.asarray(at_a), "at_b": jnp.asarray(at_a),
        "rep2a": low(rep2a), "rep2b": low(rep2b), "at2a": jnp.asarray(at2), "at2b": jnp.asarray(at2),
    }


def local(
    inputs, offsets, owners, cotangent,
    norm1_gain, norm1_bias, norm1_moments,
    norm2_gain, norm2_bias, norm2_moments,
    norm3_gain, norm3_bias, norm3_moments,
    conv1_copy, conv1_master, conv1_first, conv1_second, conv1_average, basis1,
    conv2_copy, conv2_master, conv2_first, conv2_second, conv2_average, basis2,
    project_copy, project_master, project_first, project_second, project_average, basis3,
):
    consts = make_consts()
    flip2 = lambda a: jnp.swapaxes(a, -1, -2)
    xt = flip2(inputs[0])
    offsets = offsets[None]
    owners = owners[None]
    params = [norm1_gain, norm1_bias, norm2_gain, norm2_bias, norm3_gain, norm3_bias]
    states = [
        conv1_master, conv1_first, conv1_second, conv1_average,
        conv2_master, conv2_first, conv2_second, conv2_average,
        project_master, project_first, project_second, project_average,
    ]
    out, slopes, stats, *more = run_step(
        xt, offsets, owners, cotangent[0], conv1_copy, flip2(conv2_copy), flip2(project_copy), params,
        (basis1, basis2, basis3), [flip2(a) for a in states], consts,
    )
    gathered, new = more[0:4], more[4:]
    result = run_finish(
        xt, offsets, owners, slopes, stats, gathered, out, params,
        (norm1_moments, norm2_moments, norm3_moments), new, consts,
    )
    out, gin, *vec = result[0:11]
    cp1, cp2, cp3 = result[11:14]
    nm1, nf1, nq1, na1, nm2, nf2, nq2, na2, nm3, nf3, nq3, na3 = [flip2(a) for a in result[14:]]
    return (
        out[None], jnp.transpose(gin, (1, 2, 0)), *vec,
        nm1, cp1, nf1, nq1, na1,
        nm2, flip2(cp2), nf2, nq2, na2,
        nm3, flip2(cp3), nf3, nq3, na3,
    )


def solution(mesh):
    finer = Mesh(mesh.devices.reshape(4, 4, 2, 2, mesh.shape["ch"]), SEQ_CH)
    owner3 = P(None, None, SEQ_CH)
    owner2 = P(None, SEQ_CH)
    half3 = P(None, None, "ch")
    in_specs = (
        P(SEQ, None, "ch"), P(SEQ), P(), P(SEQ, None, "ch"),
        P("ch"), P("ch"), half3, P("ch"), P("ch"), half3, P("ch"), P("ch"), half3,
        half3, owner3, owner3, owner3, owner3, P(),
        half3, owner3, owner3, owner3, owner3, P(),
        P(None, "ch"), owner2, owner2, owner2, owner2, P(),
    )
    vec = P(None, "ch")
    out_specs = (
        P(SEQ, None, "ch"), P(SEQ, None, "ch"), *[vec] * 9,
        owner3, half3, owner3, owner3, owner3,
        owner3, half3, owner3, owner3, owner3,
        owner2, vec, owner2, owner2, owner2,
    )
    return jax.shard_map(local, mesh=finer, in_specs=in_specs, out_specs=out_specs, check_vma=False)
```

```python
import math

import jax
import jax.numpy as jnp
import numpy as np
from jax import lax
from jax.experimental import pallas as pl
from jax.experimental.pallas import tpu as pltpu
from jax.sharding import Mesh
from jax.sharding import PartitionSpec as P

STEP = 8
SEQ = ("seq_0", "seq_1", "seq_2", "seq_3")
SEQ_CH = ("seq_0", "seq_1", "seq_2", "seq_3", "ch")
MESH = pl.DeviceIdType.MESH
bf16 = jnp.bfloat16
f32 = jnp.float32

eps_norm = 1e-05
beta_one = 0.9
beta_two = 0.95
adam_eps = 1e-08
decay_rate = 0.01
average_rate = 0.9
norm_rate = 0.05

C0, C1, H = 652, 768, 384
HALF0, HALF1, HALFH = 326, 384, 192
BINS = 1024
OWN = 512
WIN = 528
LANES = 1152
PAD = 768

GELU_K = math.sqrt(2.0 / math.pi)
GELU_C = 0.044715


def gelu(v):
    return 0.5 * v * (1.0 + jnp.tanh(GELU_K * (v + GELU_C * (v * v * v))))


def gelu_slope(v):
    square = v * v
    t = jnp.tanh(GELU_K * v * (1.0 + GELU_C * square))
    return 0.5 * (1.0 + t) + 0.5 * GELU_K * v * (1.0 - t * t) * (1.0 + 3.0 * GELU_C * square)


def dot(a, b, dims=((1,), (0,))):
    return lax.dot_general(a, b, (dims, ((), ())), preferred_element_type=f32)


def iota(shape, dim):
    return lax.broadcasted_iota(jnp.int32, shape, dim)


def adam_block(first, second, turned):
    first_new = beta_one * first + (1.0 - beta_one) * turned
    second_new = beta_two * second + (1.0 - beta_two) * turned * turned
    direction = (
        first_new
        / (1.0 - beta_one**STEP)
        / (jnp.sqrt(second_new / (1.0 - beta_two**STEP)) + adam_eps)
    )
    return first_new, second_new, direction


def master_block(master, update, rate, average):
    master_new = master - rate * (update + decay_rate * master)
    return master_new, average_rate * average + (1.0 - average_rate) * master_new


class Place:
    def __init__(self):
        self.x, self.y, self.zh, self.c, self.zl = [lax.axis_index(n) for n in SEQ_CH]
        self.z = 2 * self.zh + self.zl
        self.e = 2 * self.z + self.c
        self.g = 4 * self.x + self.y

    def at(self, **other):
        v = {"x": self.x, "y": self.y, "z": self.z, "c": self.c}
        v.update(other)
        z = v["z"]
        return (v["x"], v["y"], lax.div(z, 2), v["c"], lax.rem(z, 2))


def remote(src, dst, send, recv, device):
    return pltpu.make_async_remote_copy(
        src_ref=src, dst_ref=dst, send_sem=send, recv_sem=recv, device_id=device, device_id_type=MESH
    )


def column_peers(p):
    out = []
    for k in range(1, 8):
        z = lax.rem(p.z + k // 2, 4)
        c = lax.rem(p.c + k % 2, 2)
        out.append((p.at(z=z, c=c), z, c))
    return out


def plane_peers(p):
    out = []
    for k in range(1, 16):
        x = lax.rem(p.x + k // 4, 4)
        y = lax.rem(p.y + k % 4, 4)
        out.append((p.at(x=x, y=y), x, y))
    return out


def other_peers(p):
    over = lax.rem(p.z + 2, 4)
    out = [p.at(x=lax.rem(p.x + k, 4), c=1 - p.c) for k in (1, 2, 3)]
    out += [p.at(x=lax.rem(p.x + k, 4), z=over) for k in (1, 2, 3)]
    out += [p.at(y=lax.rem(p.y + k, 4), z=over) for k in (1, 2, 3)]
    return out


class Total:
    def __init__(self, p, bufs, sems):
        self.p = p
        self.b1, self.b2 = bufs
        self.s1, self.r1, self.s2, self.r2 = sems

    def start(self, value):
        p = self.p
        self.b1[p.e] = value
        self.c1 = []
        for k, (device, _, _) in enumerate(column_peers(p)):
            cp = remote(self.b1.at[p.e], self.b1.at[p.e], self.s1.at[k], self.r1.at[p.e], device)
            cp.start()
            self.c1.append(cp)

    def middle(self):
        p = self.p
        for device, z, c in column_peers(p):
            e = 2 * z + c
            remote(self.b1.at[e], self.b1.at[e], self.s1.at[0], self.r1.at[e], device).wait_recv()
        total = self.b1[0]
        for k in range(1, 8):
            total = total + self.b1[k]
        for cp in self.c1:
            cp.wait_send()
        self.b2[p.g] = total
        self.c2 = []
        for k, (device, _, _) in enumerate(plane_peers(p)):
            cp = remote(self.b2.at[p.g], self.b2.at[p.g], self.s2.at[k], self.r2.at[p.g], device)
            cp.start()
            self.c2.append(cp)

    def end(self):
        p = self.p
        for device, x, y in plane_peers(p):
            g = 4 * x + y
            remote(self.b2.at[g], self.b2.at[g], self.s2.at[0], self.r2.at[g], device).wait_recv()
        total = self.b2[0]
        for k in range(1, 16):
            total = total + self.b2[k]
        for cp in self.c2:
            cp.wait_send()
        return total


TAP_CORE = (0, 0, 1, 1, 0)
UNIT_CORE = (0, 1, 0, 1)


def step_kernel(
    xt, offsets, owners, cot, w1, w2, wp, pg1, pb1, pg2, pb2, pg3, pb3,
    e1, bw1, e2, bw2, e4, bw4, rep1, rep2, rep4, pack1, pack2, b1, b2, b3,
    *rest,
):
    states_in = rest[0:12]
    out, sl_home, stats, ga1, gb1, ga2, gb2 = rest[12:19]
    states_out = rest[19:31]
    held_in = rest[31:43]
    held_out = rest[43:55]
    step_body(
        xt, offsets, owners, cot, w1, w2, wp, pg1, pb1, pg2, pb2, pg3, pb3,
        e1, bw1, e2, bw2, e4, bw4, rep1, rep2, rep4, pack1, pack2, b1, b2, b3,
        states_in, states_out, held_in, held_out,
        out, sl_home, stats, ga1, gb1, ga2, gb2, *rest[55:],
    )


def step_body(
    xt, offsets, owners, cot, w1, w2, wp, pg1, pb1, pg2, pb2, pg3, pb3,
    e1, bw1, e2, bw2, e4, bw4, rep1, rep2, rep4, pack1, pack2, b1, b2, b3,
    states_in, states_out, held_in, held_out,
    out, sl_home, stats, ga1, gb1, ga2, gb2,
    s1, s2, xw, raw, aa, ww1, ww2, wwp, pooled, diff, cc, hid, og, no, hh, mid, gg, gp,
    slope, small, offs, offw, acc, tr, dv,
    t1, t2, ra, rb, rd, re, ua, uc, va, pz, rz, pz2, rz2, pz4, rz4,
    b1f, bb1, grad, dd, nb, near1, near2, fa1, fb1, fa2, fb2, pa1, pb1_, pa2, pb2_,
    par, ab1, ab2,
    ss, rs, ls, as1, ar1, as2, ar2, gs, gr, hs, hr, bs, ns,
):
    m1, f1, q1, a1, m2, f2, q2, a2, m3, f3, q3, a3 = held_in
    nm1, nf1, nq1, na1, nm2, nf2, nq2, na2, nm3, nf3, nq3, na3 = held_out
    loads = [pltpu.make_async_copy(states_in[k], held_in[k], ns.at[k]) for k in range(12)]
    stores = [pltpu.make_async_copy(held_out[k], states_out[k], ns.at[12 + k]) for k in range(12)]
    mm = gg.at[0:3]
    p = Place()
    offs[...] = jnp.broadcast_to(offsets[...].astype(f32), (8, 128))
    c, zl = p.c, p.zl
    flip = p.at(z=3 - p.z)
    direct = p.at(z=p.z + 1 - 2 * zl)
    other_core = p.at(c=1 - c)

    bar = pltpu.get_barrier_semaphore()
    for device, _, _ in column_peers(p):
        pl.semaphore_signal(bar, inc=1, device_id=device, device_id_type=MESH)
    for device, _, _ in plane_peers(p):
        pl.semaphore_signal(bar, inc=1, device_id=device, device_id_type=MESH)
    for device in other_peers(p):
        pl.semaphore_signal(bar, inc=1, device_id=device, device_id_type=MESH)

    mine = pl.ds(pl.multiple_of(384 * c, 128), 384)
    others = pl.ds(pl.multiple_of(384 - 384 * c, 128), 384)
    my_lanes = pl.ds(pl.multiple_of(384 * zl, 128), 384)
    its_lanes = pl.ds(pl.multiple_of(384 - 384 * zl, 128), 384)
    my_rows = pl.ds(pl.multiple_of(192 * zl, 16), 192)
    its_rows = pl.ds(pl.multiple_of(192 - 192 * zl, 16), 192)

    def unit_ref(u, rows):
        return ww2.at[u, rows, :] if u < 3 else wwp.at[rows, :]

    own_w = [pltpu.make_async_copy(w1.at[t], ww1.at[t, :, my_lanes], ls.at[t]) for t in range(5)]
    own_w += [
        pltpu.make_async_copy(w2.at[u] if u < 3 else wp, unit_ref(u, my_rows), ls.at[5 + u])
        for u in range(4)
    ]
    for cp in own_w:
        cp.start()

    pl.semaphore_wait(bar, 31)

    is_self = c == zl
    not_self = c != zl
    home_chip = 2 * p.zh + c

    PARTS = ((0, 256), (256, 256), (512, 256), (768, 384))

    def window(j, part):
        at, size = PARTS[part]
        return xt.at[:, pl.ds(pl.multiple_of(896 * j + at, 128), size)]

    def window_there(k, part):
        return xw.at[k, :, pl.ds(*PARTS[part])]

    def cot_window(j):
        return cot.at[pl.ds(pl.multiple_of(496 * j, 16), WIN), :]

    cc_mine = cc.at[:, pl.ds(pl.multiple_of(384 * zl, 128), 384)]
    x_a = [
        remote(window(c, h), window_there(zl, h), ss.at[36 + 2 * h], rs.at[36 + 2 * h + zl], p.at(z=home_chip, c=c))
        for h in range(4)
    ]
    x_b = [
        remote(
            window(1 - c, h), window_there(zl, h), ss.at[37 + 2 * h], rs.at[36 + 2 * h + zl],
            p.at(z=home_chip, c=1 - c),
        )
        for h in range(4)
    ]
    c_a = remote(cot_window(c), cc_mine, ss.at[2], rs.at[2 + zl], p.at(z=home_chip, c=c))
    c_b = remote(cot_window(1 - c), cc_mine, ss.at[3], rs.at[2 + zl], p.at(z=home_chip, c=1 - c))
    o_a = remote(offs, offw, ss.at[4], rs.at[4], other_core)

    def send_windows(h):
        pl.when(not_self)(lambda: x_a[h].start())

        def keep():
            pltpu.make_async_copy(window(c, h), window_there(zl, h), rs.at[36 + 2 * h + zl]).start()

        pl.when(is_self)(keep)
        x_b[h].start()

    send_windows(0)
    o_a.start()

    def tap_over(t):
        to = direct if t == 4 else flip
        return remote(ww1.at[t, :, my_lanes], ww1.at[t, :, my_lanes], ss.at[5 + t], rs.at[5 + t], to)

    def tap_here(t):
        return remote(
            ww1.at[t, :, its_lanes], ww1.at[t, :, its_lanes], ss.at[10 + t], rs.at[10 + t], other_core
        )

    def unit_over(u):
        return remote(
            unit_ref(u, my_rows), unit_ref(u, my_rows), ss.at[15 + u], rs.at[15 + u], flip
        )

    def unit_here(u):
        return remote(
            unit_ref(u, its_rows), unit_ref(u, its_rows), ss.at[19 + u], rs.at[19 + u], other_core
        )

    own_w[0].wait()
    pl.when(c == 0)(lambda: tap_over(0).start())

    for cp in loads:
        cp.start()

    off_home = offs[0:1, 0:1]
    total_s = jnp.zeros((8, HALF0), f32)
    total_q = jnp.zeros((8, HALF0), f32)
    for k in range(8):
        lanes = pl.ds(256 * k, 256)
        mask = ((iota((8, 256), 1) + 256 * k).astype(f32) >= 2.0 * off_home).astype(bf16)
        xb = xt[:, lanes]
        xf = xb.astype(f32)
        sq = xf * xf
        hi = sq.astype(bf16)
        lo = (sq - hi.astype(f32)).astype(bf16)
        nt = ((1,), (1,))
        total_s = total_s + dot(mask, xb, nt)
        total_q = total_q + (dot(mask, hi, nt) + dot(mask, lo, nt))
    small[...] = jnp.zeros_like(small)
    small[0:1, 0:HALF0] = total_s[0:1]
    small[1:2, 0:HALF0] = total_q[0:1]
    small[2:3, 0:HALF0] = pg1[...].reshape(1, HALF0)
    small[3:4, 0:HALF0] = pb1[...].reshape(1, HALF0)
    small[4:5, 0:HALF1] = pg2[...].reshape(1, HALF1)
    small[5:6, 0:HALF1] = pb2[...].reshape(1, HALF1)
    small[6:7, 0:HALFH] = pg3[...].reshape(1, HALFH)
    small[6:7, H : H + HALFH] = pb3[...].reshape(1, HALFH)
    here = small[...]
    half_row = iota((8, PAD), 0)
    moved = jnp.where(
        half_row < 4,
        pltpu.roll(here, HALF0, 1),
        jnp.where(half_row < 6, pltpu.roll(here, HALF1, 1), pltpu.roll(here, HALFH, 1)),
    )
    here = jnp.where(zl == 0, here, moved)
    count = jnp.maximum(BINS - off_home, 0.0)
    lane8 = iota((8, PAD), 1)
    row8 = iota((8, PAD), 0)
    params_over = remote(par.at[0], par.at[1], ss.at[35], rs.at[35], direct)
    par[0] = here
    here = here + jnp.where((lane8 == PAD - 1) & (row8 == 0), count, 0.0)
    all1 = Total(p, (ab1.at[5], ab2.at[5]), (as1.at[0], ar1.at[0], as2.at[0], ar2.at[0]))
    all1.start(here[0:2])
    params_over.start()
    for h in range(1, 4):
        send_windows(h)
    for t in range(1, 5):
        own_w[t].wait()
        pl.when(c == TAP_CORE[t])(lambda t=t: tap_over(t).start())

    @pl.when(not_self)
    def _():
        c_a.start()

    @pl.when(is_self)
    def _():
        pltpu.make_async_copy(cot_window(c), cc_mine, rs.at[2 + zl]).start()

    c_b.start()
    for u in range(4):
        own_w[5 + u].wait()
        pl.when(c == UNIT_CORE[u])(lambda u=u: unit_over(u).start())
    all1.middle()

    owners_row = jnp.broadcast_to(owners[...].astype(f32), (8, 64)).astype(bf16)
    nat1 = dot(owners_row, e1[...])[0:1] * 6.0 + bw1[0:1]
    nat2 = dot(owners_row, e2[...])[0:1] * 3.0 + bw2[0:1]
    for k in range(4):
        s1[4, k] = ((iota((192, PAD), 0) + 192 * k).astype(f32) == nat1).astype(bf16).reshape(4, 48, PAD)
    perm2 = (iota((H, H), 0).astype(f32) == nat2).astype(bf16)

    row = iota((128, 128), 0)
    pick = (iota((128, 128), 1) == jnp.where(row < 64, 2 * row, 2 * row - 127)).astype(bf16)
    def window_here(k, h):
        part = window_there(k, h)
        remote(part, part, ss.at[0], rs.at[36 + 2 * h + k], other_core).wait_recv()

    tr[...] = jnp.zeros_like(tr)

    def blocks(k, second):
        for b in range(9):
            if b in (0, 2, 4, 6):
                window_here(k, b // 2)
            buf = b % 2
            tr[buf, :, 0:HALF0] = dot(pick, xw[k, :, pl.ds(128 * b, 128)], ((1,), (1,)))
            bins = pl.ds(64 * b, 64)

            def put(value, bins=bins):
                value = value.astype(bf16)
                for par in range(2):
                    part = value[64 * par : 64 * par + 64]
                    raw[par, bins, :] = raw[par, bins, :] + part if second else part

            pl.when(k == 0)(lambda: put(tr[buf]))
            pl.when(k == 1)(lambda: put(pltpu.roll(tr[buf], HALF0, 1)))

    blocks(zl, False)
    first = all1.end()
    n1 = first[0:1, PAD - 1 : PAD]
    n2 = 0.5 * n1
    inv_n1 = 1.0 / n1
    inv_n2 = 1.0 / n2
    real = iota((1, PAD), 1) < C0
    mean1 = jnp.where(real, first[0:1], 0.0) * inv_n1
    var1 = first[1:2] * inv_n1 - mean1 * mean1
    rs1 = lax.rsqrt(var1 + eps_norm)
    params_over.wait()
    both_halves = par[0] + par[1]
    gain1, bias1 = both_halves[2:3], both_halves[3:4]
    gain2, bias2 = both_halves[4:5], both_halves[5:6]
    gain3, bias3 = both_halves[6:7, 0:H], both_halves[6:7, H : 2 * H]

    remote(offs, offw, ss.at[4], rs.at[4], other_core).wait()
    off = jnp.where(is_self, offs[0:1, 0:1], offw[0:1, 0:1])

    bin0 = 496 * c
    own0 = pl.multiple_of(16 * c, 16)
    raw0 = pl.multiple_of(48 * c, 16)
    rawown = pl.multiple_of(64 * c, 16)

    def valid_mask(rows, at=0):
        return ((iota((rows, 1), 0) + (bin0 + at)).astype(f32) >= off).astype(f32)

    def own_mask(rows, at=0):
        r = iota((rows, 1), 0) + at
        return ((r >= 16 * c) & (r < 16 * c + OWN)).astype(f32)

    not_first = (iota((WIN, 1), 0) > 0).astype(f32)
    not_last = (iota((WIN, 1), 0) < WIN - 1).astype(f32)

    def before(v):
        return (pltpu.roll(v, 1, 0) * not_first).astype(bf16)

    def after(v):
        return (pltpu.roll(v, WIN - 1, 0) * not_last).astype(bf16)

    small[0:1] = rs1 * gain1
    small[1:2] = bias1 - mean1 * (rs1 * gain1)
    small[2:3] = mean1
    small[3:4] = rs1

    def norm_tile(q):
        lanes = pl.ds(pl.multiple_of(128 * q, 128), 128)
        scale, shift = small[0:1, lanes], small[1:2, lanes]
        valid = valid_mask(WIN)
        for par in range(2):
            v = raw[par, pl.ds(raw0, WIN), lanes].astype(f32)
            v = gelu(v * scale + shift) * valid
            aa[par, :, lanes] = before(v)
            aa[2 + par, :, lanes] = v.astype(bf16)
            aa[4 + par, :, lanes] = after(v)

    def pass_on(t):
        def there():
            part = ww1.at[t, :, its_lanes]
            remote(part, part, ss.at[5 + t], rs.at[5 + t], flip).wait_recv()
            tap_here(t).start()

        pl.when(c == TAP_CORE[t])(there)

    @pl.loop(0, 2)
    def _(k):
        norm_tile(3 * zl + k)

    pass_on(0)
    blocks(1 - zl, True)
    pass_on(1)
    pass_on(2)

    @pl.loop(0, 4)
    def _(k):
        norm_tile(jnp.where(zl == 0, k + 2, jnp.where(k < 3, k, 5)))

    pass_on(3)
    pass_on(4)
    for t in range(5):
        pl.when(c != TAP_CORE[t])(lambda t=t: tap_here(t).wait_recv())

    acc[...] = jnp.zeros_like(acc)

    @pl.loop(0, 3)
    def _(k):
        rows = pl.ds(pl.multiple_of(176 * k, 16), 176)
        h0 = jnp.zeros((176, C1), f32)
        for t in range(5):
            h0 = h0 + dot(aa[t, rows, 0:C0], ww1[t])
        h1 = jnp.zeros((176, C1), f32)
        for t in range(5):
            h1 = h1 + dot(aa[t + 1, rows, 0:C0], ww1[t])
        d = h0 - h1
        v = jnp.maximum(h0, h1) + (jnp.log(1.0 + jnp.exp(-jnp.abs(d))) - math.log(2.0))
        diff[rows, :] = d
        pooled[rows, :] = v
        m = valid_mask(176, 176 * k) * own_mask(176, 176 * k)
        vm = v * m
        acc[0:1] += jnp.sum(vm, axis=0, keepdims=True)
        acc[1:2] += jnp.sum(vm * v, axis=0, keepdims=True)

    all2 = Total(p, (ab1.at[0], ab2.at[0]), (as1.at[1], ar1.at[1], as2.at[1], ar2.at[1]))
    all2.start(acc[0:2])

    def early_slopes(par):
        @pl.loop(0, 6)
        def _(q):
            lanes = pl.ds(pl.multiple_of(128 * q, 128), 128)
            xv = raw[par, pl.ds(rawown, OWN), lanes].astype(f32)
            turn = gelu_slope(xv * small[0:1, lanes] + small[1:2, lanes])
            dv[par, :, lanes] = (turn * valid_mask(OWN, 16 * c)).astype(bf16)

    early_slopes(0)
    all2.middle()
    for u in range(4):

        def there_u(u=u):
            remote(
                unit_ref(u, its_rows), unit_ref(u, its_rows), ss.at[15 + u], rs.at[15 + u], flip
            ).wait_recv()
            unit_here(u).start()

        pl.when(c == UNIT_CORE[u])(there_u)
    for k in range(2):
        part = cc.at[:, pl.ds(384 * k, 384)]
        remote(part, part, ss.at[0], rs.at[2 + k], other_core).wait_recv()
    for u in range(4):
        pl.when(c == UNIT_CORE[u])(lambda u=u: unit_here(u).wait_send())
        pl.when(c != UNIT_CORE[u])(lambda u=u: unit_here(u).wait_recv())
    og[...] = dot(cc[...], wwp[...], ((1,), (1,)))
    early_slopes(1)

    @pl.when(not_self)
    def _():
        for h in range(4):
            x_a[h].wait_send()
        c_a.wait_send()

    for h in range(4):
        x_b[h].wait_send()
    c_b.wait_send()
    for t in range(5):

        def tap_sent(t=t):
            tap_over(t).wait_send()
            tap_here(t).wait_send()

        pl.when(c == TAP_CORE[t])(tap_sent)
    for u in range(4):
        pl.when(c == UNIT_CORE[u])(lambda u=u: unit_over(u).wait_send())

    second = all2.end()
    mean2 = second[0:1] * inv_n2
    var2 = second[1:2] * inv_n2 - mean2 * mean2
    rs2 = lax.rsqrt(var2 + eps_norm)
    acc[2:3] = rs2 * gain2
    acc[3:4] = bias2 - mean2 * (rs2 * gain2)
    acc[4:5] = mean2
    acc[5:6] = rs2

    @pl.loop(0, 6)
    def _(k):
        lanes = pl.ds(pl.multiple_of(128 * k, 128), 128)
        v = gelu(pooled[:, lanes] * acc[2:3, lanes] + acc[3:4, lanes]) * valid_mask(WIN)
        mm[0, :, lanes] = before(v)
        mm[1, :, lanes] = v.astype(bf16)
        mm[2, :, lanes] = after(v)

    h2 = jnp.zeros((WIN, H), f32)
    for t in range(3):
        h2 = h2 + dot(mm[t], ww2[t], ((1,), (1,)))
    hid[...] = h2
    m = valid_mask(WIN) * own_mask(WIN)
    h2m = h2 * m
    acc[6:7, 0:H] = jnp.sum(h2m, axis=0, keepdims=True)
    acc[6:7, H : 2 * H] = jnp.sum(h2m * h2, axis=0, keepdims=True)
    all3 = Total(p, (ab1.at[1], ab2.at[1]), (as1.at[2], ar1.at[2], as2.at[2], ar2.at[2]))
    all3.start(acc[6:8])

    def basis_rows(src, first, size, buf, sem):
        return pltpu.make_async_copy(src.at[pl.ds(first, size)], buf, bs.at[sem])

    slope_buf = [slope.at[pl.ds(0, 128)], slope.at[pl.ds(128, 128)]]
    rows_buf = slope_buf + [tr.at[0], tr.at[1]]

    def rounds(n):
        got = []
        for k in range(4):
            block = 4 * n + k
            src = b2 if block < 6 else b3
            got.append(basis_rows(src, 128 * (block % 6), 128, rows_buf[k], k))
        return got

    def keep_round(n):
        for k, cp in enumerate(rounds(n)):
            cp.wait()
            block = 4 * n + k
            half, at = block // 3, 128 * (block % 3)
            value = rows_buf[k][...].astype(bf16)
            if half < 3:
                ww2[half, pl.ds(at, 128), :] = value
            else:
                wwp[pl.ds(at, 128), :] = value

    first_basis = pltpu.make_async_copy(b1, b1f, bs.at[4])
    first_basis.start()

    @pl.loop(0, 6)
    def _(q):
        lanes = pl.ds(pl.multiple_of(128 * q, 128), 128)
        turn = gelu_slope(pooled[:, lanes] * acc[2:3, lanes] + acc[3:4, lanes])
        turn = (turn * valid_mask(WIN)).astype(bf16)
        xw[0, 0:272, lanes] = turn[0:272]
        xw[1, 0:256, lanes] = turn[272:WIN]

    all3.middle()

    @pl.loop(0, 6)
    def _(q):
        lanes = pl.ds(pl.multiple_of(128 * q, 128), 128)
        diff[:, lanes] = 1.0 / (1.0 + jnp.exp(-diff[:, lanes]))

    first_basis.wait()
    bb1[...] = b1f[...].astype(bf16)
    third = all3.end()
    mean3 = third[0:1, 0:H] * inv_n2
    var3 = third[0:1, H : 2 * H] * inv_n2 - mean3 * mean3
    rs3 = lax.rsqrt(var3 + eps_norm)
    valid = valid_mask(WIN)
    own = own_mask(WIN)
    h2 = hid[...]
    scaled = (h2 - mean3) * rs3
    pre = scaled * gain3 + bias3
    no[...] = (gelu(pre) * valid).astype(bf16)
    slopes = gelu_slope(pre) * og[...] * valid
    og[...] = slopes
    hid[...] = scaled
    acc[6:7, 0:H] = jnp.sum(slopes * scaled * own, axis=0, keepdims=True)
    acc[6:7, H : 2 * H] = jnp.sum(slopes * own, axis=0, keepdims=True)
    all4 = Total(p, (ab1.at[2], ab2.at[2]), (as1.at[3], ar1.at[3], as2.at[3], ar2.at[3]))
    all4.start(acc[6:8])
    out_rows = pl.ds(pl.multiple_of(512 * c, 16), OWN)
    own_rows = pl.ds(own0, OWN)
    gp[0] = (pooled[own_rows, :] + dot(no[own_rows, :], wwp[...])).astype(bf16)
    all4.middle()

    def out_copy(k):
        return remote(
            gp.at[0, :, pl.ds(384 * k, 384)],
            out.at[out_rows, :],
            ss.at[23 + k],
            rs.at[23 + c],
            p.at(z=2 * p.zh + k, c=zl),
        )

    def out_local(k):
        return pltpu.make_async_copy(
            gp.at[0, :, pl.ds(384 * k, 384)], out.at[out_rows, :], ls.at[9]
        )

    def to_self(k):
        return (zl == k) & is_self

    for k in range(2):
        pl.when(jnp.logical_not(to_self(k)))(lambda k=k: out_copy(k).start())

        pl.when(to_self(k))(lambda k=k: out_local(k).start())

    def put2(m, value):
        s2[:, :, pl.ds(24 * m, 24), :] = value.astype(bf16).reshape(4, 4, 24, C1)

    tn = ((0,), (0,))
    nop = dot(no[own_rows, :], perm2).astype(bf16)
    put2(3, dot(nop, cc[own_rows, :], tn))
    for cp in rounds(0):
        cp.start()
    fourth = all4.end()
    stats[4:5] = fourth[0:1]
    gain_mean = fourth[0:1, 0:H] * inv_n2
    bias_mean = fourth[0:1, H : 2 * H] * inv_n2
    hg = valid_mask(WIN) * (gain3 * rs3) * (og[...] - bias_mean - hid[...] * gain_mean)
    hh[0] = after(hg)
    hh[1] = hg.astype(bf16)
    hh[2] = before(hg)
    mid_grad = jnp.zeros((WIN, C1), f32)
    for t in range(3):
        mid_grad = mid_grad + dot(hh[t], ww2[t])
    mid[...] = mid_grad

    @pl.loop(0, 6)
    def _(k):
        lanes = pl.ds(pl.multiple_of(128 * k, 128), 128)
        v = pooled[:, lanes]
        turn = jnp.concatenate([xw[0, 0:272, lanes], xw[1, 0:256, lanes]], axis=0)
        slopes = turn.astype(f32) * mid[:, lanes]
        scaled = (v - acc[4:5, lanes]) * acc[5:6, lanes]
        mid[:, lanes] = slopes
        pooled[:, lanes] = scaled
        mine = slopes * own_mask(WIN)
        acc[0:1, lanes] = jnp.sum(mine * scaled, axis=0, keepdims=True)
        acc[1:2, lanes] = jnp.sum(mine, axis=0, keepdims=True)

    all5 = Total(p, (ab1.at[3], ab2.at[3]), (as1.at[4], ar1.at[4], as2.at[4], ar2.at[4]))
    all5.start(acc[0:2])
    hp = dot(hh[1, own_rows, :], perm2).astype(bf16)
    put2(0, dot(hp, mm[0, own_rows, :], tn))
    keep_round(0)
    all5.middle()
    for cp in rounds(1):
        cp.start()
    for t in range(1, 3):
        put2(t, dot(hp, mm[t, own_rows, :], tn))
    s2_over = remote(s2.at[:, :, :, others], t2, gs.at[0], gr.at[0], other_core)
    s2_over.start()
    keep_round(1)
    for cp in rounds(2):
        cp.start()
    nat4 = dot(owners_row, e4[...])[0:1] * 6.0 + bw4[0:1]
    for r in range(3):
        for h in range(2):
            hh[r, pl.ds(256 * h, 256), :] = (
                (iota((256, 384), 0) + 256 * r).astype(f32) == nat4[:, 384 * h : 384 * h + 384]
            ).astype(bf16)
    fifth = all5.end()
    stats[2:4] = fifth
    acc[0:2] = fifth * inv_n2

    @pl.loop(0, 6)
    def _(k):
        lanes = pl.ds(pl.multiple_of(128 * k, 128), 128)
        back = acc[2:3, lanes] * (
            mid[:, lanes] - acc[1:2, lanes] - pooled[:, lanes] * acc[0:1, lanes]
        )
        pg = cc[:, lanes].astype(f32) + back * valid_mask(WIN)
        even = diff[:, lanes]
        ge = pg * even
        go = pg * (1.0 - even)
        gg[0, :, lanes] = after(go)
        gg[1, :, lanes] = after(ge)
        gg[2, :, lanes] = go.astype(bf16)
        gg[3, :, lanes] = ge.astype(bf16)
        gg[4, :, lanes] = before(go)
        gg[5, :, lanes] = before(ge)

    def total(own, parts):
        v = own.astype(f32)
        for part in parts:
            v = v + part.astype(f32)
        return v.astype(bf16)

    def along(k, axis):
        if axis == "x":
            i = lax.rem(p.x + k + 1, 4)
            return p.at(x=i), i
        if axis == "z":
            i = lax.rem(p.z + k + 1, 4)
            return p.at(z=i), i
        i = lax.rem(p.y + k + 1, 4)
        return p.at(y=i), i

    s2_over.wait()
    t2[...] = total(t2[...], [s2[:, :, :, mine]])
    flying = []

    def send(src, dst, sem, device):
        cp = remote(src, dst, gs.at[sem], gr.at[sem], device)
        cp.start()
        flying.append(cp)

    def arrived(dst, sem):
        remote(dst, dst, gs.at[0], gr.at[sem], other_core).wait_recv()

    for k in range(3):
        device, i = along(k, "z")
        send(t2.at[i], rd.at[k], 1 + k, device)
    keep_round(2)

    for k in range(2):

        def out_sent(k=k):
            out_copy(k).wait_send()

        pl.when(jnp.logical_not(to_self(k)))(out_sent)
        pl.when(to_self(k))(lambda k=k: out_local(k).wait())
    perm = s1[4].reshape(PAD, PAD)
    gp[0] = dot(gg[3, own_rows, :], perm).astype(bf16)
    gp[1] = dot(gg[2, own_rows, :], perm).astype(bf16)

    TAP_AXIS = ("x", "y", "x", "y", "z")
    SECOND = {"x": "y", "y": "x", "z": "y"}

    def for_last_tap(slot):
        g = gg[slot, own_rows, :]
        halves = []
        for h in range(2):
            v = dot(g[:, 0:256], hh[0, pl.ds(256 * h, 256), :])
            for r in (1, 2):
                v = v + dot(g[:, 256 * r : 256 * r + 256], hh[r, pl.ds(256 * h, 256), :])
            halves.append(v.astype(bf16))
        return halves

    def to_core(t):
        return remote(s1.at[t, :, :, :, others], t1.at[t], gs.at[7 + t], gr.at[7 + t], other_core)

    def to_axis(t):
        to_core(t).wait_recv()
        t1[t] = total(t1[t], [s1[t, :, :, :, mine]])
        for k in range(3):
            device, i = along(k, TAP_AXIS[t])
            src = t1.at[t, :, i] if TAP_AXIS[t] == "y" else t1.at[t, i]
            send(src, ra.at[t, k], 12 + 3 * t + k, device)

    def to_other_axis(t):
        for k in range(3):
            arrived(ra.at[t, k], 12 + 3 * t + k)
        own_part = {"x": lambda: t1[t, p.x], "y": lambda: t1[t, :, p.y], "z": lambda: t1[t, p.z]}[TAP_AXIS[t]]()
        ua[t] = total(own_part, [ra[t, k] for k in range(3)])
        for k in range(3):
            device, i = along(k, SECOND[TAP_AXIS[t]])
            send(ua.at[t, i], rb.at[t, k], 27 + 3 * t + k, device)

    def last_of(t):
        for k in range(3):
            arrived(rb.at[t, k], 27 + 3 * t + k)
        own_part = ua[t, p.x] if TAP_AXIS[t] == "y" else ua[t, p.y]
        va[t] = total(own_part, [rb[t, k] for k in range(3)])

    for t in range(5):
        if t == 4:
            for k in range(2):
                halves = for_last_tap(3 - k)
                gp[k, :, 0:384] = halves[0]
                gp[k, :, 384:768] = halves[1]
        part = dot(gp[0], aa[t, own_rows, 0:C0], tn) + dot(gp[1], aa[t + 1, own_rows, 0:C0], tn)
        part = part.astype(bf16).reshape(4, 4, 48, C0)
        s1[t, :, :, :, 0:C0] = part
        s1[t, :, :, :, C0:PAD] = jnp.zeros((4, 4, 48, PAD - C0), bf16)
        to_core(t).start()
        if t > 0:
            to_axis(t - 1)
    to_axis(4)

    def second_of_two():
        for k in range(3):
            arrived(rd.at[k], 1 + k)
        uc[...] = total(t2[p.z], [rd[k] for k in range(3)])
        for k in range(3):
            device, i = along(k, "y")
            send(uc.at[i], re.at[k], 4 + k, device)

    def xc_peers():
        for k in range(1, 8):
            xi = lax.rem(p.x + k // 2, 4)
            ci = lax.rem(c + k % 2, 2)
            yield p.at(x=xi, c=ci), 2 * xi + ci

    def slope_part(half, par, k):
        return (
            gp.at[par, pl.ds(256 * k, 256), pl.ds(384 * half, 384)],
            sl_home.at[c, par, pl.ds(256 * k, 256), :],
        )

    def slope_copy(half, par, k):
        src, dst = slope_part(half, par, k)
        n = 2 * par + k
        return remote(src, dst, ss.at[25 + 4 * half + n], rs.at[25 + 4 * c + n], p.at(z=2 * p.zh + half, c=zl))

    def slope_local(half, par, k):
        src, dst = slope_part(half, par, k)
        return pltpu.make_async_copy(src, dst, rs.at[25 + 4 * c + 2 * par + k])

    def send_slopes(par):
        for half in range(2):
            for k in range(2):

                def send_slope(half=half, k=k):
                    slope_copy(half, par, k).start()

                def keep_slope(half=half, k=k):
                    slope_local(half, par, k).start()

                pl.when(jnp.logical_not(to_self(half)))(send_slope)
                pl.when(to_self(half))(keep_slope)

    small[4:6] = jnp.zeros((2, PAD), f32)
    for par in range(2):
        for k in range(2):
            rows = pl.ds(pl.multiple_of(own0 + 256 * k, 16), 256)
            v = jnp.zeros((256, C0), f32)
            for t in range(5):
                v = v + dot(gg[t + 1 - par, rows, :], ww1[t], ((1,), (1,)))
            slope[:, 0:C0] = v
            slope[:, C0:PAD] = jnp.zeros((256, PAD - C0), f32)

            @pl.loop(0, 6)
            def _(q, par=par, k=k):
                lanes = pl.ds(pl.multiple_of(128 * q, 128), 128)
                xv = raw[par, pl.ds(pl.multiple_of(rawown + 256 * k, 16), 256), lanes].astype(f32)
                slopes = dv[par, pl.ds(256 * k, 256), lanes].astype(f32) * slope[:, lanes]
                scaled = (xv - small[2:3, lanes]) * small[3:4, lanes]
                slope[:, lanes] = slopes
                small[4:5, lanes] += jnp.sum(slopes * scaled, axis=0, keepdims=True)
                small[5:6, lanes] += jnp.sum(slopes, axis=0, keepdims=True)

            dst = pl.ds(256 * k, 256)
            gp[par, dst, 0:384] = slope[:, 0:384].astype(bf16)
            gp[par, dst, 384:768] = pltpu.roll(slope[...], PAD - HALF0, 1)[:, 0:384].astype(bf16)
            if (par, k) == (0, 1):
                second_of_two()
                send_slopes(0)
            if (par, k) == (1, 0):
                to_other_axis(0)
                to_other_axis(1)

    all6 = Total(p, (ab1.at[4], ab2.at[4]), (as1.at[5], ar1.at[5], as2.at[5], ar2.at[5]))
    all6.start(small[4:6])

    to_other_axis(2)
    to_other_axis(3)
    for k in range(3):
        arrived(re.at[k], 4 + k)
    g2 = dot(rep2[...], total(uc[p.y], [re[k] for k in range(3)]))
    e2_own = 2 * p.x + c
    for e in range(8):
        pz2[e] = g2[32 * e : 32 * e + 32].astype(bf16)
    for k, (device, e) in enumerate(xc_peers()):
        cp = remote(pz2.at[e], rz2.at[e2_own], gs.at[50 + k], gr.at[50 + e2_own], device)
        cp.start()
        flying.append(cp)
    rz2[e2_own] = pz2[e2_own]
    for t in range(2):
        last_of(t)
    to_other_axis(4)
    for t in range(2, 4):
        last_of(t)
    g1 = dot(rep1[...], va[0:4].reshape(192, 384))
    for e in range(8):
        pz[e] = g1[48 * e : 48 * e + 48].astype(bf16)
    for k, (device, zi, ci) in enumerate(column_peers(p)):
        cp = remote(pz.at[2 * zi + ci], rz.at[p.e], gs.at[42 + k], gr.at[42 + p.e], device)
        cp.start()
        flying.append(cp)
    last_of(4)
    g4 = dot(rep4[...], va[4])
    for e in range(8):
        pz4[e] = g4[16 * e : 16 * e + 16].astype(bf16)
    for k, (device, e) in enumerate(xc_peers()):
        cp = remote(pz4.at[e], rz4.at[e2_own], gs.at[58 + k], gr.at[58 + e2_own], device)
        cp.start()
        flying.append(cp)
    rz4[e2_own] = pz4[e2_own]
    rz[p.e] = pz[p.e]
    all6.middle()

    def summed(parts, half):
        v = parts[half].astype(f32)
        for k in range(1, 4):
            v = v + parts[2 * k + half].astype(f32)
        return v

    for cp in loads:
        cp.wait()
    for _, e in xc_peers():
        arrived(rz2.at[e], 50 + e)
    for half in range(2):
        grad[48:80, 384 * half : 384 * half + 384] = summed(rz2, half)
    nt = ((1,), (1,))
    nb[...] = jnp.zeros_like(nb)
    dd[...] = jnp.zeros_like(dd)

    def turn2(v):
        return dot(v[:, 0:384], ww2[0]) + dot(v[:, 384:768], ww2[1])

    def turn3(v):
        return dot(v[:, 0:384], ww2[2]) + dot(v[:, 384:768], wwp[...])

    turned = turn2(grad[48:72].astype(bf16))
    for t in range(3):
        first_new, second_new, direction = adam_block(f2[t], q2[t], turned[8 * t : 8 * t + 3])
        nf2[t] = first_new
        nq2[t] = second_new
        dd[40 + 8 * t : 43 + 8 * t, :] = direction
    turned = turn3(grad[72:80].astype(bf16))
    first_new, second_new, direction = adam_block(f3[...], q3[...], turned[0:3])
    nf3[...] = first_new
    nq3[...] = second_new
    dd[64:67] = direction
    d2 = dd[40:64].astype(bf16)
    update = jnp.concatenate([dot(d2, ww2[0], nt), dot(d2, ww2[1], nt)], axis=1)
    row_of_two = (68, 80, 84)
    for t in range(3):
        master_new, average_new = master_block(m2[t], update[8 * t : 8 * t + 3], 0.02, a2[t])
        nm2[t] = master_new
        na2[t] = average_new
        nb[row_of_two[t] : row_of_two[t] + 3, :] = master_new
    d3 = dd[64:72].astype(bf16)
    update = jnp.concatenate([dot(d3, ww2[2], nt), dot(d3, wwp[...], nt)], axis=1)
    master_new, average_new = master_block(m3[...], update[0:3], 0.05, a3[...])
    nm3[...] = master_new
    na3[...] = average_new
    nb[64:67, :] = master_new
    for cp in stores[4:12]:
        cp.start()

    def hop(src, dst, send_at, recv_at, device):
        cp = remote(src, dst, hs.at[send_at], hr.at[recv_at], device)
        cp.start()
        flying.append(cp)

    def landed(dst, sem):
        remote(dst, dst, hs.at[0], hr.at[sem], other_core).wait_recv()

    qa = 2 * p.y + p.zh
    qb = 2 * p.x + p.zh

    def near_peers(axis):
        for k in range(1, 8):
            i = lax.rem((p.y if axis == "y" else p.x) + k // 2, 4)
            zh = lax.rem(p.zh + k % 2, 2)
            z = 2 * zh + zl
            yield (p.at(y=i, z=z) if axis == "y" else p.at(x=i, z=z)), 2 * i + zh

    def gather_near(near, fa, fb, rows, base):
        fa[qa] = near[0:rows]
        fb[qb] = near[rows : 2 * rows]
        for k, (device, _) in enumerate(near_peers("y")):
            hop(near.at[pl.ds(0, rows)], fa.at[qa], base + k, base + qa, device)
        for k, (device, _) in enumerate(near_peers("x")):
            hop(near.at[pl.ds(rows, rows)], fb.at[qb], base + 8 + k, base + 8 + qb, device)

    def gather_far(fa, fb, pack, pa, pb, parts_a, parts_b, ga, gb, base):
        for _, q in near_peers("y"):
            landed(fa.at[q], base + q)
        pa[...] = dot(pack, fa[...].reshape(8 * fa.shape[1], PAD)).astype(bf16)
        for k in range(3):
            device, _ = along(k, "x")
            for n, part in enumerate(parts_a):
                hop(pa.at[part], ga.at[(c, p.x) + part], base + 16 + 8 * n + k, base + 16 + 8 * n + p.x, device)
        for _, q in near_peers("x"):
            landed(fb.at[q], base + 8 + q)
        pb[...] = dot(pack, fb[...].reshape(8 * fb.shape[1], PAD)).astype(bf16)
        for k in range(3):
            device, _ = along(k, "y")
            for n, part in enumerate(parts_b):
                hop(pb.at[part], gb.at[(c, p.y) + part], base + 20 + 8 * n + k, base + 20 + 8 * n + p.y, device)
        kept = []
        for n, part in enumerate(parts_a):
            hop(pa.at[part], ga.at[(c, p.x) + part], base + 35 + 8 * n, base + 32 + 8 * n + p.x, other_core)
            kept.append(pltpu.make_async_copy(pa.at[part], ga.at[(c, p.x) + part], bs.at[8 + n]))
        for n, part in enumerate(parts_b):
            hop(pb.at[part], gb.at[(c, p.y) + part], base + 39 + 8 * n, base + 36 + 8 * n + p.y, other_core)
            kept.append(pltpu.make_async_copy(pb.at[part], gb.at[(c, p.y) + part], bs.at[10 + n]))
        for cp in kept:
            cp.start()
        return kept

    def gather_over(parts_a, parts_b, ga, gb, base):
        for k in range(3):
            _, i = along(2 - k, "x")
            for n, part in enumerate(parts_a):
                ref = ga.at[(c, i) + part]
                landed(ref, base + 16 + 8 * n + i)
                hop(ref, ref, base + 32 + 8 * n + k, base + 32 + 8 * n + i, other_core)
            _, i = along(2 - k, "y")
            for n, part in enumerate(parts_b):
                ref = gb.at[(c, i) + part]
                landed(ref, base + 20 + 8 * n + i)
                hop(ref, ref, base + 36 + 8 * n + k, base + 36 + 8 * n + i, other_core)

    def gather_end(parts_a, parts_b, ga, gb, base):
        for i in range(4):
            for n, part in enumerate(parts_a):
                landed(ga.at[(1 - c, i) + part], base + 32 + 8 * n + i)
            for n, part in enumerate(parts_b):
                landed(gb.at[(1 - c, i) + part], base + 36 + 8 * n + i)

    whole2 = ((slice(None), slice(None)),)
    near2[...] = nb[64:96].astype(bf16)
    gather_near(near2, fa2, fb2, 16, 0)

    for device, zi, ci in column_peers(p):
        e = 2 * zi + ci
        arrived(rz.at[e], 42 + e)
    for _, e in xc_peers():
        arrived(rz4.at[e], 58 + e)
    for half in range(2):
        lanes = slice(384 * half, 384 * half + 384)
        v = summed(rz, half)
        grad[0:32, lanes] = v[0:32]
        grad[32:40, lanes] = summed(rz4, half)[0:8]
    turned = dot(grad[0:40, 0:C0].astype(bf16), bb1[...])
    for t in range(5):
        first_new, second_new, direction = adam_block(f1[t], q1[t], turned[8 * t : 8 * t + 6])
        nf1[t] = first_new
        nq1[t] = second_new
        dd[8 * t : 8 * t + 6, 0:C0] = direction
    update = dot(dd[0:40, 0:C0].astype(bf16), bb1[...], nt)
    row_of = (0, 8, 16, 32, 40)
    for t in range(5):
        master_new, average_new = master_block(m1[t], update[8 * t : 8 * t + 6], 0.02, a1[t])
        nm1[t] = master_new
        na1[t] = average_new
        nb[row_of[t] : row_of[t] + 6, 0:C0] = master_new
        if t == 2:
            nb[48:54, 0:C0] = master_new
    for cp in stores[0:4]:
        cp.start()
    near1[...] = nb[0:64].astype(bf16)
    gather_near(near1, fa1, fb1, 32, 48)
    send_slopes(1)
    kept2 = gather_far(fa2, fb2, pack2[...], pa2, pb2_, whole2, whole2, ga2, gb2, 0)
    sixth = all6.end()
    stats[0:2] = sixth
    stats[5:6] = mean1
    stats[6:7] = rs1
    stats[7:8] = rs1 * gain1
    stats[8:10] = sixth * inv_n1
    stats[10:16] = jnp.zeros((6, PAD), f32)
    taps2 = (pl.ds(0, 96), slice(None))
    parts_a = (taps2, (pl.ds(96, 48), pl.ds(0, 384)))
    parts_b = (taps2, (pl.ds(96, 48), pl.ds(384, 384)))
    kept1 = gather_far(fa1, fb1, pack1[...], pa1, pb1_, parts_a, parts_b, ga1, gb1, 48)
    gather_over(whole2, whole2, ga2, gb2, 0)
    gather_over(parts_a, parts_b, ga1, gb1, 48)
    gather_end(whole2, whole2, ga2, gb2, 0)
    gather_end(parts_a, parts_b, ga1, gb1, 48)
    for cp in kept1 + kept2 + stores:
        cp.wait()

    for t in range(5):
        to_core(t).wait_send()
    for cp in flying:
        cp.wait_send()
    for half in range(2):
        for par in range(2):
            for k in range(2):

                def slope_sent(half=half, par=par, k=k):
                    slope_copy(half, par, k).wait_send()

                pl.when(jnp.logical_not(to_self(half)))(slope_sent)
    for j in range(2):

        def out_here(j=j):
            rows = out.at[pl.ds(512 * j, 512), :]
            remote(rows, rows, ss.at[0], rs.at[23 + j], other_core).wait_recv()

        pl.when(jnp.logical_not(is_self & (c == j)))(out_here)
    for j in range(2):
        for par in range(2):
            for k in range(2):
                part = sl_home.at[j, par, pl.ds(256 * k, 256), :]
                remote(part, part, ss.at[0], rs.at[25 + 4 * j + 2 * par + k], other_core).wait_recv()


VMEM = pl.BlockSpec(memory_space=pltpu.VMEM)
ANY = pl.BlockSpec(memory_space=pl.ANY)


def run_step(xt, offsets, owners, cot, w1, w2, wp, params, bases, states, consts):
    shape = jax.ShapeDtypeStruct
    dma = pltpu.SemaphoreType.DMA
    scratch = [pltpu.VMEM(a.shape, f32) for a in states] * 2
    scratch += [
        pltpu.VMEM((5, 4, 4, 48, PAD), bf16),
        pltpu.VMEM((4, 4, 96, C1), bf16),
        pltpu.VMEM((2, HALF0, LANES), bf16),
        pltpu.VMEM((2, 576, PAD), bf16),
        pltpu.VMEM((6, WIN, PAD), bf16),
        pltpu.VMEM((5, C0, C1), bf16),
        pltpu.VMEM((3, H, C1), bf16),
        pltpu.VMEM((H, C1), bf16),
        pltpu.VMEM((WIN, C1), f32),
        pltpu.VMEM((WIN, C1), f32),
        pltpu.VMEM((WIN, C1), bf16),
        pltpu.VMEM((WIN, H), f32),
        pltpu.VMEM((WIN, H), f32),
        pltpu.VMEM((WIN, H), bf16),
        pltpu.VMEM((3, WIN, H), bf16),
        pltpu.VMEM((WIN, C1), f32),
        pltpu.VMEM((6, WIN, C1), bf16),
        pltpu.VMEM((2, OWN, C1), bf16),
        pltpu.VMEM((256, PAD), f32),
        pltpu.VMEM((8, PAD), f32),
        pltpu.VMEM((8, 128), f32),
        pltpu.VMEM((8, 128), f32),
        pltpu.VMEM((8, PAD), f32),
        pltpu.VMEM((2, 128, PAD), f32),
        pltpu.VMEM((2, OWN, PAD), bf16),
        pltpu.VMEM((5, 4, 4, 48, 384), bf16),
        pltpu.VMEM((4, 4, 96, 384), bf16),
        pltpu.VMEM((5, 3, 4, 48, 384), bf16),
        pltpu.VMEM((5, 3, 48, 384), bf16),
        pltpu.VMEM((3, 4, 96, 384), bf16),
        pltpu.VMEM((3, 96, 384), bf16),
        pltpu.VMEM((5, 4, 48, 384), bf16),
        pltpu.VMEM((4, 96, 384), bf16),
        pltpu.VMEM((5, 48, 384), bf16),
        pltpu.VMEM((8, 48, 384), bf16),
        pltpu.VMEM((8, 48, 384), bf16),
        pltpu.VMEM((8, 32, 384), bf16),
        pltpu.VMEM((8, 32, 384), bf16),
        pltpu.VMEM((8, 16, 384), bf16),
        pltpu.VMEM((8, 16, 384), bf16),
        pltpu.VMEM((C0, C0), f32),
        pltpu.VMEM((C0, C0), bf16),
        pltpu.VMEM((80, PAD), f32),
        pltpu.VMEM((72, PAD), f32),
        pltpu.VMEM((96, PAD), f32),
        pltpu.VMEM((64, PAD), bf16),
        pltpu.VMEM((32, PAD), bf16),
        pltpu.VMEM((8, 32, PAD), bf16),
        pltpu.VMEM((8, 32, PAD), bf16),
        pltpu.VMEM((8, 16, PAD), bf16),
        pltpu.VMEM((8, 16, PAD), bf16),
        pltpu.VMEM((144, PAD), bf16),
        pltpu.VMEM((144, PAD), bf16),
        pltpu.VMEM((48, PAD), bf16),
        pltpu.VMEM((48, PAD), bf16),
        pltpu.VMEM((2, 8, PAD), f32),
        pltpu.VMEM((6, 8, 2, PAD), f32),
        pltpu.VMEM((6, 16, 2, PAD), f32),
        dma((44,)),
        dma((44,)),
        dma((10,)),
        dma((6, 8)),
        dma((6, 8)),
        dma((6, 16)),
        dma((6, 16)),
        dma((68,)),
        dma((68,)),
        dma((96,)),
        dma((96,)),
        dma((12,)),
        dma((24,)),
    ]
    one = shape((2, 4, 144, PAD), bf16)
    two = shape((2, 4, 48, PAD), bf16)
    return pl.pallas_call(
        step_kernel,
        out_shape=(
            shape((BINS, 384), bf16),
            shape((2, 2, OWN, 384), bf16),
            shape((16, PAD), f32),
            one,
            one,
            two,
            two,
            *[shape(a.shape, f32) for a in states],
        ),
        in_specs=[VMEM, VMEM, VMEM, ANY, ANY, ANY, ANY] + [VMEM] * 17 + [ANY] * 15,
        out_specs=(ANY, ANY, VMEM, *[ANY] * 16),
        scratch_shapes=scratch,
        compiler_params=pltpu.CompilerParams(
            collective_id=0, has_side_effects=True, vmem_limit_bytes=63 * 2**20
        ),
    )(
        xt, offsets, owners, cot, w1, w2, wp, *params,
        *[consts[n] for n in ("e1", "bw1", "e2", "bw2", "e4", "bw4", "rep1", "rep2", "rep4", "pack1", "pack2")],
        *bases, *states,
    )


def norm_block(gradient, parameters, moments):
    first_new, second_new, direction = adam_block(moments[0], moments[1], gradient)
    return parameters - norm_rate * direction, first_new, second_new


def finish_kernel(
    xt_in, offsets, owners, slopes_in, stats, ga1, gb1, ga2, gb2, out_in, *rest,
):
    p = Place()
    zl = p.zl
    params = rest[0:6]
    moments = rest[6:9]
    rep_a, rep_b, at_a, at_b, rep2a, rep2b, at2a, at2b = rest[9:17]
    states_in = rest[17:29]
    out, gin, v1, v1f, v1s, v2, v2f, v2s, v3, v3f, v3s, cp1, cp2, cp3 = rest[29:43]
    states_out = rest[43:55]
    gav, gbv, gav2, gbv2, held, tr, xt, slopes, outv, cp1v, cp2v, cp3v, *held_states, ls, ns = rest[55:]
    third_a = (slice(None), slice(None), pl.ds(96, 48), pl.ds(0, 384))
    third_b = (slice(None), slice(None), pl.ds(96, 48), pl.ds(384, 384))
    taps2 = (slice(None), slice(None), pl.ds(0, 96))
    copies = [
        pltpu.make_async_copy(ga1.at[taps2], gav.at[taps2], ls.at[0]),
        pltpu.make_async_copy(gb1.at[taps2], gbv.at[taps2], ls.at[1]),
        pltpu.make_async_copy(ga1.at[third_a], gav.at[third_a], ls.at[4]),
        pltpu.make_async_copy(gb1.at[third_b], gbv.at[third_b], ls.at[5]),
        pltpu.make_async_copy(ga2, gav2, ls.at[6]),
        pltpu.make_async_copy(gb2, gbv2, ls.at[7]),
    ]
    first = [
        pltpu.make_async_copy(xt_in, xt, ls.at[8]),
        pltpu.make_async_copy(slopes_in.at[0], slopes.at[0], ls.at[9]),
        pltpu.make_async_copy(slopes_in.at[1], slopes.at[1], ls.at[10]),
    ]
    passed_in = [(out_in, outv)] + list(zip(states_in, held_states))
    passed_out = [(outv, out)] + list(zip(held_states, states_out))
    ins = [pltpu.make_async_copy(a, b, ns.at[k]) for k, (a, b) in enumerate(passed_in)]
    outs_ = [pltpu.make_async_copy(a, b, ns.at[13 + k]) for k, (a, b) in enumerate(passed_out)]
    for cp in first + copies + ins:
        cp.start()

    vec = stats[...]
    v326 = jnp.where(zl == 0, vec, pltpu.roll(vec, PAD - HALF0, 1))
    tr[0:16, :] = v326[:, 0:384]
    tr[16:128, :] = jnp.zeros((112, 384), f32)
    cols = jnp.transpose(tr[...])
    mean_c = cols[0:HALF0, 5:6]
    rs_c = cols[0:HALF0, 6:7]
    scale_c = cols[0:HALF0, 7:8]
    gm_c = cols[0:HALF0, 8:9]
    bm_c = cols[0:HALF0, 9:10]
    off_home = offsets[...].astype(f32)
    tn = ((0,), (0,))
    rowq = iota((128, 256), 0)
    laneq = iota((128, 256), 1)
    put_even = (laneq == 2 * rowq).astype(bf16)
    put_odd = (laneq == 2 * rowq + 1).astype(bf16)
    grads1 = v326[0:2, 0:HALF0]
    v384 = jnp.where(zl == 0, vec, pltpu.roll(vec, PAD - HALF1, 1))
    grads2 = v384[2:4, 0:HALF1]
    v192 = jnp.where(zl == 0, vec, pltpu.roll(vec, PAD - HALFH, 1))
    halves = [(grads1[0:1], grads1[1:2]), (grads2[0:1], grads2[1:2]), (v192[4:5, 0:HALFH], v192[4:5, H : H + HALFH])]
    outs = [(v1, v1f, v1s), (v2, v2f, v2s), (v3, v3f, v3s)]
    for n in range(3):
        for r in range(2):
            old = (moments[n][0, r : r + 1, :], moments[n][1, r : r + 1, :])
            new = norm_block(halves[n][r], params[2 * n + r][...].reshape(1, -1), old)
            for q in range(3):
                outs[n][q][r : r + 1, :] = new[q]

    own_row = jnp.broadcast_to(owners[...].astype(f32), (8, 64))

    def column(rep, at, width):
        own = jnp.sum(rep[...].astype(f32) * own_row[0:1], axis=1, keepdims=True)
        return own * float(width) + at[...]

    lane = iota((384, 384), 1).astype(f32)
    place_a = (lane == column(rep_a, at_a, 6)).astype(bf16)
    place_b = (lane == column(rep_b, at_b, 6)).astype(bf16)
    own8 = own_row.astype(bf16)
    place2a = (iota((H, H), 0).astype(f32) == (dot(own8, rep2a[...])[0:1] * 3.0 + at2a[...])).astype(bf16)
    place2b = (iota((H, H), 0).astype(f32) == (dot(own8, rep2b[...])[0:1] * 3.0 + at2b[...])).astype(bf16)
    back = []
    first[0].wait()
    for j in range(2):
        first[1 + j].wait()
        for k in range(4):
            bins = pl.ds(128 * k, 128)
            st = dot(slopes[j, 0, bins, :], put_even, tn) + dot(slopes[j, 1, bins, :], put_odd, tn)
            lanes = pl.ds(1024 * j + 256 * k, 256)
            xf = xt[:, lanes].astype(f32)
            scaled = (xf - mean_c) * rs_c
            ok = ((iota((1, 256), 1) + (1024 * j + 256 * k)).astype(f32) >= 2.0 * off_home).astype(f32)
            held[:, lanes] = ok * (scale_c * (st[0:HALF0] - bm_c - scaled * gm_c))
        half = pl.ds(1024 * j, 1024)
        back.append(pltpu.make_async_copy(held.at[:, half], gin.at[:, 0, half], ls.at[2 + j]))
        back[j].start()
    for cp, on in zip(ins, outs_):
        cp.wait()
        on.start()

    for cp in copies:
        cp.wait()

    def give(held_ref, result, sem):
        cp = pltpu.make_async_copy(held_ref, result, ls.at[sem])
        cp.start()
        back.append(cp)

    for t in range(2):
        block = gav[:, :, 48 * t : 48 * t + 48, :].reshape(384, PAD)
        cp1v[t] = dot(block[:, 0:C0], place_a, tn).astype(bf16)
        give(cp1v.at[t], cp1.at[t], 11 + 2 * t)
        block = gbv[:, :, 48 * t : 48 * t + 48, :].reshape(384, PAD)
        cp1v[3 + t] = dot(block[:, 0:C0], place_b, tn).astype(bf16)
        give(cp1v.at[3 + t], cp1.at[3 + t], 12 + 2 * t)
    cp1v[2, 0:384] = dot(gav[:, :, 96:144, 0:384].reshape(384, 384), place_a, tn).astype(bf16)
    cp1v[2, 384:C0] = dot(gbv[:, :, 96:144, 384:C0].reshape(384, C0 - 384), place_b, tn).astype(bf16)
    give(cp1v.at[2], cp1.at[2], 15)
    two = dot(place2a, gav2[...].reshape(384, PAD)).astype(bf16)
    cp3v[...] = two[0:HALFH]
    cp2v[0] = two[HALFH:H]
    two = dot(place2b, gbv2[...].reshape(384, PAD)).astype(bf16)
    cp2v[1] = two[0:HALFH]
    cp2v[2] = two[HALFH:H]
    give(cp3v, cp3, 16)
    give(cp2v, cp2, 17)
    back.extend(outs_)
    for cp in back:
        cp.wait()


def run_finish(xt, offsets, owners, slopes, stats, gathered, out, params, moments, states, consts):
    shape = jax.ShapeDtypeStruct
    vec = [shape((2, n), f32) for n in (HALF0,) * 3 + (HALF1,) * 3 + (HALFH,) * 3]
    names = ("rep_a", "rep_b", "at_a", "at_b", "rep2a", "rep2b", "at2a", "at2b")
    return pl.pallas_call(
        finish_kernel,
        out_shape=(
            shape((BINS, 384), bf16),
            shape((HALF0, 1, 2 * BINS), f32),
            *vec,
            shape((5, C0, 384), bf16),
            shape((3, HALFH, C1), bf16),
            shape((HALFH, C1), bf16),
            *[shape(a.shape, f32) for a in states],
        ),
        in_specs=[ANY, VMEM, VMEM, ANY, VMEM] + [ANY] * 5 + [VMEM] * 17 + [ANY] * 12,
        out_specs=(ANY, ANY, *[VMEM] * 9, *[ANY] * 15),
        scratch_shapes=[
            pltpu.VMEM((2, 4, 144, PAD), bf16),
            pltpu.VMEM((2, 4, 144, PAD), bf16),
            pltpu.VMEM((2, 4, 48, PAD), bf16),
            pltpu.VMEM((2, 4, 48, PAD), bf16),
            pltpu.VMEM((HALF0, 2 * BINS), f32),
            pltpu.VMEM((128, 384), f32),
            pltpu.VMEM((HALF0, 2 * BINS), bf16),
            pltpu.VMEM((2, 2, OWN, 384), bf16),
            pltpu.VMEM((BINS, 384), bf16),
            pltpu.VMEM((5, C0, 384), bf16),
            pltpu.VMEM((3, HALFH, C1), bf16),
            pltpu.VMEM((HALFH, C1), bf16),
            *[pltpu.VMEM(a.shape, f32) for a in states],
            pltpu.SemaphoreType.DMA((20,)),
            pltpu.SemaphoreType.DMA((26,)),
        ],
        compiler_params=pltpu.CompilerParams(vmem_limit_bytes=63 * 2**20),
    )(
        xt, offsets, owners, slopes, stats, *gathered, out, *params, *moments,
        *[consts[n] for n in names], *states,
    )


def make_consts():
    e1 = np.zeros((64, 768), np.float32)
    bw1 = np.zeros((8, 768), np.float32)
    e2 = np.zeros((64, 384), np.float32)
    bw2 = np.zeros((8, 384), np.float32)
    e4 = np.zeros((64, 768), np.float32)
    bw4 = np.zeros((8, 768), np.float32)
    for s in range(64):
        g, zh, c = s // 4, (s // 2) % 2, s % 2
        for b in range(2):
            e = (2 * zh + b) * 2 + c
            for w in range(6):
                e1[s, (g * 8 + e) * 6 + w] = 1
                bw1[:, (g * 8 + e) * 6 + w] = b * 384 + w
            block = ((2 * zh + b) * 4 + g % 4) * 8 + (g // 4) * 2 + c
            for w in range(6):
                e4[s, block * 6 + w] = 1
                bw4[:, block * 6 + w] = b * 384 + w
            for w in range(3):
                e2[s, block * 3 + w] = 1
                bw2[:, block * 3 + w] = b * 192 + w
    rep1 = np.zeros((8 * 48, 192), np.float32)
    rep4 = np.zeros((8 * 16, 48), np.float32)
    rep2 = np.zeros((8 * 32, 96), np.float32)
    for e in range(8):
        for w in range(6):
            rep4[e * 16 + w, e * 6 + w] = 1
            for t in range(4):
                rep1[e * 48 + t * 8 + w, t * 48 + e * 6 + w] = 1
        for m in range(4):
            for w in range(3):
                rep2[e * 32 + m * 8 + w, m * 24 + e * 3 + w] = 1
    pack1 = np.zeros((144, 256), np.float32)
    pack2 = np.zeros((48, 128), np.float32)
    for o in range(8):
        for w in range(6):
            for t in range(3):
                pack1[t * 48 + o * 6 + w, o * 32 + 8 * t + w] = 1
        for w in range(3):
            for m in range(2):
                pack2[m * 24 + o * 3 + w, o * 16 + 4 * m + w] = 1
    rep_a = np.zeros((384, 64), np.float32)
    rep_b = np.zeros((384, 64), np.float32)
    at_a = np.zeros((384, 1), np.float32)
    rep2a = np.zeros((64, 384), np.float32)
    rep2b = np.zeros((64, 384), np.float32)
    at2 = np.zeros((1, 384), np.float32)
    for c in range(2):
        for i in range(4):
            for o in range(8):
                j, zh = o // 2, o % 2
                s_a = ((i * 4 + j) * 2 + zh) * 2 + c
                s_b = ((j * 4 + i) * 2 + zh) * 2 + c
                for w in range(6):
                    r = (c * 4 + i) * 48 + o * 6 + w
                    rep_a[r, s_a] = 1
                    rep_b[r, s_b] = 1
                    at_a[r, 0] = w
                for m in range(2):
                    for w in range(3):
                        r = (c * 4 + i) * 48 + m * 24 + o * 3 + w
                        rep2a[s_a, r] = 1
                        rep2b[s_b, r] = 1
                        at2[0, r] = m * 192 + w
    low = lambda a: jnp.asarray(a, bf16)
    return {
        "e1": low(e1), "bw1": jnp.asarray(bw1), "e2": low(e2), "bw2": jnp.asarray(bw2),
        "e4": low(e4), "bw4": jnp.asarray(bw4),
        "rep1": low(rep1), "rep2": low(rep2), "rep4": low(rep4), "pack1": low(pack1), "pack2": low(pack2),
        "rep_a": low(rep_a), "rep_b": low(rep_b), "at_a": jnp.asarray(at_a), "at_b": jnp.asarray(at_a),
        "rep2a": low(rep2a), "rep2b": low(rep2b), "at2a": jnp.asarray(at2), "at2b": jnp.asarray(at2),
    }


def local(
    inputs, offsets, owners, cotangent,
    norm1_gain, norm1_bias, norm1_moments,
    norm2_gain, norm2_bias, norm2_moments,
    norm3_gain, norm3_bias, norm3_moments,
    conv1_copy, conv1_master, conv1_first, conv1_second, conv1_average, basis1,
    conv2_copy, conv2_master, conv2_first, conv2_second, conv2_average, basis2,
    project_copy, project_master, project_first, project_second, project_average, basis3,
):
    consts = make_consts()
    flip2 = lambda a: jnp.swapaxes(a, -1, -2)
    xt = flip2(inputs[0])
    offsets = offsets[None]
    owners = owners[None]
    params = [norm1_gain, norm1_bias, norm2_gain, norm2_bias, norm3_gain, norm3_bias]
    states = [
        conv1_master, conv1_first, conv1_second, conv1_average,
        conv2_master, conv2_first, conv2_second, conv2_average,
        project_master, project_first, project_second, project_average,
    ]
    out, slopes, stats, *more = run_step(
        xt, offsets, owners, cotangent[0], conv1_copy, flip2(conv2_copy), flip2(project_copy), params,
        (basis1, basis2, basis3), [flip2(a) for a in states], consts,
    )
    gathered, new = more[0:4], more[4:]
    result = run_finish(
        xt, offsets, owners, slopes, stats, gathered, out, params,
        (norm1_moments, norm2_moments, norm3_moments), new, consts,
    )
    out, gin, *vec = result[0:11]
    cp1, cp2, cp3 = result[11:14]
    nm1, nf1, nq1, na1, nm2, nf2, nq2, na2, nm3, nf3, nq3, na3 = [flip2(a) for a in result[14:]]
    return (
        out[None], jnp.transpose(gin, (1, 2, 0)), *vec,
        nm1, cp1, nf1, nq1, na1,
        nm2, flip2(cp2), nf2, nq2, na2,
        nm3, flip2(cp3), nf3, nq3, na3,
    )


def solution(mesh):
    finer = Mesh(mesh.devices.reshape(4, 4, 2, 2, mesh.shape["ch"]), SEQ_CH)
    owner3 = P(None, None, SEQ_CH)
    owner2 = P(None, SEQ_CH)
    half3 = P(None, None, "ch")
    in_specs = (
        P(SEQ, None, "ch"), P(SEQ), P(), P(SEQ, None, "ch"),
        P("ch"), P("ch"), half3, P("ch"), P("ch"), half3, P("ch"), P("ch"), half3,
        half3, owner3, owner3, owner3, owner3, P(),
        half3, owner3, owner3, owner3, owner3, P(),
        P(None, "ch"), owner2, owner2, owner2, owner2, P(),
    )
    vec = P(None, "ch")
    out_specs = (
        P(SEQ, None, "ch"), P(SEQ, None, "ch"), *[vec] * 9,
        owner3, half3, owner3, owner3, owner3,
        owner3, half3, owner3, owner3, owner3,
        owner2, vec, owner2, owner2, owner2,
    )
    return jax.shard_map(local, mesh=finer, in_specs=in_specs, out_specs=out_specs, check_vma=False)
```

```python
import math

import jax
import jax.numpy as jnp
import numpy as np
from jax import lax
from jax.experimental import pallas as pl
from jax.experimental.pallas import tpu as pltpu
from jax.sharding import Mesh
from jax.sharding import PartitionSpec as P

STEP = 8
SEQ = ("seq_0", "seq_1", "seq_2", "seq_3")
SEQ_CH = ("seq_0", "seq_1", "seq_2", "seq_3", "ch")
MESH = pl.DeviceIdType.MESH
bf16 = jnp.bfloat16
f32 = jnp.float32

eps_norm = 1e-05
beta_one = 0.9
beta_two = 0.95
adam_eps = 1e-08
decay_rate = 0.01
average_rate = 0.9
norm_rate = 0.05

C0, C1, H = 652, 768, 384
HALF0, HALF1, HALFH = 326, 384, 192
BINS = 1024
OWN = 512
WIN = 528
LANES = 1152
PAD = 768

GELU_K = math.sqrt(2.0 / math.pi)
GELU_C = 0.044715


def gelu(v):
    return 0.5 * v * (1.0 + jnp.tanh(GELU_K * (v + GELU_C * (v * v * v))))


def gelu_slope(v):
    square = v * v
    t = jnp.tanh(GELU_K * v * (1.0 + GELU_C * square))
    return 0.5 * (1.0 + t) + 0.5 * GELU_K * v * (1.0 - t * t) * (1.0 + 3.0 * GELU_C * square)


def dot(a, b, dims=((1,), (0,))):
    return lax.dot_general(a, b, (dims, ((), ())), preferred_element_type=f32)


def iota(shape, dim):
    return lax.broadcasted_iota(jnp.int32, shape, dim)


def adam_block(first, second, turned):
    first_new = beta_one * first + (1.0 - beta_one) * turned
    second_new = beta_two * second + (1.0 - beta_two) * turned * turned
    direction = (
        first_new
        / (1.0 - beta_one**STEP)
        / (jnp.sqrt(second_new / (1.0 - beta_two**STEP)) + adam_eps)
    )
    return first_new, second_new, direction


def master_block(master, update, rate, average):
    master_new = master - rate * (update + decay_rate * master)
    return master_new, average_rate * average + (1.0 - average_rate) * master_new


class Place:
    def __init__(self):
        self.x, self.y, self.zh, self.c, self.zl = [lax.axis_index(n) for n in SEQ_CH]
        self.z = 2 * self.zh + self.zl
        self.e = 2 * self.z + self.c
        self.g = 4 * self.x + self.y

    def at(self, **other):
        v = {"x": self.x, "y": self.y, "z": self.z, "c": self.c}
        v.update(other)
        z = v["z"]
        return (v["x"], v["y"], lax.div(z, 2), v["c"], lax.rem(z, 2))


def remote(src, dst, send, recv, device):
    return pltpu.make_async_remote_copy(
        src_ref=src, dst_ref=dst, send_sem=send, recv_sem=recv, device_id=device, device_id_type=MESH
    )


def column_peers(p):
    out = []
    for k in range(1, 8):
        z = lax.rem(p.z + k // 2, 4)
        c = lax.rem(p.c + k % 2, 2)
        out.append((p.at(z=z, c=c), z, c))
    return out


def plane_peers(p):
    out = []
    for k in range(1, 16):
        x = lax.rem(p.x + k // 4, 4)
        y = lax.rem(p.y + k % 4, 4)
        out.append((p.at(x=x, y=y), x, y))
    return out


def other_peers(p):
    over = lax.rem(p.z + 2, 4)
    out = [p.at(x=lax.rem(p.x + k, 4), c=1 - p.c) for k in (1, 2, 3)]
    out += [p.at(x=lax.rem(p.x + k, 4), z=over) for k in (1, 2, 3)]
    out += [p.at(y=lax.rem(p.y + k, 4), z=over) for k in (1, 2, 3)]
    return out


class Total:
    def __init__(self, p, bufs, sems):
        self.p = p
        self.b1, self.b2 = bufs
        self.s1, self.r1, self.s2, self.r2 = sems

    def start(self, value):
        p = self.p
        self.b1[p.e] = value
        self.c1 = []
        for k, (device, _, _) in enumerate(column_peers(p)):
            cp = remote(self.b1.at[p.e], self.b1.at[p.e], self.s1.at[k], self.r1.at[p.e], device)
            cp.start()
            self.c1.append(cp)

    def middle(self):
        p = self.p
        for device, z, c in column_peers(p):
            e = 2 * z + c
            remote(self.b1.at[e], self.b1.at[e], self.s1.at[0], self.r1.at[e], device).wait_recv()
        total = self.b1[0]
        for k in range(1, 8):
            total = total + self.b1[k]
        for cp in self.c1:
            cp.wait_send()
        self.b2[p.g] = total
        self.c2 = []
        for k, (device, _, _) in enumerate(plane_peers(p)):
            cp = remote(self.b2.at[p.g], self.b2.at[p.g], self.s2.at[k], self.r2.at[p.g], device)
            cp.start()
            self.c2.append(cp)

    def end(self):
        p = self.p
        for device, x, y in plane_peers(p):
            g = 4 * x + y
            remote(self.b2.at[g], self.b2.at[g], self.s2.at[0], self.r2.at[g], device).wait_recv()
        total = self.b2[0]
        for k in range(1, 16):
            total = total + self.b2[k]
        for cp in self.c2:
            cp.wait_send()
        return total


UNIT_CORE = (0, 1, 0, 1)


def step_kernel(
    xt, offsets, owners, cot, w1, w2, wp, pg1, pb1, pg2, pb2, pg3, pb3,
    e1, bw1, e2, bw2, e4, bw4, rep1, rep2, rep4, pack1, pack2, b1, b2, b3,
    *rest,
):
    states_in = rest[0:12]
    out, sl_home, stats, ga1, gb1, ga2, gb2 = rest[12:19]
    states_out = rest[19:31]
    held_in = rest[31:43]
    held_out = rest[43:55]
    step_body(
        xt, offsets, owners, cot, w1, w2, wp, pg1, pb1, pg2, pb2, pg3, pb3,
        e1, bw1, e2, bw2, e4, bw4, rep1, rep2, rep4, pack1, pack2, b1, b2, b3,
        states_in, states_out, held_in, held_out,
        out, sl_home, stats, ga1, gb1, ga2, gb2, *rest[55:],
    )


def step_body(
    xt, offsets, owners, cot, w1, w2, wp, pg1, pb1, pg2, pb2, pg3, pb3,
    e1, bw1, e2, bw2, e4, bw4, rep1, rep2, rep4, pack1, pack2, b1, b2, b3,
    states_in, states_out, held_in, held_out,
    out, sl_home, stats, ga1, gb1, ga2, gb2,
    s1, s2, xw, raw, aa, ww1, ww2, wwp, pooled, diff, cc, hid, og, no, hh, mid, gg, gp,
    slope, small, offs, offw, acc, tr, dv,
    t1, t2, ra, rb, rd, re, ua, uc, va, pz, rz, pz2, rz2, pz4, rz4,
    b1f, bb1, grad, dd, nb, near1, near2, fa1, fb1, fa2, fb2, pa1, pb1_, pa2, pb2_,
    par, ab1, ab2,
    ss, rs, ls, as1, ar1, as2, ar2, gs, gr, hs, hr, bs, ns, ws, wr,
):
    m1, f1, q1, a1, m2, f2, q2, a2, m3, f3, q3, a3 = held_in
    nm1, nf1, nq1, na1, nm2, nf2, nq2, na2, nm3, nf3, nq3, na3 = held_out
    loads = [pltpu.make_async_copy(states_in[k], held_in[k], ns.at[k]) for k in range(12)]
    stores = [pltpu.make_async_copy(held_out[k], states_out[k], ns.at[12 + k]) for k in range(12)]
    mm = gg.at[0:3]
    p = Place()
    offs[...] = jnp.broadcast_to(offsets[...].astype(f32), (8, 128))
    c, zl = p.c, p.zl
    flip = p.at(z=3 - p.z)
    direct = p.at(z=p.z + 1 - 2 * zl)
    other_core = p.at(c=1 - c)

    bar = pltpu.get_barrier_semaphore()
    for device, _, _ in column_peers(p):
        pl.semaphore_signal(bar, inc=1, device_id=device, device_id_type=MESH)
    for device, _, _ in plane_peers(p):
        pl.semaphore_signal(bar, inc=1, device_id=device, device_id_type=MESH)
    for device in other_peers(p):
        pl.semaphore_signal(bar, inc=1, device_id=device, device_id_type=MESH)

    mine = pl.ds(pl.multiple_of(384 * c, 128), 384)
    others = pl.ds(pl.multiple_of(384 - 384 * c, 128), 384)
    my_lanes = pl.ds(pl.multiple_of(384 * zl, 128), 384)
    its_lanes = pl.ds(pl.multiple_of(384 - 384 * zl, 128), 384)
    my_rows = pl.ds(pl.multiple_of(192 * zl, 16), 192)
    its_rows = pl.ds(pl.multiple_of(192 - 192 * zl, 16), 192)

    def unit_ref(u, rows):
        return ww2.at[u, rows, :] if u < 3 else wwp.at[rows, :]

    own_w = [pltpu.make_async_copy(w1.at[t], ww1.at[t, :, my_lanes], ls.at[t]) for t in range(5)]
    own_w += [
        pltpu.make_async_copy(w2.at[u] if u < 3 else wp, unit_ref(u, my_rows), ls.at[5 + u])
        for u in range(4)
    ]
    for cp in own_w:
        cp.start()

    pl.semaphore_wait(bar, 31)

    is_self = c == zl
    not_self = c != zl
    home_chip = 2 * p.zh + c

    PARTS = ((0, 256), (256, 256), (512, 256), (768, 384))

    def window(j, part):
        at, size = PARTS[part]
        return xt.at[:, pl.ds(pl.multiple_of(896 * j + at, 128), size)]

    def window_there(k, part):
        return xw.at[k, :, pl.ds(*PARTS[part])]

    def cot_window(j):
        return cot.at[pl.ds(pl.multiple_of(496 * j, 16), WIN), :]

    cc_mine = cc.at[:, pl.ds(pl.multiple_of(384 * zl, 128), 384)]
    x_a = [
        remote(window(c, h), window_there(zl, h), ss.at[36 + 2 * h], rs.at[36 + 2 * h + zl], p.at(z=home_chip, c=c))
        for h in range(4)
    ]
    x_b = [
        remote(
            window(1 - c, h), window_there(zl, h), ss.at[37 + 2 * h], rs.at[36 + 2 * h + zl],
            p.at(z=home_chip, c=1 - c),
        )
        for h in range(4)
    ]
    c_a = remote(cot_window(c), cc_mine, ss.at[2], rs.at[2 + zl], p.at(z=home_chip, c=c))
    c_b = remote(cot_window(1 - c), cc_mine, ss.at[3], rs.at[2 + zl], p.at(z=home_chip, c=1 - c))
    o_a = remote(offs, offw, ss.at[4], rs.at[4], other_core)

    def send_windows(h):
        pl.when(not_self)(lambda: x_a[h].start())

        def keep():
            pltpu.make_async_copy(window(c, h), window_there(zl, h), rs.at[36 + 2 * h + zl]).start()

        pl.when(is_self)(keep)
        x_b[h].start()

    send_windows(0)
    o_a.start()

    def block_at(b, ch):
        t = lax.div(b, 3)
        return ww1.at[t, :, pl.ds(pl.multiple_of(384 * ch + 128 * (b - 3 * t), 128), 128)]

    def block_of(axis, k):
        if axis == "x":
            return 2 * lax.rem(p.x + k, 4) + c
        return 8 + 2 * lax.rem(p.y + k, 4) + c

    def if_block(axis, b, do):
        if axis == "x":
            do()
        else:
            pl.when(b < 15)(do)

    def fetch(axis):
        b = block_of(axis, 0)
        part = block_at(b, zl)
        return b, remote(part, part, ws.at[0 if axis == "x" else 1], wr.at[b], flip)

    def spread(axis):
        b = block_of(axis, 0)
        part = block_at(b, 1 - zl)
        to = [p.at(**{axis: lax.rem((p.x if axis == "x" else p.y) + k, 4)}) for k in (1, 2, 3)]
        first = 2 if axis == "x" else 5
        return b, [remote(part, part, ws.at[first + k], wr.at[b], to[k]) for k in range(3)]

    def across(axis, k):
        b = block_of(axis, k)
        part = block_at(b, 1 - zl)
        return b, remote(part, part, ws.at[(8 if axis == "x" else 12) + k], wr.at[b], other_core)

    def start_fetch(axis):
        b, cp = fetch(axis)
        if_block(axis, b, cp.start)

    def block_here(b):
        part = block_at(b, 1 - zl)
        remote(part, part, ws.at[0], wr.at[b], other_core).wait_recv()

    def start_spread(axis):
        b, cps = spread(axis)

        def do():
            block_here(b)
            for cp in cps + [across(axis, 0)[1]]:
                cp.start()

        if_block(axis, b, do)

    def start_across(axis, k):
        b, cp = across(axis, k)

        def do():
            block_here(b)
            cp.start()

        if_block(axis, b, do)

    def unit_over(u):
        return remote(
            unit_ref(u, my_rows), unit_ref(u, my_rows), ss.at[15 + u], rs.at[15 + u], flip
        )

    def unit_here(u):
        return remote(
            unit_ref(u, its_rows), unit_ref(u, its_rows), ss.at[19 + u], rs.at[19 + u], other_core
        )

    for t in range(5):
        own_w[t].wait()
    start_fetch("x")

    for cp in loads:
        cp.start()

    off_home = offs[0:1, 0:1]
    total_s = jnp.zeros((8, HALF0), f32)
    total_q = jnp.zeros((8, HALF0), f32)
    for k in range(8):
        lanes = pl.ds(256 * k, 256)
        mask = ((iota((8, 256), 1) + 256 * k).astype(f32) >= 2.0 * off_home).astype(bf16)
        xb = xt[:, lanes]
        xf = xb.astype(f32)
        sq = xf * xf
        hi = sq.astype(bf16)
        lo = (sq - hi.astype(f32)).astype(bf16)
        nt = ((1,), (1,))
        total_s = total_s + dot(mask, xb, nt)
        total_q = total_q + (dot(mask, hi, nt) + dot(mask, lo, nt))
    small[...] = jnp.zeros_like(small)
    small[0:1, 0:HALF0] = total_s[0:1]
    small[1:2, 0:HALF0] = total_q[0:1]
    small[2:3, 0:HALF0] = pg1[...].reshape(1, HALF0)
    small[3:4, 0:HALF0] = pb1[...].reshape(1, HALF0)
    small[4:5, 0:HALF1] = pg2[...].reshape(1, HALF1)
    small[5:6, 0:HALF1] = pb2[...].reshape(1, HALF1)
    small[6:7, 0:HALFH] = pg3[...].reshape(1, HALFH)
    small[6:7, H : H + HALFH] = pb3[...].reshape(1, HALFH)
    here = small[...]
    half_row = iota((8, PAD), 0)
    moved = jnp.where(
        half_row < 4,
        pltpu.roll(here, HALF0, 1),
        jnp.where(half_row < 6, pltpu.roll(here, HALF1, 1), pltpu.roll(here, HALFH, 1)),
    )
    here = jnp.where(zl == 0, here, moved)
    count = jnp.maximum(BINS - off_home, 0.0)
    lane8 = iota((8, PAD), 1)
    row8 = iota((8, PAD), 0)
    params_over = remote(par.at[0], par.at[1], ss.at[35], rs.at[35], direct)
    par[0] = here
    here = here + jnp.where((lane8 == PAD - 1) & (row8 == 0), count, 0.0)
    all1 = Total(p, (ab1.at[5], ab2.at[5]), (as1.at[0], ar1.at[0], as2.at[0], ar2.at[0]))
    all1.start(here[0:2])
    params_over.start()
    start_fetch("y")
    for h in range(1, 4):
        send_windows(h)

    @pl.when(not_self)
    def _():
        c_a.start()

    @pl.when(is_self)
    def _():
        pltpu.make_async_copy(cot_window(c), cc_mine, rs.at[2 + zl]).start()

    c_b.start()
    for u in range(4):
        own_w[5 + u].wait()
        pl.when(c == UNIT_CORE[u])(lambda u=u: unit_over(u).start())
    all1.middle()
    start_spread("x")
    start_spread("y")

    owners_row = jnp.broadcast_to(owners[...].astype(f32), (8, 64)).astype(bf16)
    nat1 = dot(owners_row, e1[...])[0:1] * 6.0 + bw1[0:1]
    nat2 = dot(owners_row, e2[...])[0:1] * 3.0 + bw2[0:1]
    for k in range(4):
        s1[4, k] = ((iota((192, PAD), 0) + 192 * k).astype(f32) == nat1).astype(bf16).reshape(4, 48, PAD)
    perm2 = (iota((H, H), 0).astype(f32) == nat2).astype(bf16)

    row = iota((128, 128), 0)
    pick = (iota((128, 128), 1) == jnp.where(row < 64, 2 * row, 2 * row - 127)).astype(bf16)
    def window_here(k, h):
        part = window_there(k, h)
        remote(part, part, ss.at[0], rs.at[36 + 2 * h + k], other_core).wait_recv()

    tr[...] = jnp.zeros_like(tr)

    def blocks(k, second):
        for b in range(9):
            if b in (0, 2, 4, 6):
                window_here(k, b // 2)
            buf = b % 2
            tr[buf, :, 0:HALF0] = dot(pick, xw[k, :, pl.ds(128 * b, 128)], ((1,), (1,)))
            bins = pl.ds(64 * b, 64)

            def put(value, bins=bins):
                value = value.astype(bf16)
                for par in range(2):
                    part = value[64 * par : 64 * par + 64]
                    raw[par, bins, :] = raw[par, bins, :] + part if second else part

            pl.when(k == 0)(lambda: put(tr[buf]))
            pl.when(k == 1)(lambda: put(pltpu.roll(tr[buf], HALF0, 1)))

    blocks(zl, False)
    first = all1.end()
    n1 = first[0:1, PAD - 1 : PAD]
    n2 = 0.5 * n1
    inv_n1 = 1.0 / n1
    inv_n2 = 1.0 / n2
    real = iota((1, PAD), 1) < C0
    mean1 = jnp.where(real, first[0:1], 0.0) * inv_n1
    var1 = first[1:2] * inv_n1 - mean1 * mean1
    rs1 = lax.rsqrt(var1 + eps_norm)
    params_over.wait()
    both_halves = par[0] + par[1]
    gain1, bias1 = both_halves[2:3], both_halves[3:4]
    gain2, bias2 = both_halves[4:5], both_halves[5:6]
    gain3, bias3 = both_halves[6:7, 0:H], both_halves[6:7, H : 2 * H]

    remote(offs, offw, ss.at[4], rs.at[4], other_core).wait()
    off = jnp.where(is_self, offs[0:1, 0:1], offw[0:1, 0:1])

    bin0 = 496 * c
    own0 = pl.multiple_of(16 * c, 16)
    raw0 = pl.multiple_of(48 * c, 16)
    rawown = pl.multiple_of(64 * c, 16)

    def valid_mask(rows, at=0):
        return ((iota((rows, 1), 0) + (bin0 + at)).astype(f32) >= off).astype(f32)

    def own_mask(rows, at=0):
        r = iota((rows, 1), 0) + at
        return ((r >= 16 * c) & (r < 16 * c + OWN)).astype(f32)

    not_first = (iota((WIN, 1), 0) > 0).astype(f32)
    not_last = (iota((WIN, 1), 0) < WIN - 1).astype(f32)

    def before(v):
        return (pltpu.roll(v, 1, 0) * not_first).astype(bf16)

    def after(v):
        return (pltpu.roll(v, WIN - 1, 0) * not_last).astype(bf16)

    small[0:1] = rs1 * gain1
    small[1:2] = bias1 - mean1 * (rs1 * gain1)
    small[2:3] = mean1
    small[3:4] = rs1

    def norm_tile(q):
        lanes = pl.ds(pl.multiple_of(128 * q, 128), 128)
        scale, shift = small[0:1, lanes], small[1:2, lanes]
        valid = valid_mask(WIN)
        for par in range(2):
            v = raw[par, pl.ds(raw0, WIN), lanes].astype(f32)
            v = gelu(v * scale + shift) * valid
            aa[par, :, lanes] = before(v)
            aa[2 + par, :, lanes] = v.astype(bf16)
            aa[4 + par, :, lanes] = after(v)

    @pl.loop(0, 2)
    def _(k):
        norm_tile(3 * zl + k)

    blocks(1 - zl, True)
    for k in (1, 3, 2):
        for axis in ("x", "y"):
            start_across(axis, k)

    @pl.loop(0, 4)
    def _(k):
        norm_tile(jnp.where(zl == 0, k + 2, jnp.where(k < 3, k, 5)))

    for b in range(15):
        pl.when(c != b % 2)(lambda b=b: block_here(jnp.int32(b)))

    acc[...] = jnp.zeros_like(acc)

    @pl.loop(0, 3)
    def _(k):
        rows = pl.ds(pl.multiple_of(176 * k, 16), 176)
        h0 = jnp.zeros((176, C1), f32)
        for t in range(5):
            h0 = h0 + dot(aa[t, rows, 0:C0], ww1[t])
        h1 = jnp.zeros((176, C1), f32)
        for t in range(5):
            h1 = h1 + dot(aa[t + 1, rows, 0:C0], ww1[t])
        d = h0 - h1
        v = jnp.maximum(h0, h1) + (jnp.log(1.0 + jnp.exp(-jnp.abs(d))) - math.log(2.0))
        diff[rows, :] = d
        pooled[rows, :] = v
        m = valid_mask(176, 176 * k) * own_mask(176, 176 * k)
        vm = v * m
        acc[0:1] += jnp.sum(vm, axis=0, keepdims=True)
        acc[1:2] += jnp.sum(vm * v, axis=0, keepdims=True)

    all2 = Total(p, (ab1.at[0], ab2.at[0]), (as1.at[1], ar1.at[1], as2.at[1], ar2.at[1]))
    all2.start(acc[0:2])

    def early_slopes(par):
        @pl.loop(0, 6)
        def _(q):
            lanes = pl.ds(pl.multiple_of(128 * q, 128), 128)
            xv = raw[par, pl.ds(rawown, OWN), lanes].astype(f32)
            turn = gelu_slope(xv * small[0:1, lanes] + small[1:2, lanes])
            dv[par, :, lanes] = (turn * valid_mask(OWN, 16 * c)).astype(bf16)

    early_slopes(0)
    all2.middle()
    for u in range(4):

        def there_u(u=u):
            remote(
                unit_ref(u, its_rows), unit_ref(u, its_rows), ss.at[15 + u], rs.at[15 + u], flip
            ).wait_recv()
            unit_here(u).start()

        pl.when(c == UNIT_CORE[u])(there_u)
    for k in range(2):
        part = cc.at[:, pl.ds(384 * k, 384)]
        remote(part, part, ss.at[0], rs.at[2 + k], other_core).wait_recv()
    for u in range(4):
        pl.when(c == UNIT_CORE[u])(lambda u=u: unit_here(u).wait_send())
        pl.when(c != UNIT_CORE[u])(lambda u=u: unit_here(u).wait_recv())
    og[...] = dot(cc[...], wwp[...], ((1,), (1,)))
    early_slopes(1)

    @pl.when(not_self)
    def _():
        for h in range(4):
            x_a[h].wait_send()
        c_a.wait_send()

    for h in range(4):
        x_b[h].wait_send()
    c_b.wait_send()
    for axis in ("x", "y"):
        b, cps = spread(axis)
        own_sends = [fetch(axis)[1], *cps, across(axis, 0)[1]]

        def sent_all(own_sends=own_sends):
            for cp in own_sends:
                cp.wait_send()

        if_block(axis, b, sent_all)
        for k in (1, 2, 3):
            b, cp = across(axis, k)
            if_block(axis, b, cp.wait_send)
    for u in range(4):
        pl.when(c == UNIT_CORE[u])(lambda u=u: unit_over(u).wait_send())

    second = all2.end()
    mean2 = second[0:1] * inv_n2
    var2 = second[1:2] * inv_n2 - mean2 * mean2
    rs2 = lax.rsqrt(var2 + eps_norm)
    acc[2:3] = rs2 * gain2
    acc[3:4] = bias2 - mean2 * (rs2 * gain2)
    acc[4:5] = mean2
    acc[5:6] = rs2

    @pl.loop(0, 6)
    def _(k):
        lanes = pl.ds(pl.multiple_of(128 * k, 128), 128)
        v = gelu(pooled[:, lanes] * acc[2:3, lanes] + acc[3:4, lanes]) * valid_mask(WIN)
        mm[0, :, lanes] = before(v)
        mm[1, :, lanes] = v.astype(bf16)
        mm[2, :, lanes] = after(v)

    h2 = jnp.zeros((WIN, H), f32)
    for t in range(3):
        h2 = h2 + dot(mm[t], ww2[t], ((1,), (1,)))
    hid[...] = h2
    m = valid_mask(WIN) * own_mask(WIN)
    h2m = h2 * m
    acc[6:7, 0:H] = jnp.sum(h2m, axis=0, keepdims=True)
    acc[6:7, H : 2 * H] = jnp.sum(h2m * h2, axis=0, keepdims=True)
    all3 = Total(p, (ab1.at[1], ab2.at[1]), (as1.at[2], ar1.at[2], as2.at[2], ar2.at[2]))
    all3.start(acc[6:8])

    def basis_rows(src, first, size, buf, sem):
        return pltpu.make_async_copy(src.at[pl.ds(first, size)], buf, bs.at[sem])

    slope_buf = [slope.at[pl.ds(0, 128)], slope.at[pl.ds(128, 128)]]
    rows_buf = slope_buf + [tr.at[0], tr.at[1]]

    def rounds(n):
        got = []
        for k in range(4):
            block = 4 * n + k
            src = b2 if block < 6 else b3
            got.append(basis_rows(src, 128 * (block % 6), 128, rows_buf[k], k))
        return got

    def keep_round(n):
        for k, cp in enumerate(rounds(n)):
            cp.wait()
            block = 4 * n + k
            half, at = block // 3, 128 * (block % 3)
            value = rows_buf[k][...].astype(bf16)
            if half < 3:
                ww2[half, pl.ds(at, 128), :] = value
            else:
                wwp[pl.ds(at, 128), :] = value

    first_basis = pltpu.make_async_copy(b1, b1f, bs.at[4])
    first_basis.start()

    @pl.loop(0, 6)
    def _(q):
        lanes = pl.ds(pl.multiple_of(128 * q, 128), 128)
        turn = gelu_slope(pooled[:, lanes] * acc[2:3, lanes] + acc[3:4, lanes])
        turn = (turn * valid_mask(WIN)).astype(bf16)
        xw[0, 0:272, lanes] = turn[0:272]
        xw[1, 0:256, lanes] = turn[272:WIN]

    all3.middle()

    @pl.loop(0, 6)
    def _(q):
        lanes = pl.ds(pl.multiple_of(128 * q, 128), 128)
        diff[:, lanes] = 1.0 / (1.0 + jnp.exp(-diff[:, lanes]))

    first_basis.wait()
    bb1[...] = b1f[...].astype(bf16)
    third = all3.end()
    mean3 = third[0:1, 0:H] * inv_n2
    var3 = third[0:1, H : 2 * H] * inv_n2 - mean3 * mean3
    rs3 = lax.rsqrt(var3 + eps_norm)
    valid = valid_mask(WIN)
    own = own_mask(WIN)
    h2 = hid[...]
    scaled = (h2 - mean3) * rs3
    pre = scaled * gain3 + bias3
    no[...] = (gelu(pre) * valid).astype(bf16)
    slopes = gelu_slope(pre) * og[...] * valid
    og[...] = slopes
    hid[...] = scaled
    acc[6:7, 0:H] = jnp.sum(slopes * scaled * own, axis=0, keepdims=True)
    acc[6:7, H : 2 * H] = jnp.sum(slopes * own, axis=0, keepdims=True)
    all4 = Total(p, (ab1.at[2], ab2.at[2]), (as1.at[3], ar1.at[3], as2.at[3], ar2.at[3]))
    all4.start(acc[6:8])
    out_rows = pl.ds(pl.multiple_of(512 * c, 16), OWN)
    own_rows = pl.ds(own0, OWN)
    gp[0] = (pooled[own_rows, :] + dot(no[own_rows, :], wwp[...])).astype(bf16)
    all4.middle()

    def out_copy(k):
        return remote(
            gp.at[0, :, pl.ds(384 * k, 384)],
            out.at[out_rows, :],
            ss.at[23 + k],
            rs.at[23 + c],
            p.at(z=2 * p.zh + k, c=zl),
        )

    def out_local(k):
        return pltpu.make_async_copy(
            gp.at[0, :, pl.ds(384 * k, 384)], out.at[out_rows, :], ls.at[9]
        )

    def to_self(k):
        return (zl == k) & is_self

    for k in range(2):
        pl.when(jnp.logical_not(to_self(k)))(lambda k=k: out_copy(k).start())

        pl.when(to_self(k))(lambda k=k: out_local(k).start())

    def put2(m, value):
        s2[:, :, pl.ds(24 * m, 24), :] = value.astype(bf16).reshape(4, 4, 24, C1)

    tn = ((0,), (0,))
    nop = dot(no[own_rows, :], perm2).astype(bf16)
    put2(3, dot(nop, cc[own_rows, :], tn))
    for cp in rounds(0):
        cp.start()
    fourth = all4.end()
    stats[4:5] = fourth[0:1]
    gain_mean = fourth[0:1, 0:H] * inv_n2
    bias_mean = fourth[0:1, H : 2 * H] * inv_n2
    hg = valid_mask(WIN) * (gain3 * rs3) * (og[...] - bias_mean - hid[...] * gain_mean)
    hh[0] = after(hg)
    hh[1] = hg.astype(bf16)
    hh[2] = before(hg)
    mid_grad = jnp.zeros((WIN, C1), f32)
    for t in range(3):
        mid_grad = mid_grad + dot(hh[t], ww2[t])
    mid[...] = mid_grad

    @pl.loop(0, 6)
    def _(k):
        lanes = pl.ds(pl.multiple_of(128 * k, 128), 128)
        v = pooled[:, lanes]
        turn = jnp.concatenate([xw[0, 0:272, lanes], xw[1, 0:256, lanes]], axis=0)
        slopes = turn.astype(f32) * mid[:, lanes]
        scaled = (v - acc[4:5, lanes]) * acc[5:6, lanes]
        mid[:, lanes] = slopes
        pooled[:, lanes] = scaled
        mine = slopes * own_mask(WIN)
        acc[0:1, lanes] = jnp.sum(mine * scaled, axis=0, keepdims=True)
        acc[1:2, lanes] = jnp.sum(mine, axis=0, keepdims=True)

    all5 = Total(p, (ab1.at[3], ab2.at[3]), (as1.at[4], ar1.at[4], as2.at[4], ar2.at[4]))
    all5.start(acc[0:2])
    hp = dot(hh[1, own_rows, :], perm2).astype(bf16)
    put2(0, dot(hp, mm[0, own_rows, :], tn))
    keep_round(0)
    all5.middle()
    for cp in rounds(1):
        cp.start()
    for t in range(1, 3):
        put2(t, dot(hp, mm[t, own_rows, :], tn))
    s2_over = remote(s2.at[:, :, :, others], t2, gs.at[0], gr.at[0], other_core)
    s2_over.start()
    keep_round(1)
    for cp in rounds(2):
        cp.start()
    nat4 = dot(owners_row, e4[...])[0:1] * 6.0 + bw4[0:1]
    for r in range(3):
        for h in range(2):
            hh[r, pl.ds(256 * h, 256), :] = (
                (iota((256, 384), 0) + 256 * r).astype(f32) == nat4[:, 384 * h : 384 * h + 384]
            ).astype(bf16)
    fifth = all5.end()
    stats[2:4] = fifth
    acc[0:2] = fifth * inv_n2

    @pl.loop(0, 6)
    def _(k):
        lanes = pl.ds(pl.multiple_of(128 * k, 128), 128)
        back = acc[2:3, lanes] * (
            mid[:, lanes] - acc[1:2, lanes] - pooled[:, lanes] * acc[0:1, lanes]
        )
        pg = cc[:, lanes].astype(f32) + back * valid_mask(WIN)
        even = diff[:, lanes]
        ge = pg * even
        go = pg * (1.0 - even)
        gg[0, :, lanes] = after(go)
        gg[1, :, lanes] = after(ge)
        gg[2, :, lanes] = go.astype(bf16)
        gg[3, :, lanes] = ge.astype(bf16)
        gg[4, :, lanes] = before(go)
        gg[5, :, lanes] = before(ge)

    def total(own, parts):
        v = own.astype(f32)
        for part in parts:
            v = v + part.astype(f32)
        return v.astype(bf16)

    def along(k, axis):
        if axis == "x":
            i = lax.rem(p.x + k + 1, 4)
            return p.at(x=i), i
        if axis == "z":
            i = lax.rem(p.z + k + 1, 4)
            return p.at(z=i), i
        i = lax.rem(p.y + k + 1, 4)
        return p.at(y=i), i

    s2_over.wait()
    t2[...] = total(t2[...], [s2[:, :, :, mine]])
    flying = []

    def send(src, dst, sem, device):
        cp = remote(src, dst, gs.at[sem], gr.at[sem], device)
        cp.start()
        flying.append(cp)

    def arrived(dst, sem):
        remote(dst, dst, gs.at[0], gr.at[sem], other_core).wait_recv()

    for k in range(3):
        device, i = along(k, "z")
        send(t2.at[i], rd.at[k], 1 + k, device)
    keep_round(2)

    for k in range(2):

        def out_sent(k=k):
            out_copy(k).wait_send()

        pl.when(jnp.logical_not(to_self(k)))(out_sent)
        pl.when(to_self(k))(lambda k=k: out_local(k).wait())
    perm = s1[4].reshape(PAD, PAD)
    gp[0] = dot(gg[3, own_rows, :], perm).astype(bf16)
    gp[1] = dot(gg[2, own_rows, :], perm).astype(bf16)

    TAP_AXIS = ("x", "y", "x", "y", "z")
    SECOND = {"x": "y", "y": "x", "z": "y"}

    def for_last_tap(slot):
        g = gg[slot, own_rows, :]
        halves = []
        for h in range(2):
            v = dot(g[:, 0:256], hh[0, pl.ds(256 * h, 256), :])
            for r in (1, 2):
                v = v + dot(g[:, 256 * r : 256 * r + 256], hh[r, pl.ds(256 * h, 256), :])
            halves.append(v.astype(bf16))
        return halves

    def to_core(t):
        return remote(s1.at[t, :, :, :, others], t1.at[t], gs.at[7 + t], gr.at[7 + t], other_core)

    def to_axis(t):
        to_core(t).wait_recv()
        t1[t] = total(t1[t], [s1[t, :, :, :, mine]])
        for k in range(3):
            device, i = along(k, TAP_AXIS[t])
            src = t1.at[t, :, i] if TAP_AXIS[t] == "y" else t1.at[t, i]
            send(src, ra.at[t, k], 12 + 3 * t + k, device)

    def to_other_axis(t):
        for k in range(3):
            arrived(ra.at[t, k], 12 + 3 * t + k)
        own_part = {"x": lambda: t1[t, p.x], "y": lambda: t1[t, :, p.y], "z": lambda: t1[t, p.z]}[TAP_AXIS[t]]()
        ua[t] = total(own_part, [ra[t, k] for k in range(3)])
        for k in range(3):
            device, i = along(k, SECOND[TAP_AXIS[t]])
            send(ua.at[t, i], rb.at[t, k], 27 + 3 * t + k, device)

    def last_of(t):
        for k in range(3):
            arrived(rb.at[t, k], 27 + 3 * t + k)
        own_part = ua[t, p.x] if TAP_AXIS[t] == "y" else ua[t, p.y]
        va[t] = total(own_part, [rb[t, k] for k in range(3)])

    for t in range(5):
        if t == 4:
            for k in range(2):
                halves = for_last_tap(3 - k)
                gp[k, :, 0:384] = halves[0]
                gp[k, :, 384:768] = halves[1]
        part = dot(gp[0], aa[t, own_rows, 0:C0], tn) + dot(gp[1], aa[t + 1, own_rows, 0:C0], tn)
        part = part.astype(bf16).reshape(4, 4, 48, C0)
        s1[t, :, :, :, 0:C0] = part
        s1[t, :, :, :, C0:PAD] = jnp.zeros((4, 4, 48, PAD - C0), bf16)
        to_core(t).start()
        if t > 0:
            to_axis(t - 1)
    to_axis(4)

    def second_of_two():
        for k in range(3):
            arrived(rd.at[k], 1 + k)
        uc[...] = total(t2[p.z], [rd[k] for k in range(3)])
        for k in range(3):
            device, i = along(k, "y")
            send(uc.at[i], re.at[k], 4 + k, device)

    def xc_peers():
        for k in range(1, 8):
            xi = lax.rem(p.x + k // 2, 4)
            ci = lax.rem(c + k % 2, 2)
            yield p.at(x=xi, c=ci), 2 * xi + ci

    def slope_part(half, par, k):
        return (
            gp.at[par, pl.ds(256 * k, 256), pl.ds(384 * half, 384)],
            sl_home.at[c, par, pl.ds(256 * k, 256), :],
        )

    def slope_copy(half, par, k):
        src, dst = slope_part(half, par, k)
        n = 2 * par + k
        return remote(src, dst, ss.at[25 + 4 * half + n], rs.at[25 + 4 * c + n], p.at(z=2 * p.zh + half, c=zl))

    def slope_local(half, par, k):
        src, dst = slope_part(half, par, k)
        return pltpu.make_async_copy(src, dst, rs.at[25 + 4 * c + 2 * par + k])

    def send_slopes(par):
        for half in range(2):
            for k in range(2):

                def send_slope(half=half, k=k):
                    slope_copy(half, par, k).start()

                def keep_slope(half=half, k=k):
                    slope_local(half, par, k).start()

                pl.when(jnp.logical_not(to_self(half)))(send_slope)
                pl.when(to_self(half))(keep_slope)

    small[4:6] = jnp.zeros((2, PAD), f32)
    for par in range(2):
        for k in range(2):
            rows = pl.ds(pl.multiple_of(own0 + 256 * k, 16), 256)
            v = jnp.zeros((256, C0), f32)
            for t in range(5):
                v = v + dot(gg[t + 1 - par, rows, :], ww1[t], ((1,), (1,)))
            slope[:, 0:C0] = v
            slope[:, C0:PAD] = jnp.zeros((256, PAD - C0), f32)

            @pl.loop(0, 6)
            def _(q, par=par, k=k):
                lanes = pl.ds(pl.multiple_of(128 * q, 128), 128)
                xv = raw[par, pl.ds(pl.multiple_of(rawown + 256 * k, 16), 256), lanes].astype(f32)
                slopes = dv[par, pl.ds(256 * k, 256), lanes].astype(f32) * slope[:, lanes]
                scaled = (xv - small[2:3, lanes]) * small[3:4, lanes]
                slope[:, lanes] = slopes
                small[4:5, lanes] += jnp.sum(slopes * scaled, axis=0, keepdims=True)
                small[5:6, lanes] += jnp.sum(slopes, axis=0, keepdims=True)

            dst = pl.ds(256 * k, 256)
            gp[par, dst, 0:384] = slope[:, 0:384].astype(bf16)
            gp[par, dst, 384:768] = pltpu.roll(slope[...], PAD - HALF0, 1)[:, 0:384].astype(bf16)
            if (par, k) == (0, 1):
                second_of_two()
                send_slopes(0)
            if (par, k) == (1, 0):
                to_other_axis(0)
                to_other_axis(1)

    all6 = Total(p, (ab1.at[4], ab2.at[4]), (as1.at[5], ar1.at[5], as2.at[5], ar2.at[5]))
    all6.start(small[4:6])

    to_other_axis(2)
    to_other_axis(3)
    for k in range(3):
        arrived(re.at[k], 4 + k)
    g2 = dot(rep2[...], total(uc[p.y], [re[k] for k in range(3)]))
    e2_own = 2 * p.x + c
    for e in range(8):
        pz2[e] = g2[32 * e : 32 * e + 32].astype(bf16)
    for k, (device, e) in enumerate(xc_peers()):
        cp = remote(pz2.at[e], rz2.at[e2_own], gs.at[50 + k], gr.at[50 + e2_own], device)
        cp.start()
        flying.append(cp)
    rz2[e2_own] = pz2[e2_own]
    for t in range(2):
        last_of(t)
    to_other_axis(4)
    for t in range(2, 4):
        last_of(t)
    g1 = dot(rep1[...], va[0:4].reshape(192, 384))
    for e in range(8):
        pz[e] = g1[48 * e : 48 * e + 48].astype(bf16)
    for k, (device, zi, ci) in enumerate(column_peers(p)):
        cp = remote(pz.at[2 * zi + ci], rz.at[p.e], gs.at[42 + k], gr.at[42 + p.e], device)
        cp.start()
        flying.append(cp)
    last_of(4)
    g4 = dot(rep4[...], va[4])
    for e in range(8):
        pz4[e] = g4[16 * e : 16 * e + 16].astype(bf16)
    for k, (device, e) in enumerate(xc_peers()):
        cp = remote(pz4.at[e], rz4.at[e2_own], gs.at[58 + k], gr.at[58 + e2_own], device)
        cp.start()
        flying.append(cp)
    rz4[e2_own] = pz4[e2_own]
    rz[p.e] = pz[p.e]
    all6.middle()

    def summed(parts, half):
        v = parts[half].astype(f32)
        for k in range(1, 4):
            v = v + parts[2 * k + half].astype(f32)
        return v

    for cp in loads:
        cp.wait()
    for _, e in xc_peers():
        arrived(rz2.at[e], 50 + e)
    for half in range(2):
        grad[48:80, 384 * half : 384 * half + 384] = summed(rz2, half)
    nt = ((1,), (1,))
    nb[...] = jnp.zeros_like(nb)
    dd[...] = jnp.zeros_like(dd)

    def turn2(v):
        return dot(v[:, 0:384], ww2[0]) + dot(v[:, 384:768], ww2[1])

    def turn3(v):
        return dot(v[:, 0:384], ww2[2]) + dot(v[:, 384:768], wwp[...])

    turned = turn2(grad[48:72].astype(bf16))
    for t in range(3):
        first_new, second_new, direction = adam_block(f2[t], q2[t], turned[8 * t : 8 * t + 3])
        nf2[t] = first_new
        nq2[t] = second_new
        dd[40 + 8 * t : 43 + 8 * t, :] = direction
    turned = turn3(grad[72:80].astype(bf16))
    first_new, second_new, direction = adam_block(f3[...], q3[...], turned[0:3])
    nf3[...] = first_new
    nq3[...] = second_new
    dd[64:67] = direction
    d2 = dd[40:64].astype(bf16)
    update = jnp.concatenate([dot(d2, ww2[0], nt), dot(d2, ww2[1], nt)], axis=1)
    row_of_two = (68, 80, 84)
    for t in range(3):
        master_new, average_new = master_block(m2[t], update[8 * t : 8 * t + 3], 0.02, a2[t])
        nm2[t] = master_new
        na2[t] = average_new
        nb[row_of_two[t] : row_of_two[t] + 3, :] = master_new
    d3 = dd[64:72].astype(bf16)
    update = jnp.concatenate([dot(d3, ww2[2], nt), dot(d3, wwp[...], nt)], axis=1)
    master_new, average_new = master_block(m3[...], update[0:3], 0.05, a3[...])
    nm3[...] = master_new
    na3[...] = average_new
    nb[64:67, :] = master_new
    for cp in stores[4:12]:
        cp.start()

    def hop(src, dst, send_at, recv_at, device):
        cp = remote(src, dst, hs.at[send_at], hr.at[recv_at], device)
        cp.start()
        flying.append(cp)

    def landed(dst, sem):
        remote(dst, dst, hs.at[0], hr.at[sem], other_core).wait_recv()

    qa = 2 * p.y + p.zh
    qb = 2 * p.x + p.zh

    def near_peers(axis):
        for k in range(1, 8):
            i = lax.rem((p.y if axis == "y" else p.x) + k // 2, 4)
            zh = lax.rem(p.zh + k % 2, 2)
            z = 2 * zh + zl
            yield (p.at(y=i, z=z) if axis == "y" else p.at(x=i, z=z)), 2 * i + zh

    def gather_near(near, fa, fb, rows, base):
        fa[qa] = near[0:rows]
        fb[qb] = near[rows : 2 * rows]
        for k, (device, _) in enumerate(near_peers("y")):
            hop(near.at[pl.ds(0, rows)], fa.at[qa], base + k, base + qa, device)
        for k, (device, _) in enumerate(near_peers("x")):
            hop(near.at[pl.ds(rows, rows)], fb.at[qb], base + 8 + k, base + 8 + qb, device)

    def gather_far(fa, fb, pack, pa, pb, parts_a, parts_b, ga, gb, base):
        for _, q in near_peers("y"):
            landed(fa.at[q], base + q)
        pa[...] = dot(pack, fa[...].reshape(8 * fa.shape[1], PAD)).astype(bf16)
        for k in range(3):
            device, _ = along(k, "x")
            for n, part in enumerate(parts_a):
                hop(pa.at[part], ga.at[(c, p.x) + part], base + 16 + 8 * n + k, base + 16 + 8 * n + p.x, device)
        for _, q in near_peers("x"):
            landed(fb.at[q], base + 8 + q)
        pb[...] = dot(pack, fb[...].reshape(8 * fb.shape[1], PAD)).astype(bf16)
        for k in range(3):
            device, _ = along(k, "y")
            for n, part in enumerate(parts_b):
                hop(pb.at[part], gb.at[(c, p.y) + part], base + 20 + 8 * n + k, base + 20 + 8 * n + p.y, device)
        kept = []
        for n, part in enumerate(parts_a):
            hop(pa.at[part], ga.at[(c, p.x) + part], base + 35 + 8 * n, base + 32 + 8 * n + p.x, other_core)
            kept.append(pltpu.make_async_copy(pa.at[part], ga.at[(c, p.x) + part], bs.at[8 + n]))
        for n, part in enumerate(parts_b):
            hop(pb.at[part], gb.at[(c, p.y) + part], base + 39 + 8 * n, base + 36 + 8 * n + p.y, other_core)
            kept.append(pltpu.make_async_copy(pb.at[part], gb.at[(c, p.y) + part], bs.at[10 + n]))
        for cp in kept:
            cp.start()
        return kept

    def gather_over(parts_a, parts_b, ga, gb, base):
        for k in range(3):
            _, i = along(2 - k, "x")
            for n, part in enumerate(parts_a):
                ref = ga.at[(c, i) + part]
                landed(ref, base + 16 + 8 * n + i)
                hop(ref, ref, base + 32 + 8 * n + k, base + 32 + 8 * n + i, other_core)
            _, i = along(2 - k, "y")
            for n, part in enumerate(parts_b):
                ref = gb.at[(c, i) + part]
                landed(ref, base + 20 + 8 * n + i)
                hop(ref, ref, base + 36 + 8 * n + k, base + 36 + 8 * n + i, other_core)

    def gather_end(parts_a, parts_b, ga, gb, base):
        for i in range(4):
            for n, part in enumerate(parts_a):
                landed(ga.at[(1 - c, i) + part], base + 32 + 8 * n + i)
            for n, part in enumerate(parts_b):
                landed(gb.at[(1 - c, i) + part], base + 36 + 8 * n + i)

    whole2 = ((slice(None), slice(None)),)
    near2[...] = nb[64:96].astype(bf16)
    gather_near(near2, fa2, fb2, 16, 0)

    for device, zi, ci in column_peers(p):
        e = 2 * zi + ci
        arrived(rz.at[e], 42 + e)
    for _, e in xc_peers():
        arrived(rz4.at[e], 58 + e)
    for half in range(2):
        lanes = slice(384 * half, 384 * half + 384)
        v = summed(rz, half)
        grad[0:32, lanes] = v[0:32]
        grad[32:40, lanes] = summed(rz4, half)[0:8]
    turned = dot(grad[0:40, 0:C0].astype(bf16), bb1[...])
    for t in range(5):
        first_new, second_new, direction = adam_block(f1[t], q1[t], turned[8 * t : 8 * t + 6])
        nf1[t] = first_new
        nq1[t] = second_new
        dd[8 * t : 8 * t + 6, 0:C0] = direction
    update = dot(dd[0:40, 0:C0].astype(bf16), bb1[...], nt)
    row_of = (0, 8, 16, 32, 40)
    for t in range(5):
        master_new, average_new = master_block(m1[t], update[8 * t : 8 * t + 6], 0.02, a1[t])
        nm1[t] = master_new
        na1[t] = average_new
        nb[row_of[t] : row_of[t] + 6, 0:C0] = master_new
        if t == 2:
            nb[48:54, 0:C0] = master_new
    for cp in stores[0:4]:
        cp.start()
    near1[...] = nb[0:64].astype(bf16)
    gather_near(near1, fa1, fb1, 32, 48)
    send_slopes(1)
    kept2 = gather_far(fa2, fb2, pack2[...], pa2, pb2_, whole2, whole2, ga2, gb2, 0)
    sixth = all6.end()
    stats[0:2] = sixth
    stats[5:6] = mean1
    stats[6:7] = rs1
    stats[7:8] = rs1 * gain1
    stats[8:10] = sixth * inv_n1
    stats[10:16] = jnp.zeros((6, PAD), f32)
    taps2 = (pl.ds(0, 96), slice(None))
    parts_a = (taps2, (pl.ds(96, 48), pl.ds(0, 384)))
    parts_b = (taps2, (pl.ds(96, 48), pl.ds(384, 384)))
    kept1 = gather_far(fa1, fb1, pack1[...], pa1, pb1_, parts_a, parts_b, ga1, gb1, 48)
    gather_over(whole2, whole2, ga2, gb2, 0)
    gather_over(parts_a, parts_b, ga1, gb1, 48)
    gather_end(whole2, whole2, ga2, gb2, 0)
    gather_end(parts_a, parts_b, ga1, gb1, 48)
    for cp in kept1 + kept2 + stores:
        cp.wait()

    for t in range(5):
        to_core(t).wait_send()
    for cp in flying:
        cp.wait_send()
    for half in range(2):
        for par in range(2):
            for k in range(2):

                def slope_sent(half=half, par=par, k=k):
                    slope_copy(half, par, k).wait_send()

                pl.when(jnp.logical_not(to_self(half)))(slope_sent)
    for j in range(2):

        def out_here(j=j):
            rows = out.at[pl.ds(512 * j, 512), :]
            remote(rows, rows, ss.at[0], rs.at[23 + j], other_core).wait_recv()

        pl.when(jnp.logical_not(is_self & (c == j)))(out_here)
    for j in range(2):
        for par in range(2):
            for k in range(2):
                part = sl_home.at[j, par, pl.ds(256 * k, 256), :]
                remote(part, part, ss.at[0], rs.at[25 + 4 * j + 2 * par + k], other_core).wait_recv()


VMEM = pl.BlockSpec(memory_space=pltpu.VMEM)
ANY = pl.BlockSpec(memory_space=pl.ANY)


def run_step(xt, offsets, owners, cot, w1, w2, wp, params, bases, states, consts):
    shape = jax.ShapeDtypeStruct
    dma = pltpu.SemaphoreType.DMA
    scratch = [pltpu.VMEM(a.shape, f32) for a in states] * 2
    scratch += [
        pltpu.VMEM((5, 4, 4, 48, PAD), bf16),
        pltpu.VMEM((4, 4, 96, C1), bf16),
        pltpu.VMEM((2, HALF0, LANES), bf16),
        pltpu.VMEM((2, 576, PAD), bf16),
        pltpu.VMEM((6, WIN, PAD), bf16),
        pltpu.VMEM((5, C0, C1), bf16),
        pltpu.VMEM((3, H, C1), bf16),
        pltpu.VMEM((H, C1), bf16),
        pltpu.VMEM((WIN, C1), f32),
        pltpu.VMEM((WIN, C1), f32),
        pltpu.VMEM((WIN, C1), bf16),
        pltpu.VMEM((WIN, H), f32),
        pltpu.VMEM((WIN, H), f32),
        pltpu.VMEM((WIN, H), bf16),
        pltpu.VMEM((3, WIN, H), bf16),
        pltpu.VMEM((WIN, C1), f32),
        pltpu.VMEM((6, WIN, C1), bf16),
        pltpu.VMEM((2, OWN, C1), bf16),
        pltpu.VMEM((256, PAD), f32),
        pltpu.VMEM((8, PAD), f32),
        pltpu.VMEM((8, 128), f32),
        pltpu.VMEM((8, 128), f32),
        pltpu.VMEM((8, PAD), f32),
        pltpu.VMEM((2, 128, PAD), f32),
        pltpu.VMEM((2, OWN, PAD), bf16),
        pltpu.VMEM((5, 4, 4, 48, 384), bf16),
        pltpu.VMEM((4, 4, 96, 384), bf16),
        pltpu.VMEM((5, 3, 4, 48, 384), bf16),
        pltpu.VMEM((5, 3, 48, 384), bf16),
        pltpu.VMEM((3, 4, 96, 384), bf16),
        pltpu.VMEM((3, 96, 384), bf16),
        pltpu.VMEM((5, 4, 48, 384), bf16),
        pltpu.VMEM((4, 96, 384), bf16),
        pltpu.VMEM((5, 48, 384), bf16),
        pltpu.VMEM((8, 48, 384), bf16),
        pltpu.VMEM((8, 48, 384), bf16),
        pltpu.VMEM((8, 32, 384), bf16),
        pltpu.VMEM((8, 32, 384), bf16),
        pltpu.VMEM((8, 16, 384), bf16),
        pltpu.VMEM((8, 16, 384), bf16),
        pltpu.VMEM((C0, C0), f32),
        pltpu.VMEM((C0, C0), bf16),
        pltpu.VMEM((80, PAD), f32),
        pltpu.VMEM((72, PAD), f32),
        pltpu.VMEM((96, PAD), f32),
        pltpu.VMEM((64, PAD), bf16),
        pltpu.VMEM((32, PAD), bf16),
        pltpu.VMEM((8, 32, PAD), bf16),
        pltpu.VMEM((8, 32, PAD), bf16),
        pltpu.VMEM((8, 16, PAD), bf16),
        pltpu.VMEM((8, 16, PAD), bf16),
        pltpu.VMEM((144, PAD), bf16),
        pltpu.VMEM((144, PAD), bf16),
        pltpu.VMEM((48, PAD), bf16),
        pltpu.VMEM((48, PAD), bf16),
        pltpu.VMEM((2, 8, PAD), f32),
        pltpu.VMEM((6, 8, 2, PAD), f32),
        pltpu.VMEM((6, 16, 2, PAD), f32),
        dma((44,)),
        dma((44,)),
        dma((10,)),
        dma((6, 8)),
        dma((6, 8)),
        dma((6, 16)),
        dma((6, 16)),
        dma((68,)),
        dma((68,)),
        dma((96,)),
        dma((96,)),
        dma((12,)),
        dma((24,)),
        dma((16,)),
        dma((16,)),
    ]
    one = shape((2, 4, 144, PAD), bf16)
    two = shape((2, 4, 48, PAD), bf16)
    return pl.pallas_call(
        step_kernel,
        out_shape=(
            shape((BINS, 384), bf16),
            shape((2, 2, OWN, 384), bf16),
            shape((16, PAD), f32),
            one,
            one,
            two,
            two,
            *[shape(a.shape, f32) for a in states],
        ),
        in_specs=[VMEM, VMEM, VMEM, ANY, ANY, ANY, ANY] + [VMEM] * 17 + [ANY] * 15,
        out_specs=(ANY, ANY, VMEM, *[ANY] * 16),
        scratch_shapes=scratch,
        compiler_params=pltpu.CompilerParams(
            collective_id=0, has_side_effects=True, vmem_limit_bytes=63 * 2**20
        ),
    )(
        xt, offsets, owners, cot, w1, w2, wp, *params,
        *[consts[n] for n in ("e1", "bw1", "e2", "bw2", "e4", "bw4", "rep1", "rep2", "rep4", "pack1", "pack2")],
        *bases, *states,
    )


def norm_block(gradient, parameters, moments):
    first_new, second_new, direction = adam_block(moments[0], moments[1], gradient)
    return parameters - norm_rate * direction, first_new, second_new


def finish_kernel(
    xt_in, offsets, owners, slopes_in, stats, ga1, gb1, ga2, gb2, out_in, *rest,
):
    p = Place()
    zl = p.zl
    params = rest[0:6]
    moments = rest[6:9]
    rep_a, rep_b, at_a, at_b, rep2a, rep2b, at2a, at2b = rest[9:17]
    states_in = rest[17:29]
    out, gin, v1, v1f, v1s, v2, v2f, v2s, v3, v3f, v3s, cp1, cp2, cp3 = rest[29:43]
    states_out = rest[43:55]
    gav, gbv, gav2, gbv2, held, tr, xt, slopes, outv, cp1v, cp2v, cp3v, *held_states, ls, ns = rest[55:]
    third_a = (slice(None), slice(None), pl.ds(96, 48), pl.ds(0, 384))
    third_b = (slice(None), slice(None), pl.ds(96, 48), pl.ds(384, 384))
    taps2 = (slice(None), slice(None), pl.ds(0, 96))
    copies = [
        pltpu.make_async_copy(ga1.at[taps2], gav.at[taps2], ls.at[0]),
        pltpu.make_async_copy(gb1.at[taps2], gbv.at[taps2], ls.at[1]),
        pltpu.make_async_copy(ga1.at[third_a], gav.at[third_a], ls.at[4]),
        pltpu.make_async_copy(gb1.at[third_b], gbv.at[third_b], ls.at[5]),
        pltpu.make_async_copy(ga2, gav2, ls.at[6]),
        pltpu.make_async_copy(gb2, gbv2, ls.at[7]),
    ]
    first = [
        pltpu.make_async_copy(xt_in, xt, ls.at[8]),
        pltpu.make_async_copy(slopes_in.at[0], slopes.at[0], ls.at[9]),
        pltpu.make_async_copy(slopes_in.at[1], slopes.at[1], ls.at[10]),
    ]
    passed_in = [(out_in, outv)] + list(zip(states_in, held_states))
    passed_out = [(outv, out)] + list(zip(held_states, states_out))
    ins = [pltpu.make_async_copy(a, b, ns.at[k]) for k, (a, b) in enumerate(passed_in)]
    outs_ = [pltpu.make_async_copy(a, b, ns.at[13 + k]) for k, (a, b) in enumerate(passed_out)]
    for cp in first + copies + ins:
        cp.start()

    vec = stats[...]
    v326 = jnp.where(zl == 0, vec, pltpu.roll(vec, PAD - HALF0, 1))
    tr[0:16, :] = v326[:, 0:384]
    tr[16:128, :] = jnp.zeros((112, 384), f32)
    cols = jnp.transpose(tr[...])
    mean_c = cols[0:HALF0, 5:6]
    rs_c = cols[0:HALF0, 6:7]
    scale_c = cols[0:HALF0, 7:8]
    gm_c = cols[0:HALF0, 8:9]
    bm_c = cols[0:HALF0, 9:10]
    off_home = offsets[...].astype(f32)
    tn = ((0,), (0,))
    rowq = iota((128, 256), 0)
    laneq = iota((128, 256), 1)
    put_even = (laneq == 2 * rowq).astype(bf16)
    put_odd = (laneq == 2 * rowq + 1).astype(bf16)
    grads1 = v326[0:2, 0:HALF0]
    v384 = jnp.where(zl == 0, vec, pltpu.roll(vec, PAD - HALF1, 1))
    grads2 = v384[2:4, 0:HALF1]
    v192 = jnp.where(zl == 0, vec, pltpu.roll(vec, PAD - HALFH, 1))
    halves = [(grads1[0:1], grads1[1:2]), (grads2[0:1], grads2[1:2]), (v192[4:5, 0:HALFH], v192[4:5, H : H + HALFH])]
    outs = [(v1, v1f, v1s), (v2, v2f, v2s), (v3, v3f, v3s)]
    for n in range(3):
        for r in range(2):
            old = (moments[n][0, r : r + 1, :], moments[n][1, r : r + 1, :])
            new = norm_block(halves[n][r], params[2 * n + r][...].reshape(1, -1), old)
            for q in range(3):
                outs[n][q][r : r + 1, :] = new[q]

    own_row = jnp.broadcast_to(owners[...].astype(f32), (8, 64))

    def column(rep, at, width):
        own = jnp.sum(rep[...].astype(f32) * own_row[0:1], axis=1, keepdims=True)
        return own * float(width) + at[...]

    lane = iota((384, 384), 1).astype(f32)
    place_a = (lane == column(rep_a, at_a, 6)).astype(bf16)
    place_b = (lane == column(rep_b, at_b, 6)).astype(bf16)
    own8 = own_row.astype(bf16)
    place2a = (iota((H, H), 0).astype(f32) == (dot(own8, rep2a[...])[0:1] * 3.0 + at2a[...])).astype(bf16)
    place2b = (iota((H, H), 0).astype(f32) == (dot(own8, rep2b[...])[0:1] * 3.0 + at2b[...])).astype(bf16)
    back = []
    first[0].wait()
    for j in range(2):
        first[1 + j].wait()
        for k in range(4):
            bins = pl.ds(128 * k, 128)
            st = dot(slopes[j, 0, bins, :], put_even, tn) + dot(slopes[j, 1, bins, :], put_odd, tn)
            lanes = pl.ds(1024 * j + 256 * k, 256)
            xf = xt[:, lanes].astype(f32)
            scaled = (xf - mean_c) * rs_c
            ok = ((iota((1, 256), 1) + (1024 * j + 256 * k)).astype(f32) >= 2.0 * off_home).astype(f32)
            held[:, lanes] = ok * (scale_c * (st[0:HALF0] - bm_c - scaled * gm_c))
        half = pl.ds(1024 * j, 1024)
        back.append(pltpu.make_async_copy(held.at[:, half], gin.at[:, 0, half], ls.at[2 + j]))
        back[j].start()
    for cp, on in zip(ins, outs_):
        cp.wait()
        on.start()

    for cp in copies:
        cp.wait()

    def give(held_ref, result, sem):
        cp = pltpu.make_async_copy(held_ref, result, ls.at[sem])
        cp.start()
        back.append(cp)

    for t in range(2):
        block = gav[:, :, 48 * t : 48 * t + 48, :].reshape(384, PAD)
        cp1v[t] = dot(block[:, 0:C0], place_a, tn).astype(bf16)
        give(cp1v.at[t], cp1.at[t], 11 + 2 * t)
        block = gbv[:, :, 48 * t : 48 * t + 48, :].reshape(384, PAD)
        cp1v[3 + t] = dot(block[:, 0:C0], place_b, tn).astype(bf16)
        give(cp1v.at[3 + t], cp1.at[3 + t], 12 + 2 * t)
    cp1v[2, 0:384] = dot(gav[:, :, 96:144, 0:384].reshape(384, 384), place_a, tn).astype(bf16)
    cp1v[2, 384:C0] = dot(gbv[:, :, 96:144, 384:C0].reshape(384, C0 - 384), place_b, tn).astype(bf16)
    give(cp1v.at[2], cp1.at[2], 15)
    two = dot(place2a, gav2[...].reshape(384, PAD)).astype(bf16)
    cp3v[...] = two[0:HALFH]
    cp2v[0] = two[HALFH:H]
    two = dot(place2b, gbv2[...].reshape(384, PAD)).astype(bf16)
    cp2v[1] = two[0:HALFH]
    cp2v[2] = two[HALFH:H]
    give(cp3v, cp3, 16)
    give(cp2v, cp2, 17)
    back.extend(outs_)
    for cp in back:
        cp.wait()


def run_finish(xt, offsets, owners, slopes, stats, gathered, out, params, moments, states, consts):
    shape = jax.ShapeDtypeStruct
    vec = [shape((2, n), f32) for n in (HALF0,) * 3 + (HALF1,) * 3 + (HALFH,) * 3]
    names = ("rep_a", "rep_b", "at_a", "at_b", "rep2a", "rep2b", "at2a", "at2b")
    return pl.pallas_call(
        finish_kernel,
        out_shape=(
            shape((BINS, 384), bf16),
            shape((HALF0, 1, 2 * BINS), f32),
            *vec,
            shape((5, C0, 384), bf16),
            shape((3, HALFH, C1), bf16),
            shape((HALFH, C1), bf16),
            *[shape(a.shape, f32) for a in states],
        ),
        in_specs=[ANY, VMEM, VMEM, ANY, VMEM] + [ANY] * 5 + [VMEM] * 17 + [ANY] * 12,
        out_specs=(ANY, ANY, *[VMEM] * 9, *[ANY] * 15),
        scratch_shapes=[
            pltpu.VMEM((2, 4, 144, PAD), bf16),
            pltpu.VMEM((2, 4, 144, PAD), bf16),
            pltpu.VMEM((2, 4, 48, PAD), bf16),
            pltpu.VMEM((2, 4, 48, PAD), bf16),
            pltpu.VMEM((HALF0, 2 * BINS), f32),
            pltpu.VMEM((128, 384), f32),
            pltpu.VMEM((HALF0, 2 * BINS), bf16),
            pltpu.VMEM((2, 2, OWN, 384), bf16),
            pltpu.VMEM((BINS, 384), bf16),
            pltpu.VMEM((5, C0, 384), bf16),
            pltpu.VMEM((3, HALFH, C1), bf16),
            pltpu.VMEM((HALFH, C1), bf16),
            *[pltpu.VMEM(a.shape, f32) for a in states],
            pltpu.SemaphoreType.DMA((20,)),
            pltpu.SemaphoreType.DMA((26,)),
        ],
        compiler_params=pltpu.CompilerParams(vmem_limit_bytes=63 * 2**20),
    )(
        xt, offsets, owners, slopes, stats, *gathered, out, *params, *moments,
        *[consts[n] for n in names], *states,
    )


def make_consts():
    e1 = np.zeros((64, 768), np.float32)
    bw1 = np.zeros((8, 768), np.float32)
    e2 = np.zeros((64, 384), np.float32)
    bw2 = np.zeros((8, 384), np.float32)
    e4 = np.zeros((64, 768), np.float32)
    bw4 = np.zeros((8, 768), np.float32)
    for s in range(64):
        g, zh, c = s // 4, (s // 2) % 2, s % 2
        for b in range(2):
            e = (2 * zh + b) * 2 + c
            for w in range(6):
                e1[s, (g * 8 + e) * 6 + w] = 1
                bw1[:, (g * 8 + e) * 6 + w] = b * 384 + w
            block = ((2 * zh + b) * 4 + g % 4) * 8 + (g // 4) * 2 + c
            for w in range(6):
                e4[s, block * 6 + w] = 1
                bw4[:, block * 6 + w] = b * 384 + w
            for w in range(3):
                e2[s, block * 3 + w] = 1
                bw2[:, block * 3 + w] = b * 192 + w
    rep1 = np.zeros((8 * 48, 192), np.float32)
    rep4 = np.zeros((8 * 16, 48), np.float32)
    rep2 = np.zeros((8 * 32, 96), np.float32)
    for e in range(8):
        for w in range(6):
            rep4[e * 16 + w, e * 6 + w] = 1
            for t in range(4):
                rep1[e * 48 + t * 8 + w, t * 48 + e * 6 + w] = 1
        for m in range(4):
            for w in range(3):
                rep2[e * 32 + m * 8 + w, m * 24 + e * 3 + w] = 1
    pack1 = np.zeros((144, 256), np.float32)
    pack2 = np.zeros((48, 128), np.float32)
    for o in range(8):
        for w in range(6):
            for t in range(3):
                pack1[t * 48 + o * 6 + w, o * 32 + 8 * t + w] = 1
        for w in range(3):
            for m in range(2):
                pack2[m * 24 + o * 3 + w, o * 16 + 4 * m + w] = 1
    rep_a = np.zeros((384, 64), np.float32)
    rep_b = np.zeros((384, 64), np.float32)
    at_a = np.zeros((384, 1), np.float32)
    rep2a = np.zeros((64, 384), np.float32)
    rep2b = np.zeros((64, 384), np.float32)
    at2 = np.zeros((1, 384), np.float32)
    for c in range(2):
        for i in range(4):
            for o in range(8):
                j, zh = o // 2, o % 2
                s_a = ((i * 4 + j) * 2 + zh) * 2 + c
                s_b = ((j * 4 + i) * 2 + zh) * 2 + c
                for w in range(6):
                    r = (c * 4 + i) * 48 + o * 6 + w
                    rep_a[r, s_a] = 1
                    rep_b[r, s_b] = 1
                    at_a[r, 0] = w
                for m in range(2):
                    for w in range(3):
                        r = (c * 4 + i) * 48 + m * 24 + o * 3 + w
                        rep2a[s_a, r] = 1
                        rep2b[s_b, r] = 1
                        at2[0, r] = m * 192 + w
    low = lambda a: jnp.asarray(a, bf16)
    return {
        "e1": low(e1), "bw1": jnp.asarray(bw1), "e2": low(e2), "bw2": jnp.asarray(bw2),
        "e4": low(e4), "bw4": jnp.asarray(bw4),
        "rep1": low(rep1), "rep2": low(rep2), "rep4": low(rep4), "pack1": low(pack1), "pack2": low(pack2),
        "rep_a": low(rep_a), "rep_b": low(rep_b), "at_a": jnp.asarray(at_a), "at_b": jnp.asarray(at_a),
        "rep2a": low(rep2a), "rep2b": low(rep2b), "at2a": jnp.asarray(at2), "at2b": jnp.asarray(at2),
    }


def local(
    inputs, offsets, owners, cotangent,
    norm1_gain, norm1_bias, norm1_moments,
    norm2_gain, norm2_bias, norm2_moments,
    norm3_gain, norm3_bias, norm3_moments,
    conv1_copy, conv1_master, conv1_first, conv1_second, conv1_average, basis1,
    conv2_copy, conv2_master, conv2_first, conv2_second, conv2_average, basis2,
    project_copy, project_master, project_first, project_second, project_average, basis3,
):
    consts = make_consts()
    flip2 = lambda a: jnp.swapaxes(a, -1, -2)
    xt = flip2(inputs[0])
    offsets = offsets[None]
    owners = owners[None]
    params = [norm1_gain, norm1_bias, norm2_gain, norm2_bias, norm3_gain, norm3_bias]
    states = [
        conv1_master, conv1_first, conv1_second, conv1_average,
        conv2_master, conv2_first, conv2_second, conv2_average,
        project_master, project_first, project_second, project_average,
    ]
    out, slopes, stats, *more = run_step(
        xt, offsets, owners, cotangent[0], conv1_copy, flip2(conv2_copy), flip2(project_copy), params,
        (basis1, basis2, basis3), [flip2(a) for a in states], consts,
    )
    gathered, new = more[0:4], more[4:]
    result = run_finish(
        xt, offsets, owners, slopes, stats, gathered, out, params,
        (norm1_moments, norm2_moments, norm3_moments), new, consts,
    )
    out, gin, *vec = result[0:11]
    cp1, cp2, cp3 = result[11:14]
    nm1, nf1, nq1, na1, nm2, nf2, nq2, na2, nm3, nf3, nq3, na3 = [flip2(a) for a in result[14:]]
    return (
        out[None], jnp.transpose(gin, (1, 2, 0)), *vec,
        nm1, cp1, nf1, nq1, na1,
        nm2, flip2(cp2), nf2, nq2, na2,
        nm3, flip2(cp3), nf3, nq3, na3,
    )


def solution(mesh):
    finer = Mesh(mesh.devices.reshape(4, 4, 2, 2, mesh.shape["ch"]), SEQ_CH)
    owner3 = P(None, None, SEQ_CH)
    owner2 = P(None, SEQ_CH)
    half3 = P(None, None, "ch")
    in_specs = (
        P(SEQ, None, "ch"), P(SEQ), P(), P(SEQ, None, "ch"),
        P("ch"), P("ch"), half3, P("ch"), P("ch"), half3, P("ch"), P("ch"), half3,
        half3, owner3, owner3, owner3, owner3, P(),
        half3, owner3, owner3, owner3, owner3, P(),
        P(None, "ch"), owner2, owner2, owner2, owner2, P(),
    )
    vec = P(None, "ch")
    out_specs = (
        P(SEQ, None, "ch"), P(SEQ, None, "ch"), *[vec] * 9,
        owner3, half3, owner3, owner3, owner3,
        owner3, half3, owner3, owner3, owner3,
        owner2, vec, owner2, owner2, owner2,
    )
    return jax.shard_map(local, mesh=finer, in_specs=in_specs, out_specs=out_specs, check_vma=False)
```

```python
import math

import jax
import jax.numpy as jnp
import numpy as np
from jax import lax
from jax.experimental import pallas as pl
from jax.experimental.pallas import tpu as pltpu
from jax.sharding import Mesh
from jax.sharding import PartitionSpec as P

STEP = 8
SEQ = ("seq_0", "seq_1", "seq_2", "seq_3")
SEQ_CH = ("seq_0", "seq_1", "seq_2", "seq_3", "ch")
MESH = pl.DeviceIdType.MESH
bf16 = jnp.bfloat16
f32 = jnp.float32

eps_norm = 1e-05
beta_one = 0.9
beta_two = 0.95
adam_eps = 1e-08
decay_rate = 0.01
average_rate = 0.9
norm_rate = 0.05

C0, C1, H = 652, 768, 384
HALF0, HALF1, HALFH = 326, 384, 192
BINS = 1024
OWN = 512
WIN = 528
LANES = 1152
PAD = 768

GELU_K = math.sqrt(2.0 / math.pi)
GELU_C = 0.044715


def gelu(v):
    return 0.5 * v * (1.0 + jnp.tanh(GELU_K * (v + GELU_C * (v * v * v))))


def gelu_slope(v):
    square = v * v
    t = jnp.tanh(GELU_K * v * (1.0 + GELU_C * square))
    return 0.5 * (1.0 + t) + 0.5 * GELU_K * v * (1.0 - t * t) * (1.0 + 3.0 * GELU_C * square)


def dot(a, b, dims=((1,), (0,))):
    return lax.dot_general(a, b, (dims, ((), ())), preferred_element_type=f32)


def iota(shape, dim):
    return lax.broadcasted_iota(jnp.int32, shape, dim)


def adam_block(first, second, turned):
    first_new = beta_one * first + (1.0 - beta_one) * turned
    second_new = beta_two * second + (1.0 - beta_two) * turned * turned
    direction = (
        first_new
        / (1.0 - beta_one**STEP)
        / (jnp.sqrt(second_new / (1.0 - beta_two**STEP)) + adam_eps)
    )
    return first_new, second_new, direction


def master_block(master, update, rate, average):
    master_new = master - rate * (update + decay_rate * master)
    return master_new, average_rate * average + (1.0 - average_rate) * master_new


class Place:
    def __init__(self):
        self.x, self.y, self.zh, self.c, self.zl = [lax.axis_index(n) for n in SEQ_CH]
        self.z = 2 * self.zh + self.zl
        self.e = 2 * self.z + self.c
        self.g = 4 * self.x + self.y

    def at(self, **other):
        v = {"x": self.x, "y": self.y, "z": self.z, "c": self.c}
        v.update(other)
        z = v["z"]
        return (v["x"], v["y"], lax.div(z, 2), v["c"], lax.rem(z, 2))


def remote(src, dst, send, recv, device):
    return pltpu.make_async_remote_copy(
        src_ref=src, dst_ref=dst, send_sem=send, recv_sem=recv, device_id=device, device_id_type=MESH
    )


def column_peers(p):
    out = []
    for k in range(1, 8):
        z = lax.rem(p.z + k // 2, 4)
        c = lax.rem(p.c + k % 2, 2)
        out.append((p.at(z=z, c=c), z, c))
    return out


def plane_peers(p):
    out = []
    for k in range(1, 16):
        x = lax.rem(p.x + k // 4, 4)
        y = lax.rem(p.y + k % 4, 4)
        out.append((p.at(x=x, y=y), x, y))
    return out


def other_peers(p):
    over = lax.rem(p.z + 2, 4)
    out = [p.at(x=lax.rem(p.x + k, 4), c=1 - p.c) for k in (1, 2, 3)]
    out += [p.at(x=lax.rem(p.x + k, 4), z=over) for k in (1, 2, 3)]
    out += [p.at(y=lax.rem(p.y + k, 4), z=over) for k in (1, 2, 3)]
    return out


class Total:
    def __init__(self, p, bufs, sems):
        self.p = p
        self.b1, self.b2 = bufs
        self.s1, self.r1, self.s2, self.r2 = sems

    def start(self, value):
        p = self.p
        self.b1[p.e] = value
        self.c1 = []
        for k, (device, _, _) in enumerate(column_peers(p)):
            cp = remote(self.b1.at[p.e], self.b1.at[p.e], self.s1.at[k], self.r1.at[p.e], device)
            cp.start()
            self.c1.append(cp)

    def middle(self):
        p = self.p
        for device, z, c in column_peers(p):
            e = 2 * z + c
            remote(self.b1.at[e], self.b1.at[e], self.s1.at[0], self.r1.at[e], device).wait_recv()
        total = self.b1[0]
        for k in range(1, 8):
            total = total + self.b1[k]
        for cp in self.c1:
            cp.wait_send()
        self.b2[p.g] = total
        self.c2 = []
        for k, (device, _, _) in enumerate(plane_peers(p)):
            cp = remote(self.b2.at[p.g], self.b2.at[p.g], self.s2.at[k], self.r2.at[p.g], device)
            cp.start()
            self.c2.append(cp)

    def end(self):
        p = self.p
        for device, x, y in plane_peers(p):
            g = 4 * x + y
            remote(self.b2.at[g], self.b2.at[g], self.s2.at[0], self.r2.at[g], device).wait_recv()
        total = self.b2[0]
        for k in range(1, 16):
            total = total + self.b2[k]
        for cp in self.c2:
            cp.wait_send()
        return total


UNIT_CORE = (0, 1, 0, 1)


def step_kernel(
    xt, offsets, owners, cot, w1, w2, wp, pg1, pb1, pg2, pb2, pg3, pb3,
    e1, bw1, e2, bw2, e4, bw4, rep1, rep2, rep4, pack1, pack2, b1, b2, b3,
    *rest,
):
    states_in = rest[0:12]
    out, sl_home, stats, ga1, gb1, ga2, gb2 = rest[12:19]
    states_out = rest[19:31]
    held_in = rest[31:43]
    held_out = rest[43:55]
    step_body(
        xt, offsets, owners, cot, w1, w2, wp, pg1, pb1, pg2, pb2, pg3, pb3,
        e1, bw1, e2, bw2, e4, bw4, rep1, rep2, rep4, pack1, pack2, b1, b2, b3,
        states_in, states_out, held_in, held_out,
        out, sl_home, stats, ga1, gb1, ga2, gb2, *rest[55:],
    )


def step_body(
    xt, offsets, owners, cot, w1, w2, wp, pg1, pb1, pg2, pb2, pg3, pb3,
    e1, bw1, e2, bw2, e4, bw4, rep1, rep2, rep4, pack1, pack2, b1, b2, b3,
    states_in, states_out, held_in, held_out,
    out, sl_home, stats, ga1, gb1, ga2, gb2,
    s1, s2, xw, raw, aa, ww1, ww2, wwp, pooled, diff, cc, hid, og, no, hh, mid, gg, gp,
    slope, small, offs, offw, acc, tr, dv,
    t1, t2, ra, rb, rd, re, ua, uc, va, pz, rz, pz2, rz2, pz4, rz4,
    b1f, bb1, grad, dd, nb, near1, near2, fa1, fb1, fa2, fb2, pa1, pb1_, pa2, pb2_,
    par, ab1, ab2,
    ss, rs, ls, as1, ar1, as2, ar2, gs, gr, hs, hr, bs, ns, ws, wr,
):
    m1, f1, q1, a1, m2, f2, q2, a2, m3, f3, q3, a3 = held_in
    nm1, nf1, nq1, na1, nm2, nf2, nq2, na2, nm3, nf3, nq3, na3 = held_out
    loads = [pltpu.make_async_copy(states_in[k], held_in[k], ns.at[k]) for k in range(12)]
    stores = [pltpu.make_async_copy(held_out[k], states_out[k], ns.at[12 + k]) for k in range(12)]
    mm = gg.at[0:3]
    p = Place()
    offs[...] = jnp.broadcast_to(offsets[...].astype(f32), (8, 128))
    c, zl = p.c, p.zl
    flip = p.at(z=3 - p.z)
    direct = p.at(z=p.z + 1 - 2 * zl)
    other_core = p.at(c=1 - c)

    bar = pltpu.get_barrier_semaphore()
    for device, _, _ in column_peers(p):
        pl.semaphore_signal(bar, inc=1, device_id=device, device_id_type=MESH)
    for device, _, _ in plane_peers(p):
        pl.semaphore_signal(bar, inc=1, device_id=device, device_id_type=MESH)
    for device in other_peers(p):
        pl.semaphore_signal(bar, inc=1, device_id=device, device_id_type=MESH)

    mine = pl.ds(pl.multiple_of(384 * c, 128), 384)
    others = pl.ds(pl.multiple_of(384 - 384 * c, 128), 384)
    my_lanes = pl.ds(pl.multiple_of(384 * zl, 128), 384)
    its_lanes = pl.ds(pl.multiple_of(384 - 384 * zl, 128), 384)
    my_rows = pl.ds(pl.multiple_of(192 * zl, 16), 192)
    its_rows = pl.ds(pl.multiple_of(192 - 192 * zl, 16), 192)

    def unit_ref(u, rows):
        return ww2.at[u, rows, :] if u < 3 else wwp.at[rows, :]

    own_w = [pltpu.make_async_copy(w1.at[t], ww1.at[t, :, my_lanes], ls.at[t]) for t in range(5)]
    own_w += [
        pltpu.make_async_copy(w2.at[u] if u < 3 else wp, unit_ref(u, my_rows), ls.at[5 + u])
        for u in range(4)
    ]
    for cp in own_w:
        cp.start()

    pl.semaphore_wait(bar, 31)

    is_self = c == zl
    not_self = c != zl
    home_chip = 2 * p.zh + c

    PARTS = ((0, 256), (256, 256), (512, 256), (768, 384))

    def window(j, part):
        at, size = PARTS[part]
        return xt.at[:, pl.ds(pl.multiple_of(896 * j + at, 128), size)]

    def window_there(k, part):
        return xw.at[k, :, pl.ds(*PARTS[part])]

    def cot_window(j):
        return cot.at[pl.ds(pl.multiple_of(496 * j, 16), WIN), :]

    cc_mine = cc.at[:, pl.ds(pl.multiple_of(384 * zl, 128), 384)]
    x_a = [
        remote(window(c, h), window_there(zl, h), ss.at[36 + 2 * h], rs.at[36 + 2 * h + zl], p.at(z=home_chip, c=c))
        for h in range(4)
    ]
    x_b = [
        remote(
            window(1 - c, h), window_there(zl, h), ss.at[37 + 2 * h], rs.at[36 + 2 * h + zl],
            p.at(z=home_chip, c=1 - c),
        )
        for h in range(4)
    ]
    c_a = remote(cot_window(c), cc_mine, ss.at[2], rs.at[2 + zl], p.at(z=home_chip, c=c))
    c_b = remote(cot_window(1 - c), cc_mine, ss.at[3], rs.at[2 + zl], p.at(z=home_chip, c=1 - c))
    o_a = remote(offs, offw, ss.at[4], rs.at[4], other_core)

    def send_windows(h):
        pl.when(not_self)(lambda: x_a[h].start())

        def keep():
            pltpu.make_async_copy(window(c, h), window_there(zl, h), rs.at[36 + 2 * h + zl]).start()

        pl.when(is_self)(keep)
        x_b[h].start()

    send_windows(0)
    o_a.start()

    def block_at(b, ch):
        t = lax.div(b, 3)
        return ww1.at[t, :, pl.ds(pl.multiple_of(384 * ch + 128 * (b - 3 * t), 128), 128)]

    def block_of(axis, k):
        if axis == "x":
            return 2 * lax.rem(p.x + k, 4) + c
        return 8 + 2 * lax.rem(p.y + k, 4) + c

    def if_block(axis, b, do):
        if axis == "x":
            do()
        else:
            pl.when(b < 15)(do)

    def fetch(axis):
        b = block_of(axis, 0)
        part = block_at(b, zl)
        return b, remote(part, part, ws.at[0 if axis == "x" else 1], wr.at[b], flip)

    def spread(axis):
        b = block_of(axis, 0)
        part = block_at(b, 1 - zl)
        to = [p.at(**{axis: lax.rem((p.x if axis == "x" else p.y) + k, 4)}) for k in (1, 2, 3)]
        first = 2 if axis == "x" else 5
        return b, [remote(part, part, ws.at[first + k], wr.at[b], to[k]) for k in range(3)]

    def across(axis, k):
        b = block_of(axis, k)
        part = block_at(b, 1 - zl)
        return b, remote(part, part, ws.at[(8 if axis == "x" else 12) + k], wr.at[b], other_core)

    def start_fetch(axis):
        b, cp = fetch(axis)
        if_block(axis, b, cp.start)

    def block_here(b):
        part = block_at(b, 1 - zl)
        remote(part, part, ws.at[0], wr.at[b], other_core).wait_recv()

    def start_spread(axis):
        b, cps = spread(axis)

        def do():
            block_here(b)
            for cp in cps + [across(axis, 0)[1]]:
                cp.start()

        if_block(axis, b, do)

    def start_across(axis, k):
        b, cp = across(axis, k)

        def do():
            block_here(b)
            cp.start()

        if_block(axis, b, do)

    def unit_over(u):
        return remote(
            unit_ref(u, my_rows), unit_ref(u, my_rows), ss.at[15 + u], rs.at[15 + u], flip
        )

    def unit_here(u):
        return remote(
            unit_ref(u, its_rows), unit_ref(u, its_rows), ss.at[19 + u], rs.at[19 + u], other_core
        )

    for t in range(5):
        own_w[t].wait()
    start_fetch("x")

    for cp in loads:
        cp.start()

    off_home = offs[0:1, 0:1]
    total_s = jnp.zeros((8, HALF0), f32)
    total_q = jnp.zeros((8, HALF0), f32)
    for k in range(8):
        lanes = pl.ds(256 * k, 256)
        mask = ((iota((8, 256), 1) + 256 * k).astype(f32) >= 2.0 * off_home).astype(bf16)
        xb = xt[:, lanes]
        xf = xb.astype(f32)
        sq = xf * xf
        hi = sq.astype(bf16)
        lo = (sq - hi.astype(f32)).astype(bf16)
        nt = ((1,), (1,))
        total_s = total_s + dot(mask, xb, nt)
        total_q = total_q + (dot(mask, hi, nt) + dot(mask, lo, nt))
    small[...] = jnp.zeros_like(small)
    small[0:1, 0:HALF0] = total_s[0:1]
    small[1:2, 0:HALF0] = total_q[0:1]
    small[2:3, 0:HALF0] = pg1[...].reshape(1, HALF0)
    small[3:4, 0:HALF0] = pb1[...].reshape(1, HALF0)
    small[4:5, 0:HALF1] = pg2[...].reshape(1, HALF1)
    small[5:6, 0:HALF1] = pb2[...].reshape(1, HALF1)
    small[6:7, 0:HALFH] = pg3[...].reshape(1, HALFH)
    small[6:7, H : H + HALFH] = pb3[...].reshape(1, HALFH)
    here = small[...]
    half_row = iota((8, PAD), 0)
    moved = jnp.where(
        half_row < 4,
        pltpu.roll(here, HALF0, 1),
        jnp.where(half_row < 6, pltpu.roll(here, HALF1, 1), pltpu.roll(here, HALFH, 1)),
    )
    here = jnp.where(zl == 0, here, moved)
    count = jnp.maximum(BINS - off_home, 0.0)
    lane8 = iota((8, PAD), 1)
    row8 = iota((8, PAD), 0)
    params_over = remote(par.at[0], par.at[1], ss.at[35], rs.at[35], direct)
    par[0] = here
    here = here + jnp.where((lane8 == PAD - 1) & (row8 == 0), count, 0.0)
    all1 = Total(p, (ab1.at[5], ab2.at[5]), (as1.at[0], ar1.at[0], as2.at[0], ar2.at[0]))
    all1.start(here[0:2])
    params_over.start()
    start_fetch("y")
    for h in range(1, 4):
        send_windows(h)

    @pl.when(not_self)
    def _():
        c_a.start()

    @pl.when(is_self)
    def _():
        pltpu.make_async_copy(cot_window(c), cc_mine, rs.at[2 + zl]).start()

    c_b.start()
    for u in range(4):
        own_w[5 + u].wait()
        pl.when(c == UNIT_CORE[u])(lambda u=u: unit_over(u).start())
    all1.middle()
    start_spread("x")
    start_spread("y")

    owners_row = jnp.broadcast_to(owners[...].astype(f32), (8, 64)).astype(bf16)
    nat1 = dot(owners_row, e1[...])[0:1] * 6.0 + bw1[0:1]
    nat2 = dot(owners_row, e2[...])[0:1] * 3.0 + bw2[0:1]
    for k in range(4):
        s1[4, k] = ((iota((192, PAD), 0) + 192 * k).astype(f32) == nat1).astype(bf16).reshape(4, 48, PAD)
    perm2 = (iota((H, H), 0).astype(f32) == nat2).astype(bf16)

    row = iota((128, 128), 0)
    pick = (iota((128, 128), 1) == jnp.where(row < 64, 2 * row, 2 * row - 127)).astype(bf16)
    def window_here(k, h):
        part = window_there(k, h)
        remote(part, part, ss.at[0], rs.at[36 + 2 * h + k], other_core).wait_recv()

    tr[...] = jnp.zeros_like(tr)

    def blocks(k, second):
        for b in range(9):
            if b in (0, 2, 4, 6):
                window_here(k, b // 2)
            buf = b % 2
            tr[buf, :, 0:HALF0] = dot(pick, xw[k, :, pl.ds(128 * b, 128)], ((1,), (1,)))
            bins = pl.ds(64 * b, 64)

            def put(value, bins=bins):
                value = value.astype(bf16)
                for par in range(2):
                    part = value[64 * par : 64 * par + 64]
                    raw[par, bins, :] = raw[par, bins, :] + part if second else part

            pl.when(k == 0)(lambda: put(tr[buf]))
            pl.when(k == 1)(lambda: put(pltpu.roll(tr[buf], HALF0, 1)))

    blocks(zl, False)
    first = all1.end()
    n1 = first[0:1, PAD - 1 : PAD]
    n2 = 0.5 * n1
    inv_n1 = 1.0 / n1
    inv_n2 = 1.0 / n2
    real = iota((1, PAD), 1) < C0
    mean1 = jnp.where(real, first[0:1], 0.0) * inv_n1
    var1 = jnp.maximum(first[1:2] * inv_n1 - mean1 * mean1, 0.0)
    rs1 = lax.rsqrt(var1 + eps_norm)
    params_over.wait()
    both_halves = par[0] + par[1]
    gain1, bias1 = both_halves[2:3], both_halves[3:4]
    gain2, bias2 = both_halves[4:5], both_halves[5:6]
    gain3, bias3 = both_halves[6:7, 0:H], both_halves[6:7, H : 2 * H]

    remote(offs, offw, ss.at[4], rs.at[4], other_core).wait()
    off = jnp.where(is_self, offs[0:1, 0:1], offw[0:1, 0:1])

    bin0 = 496 * c
    own0 = pl.multiple_of(16 * c, 16)
    raw0 = pl.multiple_of(48 * c, 16)
    rawown = pl.multiple_of(64 * c, 16)

    def valid_mask(rows, at=0):
        return ((iota((rows, 1), 0) + (bin0 + at)).astype(f32) >= off).astype(f32)

    def own_mask(rows, at=0):
        r = iota((rows, 1), 0) + at
        return ((r >= 16 * c) & (r < 16 * c + OWN)).astype(f32)

    not_first = (iota((WIN, 1), 0) > 0).astype(f32)
    not_last = (iota((WIN, 1), 0) < WIN - 1).astype(f32)

    def before(v):
        return (pltpu.roll(v, 1, 0) * not_first).astype(bf16)

    def after(v):
        return (pltpu.roll(v, WIN - 1, 0) * not_last).astype(bf16)

    small[0:1] = rs1 * gain1
    small[1:2] = bias1 - mean1 * (rs1 * gain1)
    small[2:3] = mean1
    small[3:4] = rs1

    def norm_tile(q):
        lanes = pl.ds(pl.multiple_of(128 * q, 128), 128)
        scale, shift = small[0:1, lanes], small[1:2, lanes]
        valid = valid_mask(WIN)
        for par in range(2):
            v = raw[par, pl.ds(raw0, WIN), lanes].astype(f32)
            v = gelu(v * scale + shift) * valid
            aa[par, :, lanes] = before(v)
            aa[2 + par, :, lanes] = v.astype(bf16)
            aa[4 + par, :, lanes] = after(v)

    @pl.loop(0, 2)
    def _(k):
        norm_tile(3 * zl + k)

    blocks(1 - zl, True)
    for k in (1, 3, 2):
        for axis in ("x", "y"):
            start_across(axis, k)

    @pl.loop(0, 4)
    def _(k):
        norm_tile(jnp.where(zl == 0, k + 2, jnp.where(k < 3, k, 5)))

    for b in range(15):
        pl.when(c != b % 2)(lambda b=b: block_here(jnp.int32(b)))

    acc[...] = jnp.zeros_like(acc)

    @pl.loop(0, 3)
    def _(k):
        rows = pl.ds(pl.multiple_of(176 * k, 16), 176)
        h0 = jnp.zeros((176, C1), f32)
        for t in range(5):
            h0 = h0 + dot(aa[t, rows, 0:C0], ww1[t])
        h1 = jnp.zeros((176, C1), f32)
        for t in range(5):
            h1 = h1 + dot(aa[t + 1, rows, 0:C0], ww1[t])
        d = h0 - h1
        v = jnp.maximum(h0, h1) + (jnp.log(1.0 + jnp.exp(-jnp.abs(d))) - math.log(2.0))
        diff[rows, :] = d
        pooled[rows, :] = v
        m = valid_mask(176, 176 * k) * own_mask(176, 176 * k)
        vm = v * m
        acc[0:1] += jnp.sum(vm, axis=0, keepdims=True)
        acc[1:2] += jnp.sum(vm * v, axis=0, keepdims=True)

    all2 = Total(p, (ab1.at[0], ab2.at[0]), (as1.at[1], ar1.at[1], as2.at[1], ar2.at[1]))
    all2.start(acc[0:2])

    def early_slopes(par):
        @pl.loop(0, 6)
        def _(q):
            lanes = pl.ds(pl.multiple_of(128 * q, 128), 128)
            xv = raw[par, pl.ds(rawown, OWN), lanes].astype(f32)
            turn = gelu_slope(xv * small[0:1, lanes] + small[1:2, lanes])
            dv[par, :, lanes] = (turn * valid_mask(OWN, 16 * c)).astype(bf16)

    early_slopes(0)
    all2.middle()
    for u in range(4):

        def there_u(u=u):
            remote(
                unit_ref(u, its_rows), unit_ref(u, its_rows), ss.at[15 + u], rs.at[15 + u], flip
            ).wait_recv()
            unit_here(u).start()

        pl.when(c == UNIT_CORE[u])(there_u)
    for k in range(2):
        part = cc.at[:, pl.ds(384 * k, 384)]
        remote(part, part, ss.at[0], rs.at[2 + k], other_core).wait_recv()
    for u in range(4):
        pl.when(c == UNIT_CORE[u])(lambda u=u: unit_here(u).wait_send())
        pl.when(c != UNIT_CORE[u])(lambda u=u: unit_here(u).wait_recv())
    og[...] = dot(cc[...], wwp[...], ((1,), (1,)))
    early_slopes(1)

    @pl.when(not_self)
    def _():
        for h in range(4):
            x_a[h].wait_send()
        c_a.wait_send()

    for h in range(4):
        x_b[h].wait_send()
    c_b.wait_send()
    for axis in ("x", "y"):
        b, cps = spread(axis)
        own_sends = [fetch(axis)[1], *cps, across(axis, 0)[1]]

        def sent_all(own_sends=own_sends):
            for cp in own_sends:
                cp.wait_send()

        if_block(axis, b, sent_all)
        for k in (1, 2, 3):
            b, cp = across(axis, k)
            if_block(axis, b, cp.wait_send)
    for u in range(4):
        pl.when(c == UNIT_CORE[u])(lambda u=u: unit_over(u).wait_send())

    second = all2.end()
    mean2 = second[0:1] * inv_n2
    var2 = jnp.maximum(second[1:2] * inv_n2 - mean2 * mean2, 0.0)
    rs2 = lax.rsqrt(var2 + eps_norm)
    acc[2:3] = rs2 * gain2
    acc[3:4] = bias2 - mean2 * (rs2 * gain2)
    acc[4:5] = mean2
    acc[5:6] = rs2

    @pl.loop(0, 6)
    def _(k):
        lanes = pl.ds(pl.multiple_of(128 * k, 128), 128)
        v = gelu(pooled[:, lanes] * acc[2:3, lanes] + acc[3:4, lanes]) * valid_mask(WIN)
        mm[0, :, lanes] = before(v)
        mm[1, :, lanes] = v.astype(bf16)
        mm[2, :, lanes] = after(v)

    h2 = jnp.zeros((WIN, H), f32)
    for t in range(3):
        h2 = h2 + dot(mm[t], ww2[t], ((1,), (1,)))
    hid[...] = h2
    m = valid_mask(WIN) * own_mask(WIN)
    h2m = h2 * m
    acc[6:7, 0:H] = jnp.sum(h2m, axis=0, keepdims=True)
    acc[6:7, H : 2 * H] = jnp.sum(h2m * h2, axis=0, keepdims=True)
    all3 = Total(p, (ab1.at[1], ab2.at[1]), (as1.at[2], ar1.at[2], as2.at[2], ar2.at[2]))
    all3.start(acc[6:8])

    def basis_rows(src, first, size, buf, sem):
        return pltpu.make_async_copy(src.at[pl.ds(first, size)], buf, bs.at[sem])

    slope_buf = [slope.at[pl.ds(0, 128)], slope.at[pl.ds(128, 128)]]
    rows_buf = slope_buf + [tr.at[0], tr.at[1]]

    def rounds(n):
        got = []
        for k in range(4):
            block = 4 * n + k
            src = b2 if block < 6 else b3
            got.append(basis_rows(src, 128 * (block % 6), 128, rows_buf[k], k))
        return got

    def keep_round(n):
        for k, cp in enumerate(rounds(n)):
            cp.wait()
            block = 4 * n + k
            half, at = block // 3, 128 * (block % 3)
            value = rows_buf[k][...].astype(bf16)
            if half < 3:
                ww2[half, pl.ds(at, 128), :] = value
            else:
                wwp[pl.ds(at, 128), :] = value

    first_basis = pltpu.make_async_copy(b1, b1f, bs.at[4])
    first_basis.start()

    @pl.loop(0, 6)
    def _(q):
        lanes = pl.ds(pl.multiple_of(128 * q, 128), 128)
        turn = gelu_slope(pooled[:, lanes] * acc[2:3, lanes] + acc[3:4, lanes])
        turn = (turn * valid_mask(WIN)).astype(bf16)
        xw[0, 0:272, lanes] = turn[0:272]
        xw[1, 0:256, lanes] = turn[272:WIN]

    all3.middle()

    @pl.loop(0, 6)
    def _(q):
        lanes = pl.ds(pl.multiple_of(128 * q, 128), 128)
        diff[:, lanes] = 1.0 / (1.0 + jnp.exp(-diff[:, lanes]))

    first_basis.wait()
    bb1[...] = b1f[...].astype(bf16)
    third = all3.end()
    mean3 = third[0:1, 0:H] * inv_n2
    var3 = jnp.maximum(third[0:1, H : 2 * H] * inv_n2 - mean3 * mean3, 0.0)
    rs3 = lax.rsqrt(var3 + eps_norm)
    valid = valid_mask(WIN)
    own = own_mask(WIN)
    h2 = hid[...]
    scaled = (h2 - mean3) * rs3
    pre = scaled * gain3 + bias3
    no[...] = (gelu(pre) * valid).astype(bf16)
    slopes = gelu_slope(pre) * og[...] * valid
    og[...] = slopes
    hid[...] = scaled
    acc[6:7, 0:H] = jnp.sum(slopes * scaled * own, axis=0, keepdims=True)
    acc[6:7, H : 2 * H] = jnp.sum(slopes * own, axis=0, keepdims=True)
    all4 = Total(p, (ab1.at[2], ab2.at[2]), (as1.at[3], ar1.at[3], as2.at[3], ar2.at[3]))
    all4.start(acc[6:8])
    out_rows = pl.ds(pl.multiple_of(512 * c, 16), OWN)
    own_rows = pl.ds(own0, OWN)
    gp[0] = (pooled[own_rows, :] + dot(no[own_rows, :], wwp[...])).astype(bf16)
    all4.middle()

    def out_copy(k):
        return remote(
            gp.at[0, :, pl.ds(384 * k, 384)],
            out.at[out_rows, :],
            ss.at[23 + k],
            rs.at[23 + c],
            p.at(z=2 * p.zh + k, c=zl),
        )

    def out_local(k):
        return pltpu.make_async_copy(
            gp.at[0, :, pl.ds(384 * k, 384)], out.at[out_rows, :], ls.at[9]
        )

    def to_self(k):
        return (zl == k) & is_self

    for k in range(2):
        pl.when(jnp.logical_not(to_self(k)))(lambda k=k: out_copy(k).start())

        pl.when(to_self(k))(lambda k=k: out_local(k).start())

    def put2(m, value):
        s2[:, :, pl.ds(24 * m, 24), :] = value.astype(bf16).reshape(4, 4, 24, C1)

    tn = ((0,), (0,))
    nop = dot(no[own_rows, :], perm2).astype(bf16)
    put2(3, dot(nop, cc[own_rows, :], tn))
    for cp in rounds(0):
        cp.start()
    fourth = all4.end()
    stats[4:5] = fourth[0:1]
    gain_mean = fourth[0:1, 0:H] * inv_n2
    bias_mean = fourth[0:1, H : 2 * H] * inv_n2
    hg = valid_mask(WIN) * (gain3 * rs3) * (og[...] - bias_mean - hid[...] * gain_mean)
    hh[0] = after(hg)
    hh[1] = hg.astype(bf16)
    hh[2] = before(hg)
    mid_grad = jnp.zeros((WIN, C1), f32)
    for t in range(3):
        mid_grad = mid_grad + dot(hh[t], ww2[t])
    mid[...] = mid_grad

    @pl.loop(0, 6)
    def _(k):
        lanes = pl.ds(pl.multiple_of(128 * k, 128), 128)
        v = pooled[:, lanes]
        turn = jnp.concatenate([xw[0, 0:272, lanes], xw[1, 0:256, lanes]], axis=0)
        slopes = turn.astype(f32) * mid[:, lanes]
        scaled = (v - acc[4:5, lanes]) * acc[5:6, lanes]
        mid[:, lanes] = slopes
        pooled[:, lanes] = scaled
        mine = slopes * own_mask(WIN)
        acc[0:1, lanes] = jnp.sum(mine * scaled, axis=0, keepdims=True)
        acc[1:2, lanes] = jnp.sum(mine, axis=0, keepdims=True)

    all5 = Total(p, (ab1.at[3], ab2.at[3]), (as1.at[4], ar1.at[4], as2.at[4], ar2.at[4]))
    all5.start(acc[0:2])
    hp = dot(hh[1, own_rows, :], perm2).astype(bf16)
    put2(0, dot(hp, mm[0, own_rows, :], tn))
    keep_round(0)
    all5.middle()
    for cp in rounds(1):
        cp.start()
    for t in range(1, 3):
        put2(t, dot(hp, mm[t, own_rows, :], tn))
    s2_over = remote(s2.at[:, :, :, others], t2, gs.at[0], gr.at[0], other_core)
    s2_over.start()
    keep_round(1)
    for cp in rounds(2):
        cp.start()
    nat4 = dot(owners_row, e4[...])[0:1] * 6.0 + bw4[0:1]
    for r in range(3):
        for h in range(2):
            hh[r, pl.ds(256 * h, 256), :] = (
                (iota((256, 384), 0) + 256 * r).astype(f32) == nat4[:, 384 * h : 384 * h + 384]
            ).astype(bf16)
    fifth = all5.end()
    stats[2:4] = fifth
    acc[0:2] = fifth * inv_n2

    @pl.loop(0, 6)
    def _(k):
        lanes = pl.ds(pl.multiple_of(128 * k, 128), 128)
        back = acc[2:3, lanes] * (
            mid[:, lanes] - acc[1:2, lanes] - pooled[:, lanes] * acc[0:1, lanes]
        )
        pg = cc[:, lanes].astype(f32) + back * valid_mask(WIN)
        even = diff[:, lanes]
        ge = pg * even
        go = pg * (1.0 - even)
        gg[0, :, lanes] = after(go)
        gg[1, :, lanes] = after(ge)
        gg[2, :, lanes] = go.astype(bf16)
        gg[3, :, lanes] = ge.astype(bf16)
        gg[4, :, lanes] = before(go)
        gg[5, :, lanes] = before(ge)

    def total(own, parts):
        v = own.astype(f32)
        for part in parts:
            v = v + part.astype(f32)
        return v.astype(bf16)

    def along(k, axis):
        if axis == "x":
            i = lax.rem(p.x + k + 1, 4)
            return p.at(x=i), i
        if axis == "z":
            i = lax.rem(p.z + k + 1, 4)
            return p.at(z=i), i
        i = lax.rem(p.y + k + 1, 4)
        return p.at(y=i), i

    s2_over.wait()
    t2[...] = t2[...] + s2[:, :, :, mine]
    flying = []

    def send(src, dst, sem, device):
        cp = remote(src, dst, gs.at[sem], gr.at[sem], device)
        cp.start()
        flying.append(cp)

    def arrived(dst, sem):
        remote(dst, dst, gs.at[0], gr.at[sem], other_core).wait_recv()

    for k in range(3):
        device, i = along(k, "z")
        send(t2.at[i], rd.at[k], 1 + k, device)

    for k in range(2):

        def out_sent(k=k):
            out_copy(k).wait_send()

        pl.when(jnp.logical_not(to_self(k)))(out_sent)
        pl.when(to_self(k))(lambda k=k: out_local(k).wait())
    perm = s1[4].reshape(PAD, PAD)
    gp[0] = dot(gg[3, own_rows, :], perm).astype(bf16)
    gp[1] = dot(gg[2, own_rows, :], perm).astype(bf16)

    TAP_AXIS = ("x", "y", "x", "y", "z")
    SECOND = {"x": "y", "y": "x", "z": "y"}

    def for_last_tap(slot):
        g = gg[slot, own_rows, :]
        halves = []
        for h in range(2):
            v = dot(g[:, 0:256], hh[0, pl.ds(256 * h, 256), :])
            for r in (1, 2):
                v = v + dot(g[:, 256 * r : 256 * r + 256], hh[r, pl.ds(256 * h, 256), :])
            halves.append(v.astype(bf16))
        return halves

    def to_core(t):
        return remote(s1.at[t, :, :, :, others], t1.at[t], gs.at[7 + t], gr.at[7 + t], other_core)

    def to_axis(t):
        to_core(t).wait_recv()
        t1[t] = t1[t] + s1[t, :, :, :, mine]
        for k in range(3):
            device, i = along(k, TAP_AXIS[t])
            src = t1.at[t, :, i] if TAP_AXIS[t] == "y" else t1.at[t, i]
            send(src, ra.at[t, k], 12 + 3 * t + k, device)

    def to_other_axis(t):
        for k in range(3):
            arrived(ra.at[t, k], 12 + 3 * t + k)
        own_part = {"x": lambda: t1[t, p.x], "y": lambda: t1[t, :, p.y], "z": lambda: t1[t, p.z]}[TAP_AXIS[t]]()
        ua[t] = total(own_part, [ra[t, k] for k in range(3)])
        for k in range(3):
            device, i = along(k, SECOND[TAP_AXIS[t]])
            send(ua.at[t, i], rb.at[t, k], 27 + 3 * t + k, device)

    def last_of(t):
        for k in range(3):
            arrived(rb.at[t, k], 27 + 3 * t + k)
        own_part = ua[t, p.x] if TAP_AXIS[t] == "y" else ua[t, p.y]
        va[t] = total(own_part, [rb[t, k] for k in range(3)])

    for t in range(5):
        if t == 4:
            for k in range(2):
                halves = for_last_tap(3 - k)
                gp[k, :, 0:384] = halves[0]
                gp[k, :, 384:768] = halves[1]
        part = dot(gp[0], aa[t, own_rows, 0:C0], tn) + dot(gp[1], aa[t + 1, own_rows, 0:C0], tn)
        part = part.astype(bf16).reshape(4, 4, 48, C0)
        s1[t, :, :, :, 0:C0] = part
        s1[t, :, :, :, C0:PAD] = jnp.zeros((4, 4, 48, PAD - C0), bf16)
        to_core(t).start()
        if t > 0:
            to_axis(t - 1)
    to_axis(4)
    keep_round(2)

    def second_of_two():
        for k in range(3):
            arrived(rd.at[k], 1 + k)
        uc[...] = total(t2[p.z], [rd[k] for k in range(3)])
        for k in range(3):
            device, i = along(k, "y")
            send(uc.at[i], re.at[k], 4 + k, device)

    def xc_peers():
        for k in range(1, 8):
            xi = lax.rem(p.x + k // 2, 4)
            ci = lax.rem(c + k % 2, 2)
            yield p.at(x=xi, c=ci), 2 * xi + ci

    def slope_part(half, par, k):
        return (
            gp.at[par, pl.ds(256 * k, 256), pl.ds(384 * half, 384)],
            sl_home.at[c, par, pl.ds(256 * k, 256), :],
        )

    def slope_copy(half, par, k):
        src, dst = slope_part(half, par, k)
        n = 2 * par + k
        return remote(src, dst, ss.at[25 + 4 * half + n], rs.at[25 + 4 * c + n], p.at(z=2 * p.zh + half, c=zl))

    def slope_local(half, par, k):
        src, dst = slope_part(half, par, k)
        return pltpu.make_async_copy(src, dst, rs.at[25 + 4 * c + 2 * par + k])

    def send_slopes(par):
        for half in range(2):
            for k in range(2):

                def send_slope(half=half, k=k):
                    slope_copy(half, par, k).start()

                def keep_slope(half=half, k=k):
                    slope_local(half, par, k).start()

                pl.when(jnp.logical_not(to_self(half)))(send_slope)
                pl.when(to_self(half))(keep_slope)

    small[4:6] = jnp.zeros((2, PAD), f32)
    for par in range(2):
        for k in range(2):
            rows = pl.ds(pl.multiple_of(own0 + 256 * k, 16), 256)
            v = jnp.zeros((256, C0), f32)
            for t in range(5):
                v = v + dot(gg[t + 1 - par, rows, :], ww1[t], ((1,), (1,)))
            slope[:, 0:C0] = v
            slope[:, C0:PAD] = jnp.zeros((256, PAD - C0), f32)

            @pl.loop(0, 6)
            def _(q, par=par, k=k):
                lanes = pl.ds(pl.multiple_of(128 * q, 128), 128)
                xv = raw[par, pl.ds(pl.multiple_of(rawown + 256 * k, 16), 256), lanes].astype(f32)
                slopes = dv[par, pl.ds(256 * k, 256), lanes].astype(f32) * slope[:, lanes]
                scaled = (xv - small[2:3, lanes]) * small[3:4, lanes]
                slope[:, lanes] = slopes
                small[4:5, lanes] += jnp.sum(slopes * scaled, axis=0, keepdims=True)
                small[5:6, lanes] += jnp.sum(slopes, axis=0, keepdims=True)

            dst = pl.ds(256 * k, 256)
            gp[par, dst, 0:384] = slope[:, 0:384].astype(bf16)
            gp[par, dst, 384:768] = pltpu.roll(slope[...], PAD - HALF0, 1)[:, 0:384].astype(bf16)
            if (par, k) == (0, 1):
                second_of_two()
                send_slopes(0)
            if (par, k) == (1, 0):
                to_other_axis(0)
                to_other_axis(1)

    all6 = Total(p, (ab1.at[4], ab2.at[4]), (as1.at[5], ar1.at[5], as2.at[5], ar2.at[5]))
    all6.start(small[4:6])

    to_other_axis(2)
    to_other_axis(3)
    for k in range(3):
        arrived(re.at[k], 4 + k)
    g2 = dot(rep2[...], total(uc[p.y], [re[k] for k in range(3)]))
    e2_own = 2 * p.x + c
    for e in range(8):
        pz2[e] = g2[32 * e : 32 * e + 32].astype(bf16)
    for k, (device, e) in enumerate(xc_peers()):
        cp = remote(pz2.at[e], rz2.at[e2_own], gs.at[50 + k], gr.at[50 + e2_own], device)
        cp.start()
        flying.append(cp)
    rz2[e2_own] = pz2[e2_own]
    for t in range(2):
        last_of(t)
    to_other_axis(4)
    for t in range(2, 4):
        last_of(t)
    g1 = dot(rep1[...], va[0:4].reshape(192, 384))
    for e in range(8):
        pz[e] = g1[48 * e : 48 * e + 48].astype(bf16)
    for k, (device, zi, ci) in enumerate(column_peers(p)):
        cp = remote(pz.at[2 * zi + ci], rz.at[p.e], gs.at[42 + k], gr.at[42 + p.e], device)
        cp.start()
        flying.append(cp)
    last_of(4)
    g4 = dot(rep4[...], va[4])
    for e in range(8):
        pz4[e] = g4[16 * e : 16 * e + 16].astype(bf16)
    for k, (device, e) in enumerate(xc_peers()):
        cp = remote(pz4.at[e], rz4.at[e2_own], gs.at[58 + k], gr.at[58 + e2_own], device)
        cp.start()
        flying.append(cp)
    rz4[e2_own] = pz4[e2_own]
    rz[p.e] = pz[p.e]
    all6.middle()

    def summed(parts, half):
        v = parts[half].astype(f32)
        for k in range(1, 4):
            v = v + parts[2 * k + half].astype(f32)
        return v

    for cp in loads:
        cp.wait()
    for _, e in xc_peers():
        arrived(rz2.at[e], 50 + e)
    for half in range(2):
        grad[48:80, 384 * half : 384 * half + 384] = summed(rz2, half)
    nt = ((1,), (1,))
    nb[...] = jnp.zeros_like(nb)
    dd[...] = jnp.zeros_like(dd)

    def turn2(v):
        return dot(v[:, 0:384], ww2[0]) + dot(v[:, 384:768], ww2[1])

    def turn3(v):
        return dot(v[:, 0:384], ww2[2]) + dot(v[:, 384:768], wwp[...])

    turned = turn2(grad[48:72].astype(bf16))
    for t in range(3):
        first_new, second_new, direction = adam_block(f2[t], q2[t], turned[8 * t : 8 * t + 3])
        nf2[t] = first_new
        nq2[t] = second_new
        dd[40 + 8 * t : 43 + 8 * t, :] = direction
    turned = turn3(grad[72:80].astype(bf16))
    first_new, second_new, direction = adam_block(f3[...], q3[...], turned[0:3])
    nf3[...] = first_new
    nq3[...] = second_new
    dd[64:67] = direction
    d2 = dd[40:64].astype(bf16)
    update = jnp.concatenate([dot(d2, ww2[0], nt), dot(d2, ww2[1], nt)], axis=1)
    row_of_two = (68, 80, 84)
    for t in range(3):
        master_new, average_new = master_block(m2[t], update[8 * t : 8 * t + 3], 0.02, a2[t])
        nm2[t] = master_new
        na2[t] = average_new
        nb[row_of_two[t] : row_of_two[t] + 3, :] = master_new
    d3 = dd[64:72].astype(bf16)
    update = jnp.concatenate([dot(d3, ww2[2], nt), dot(d3, wwp[...], nt)], axis=1)
    master_new, average_new = master_block(m3[...], update[0:3], 0.05, a3[...])
    nm3[...] = master_new
    na3[...] = average_new
    nb[64:67, :] = master_new
    for cp in stores[4:12]:
        cp.start()

    def hop(src, dst, send_at, recv_at, device):
        cp = remote(src, dst, hs.at[send_at], hr.at[recv_at], device)
        cp.start()
        flying.append(cp)

    def landed(dst, sem):
        remote(dst, dst, hs.at[0], hr.at[sem], other_core).wait_recv()

    qa = 2 * p.y + p.zh
    qb = 2 * p.x + p.zh

    def near_peers(axis):
        for k in range(1, 8):
            i = lax.rem((p.y if axis == "y" else p.x) + k // 2, 4)
            zh = lax.rem(p.zh + k % 2, 2)
            z = 2 * zh + zl
            yield (p.at(y=i, z=z) if axis == "y" else p.at(x=i, z=z)), 2 * i + zh

    def gather_near(near, fa, fb, rows, base):
        fa[qa] = near[0:rows]
        fb[qb] = near[rows : 2 * rows]
        for k, (device, _) in enumerate(near_peers("y")):
            hop(near.at[pl.ds(0, rows)], fa.at[qa], base + k, base + qa, device)
        for k, (device, _) in enumerate(near_peers("x")):
            hop(near.at[pl.ds(rows, rows)], fb.at[qb], base + 8 + k, base + 8 + qb, device)

    def gather_far(fa, fb, pack, pa, pb, parts_a, parts_b, ga, gb, base):
        for _, q in near_peers("y"):
            landed(fa.at[q], base + q)
        pa[...] = dot(pack, fa[...].reshape(8 * fa.shape[1], PAD)).astype(bf16)
        for k in range(3):
            device, _ = along(k, "x")
            for n, part in enumerate(parts_a):
                hop(pa.at[part], ga.at[(c, p.x) + part], base + 16 + 8 * n + k, base + 16 + 8 * n + p.x, device)
        for _, q in near_peers("x"):
            landed(fb.at[q], base + 8 + q)
        pb[...] = dot(pack, fb[...].reshape(8 * fb.shape[1], PAD)).astype(bf16)
        for k in range(3):
            device, _ = along(k, "y")
            for n, part in enumerate(parts_b):
                hop(pb.at[part], gb.at[(c, p.y) + part], base + 20 + 8 * n + k, base + 20 + 8 * n + p.y, device)
        kept = []
        for n, part in enumerate(parts_a):
            hop(pa.at[part], ga.at[(c, p.x) + part], base + 35 + 8 * n, base + 32 + 8 * n + p.x, other_core)
            kept.append(pltpu.make_async_copy(pa.at[part], ga.at[(c, p.x) + part], bs.at[8 + n]))
        for n, part in enumerate(parts_b):
            hop(pb.at[part], gb.at[(c, p.y) + part], base + 39 + 8 * n, base + 36 + 8 * n + p.y, other_core)
            kept.append(pltpu.make_async_copy(pb.at[part], gb.at[(c, p.y) + part], bs.at[10 + n]))
        for cp in kept:
            cp.start()
        return kept

    def gather_over(parts_a, parts_b, ga, gb, base):
        for k in range(3):
            _, i = along(2 - k, "x")
            for n, part in enumerate(parts_a):
                ref = ga.at[(c, i) + part]
                landed(ref, base + 16 + 8 * n + i)
                hop(ref, ref, base + 32 + 8 * n + k, base + 32 + 8 * n + i, other_core)
            _, i = along(2 - k, "y")
            for n, part in enumerate(parts_b):
                ref = gb.at[(c, i) + part]
                landed(ref, base + 20 + 8 * n + i)
                hop(ref, ref, base + 36 + 8 * n + k, base + 36 + 8 * n + i, other_core)

    def gather_end(parts_a, parts_b, ga, gb, base):
        for i in range(4):
            for n, part in enumerate(parts_a):
                landed(ga.at[(1 - c, i) + part], base + 32 + 8 * n + i)
            for n, part in enumerate(parts_b):
                landed(gb.at[(1 - c, i) + part], base + 36 + 8 * n + i)

    whole2 = ((slice(None), slice(None)),)
    near2[...] = nb[64:96].astype(bf16)
    gather_near(near2, fa2, fb2, 16, 0)

    for device, zi, ci in column_peers(p):
        e = 2 * zi + ci
        arrived(rz.at[e], 42 + e)
    for _, e in xc_peers():
        arrived(rz4.at[e], 58 + e)
    for half in range(2):
        lanes = slice(384 * half, 384 * half + 384)
        v = summed(rz, half)
        grad[0:32, lanes] = v[0:32]
        grad[32:40, lanes] = summed(rz4, half)[0:8]
    turned = dot(grad[0:40, 0:C0].astype(bf16), bb1[...])
    for t in range(5):
        first_new, second_new, direction = adam_block(f1[t], q1[t], turned[8 * t : 8 * t + 6])
        nf1[t] = first_new
        nq1[t] = second_new
        dd[8 * t : 8 * t + 6, 0:C0] = direction
    update = dot(dd[0:40, 0:C0].astype(bf16), bb1[...], nt)
    row_of = (0, 8, 16, 32, 40)
    for t in range(5):
        master_new, average_new = master_block(m1[t], update[8 * t : 8 * t + 6], 0.02, a1[t])
        nm1[t] = master_new
        na1[t] = average_new
        nb[row_of[t] : row_of[t] + 6, 0:C0] = master_new
        if t == 2:
            nb[48:54, 0:C0] = master_new
    for cp in stores[0:4]:
        cp.start()
    near1[...] = nb[0:64].astype(bf16)
    gather_near(near1, fa1, fb1, 32, 48)
    send_slopes(1)
    kept2 = gather_far(fa2, fb2, pack2[...], pa2, pb2_, whole2, whole2, ga2, gb2, 0)
    sixth = all6.end()
    stats[0:2] = sixth
    stats[5:6] = mean1
    stats[6:7] = rs1
    stats[7:8] = rs1 * gain1
    stats[8:10] = sixth * inv_n1
    stats[10:16] = jnp.zeros((6, PAD), f32)
    taps2 = (pl.ds(0, 96), slice(None))
    parts_a = (taps2, (pl.ds(96, 48), pl.ds(0, 384)))
    parts_b = (taps2, (pl.ds(96, 48), pl.ds(384, 384)))
    kept1 = gather_far(fa1, fb1, pack1[...], pa1, pb1_, parts_a, parts_b, ga1, gb1, 48)
    gather_over(whole2, whole2, ga2, gb2, 0)
    gather_over(parts_a, parts_b, ga1, gb1, 48)
    gather_end(whole2, whole2, ga2, gb2, 0)
    gather_end(parts_a, parts_b, ga1, gb1, 48)
    for cp in kept1 + kept2 + stores:
        cp.wait()

    for t in range(5):
        to_core(t).wait_send()
    for cp in flying:
        cp.wait_send()
    for half in range(2):
        for par in range(2):
            for k in range(2):

                def slope_sent(half=half, par=par, k=k):
                    slope_copy(half, par, k).wait_send()

                pl.when(jnp.logical_not(to_self(half)))(slope_sent)
    for j in range(2):

        def out_here(j=j):
            rows = out.at[pl.ds(512 * j, 512), :]
            remote(rows, rows, ss.at[0], rs.at[23 + j], other_core).wait_recv()

        pl.when(jnp.logical_not(is_self & (c == j)))(out_here)
    for j in range(2):
        for par in range(2):
            for k in range(2):
                part = sl_home.at[j, par, pl.ds(256 * k, 256), :]
                remote(part, part, ss.at[0], rs.at[25 + 4 * j + 2 * par + k], other_core).wait_recv()


VMEM = pl.BlockSpec(memory_space=pltpu.VMEM)
ANY = pl.BlockSpec(memory_space=pl.ANY)


def run_step(xt, offsets, owners, cot, w1, w2, wp, params, bases, states, consts):
    shape = jax.ShapeDtypeStruct
    dma = pltpu.SemaphoreType.DMA
    scratch = [pltpu.VMEM(a.shape, f32) for a in states] * 2
    scratch += [
        pltpu.VMEM((5, 4, 4, 48, PAD), bf16),
        pltpu.VMEM((4, 4, 96, C1), bf16),
        pltpu.VMEM((2, HALF0, LANES), bf16),
        pltpu.VMEM((2, 576, PAD), bf16),
        pltpu.VMEM((6, WIN, PAD), bf16),
        pltpu.VMEM((5, C0, C1), bf16),
        pltpu.VMEM((3, H, C1), bf16),
        pltpu.VMEM((H, C1), bf16),
        pltpu.VMEM((WIN, C1), f32),
        pltpu.VMEM((WIN, C1), f32),
        pltpu.VMEM((WIN, C1), bf16),
        pltpu.VMEM((WIN, H), f32),
        pltpu.VMEM((WIN, H), f32),
        pltpu.VMEM((WIN, H), bf16),
        pltpu.VMEM((3, WIN, H), bf16),
        pltpu.VMEM((WIN, C1), f32),
        pltpu.VMEM((6, WIN, C1), bf16),
        pltpu.VMEM((2, OWN, C1), bf16),
        pltpu.VMEM((256, PAD), f32),
        pltpu.VMEM((8, PAD), f32),
        pltpu.VMEM((8, 128), f32),
        pltpu.VMEM((8, 128), f32),
        pltpu.VMEM((8, PAD), f32),
        pltpu.VMEM((2, 128, PAD), f32),
        pltpu.VMEM((2, OWN, PAD), bf16),
        pltpu.VMEM((5, 4, 4, 48, 384), bf16),
        pltpu.VMEM((4, 4, 96, 384), bf16),
        pltpu.VMEM((5, 3, 4, 48, 384), bf16),
        pltpu.VMEM((5, 3, 48, 384), bf16),
        pltpu.VMEM((3, 4, 96, 384), bf16),
        pltpu.VMEM((3, 96, 384), bf16),
        pltpu.VMEM((5, 4, 48, 384), bf16),
        pltpu.VMEM((4, 96, 384), bf16),
        pltpu.VMEM((5, 48, 384), bf16),
        pltpu.VMEM((8, 48, 384), bf16),
        pltpu.VMEM((8, 48, 384), bf16),
        pltpu.VMEM((8, 32, 384), bf16),
        pltpu.VMEM((8, 32, 384), bf16),
        pltpu.VMEM((8, 16, 384), bf16),
        pltpu.VMEM((8, 16, 384), bf16),
        pltpu.VMEM((C0, C0), f32),
        pltpu.VMEM((C0, C0), bf16),
        pltpu.VMEM((80, PAD), f32),
        pltpu.VMEM((72, PAD), f32),
        pltpu.VMEM((96, PAD), f32),
        pltpu.VMEM((64, PAD), bf16),
        pltpu.VMEM((32, PAD), bf16),
        pltpu.VMEM((8, 32, PAD), bf16),
        pltpu.VMEM((8, 32, PAD), bf16),
        pltpu.VMEM((8, 16, PAD), bf16),
        pltpu.VMEM((8, 16, PAD), bf16),
        pltpu.VMEM((144, PAD), bf16),
        pltpu.VMEM((144, PAD), bf16),
        pltpu.VMEM((48, PAD), bf16),
        pltpu.VMEM((48, PAD), bf16),
        pltpu.VMEM((2, 8, PAD), f32),
        pltpu.VMEM((6, 8, 2, PAD), f32),
        pltpu.VMEM((6, 16, 2, PAD), f32),
        dma((44,)),
        dma((44,)),
        dma((10,)),
        dma((6, 8)),
        dma((6, 8)),
        dma((6, 16)),
        dma((6, 16)),
        dma((68,)),
        dma((68,)),
        dma((96,)),
        dma((96,)),
        dma((12,)),
        dma((24,)),
        dma((16,)),
        dma((16,)),
    ]
    one = shape((2, 4, 144, PAD), bf16)
    two = shape((2, 4, 48, PAD), bf16)
    return pl.pallas_call(
        step_kernel,
        out_shape=(
            shape((BINS, 384), bf16),
            shape((2, 2, OWN, 384), bf16),
            shape((16, PAD), f32),
            one,
            one,
            two,
            two,
            *[shape(a.shape, f32) for a in states],
        ),
        in_specs=[VMEM, VMEM, VMEM, ANY, ANY, ANY, ANY] + [VMEM] * 17 + [ANY] * 15,
        out_specs=(ANY, ANY, VMEM, *[ANY] * 16),
        scratch_shapes=scratch,
        compiler_params=pltpu.CompilerParams(
            collective_id=0, has_side_effects=True, vmem_limit_bytes=63 * 2**20
        ),
    )(
        xt, offsets, owners, cot, w1, w2, wp, *params,
        *[consts[n] for n in ("e1", "bw1", "e2", "bw2", "e4", "bw4", "rep1", "rep2", "rep4", "pack1", "pack2")],
        *bases, *states,
    )


def norm_block(gradient, parameters, moments):
    first_new, second_new, direction = adam_block(moments[0], moments[1], gradient)
    return parameters - norm_rate * direction, first_new, second_new


def finish_kernel(
    xt_in, offsets, owners, slopes_in, stats, ga1, gb1, ga2, gb2, out_in, *rest,
):
    p = Place()
    zl = p.zl
    params = rest[0:6]
    moments = rest[6:9]
    rep_a, rep_b, at_a, at_b, rep2a, rep2b, at2a, at2b = rest[9:17]
    states_in = rest[17:29]
    out, gin, v1, v1f, v1s, v2, v2f, v2s, v3, v3f, v3s, cp1, cp2, cp3 = rest[29:43]
    states_out = rest[43:55]
    gav, gbv, gav2, gbv2, held, tr, xt, slopes, outv, cp1v, cp2v, cp3v, *held_states, ls, ns = rest[55:]
    third_a = (slice(None), slice(None), pl.ds(96, 48), pl.ds(0, 384))
    third_b = (slice(None), slice(None), pl.ds(96, 48), pl.ds(384, 384))
    taps2 = (slice(None), slice(None), pl.ds(0, 96))
    copies = [
        pltpu.make_async_copy(ga1.at[taps2], gav.at[taps2], ls.at[0]),
        pltpu.make_async_copy(gb1.at[taps2], gbv.at[taps2], ls.at[1]),
        pltpu.make_async_copy(ga1.at[third_a], gav.at[third_a], ls.at[4]),
        pltpu.make_async_copy(gb1.at[third_b], gbv.at[third_b], ls.at[5]),
        pltpu.make_async_copy(ga2, gav2, ls.at[6]),
        pltpu.make_async_copy(gb2, gbv2, ls.at[7]),
    ]
    first = [
        pltpu.make_async_copy(xt_in, xt, ls.at[8]),
        pltpu.make_async_copy(slopes_in.at[0], slopes.at[0], ls.at[9]),
        pltpu.make_async_copy(slopes_in.at[1], slopes.at[1], ls.at[10]),
    ]
    passed_in = [(out_in, outv)] + list(zip(states_in, held_states))
    passed_out = [(outv, out)] + list(zip(held_states, states_out))
    ins = [pltpu.make_async_copy(a, b, ns.at[k]) for k, (a, b) in enumerate(passed_in)]
    outs_ = [pltpu.make_async_copy(a, b, ns.at[13 + k]) for k, (a, b) in enumerate(passed_out)]
    for cp in first + copies + ins:
        cp.start()

    vec = stats[...]
    v326 = jnp.where(zl == 0, vec, pltpu.roll(vec, PAD - HALF0, 1))
    tr[0:16, :] = v326[:, 0:384]
    tr[16:128, :] = jnp.zeros((112, 384), f32)
    cols = jnp.transpose(tr[...])
    mean_c = cols[0:HALF0, 5:6]
    rs_c = cols[0:HALF0, 6:7]
    scale_c = cols[0:HALF0, 7:8]
    gm_c = cols[0:HALF0, 8:9]
    bm_c = cols[0:HALF0, 9:10]
    off_home = offsets[...].astype(f32)
    tn = ((0,), (0,))
    rowq = iota((128, 256), 0)
    laneq = iota((128, 256), 1)
    put_even = (laneq == 2 * rowq).astype(bf16)
    put_odd = (laneq == 2 * rowq + 1).astype(bf16)
    grads1 = v326[0:2, 0:HALF0]
    v384 = jnp.where(zl == 0, vec, pltpu.roll(vec, PAD - HALF1, 1))
    grads2 = v384[2:4, 0:HALF1]
    v192 = jnp.where(zl == 0, vec, pltpu.roll(vec, PAD - HALFH, 1))
    halves = [(grads1[0:1], grads1[1:2]), (grads2[0:1], grads2[1:2]), (v192[4:5, 0:HALFH], v192[4:5, H : H + HALFH])]
    outs = [(v1, v1f, v1s), (v2, v2f, v2s), (v3, v3f, v3s)]
    for n in range(3):
        for r in range(2):
            old = (moments[n][0, r : r + 1, :], moments[n][1, r : r + 1, :])
            new = norm_block(halves[n][r], params[2 * n + r][...].reshape(1, -1), old)
            for q in range(3):
                outs[n][q][r : r + 1, :] = new[q]

    own_row = jnp.broadcast_to(owners[...].astype(f32), (8, 64))

    def column(rep, at, width):
        own = jnp.sum(rep[...].astype(f32) * own_row[0:1], axis=1, keepdims=True)
        return own * float(width) + at[...]

    lane = iota((384, 384), 1).astype(f32)
    place_a = (lane == column(rep_a, at_a, 6)).astype(bf16)
    place_b = (lane == column(rep_b, at_b, 6)).astype(bf16)
    own8 = own_row.astype(bf16)
    place2a = (iota((H, H), 0).astype(f32) == (dot(own8, rep2a[...])[0:1] * 3.0 + at2a[...])).astype(bf16)
    place2b = (iota((H, H), 0).astype(f32) == (dot(own8, rep2b[...])[0:1] * 3.0 + at2b[...])).astype(bf16)
    back = []
    first[0].wait()
    for j in range(2):
        first[1 + j].wait()
        for k in range(4):
            bins = pl.ds(128 * k, 128)
            st = dot(slopes[j, 0, bins, :], put_even, tn) + dot(slopes[j, 1, bins, :], put_odd, tn)
            lanes = pl.ds(1024 * j + 256 * k, 256)
            xf = xt[:, lanes].astype(f32)
            scaled = (xf - mean_c) * rs_c
            ok = ((iota((1, 256), 1) + (1024 * j + 256 * k)).astype(f32) >= 2.0 * off_home).astype(f32)
            held[:, lanes] = ok * (scale_c * (st[0:HALF0] - bm_c - scaled * gm_c))
        half = pl.ds(1024 * j, 1024)
        back.append(pltpu.make_async_copy(held.at[:, half], gin.at[:, 0, half], ls.at[2 + j]))
        back[j].start()
    for cp, on in zip(ins, outs_):
        cp.wait()
        on.start()

    for cp in copies:
        cp.wait()

    def give(held_ref, result, sem):
        cp = pltpu.make_async_copy(held_ref, result, ls.at[sem])
        cp.start()
        back.append(cp)

    for t in range(2):
        block = gav[:, :, 48 * t : 48 * t + 48, :].reshape(384, PAD)
        cp1v[t] = dot(block[:, 0:C0], place_a, tn).astype(bf16)
        give(cp1v.at[t], cp1.at[t], 11 + 2 * t)
        block = gbv[:, :, 48 * t : 48 * t + 48, :].reshape(384, PAD)
        cp1v[3 + t] = dot(block[:, 0:C0], place_b, tn).astype(bf16)
        give(cp1v.at[3 + t], cp1.at[3 + t], 12 + 2 * t)
    cp1v[2, 0:384] = dot(gav[:, :, 96:144, 0:384].reshape(384, 384), place_a, tn).astype(bf16)
    cp1v[2, 384:C0] = dot(gbv[:, :, 96:144, 384:C0].reshape(384, C0 - 384), place_b, tn).astype(bf16)
    give(cp1v.at[2], cp1.at[2], 15)
    two = dot(place2a, gav2[...].reshape(384, PAD)).astype(bf16)
    cp3v[...] = two[0:HALFH]
    cp2v[0] = two[HALFH:H]
    two = dot(place2b, gbv2[...].reshape(384, PAD)).astype(bf16)
    cp2v[1] = two[0:HALFH]
    cp2v[2] = two[HALFH:H]
    give(cp3v, cp3, 16)
    give(cp2v, cp2, 17)
    back.extend(outs_)
    for cp in back:
        cp.wait()


def run_finish(xt, offsets, owners, slopes, stats, gathered, out, params, moments, states, consts):
    shape = jax.ShapeDtypeStruct
    vec = [shape((2, n), f32) for n in (HALF0,) * 3 + (HALF1,) * 3 + (HALFH,) * 3]
    names = ("rep_a", "rep_b", "at_a", "at_b", "rep2a", "rep2b", "at2a", "at2b")
    return pl.pallas_call(
        finish_kernel,
        out_shape=(
            shape((BINS, 384), bf16),
            shape((HALF0, 1, 2 * BINS), f32),
            *vec,
            shape((5, C0, 384), bf16),
            shape((3, HALFH, C1), bf16),
            shape((HALFH, C1), bf16),
            *[shape(a.shape, f32) for a in states],
        ),
        in_specs=[ANY, VMEM, VMEM, ANY, VMEM] + [ANY] * 5 + [VMEM] * 17 + [ANY] * 12,
        out_specs=(ANY, ANY, *[VMEM] * 9, *[ANY] * 15),
        scratch_shapes=[
            pltpu.VMEM((2, 4, 144, PAD), bf16),
            pltpu.VMEM((2, 4, 144, PAD), bf16),
            pltpu.VMEM((2, 4, 48, PAD), bf16),
            pltpu.VMEM((2, 4, 48, PAD), bf16),
            pltpu.VMEM((HALF0, 2 * BINS), f32),
            pltpu.VMEM((128, 384), f32),
            pltpu.VMEM((HALF0, 2 * BINS), bf16),
            pltpu.VMEM((2, 2, OWN, 384), bf16),
            pltpu.VMEM((BINS, 384), bf16),
            pltpu.VMEM((5, C0, 384), bf16),
            pltpu.VMEM((3, HALFH, C1), bf16),
            pltpu.VMEM((HALFH, C1), bf16),
            *[pltpu.VMEM(a.shape, f32) for a in states],
            pltpu.SemaphoreType.DMA((20,)),
            pltpu.SemaphoreType.DMA((26,)),
        ],
        compiler_params=pltpu.CompilerParams(vmem_limit_bytes=63 * 2**20),
    )(
        xt, offsets, owners, slopes, stats, *gathered, out, *params, *moments,
        *[consts[n] for n in names], *states,
    )


def make_consts():
    e1 = np.zeros((64, 768), np.float32)
    bw1 = np.zeros((8, 768), np.float32)
    e2 = np.zeros((64, 384), np.float32)
    bw2 = np.zeros((8, 384), np.float32)
    e4 = np.zeros((64, 768), np.float32)
    bw4 = np.zeros((8, 768), np.float32)
    for s in range(64):
        g, zh, c = s // 4, (s // 2) % 2, s % 2
        for b in range(2):
            e = (2 * zh + b) * 2 + c
            for w in range(6):
                e1[s, (g * 8 + e) * 6 + w] = 1
                bw1[:, (g * 8 + e) * 6 + w] = b * 384 + w
            block = ((2 * zh + b) * 4 + g % 4) * 8 + (g // 4) * 2 + c
            for w in range(6):
                e4[s, block * 6 + w] = 1
                bw4[:, block * 6 + w] = b * 384 + w
            for w in range(3):
                e2[s, block * 3 + w] = 1
                bw2[:, block * 3 + w] = b * 192 + w
    rep1 = np.zeros((8 * 48, 192), np.float32)
    rep4 = np.zeros((8 * 16, 48), np.float32)
    rep2 = np.zeros((8 * 32, 96), np.float32)
    for e in range(8):
        for w in range(6):
            rep4[e * 16 + w, e * 6 + w] = 1
            for t in range(4):
                rep1[e * 48 + t * 8 + w, t * 48 + e * 6 + w] = 1
        for m in range(4):
            for w in range(3):
                rep2[e * 32 + m * 8 + w, m * 24 + e * 3 + w] = 1
    pack1 = np.zeros((144, 256), np.float32)
    pack2 = np.zeros((48, 128), np.float32)
    for o in range(8):
        for w in range(6):
            for t in range(3):
                pack1[t * 48 + o * 6 + w, o * 32 + 8 * t + w] = 1
        for w in range(3):
            for m in range(2):
                pack2[m * 24 + o * 3 + w, o * 16 + 4 * m + w] = 1
    rep_a = np.zeros((384, 64), np.float32)
    rep_b = np.zeros((384, 64), np.float32)
    at_a = np.zeros((384, 1), np.float32)
    rep2a = np.zeros((64, 384), np.float32)
    rep2b = np.zeros((64, 384), np.float32)
    at2 = np.zeros((1, 384), np.float32)
    for c in range(2):
        for i in range(4):
            for o in range(8):
                j, zh = o // 2, o % 2
                s_a = ((i * 4 + j) * 2 + zh) * 2 + c
                s_b = ((j * 4 + i) * 2 + zh) * 2 + c
                for w in range(6):
                    r = (c * 4 + i) * 48 + o * 6 + w
                    rep_a[r, s_a] = 1
                    rep_b[r, s_b] = 1
                    at_a[r, 0] = w
                for m in range(2):
                    for w in range(3):
                        r = (c * 4 + i) * 48 + m * 24 + o * 3 + w
                        rep2a[s_a, r] = 1
                        rep2b[s_b, r] = 1
                        at2[0, r] = m * 192 + w
    low = lambda a: jnp.asarray(a, bf16)
    return {
        "e1": low(e1), "bw1": jnp.asarray(bw1), "e2": low(e2), "bw2": jnp.asarray(bw2),
        "e4": low(e4), "bw4": jnp.asarray(bw4),
        "rep1": low(rep1), "rep2": low(rep2), "rep4": low(rep4), "pack1": low(pack1), "pack2": low(pack2),
        "rep_a": low(rep_a), "rep_b": low(rep_b), "at_a": jnp.asarray(at_a), "at_b": jnp.asarray(at_a),
        "rep2a": low(rep2a), "rep2b": low(rep2b), "at2a": jnp.asarray(at2), "at2b": jnp.asarray(at2),
    }


def local(
    inputs, offsets, owners, cotangent,
    norm1_gain, norm1_bias, norm1_moments,
    norm2_gain, norm2_bias, norm2_moments,
    norm3_gain, norm3_bias, norm3_moments,
    conv1_copy, conv1_master, conv1_first, conv1_second, conv1_average, basis1,
    conv2_copy, conv2_master, conv2_first, conv2_second, conv2_average, basis2,
    project_copy, project_master, project_first, project_second, project_average, basis3,
):
    consts = make_consts()
    flip2 = lambda a: jnp.swapaxes(a, -1, -2)
    xt = flip2(inputs[0])
    offsets = offsets[None]
    owners = owners[None]
    params = [norm1_gain, norm1_bias, norm2_gain, norm2_bias, norm3_gain, norm3_bias]
    states = [
        conv1_master, conv1_first, conv1_second, conv1_average,
        conv2_master, conv2_first, conv2_second, conv2_average,
        project_master, project_first, project_second, project_average,
    ]
    out, slopes, stats, *more = run_step(
        xt, offsets, owners, cotangent[0], conv1_copy, flip2(conv2_copy), flip2(project_copy), params,
        (basis1, basis2, basis3), [flip2(a) for a in states], consts,
    )
    gathered, new = more[0:4], more[4:]
    result = run_finish(
        xt, offsets, owners, slopes, stats, gathered, out, params,
        (norm1_moments, norm2_moments, norm3_moments), new, consts,
    )
    out, gin, *vec = result[0:11]
    cp1, cp2, cp3 = result[11:14]
    nm1, nf1, nq1, na1, nm2, nf2, nq2, na2, nm3, nf3, nq3, na3 = [flip2(a) for a in result[14:]]
    return (
        out[None], jnp.transpose(gin, (1, 2, 0)), *vec,
        nm1, cp1, nf1, nq1, na1,
        nm2, flip2(cp2), nf2, nq2, na2,
        nm3, flip2(cp3), nf3, nq3, na3,
    )


def solution(mesh):
    finer = Mesh(mesh.devices.reshape(4, 4, 2, 2, mesh.shape["ch"]), SEQ_CH)
    owner3 = P(None, None, SEQ_CH)
    owner2 = P(None, SEQ_CH)
    half3 = P(None, None, "ch")
    in_specs = (
        P(SEQ, None, "ch"), P(SEQ), P(), P(SEQ, None, "ch"),
        P("ch"), P("ch"), half3, P("ch"), P("ch"), half3, P("ch"), P("ch"), half3,
        half3, owner3, owner3, owner3, owner3, P(),
        half3, owner3, owner3, owner3, owner3, P(),
        P(None, "ch"), owner2, owner2, owner2, owner2, P(),
    )
    vec = P(None, "ch")
    out_specs = (
        P(SEQ, None, "ch"), P(SEQ, None, "ch"), *[vec] * 9,
        owner3, half3, owner3, owner3, owner3,
        owner3, half3, owner3, owner3, owner3,
        owner2, vec, owner2, owner2, owner2,
    )
    return jax.shard_map(local, mesh=finer, in_specs=in_specs, out_specs=out_specs, check_vma=False)
```
